32 devices in a mesh: dom: 8 (over z, y), rel: 4 (over x, core).
Axes of the slice: x: 2, y: 2, z: 4, core: 2. Of those that a mesh axis runs over, the one named last changes fastest.
Arguments:
- partitions: bfloat16 [4096, 400], P('dom'), may hold values from -1.5 to 1.5
- remainder: bfloat16 [256, 400], replicated, may hold values from -1.5 to 1.5
- relations: float32 [2560, 400], replicated, may hold values from -4 to 4
- counts: int32 [8, 8, 4], P('dom', None, 'rel'), may hold values from 0 to 1, as said below
- lhs_rows: int32 [8, 8, 4, 128], P('dom', None, 'rel'), may hold values from 0 to 511
- lhs_rems: int32 [8, 8, 4, 128], P('dom', None, 'rel'), may hold values from 0 to 255
- rel_ids: int32 [8, 8, 4, 128], P('dom', None, 'rel'), may hold values from 0 to 2559
- rhs_rows: int32 [8, 8, 4, 128], P('dom', None, 'rel'), may hold values from 0 to 511
- rhs_rems: int32 [8, 8, 4, 128], P('dom', None, 'rel'), may hold values from 0 to 255
- neg_rows: int32 [8, 8, 4, 128], P('dom', None, 'rel'), may hold values from 0 to 511
- neg_rems: int32 [8, 8, 4, 128], P('dom', None, 'rel'), may hold values from 0 to 255
Outputs:
- grad_partitions: float32 [4096, 400], P('dom')
- grad_remainder: float32 [256, 400], replicated
- grad_relations: float32 [2560, 400], replicated
The draws below stay inside these ranges and needn't reach their ends.
Inputs may be any that keep to these rules, and one draw needn't show every extreme that they name: In every bucket (p, t) some device j of rel has counts[p, t, j] = 1.
All inputs are finite; a program needn't handle non-finite values.
Results may differ from the reference program's by a relative error of at most 0.009.
Values may be sent and summed in bfloat16 or wider, within the bound.
No kernel may reach another device: no remote copies, remote signals or barrier semaphores. Data moves between devices by JAX's collectives and lax.ppermute only.
A program may use at most 128 MiB of HBM per device.

```python
import jax
import jax.numpy as jnp
from jax import lax

D = 400
NRELS = 2560
REM = 256
PROWS = 512
BLOCK = 128
NUNI = 128
MAXB = 1
STOPS = 8
SLOTS = 4
ENT = 4096


def draw_counts(key, part):
    first_key, second_key = jax.random.split(jax.random.fold_in(key, 11))
    sharers = SLOTS // MAXB
    base = jax.random.randint(first_key, (STOPS, STOPS, sharers), 0, MAXB + 1)
    fullest = jax.random.randint(second_key, (STOPS, STOPS, 1), 0, sharers)
    chosen = fullest == lax.broadcasted_iota(jnp.int32, (STOPS, STOPS, sharers), 2)
    return jnp.where(chosen, MAXB, base).astype(jnp.int32)


def with_ends(result, stream_key, low, high):
    extent = result.shape
    index_at = [jax.random.randint(jax.random.fold_in(stream_key, axis), (), 0, extent[axis]) for axis in range(len(extent))]
    result = result.at[tuple(index_at)].set(low)
    longest = extent.index(max(extent))
    index_at[longest] = (index_at[longest] + 1) % extent[longest]
    return result.at[tuple(index_at)].set(high)


def block_levels(own_key, shape, cuts, smallest, top_value):
    loudness = 1.0
    for position, shards_of in cuts:
        steps = jax.random.uniform(jax.random.fold_in(jax.random.fold_in(own_key, 6), position), (shards_of,), jnp.float32, smallest / len(cuts), top_value / len(cuts))
        loudness = loudness * jnp.repeat(jnp.exp(steps), shape[position] // shards_of).reshape((-1,) + (1,) * (len(shape) - 1 - position))
    return loudness


def centred(key, extent, scale, reach, cuts=(), kind=jnp.bfloat16):
    array = scale * jax.random.normal(key, extent, jnp.float32)
    if cuts:
        array = array * block_levels(key, extent, cuts, -0.22, 0.18)
    return jnp.clip(array, -reach, reach).astype(kind)


def setup_inputs(seed: int = 0) -> dict:
    streams_of = jax.random.split(jax.random.key(seed), 12)
    return {
        "partitions": centred(streams_of[0], (ENT, D), 0.25, 1.5, ((0, 8),)),
        "remainder": centred(streams_of[1], (REM, D), 0.25, 1.5),
        "relations": centred(streams_of[2], (NRELS, D), 1.0, 4.0, (), jnp.float32),
        "counts": draw_counts(jax.random.fold_in(streams_of[11], 71), 0),
        "lhs_rows": with_ends(jax.random.randint(streams_of[4], (STOPS, STOPS, SLOTS, BLOCK), 0, PROWS), jax.random.fold_in(streams_of[4], 1), 0, PROWS - 1).astype(jnp.int32),
        "lhs_rems": with_ends(jax.random.randint(streams_of[5], (STOPS, STOPS, SLOTS, BLOCK), 0, REM), jax.random.fold_in(streams_of[5], 1), 0, REM - 1).astype(jnp.int32),
        "rel_ids": with_ends(jax.random.randint(streams_of[6], (STOPS, STOPS, SLOTS, BLOCK), 0, NRELS), jax.random.fold_in(streams_of[6], 1), 0, NRELS - 1).astype(jnp.int32),
        "rhs_rows": with_ends(jax.random.randint(streams_of[7], (STOPS, STOPS, SLOTS, BLOCK), 0, PROWS), jax.random.fold_in(streams_of[7], 1), 0, PROWS - 1).astype(jnp.int32),
        "rhs_rems": with_ends(jax.random.randint(streams_of[8], (STOPS, STOPS, SLOTS, BLOCK), 0, REM), jax.random.fold_in(streams_of[8], 1), 0, REM - 1).astype(jnp.int32),
        "neg_rows": with_ends(jax.random.randint(streams_of[9], (STOPS, STOPS, SLOTS, NUNI), 0, PROWS), jax.random.fold_in(streams_of[9], 1), 0, PROWS - 1).astype(jnp.int32),
        "neg_rems": with_ends(jax.random.randint(streams_of[10], (STOPS, STOPS, SLOTS, NUNI), 0, REM), jax.random.fold_in(streams_of[10], 1), 0, REM - 1).astype(jnp.int32),
    }


def complex_product(left, right):
    half = left.shape[-1] // 2
    left_re, left_im = left[..., :half], left[..., half:]
    right_re, right_im = right[..., :half], right[..., half:]
    return jnp.concatenate([left_re * right_re - left_im * right_im, left_re * right_im + left_im * right_re], -1)


def conjugate_product(grad, other):
    half = grad.shape[-1] // 2
    grad_re, grad_im = grad[..., :half], grad[..., half:]
    other_re, other_im = other[..., :half], other[..., half:]
    return jnp.concatenate([grad_re * other_re + grad_im * other_im, grad_im * other_re - grad_re * other_im], -1)


def edge_terms(lhs, rel_vec, cand, width):
    high = lax.Precision.HIGHEST
    total = cand.shape[0]
    u_vec = complex_product(lhs, rel_vec)
    rhs = cand[:width]
    positive = jnp.sum(u_vec * rhs, -1)
    negative = lax.dot_general(u_vec, cand, (((1,), (1,)), ((), ())), precision=high, preferred_element_type=jnp.float32)
    keep = 1.0 - jnp.eye(width, total, dtype=jnp.float32)
    grad_pos = -jax.nn.sigmoid(-positive)
    grad_neg = jax.nn.sigmoid(negative) * keep / total
    grad_u = grad_pos[:, None] * rhs + jnp.dot(grad_neg, cand, precision=high, preferred_element_type=jnp.float32)
    extra = jnp.concatenate([grad_pos[:, None] * u_vec, jnp.zeros((total - width, u_vec.shape[1]), jnp.float32)], 0)
    grad_cand = lax.dot_general(grad_neg, u_vec, (((0,), (0,)), ((), ())), precision=high, preferred_element_type=jnp.float32) + extra
    grad_lhs = conjugate_product(grad_u, rel_vec)
    grad_rel = conjugate_product(grad_u, lhs)
    return grad_lhs, grad_rel, grad_cand


def flatten_rows(table):
    return table.reshape((-1, table.shape[-1]))


def reference(partitions, remainder, relations, counts, lhs_rows, lhs_rems, rel_ids, rhs_rows, rhs_rems, neg_rows, neg_rems):
    shape = (STOPS, STOPS, SLOTS)
    source = lax.broadcasted_iota(jnp.int32, shape, 0)
    stop = lax.broadcasted_iota(jnp.int32, shape, 1)
    slot = lax.broadcasted_iota(jnp.int32, shape, 2)
    target = (source - stop) % STOPS
    limit = counts[source, stop, slot // MAXB]
    live = ((slot % MAXB) < limit).astype(jnp.float32).reshape(-1)
    items = (source.reshape(-1), target.reshape(-1), live, flatten_rows(lhs_rows), flatten_rows(lhs_rems), flatten_rows(rel_ids), flatten_rows(rhs_rows), flatten_rows(rhs_rems), flatten_rows(neg_rows), flatten_rows(neg_rems))

    def step(carry, item):
        part_grad, rem_grad, rel_grad = carry
        src, dst, weight, lrow, lrem, rel, rrow, rrem, nrow, nrem = item
        lhs_index = (src * PROWS + lrow).astype(jnp.int32)
        cand_index = (dst * PROWS + jnp.concatenate([rrow, nrow])).astype(jnp.int32)
        cand_rem = jnp.concatenate([rrem, nrem]).astype(jnp.int32)
        lhs = partitions[lhs_index].astype(jnp.float32) + remainder[lrem].astype(jnp.float32)
        cand = partitions[cand_index].astype(jnp.float32) + remainder[cand_rem].astype(jnp.float32)
        grad_lhs, grad_rel, grad_cand = edge_terms(lhs, relations[rel], cand, BLOCK)
        part_grad = part_grad.at[lhs_index].add(weight * grad_lhs).at[cand_index].add(weight * grad_cand)
        rem_grad = rem_grad.at[lrem].add(weight * grad_lhs).at[cand_rem].add(weight * grad_cand)
        rel_grad = rel_grad.at[rel].add(weight * grad_rel)
        return (part_grad, rem_grad, rel_grad), None

    start = (jnp.zeros((ENT, D), jnp.float32), jnp.zeros((REM, D), jnp.float32), jnp.zeros((NRELS, D), jnp.float32))
    final, unused = lax.scan(step, start, items)
    return final[0], final[1], final[2]
```

```python
import functools

import jax
import jax.numpy as jnp
from jax import lax
from jax.experimental import pallas as pl
from jax.experimental.pallas import tpu as pltpu
from jax.sharding import PartitionSpec as P

F32 = jnp.float32
BF16 = jnp.bfloat16
LANES = 128
VMEM_LIMIT = 56 * 2**20
NT = (((1,), (1,)), ((), ()))
NN = (((1,), (0,)), ((), ()))
TN = (((0,), (0,)), ((), ()))


def params():
    return pltpu.CompilerParams(vmem_limit_bytes=VMEM_LIMIT)


def bits_of(count):
    return count.bit_length() - 1


def reverse_bits(value, count):
    out = 0
    for bit in range(bits_of(count)):
        out = out * 2 + ((value >> bit) & 1)
    return out


def split(value):
    high = value.astype(BF16)
    low = (value - high.astype(F32)).astype(BF16)
    return high, low


def dot(left, right, dims):
    return lax.dot_general(left, right, dims, preferred_element_type=F32)


def dot3(left, right, dims):
    left_high, left_low = split(left)
    right_high, right_low = split(right)
    return (
        dot(left_high, right_high, dims)
        + dot(left_high, right_low, dims)
        + dot(left_low, right_high, dims)
    )


def one_hot(ids, rows, base=0):
    place = lax.broadcasted_iota(jnp.int32, (rows, ids.shape[1]), 0)
    return jnp.where(place == ids - base, 1.0, 0.0).astype(BF16)


def store_split(ref, cols, value):
    high, low = split(value)
    depth = value.shape[0]
    ref[0:depth, cols] = high
    ref[depth : 2 * depth, cols] = low


def folded(value):
    depth = value.shape[0] // 2
    return value[:depth] + value[depth:]


def quantized(value):
    top = jnp.max(jnp.abs(value), axis=0, keepdims=True)
    exponent = jnp.floor(jnp.log2(jnp.maximum(top, 1e-30))) + 1.0
    scaled = jnp.round(value * jnp.exp2(15.0 - exponent))
    return jnp.clip(scaled, -32767.0, 32767.0), exponent


def to_words(value):
    return value.astype(jnp.int32).astype(jnp.int16)


def from_words(words):
    return words.astype(jnp.int32).astype(F32)


def pack_table(value):
    scaled, exponent = quantized(value)
    tail = jnp.broadcast_to(exponent, (16, value.shape[1]))
    return to_words(jnp.concatenate([scaled, tail], axis=0))


def unpack_table(words):
    depth = words.shape[0] - 16
    value = from_words(words)
    return value[:depth] * jnp.exp2(value[depth : depth + 1] - 15.0)


def pack_chunk(value):
    scaled, exponent = quantized(value)
    rows = value.shape[0]
    place = lax.broadcasted_iota(jnp.int32, value.shape, 0)
    return to_words(jnp.where(place >= rows - 8, exponent, scaled))


def unpack_chunk(words):
    value = from_words(words)
    rows = value.shape[0]
    place = lax.broadcasted_iota(jnp.int32, value.shape, 0)
    scale = jnp.exp2(value[rows - 1 : rows] - 15.0)
    return jnp.where(place >= rows - 8, 0.0, value * scale)


class Plan:
    def __init__(self, doms, rels, prows, width, rems, nrels, maxb):
        self.doms, self.rels, self.maxb = doms, rels, maxb
        self.devices = doms * rels
        self.prows, self.width, self.rems, self.nrels = prows, width, rems, nrels
        self.buckets = doms // rels
        self.slots = rels * maxb
        self.bucket_edges = self.slots * LANES
        self.edges = self.buckets * self.bucket_edges
        self.part_lanes = prows // rels
        self.half_rel, self.half_rem = nrels // 2, rems // 2
        self.half_lanes = self.half_rel + self.half_rem
        self.subs = width // 8
        self.units = (self.half_lanes // LANES) * self.subs
        self.half_chunks = self.devices // 2
        self.chunk_units = -(-self.units // self.half_chunks)
        self.chunk_rows = (self.chunk_units + 2) // 2 * 16
        rel_bits = bits_of(rels)
        all_bits = rel_bits + bits_of(doms)
        self.groups = [
            [0],
            list(range(1, rel_bits + 1)),
            list(range(rel_bits + 1, all_bits)),
        ]
        self.masks = [self.group_masks(bits) for bits in self.groups]
        order = [bit for group in self.groups for bit in reversed(group)]
        self.place = {bit: all_bits - 1 - at for at, bit in enumerate(order)}

    @staticmethod
    def group_masks(bits):
        masks = []
        for index in range(2 ** len(bits)):
            masks.append(sum(((index >> at) & 1) << bit for at, bit in enumerate(bits)))
        return masks

    def me(self):
        return lax.axis_index("dom") * self.rels + lax.axis_index("rel")

    def low_chunk(self, device):
        return device >> 1

    def position(self, chunk, me):
        relative = chunk ^ (me >> 1)
        out = 0
        for bit, at in self.place.items():
            if bit:
                out = out + (((relative >> (bit - 1)) & 1) << at)
        return out

    def bucket_mask(self, rel, bucket):
        return reverse_bits(rel, self.rels) * self.buckets + bucket

    def dynamic_mask(self, rel, bucket):
        out = 0
        width = bits_of(self.rels)
        for bit in range(width):
            out = out + (((rel >> bit) & 1) << (width - 1 - bit))
        return out * self.buckets + bucket


def send(value, plan, target):
    pairs = [(device, target(device)) for device in range(plan.devices)]
    return lax.ppermute(value, ("dom", "rel"), pairs)


def lists_kernel(plan, *refs):
    tables, counts, outs = refs[:7], refs[7], refs[8:]
    source = lax.axis_index("dom")
    rel = lax.axis_index("rel")
    for mask, out in enumerate(outs):
        for bucket in range(plan.buckets):
            target = source ^ plan.dynamic_mask(rel ^ mask, bucket)
            stop = lax.rem(source - target + plan.doms, plan.doms)
            for turn in range(plan.maxb):
                block = bucket * plan.maxb + turn
                for at, table in enumerate(tables):
                    out[block, at : at + 1, :] = table[0, stop, turn : turn + 1, :]
                live = jnp.where(turn < counts[stop], 1, 0)
                out[block, 7:8, :] = jnp.full((1, LANES), live, jnp.int32)


def prep_kernel(plan, *refs):
    labels = refs[: plan.rels]
    own, rem, relations, lhs_out, rel_out, u_out, rem_out, rel_split = refs[plan.rels :]
    depth, half = plan.width, plan.width // 2
    high, low = split(relations[...])
    rel_split[0:depth, :] = high
    rel_split[depth : 2 * depth, :] = low
    for bucket in range(plan.buckets):
        for pair in range(0, plan.slots, 2):
            blocks = [divmod(slot, plan.maxb) for slot in range(pair, min(pair + 2, plan.slots))]
            row = lambda at: jnp.concatenate(
                [
                    labels[mask][bucket * plan.maxb + turn, at : at + 1, :]
                    for mask, turn in blocks
                ],
                axis=1,
            )
            start = bucket * plan.bucket_edges + pair * LANES
            wide = len(blocks) * LANES
            cols = slice(start, start + wide)
            lhs = dot(own[...], one_hot(row(0), plan.prows), NN) + dot(
                rem[...], one_hot(row(1), plan.rems), NN
            )
            vec = folded(dot(rel_split[...], one_hot(row(2), plan.nrels), NN))
            lhs_out[:, cols] = lhs
            rel_out[:, cols] = vec
            u_out[0:half, cols] = lhs[:half] * vec[:half] - lhs[half:] * vec[half:]
            u_out[half:, cols] = lhs[:half] * vec[half:] + lhs[half:] * vec[:half]
            for at, (mask, turn) in enumerate(blocks):
                block = labels[mask]
                place = bucket * plan.maxb + turn
                ids = jnp.concatenate([block[place, 4:5, :], block[place, 6:7, :]], axis=1)
                begin = 2 * (start + at * LANES)
                rem_out[:, begin : begin + 2 * LANES] = dot(
                    rem[...], one_hot(ids, plan.rems), NN
                ).astype(BF16)


def conjugate_parts(grad, other):
    half = grad.shape[0] // 2
    grad_re, grad_im = grad[:half], grad[half:]
    other_re, other_im = other[:half], other[half:]
    return jnp.concatenate(
        [grad_re * other_re + grad_im * other_im, grad_im * other_re - grad_re * other_im], 0
    )


def bucket_kernel(plan, bucket, packed, *refs):
    labels = refs[: plan.rels]
    target, lhs_in, rel_in, u_in, rem_in = refs[plan.rels : plan.rels + 5]
    lhs_out, rel_out, cand_out, part_out = refs[plan.rels + 5 :]
    total = 2 * LANES
    blocks = [
        (labels[mask], bucket * plan.maxb + turn)
        for mask, turn in (divmod(slot, plan.maxb) for slot in range(plan.slots))
    ]
    edge = lax.broadcasted_iota(jnp.int32, (LANES, total), 0)
    column = lax.broadcasted_iota(jnp.int32, (LANES, total), 1)
    keep = jnp.where(edge == column, 0.0, 1.0 / total)
    cand_ids = [
        jnp.concatenate([label[at, 3:4, :], label[at, 5:6, :]], axis=1) for label, at in blocks
    ]
    for slot, (label, at) in enumerate(blocks):
        cols = slice(slot * LANES, (slot + 1) * LANES)
        wide = slice(slot * total, (slot + 1) * total)
        cand = dot(target[...], one_hot(cand_ids[slot], plan.prows), NN) + rem_in[
            :, wide
        ].astype(F32)
        rhs = cand[:, :LANES]
        u_vec = u_in[:, cols]
        live = label[at, 7:8, :].astype(F32)
        positive = jnp.sum(u_vec * rhs, axis=0, keepdims=True)
        negative = dot3(u_vec, cand, TN)
        grad_pos = -jax.nn.sigmoid(-positive) * live
        grad_neg = jax.nn.sigmoid(negative) * keep * live[0:1, 0:1]
        grad_u = grad_pos * rhs + dot3(cand, grad_neg, NT)
        from_neg = dot3(u_vec, grad_neg, NN)
        grad_cand = jnp.concatenate(
            [from_neg[:, :LANES] + grad_pos * u_vec, from_neg[:, LANES:]], axis=1
        )
        store_split(lhs_out, cols, conjugate_parts(grad_u, rel_in[:, cols]))
        store_split(rel_out, cols, conjugate_parts(grad_u, lhs_in[:, cols]))
        store_split(cand_out, wide, grad_cand)
    ids = jnp.concatenate(cand_ids, axis=1) ^ (lax.axis_index("rel") * plan.part_lanes)
    part = folded(dot(cand_out[...], one_hot(ids, plan.prows), NT))
    part_out[...] = pack_table(part) if packed else part


def reduce_kernel(plan, away, *refs):
    labels = refs[: plan.rels]
    grads = refs[plan.rels : plan.rels + 3 * plan.buckets]
    out, table = refs[plan.rels + 3 * plan.buckets :]
    me = plan.me()
    half = (me & 1) ^ (1 if away else 0)
    blocks = lambda bucket: [
        (labels[mask], bucket * plan.maxb + turn)
        for mask, turn in (divmod(slot, plan.maxb) for slot in range(plan.slots))
    ]
    row = lambda bucket, at: jnp.concatenate(
        [label[place, at : at + 1, :] for label, place in blocks(bucket)], axis=1
    )
    pairs = lambda bucket, first, second: jnp.concatenate(
        [
            label[place, at : at + 1, :]
            for label, place in blocks(bucket)
            for at in (first, second)
        ],
        axis=1,
    )
    depth = plan.width
    step = 2 * LANES if plan.half_rel % (2 * LANES) == 0 else LANES
    for start in range(0, plan.half_rel, step):
        total = 0.0
        for bucket in range(plan.buckets):
            hot = one_hot(row(bucket, 2), step, half * plan.half_rel + start)
            total = total + dot(grads[3 * bucket + 1][...], hot, NT)
        table[:, start : start + step] = folded(total)
    total = 0.0
    base = half * plan.half_rem
    for bucket in range(plan.buckets):
        hot = one_hot(row(bucket, 1), plan.half_rem, base)
        total = total + dot(grads[3 * bucket][...], hot, NT)
        hot = one_hot(pairs(bucket, 4, 6), plan.half_rem, base)
        total = total + dot(grads[3 * bucket + 2][...], hot, NT)
    table[:, plan.half_rel :] = folded(total)
    for chunk in range(plan.half_chunks):
        parts = []
        for unit in range(chunk * plan.chunk_units, (chunk + 1) * plan.chunk_units):
            if unit < plan.units:
                lane, sub = divmod(unit, plan.subs)
                parts.append(table[8 * sub : 8 * sub + 8, lane * LANES : (lane + 1) * LANES])
            else:
                parts.append(jnp.zeros((8, LANES), F32))
        spare = plan.chunk_rows - 8 * plan.chunk_units
        parts.append(jnp.zeros((spare, LANES), F32))
        value = jnp.concatenate(parts, axis=0)
        out[plan.position(chunk, me)] = pack_chunk(value) if away else value


def combine_kernel(group, last, *refs):
    keep, arrived = refs[0], refs[1:group]
    outs = refs[group:]
    count = keep.shape[0]
    share = count // len(outs)
    for at in range(count):
        value = keep[at]
        for ref in arrived:
            value = value + unpack_chunk(ref[at])
        which, place = divmod(at, share)
        outs[which][place] = pack_chunk(value) if (which or last) else value


def spread_kernel(plan, count, *refs):
    pieces, (rel_out, rem_out, held) = refs[:count], refs[count:]
    at = 0
    for piece in pieces:
        held[at : at + piece.shape[0]] = piece[...]
        at += piece.shape[0]
    me = plan.me()
    core = me & 1
    for half in range(2):
        first = (half ^ core) * plan.half_chunks
        for chunk in range(plan.half_chunks):
            value = unpack_chunk(held[first + plan.position(chunk, me)])
            for index in range(plan.chunk_units):
                unit = chunk * plan.chunk_units + index
                if unit >= plan.units:
                    break
                lane, sub = divmod(unit, plan.subs)
                lane = lane * LANES
                rows = slice(8 * sub, 8 * sub + 8)
                block = value[8 * index : 8 * index + 8]
                if lane < plan.half_rel:
                    lane += half * plan.half_rel
                    rel_out[rows, lane : lane + LANES] = block
                else:
                    lane += half * plan.half_rem - plan.half_rel
                    rem_out[rows, lane : lane + LANES] = block


def add_pack_kernel(*refs):
    value = refs[0][...]
    for ref in refs[1:-1]:
        value = value + unpack_table(ref[...])
    refs[-1][...] = pack_table(value)


def source_kernel(plan, *refs):
    labels = refs[: plan.rels]
    grads, out = refs[plan.rels : -1], refs[-1]
    shift = lax.axis_index("rel") * plan.part_lanes
    total = 0.0
    for bucket in range(plan.buckets):
        ids = jnp.concatenate(
            [
                labels[mask][bucket * plan.maxb + turn, 0:1, :]
                for mask, turn in (divmod(slot, plan.maxb) for slot in range(plan.slots))
            ],
            axis=1,
        )
        total = total + dot(grads[bucket][...], one_hot(ids ^ shift, plan.prows), NT)
    out[...] = folded(total)


def share_kernel(plan, table, arrived, keep, *outs):
    value = table[...] + unpack_table(arrived[...])
    lanes = plan.part_lanes
    keep[...] = value[:, :lanes]
    for at, out in enumerate(outs):
        out[...] = pack_table(value[:, (at + 1) * lanes : (at + 2) * lanes])


def part_out_kernel(plan, *refs):
    out = refs[-1]
    rel = lax.axis_index("rel")
    lanes = plan.part_lanes
    for mask, ref in enumerate(refs[:-1]):
        if lanes % LANES:
            out[:, mask * lanes : (mask + 1) * lanes] = unpack_table(ref[...])
        else:
            start = pl.multiple_of((rel ^ mask) * lanes, lanes)
            out[:, pl.ds(start, lanes)] = unpack_table(ref[...])


def shape(extent, kind):
    return jax.ShapeDtypeStruct(extent, kind)


def call(kernel, outs, args, scratch=(), in_specs=None, name=None):
    return pl.pallas_call(
        kernel,
        out_shape=outs,
        in_specs=in_specs or [pl.BlockSpec(memory_space=pltpu.VMEM)] * len(args),
        out_specs=[pl.BlockSpec(memory_space=pltpu.VMEM)] * len(outs),
        scratch_shapes=list(scratch),
        compiler_params=params(),
        name=name,
    )(*args)


def body(
    partitions,
    remainder,
    relations,
    counts,
    lhs_rows,
    lhs_rems,
    rel_ids,
    rhs_rows,
    rhs_rems,
    neg_rows,
    neg_rems,
):
    prows, width = partitions.shape
    plan = Plan(
        lax.axis_size("dom"),
        lax.axis_size("rel"),
        prows,
        width,
        remainder.shape[0],
        relations.shape[0],
        lhs_rows.shape[2],
    )
    vmem = pl.BlockSpec(memory_space=pltpu.VMEM)
    smem = pl.BlockSpec(memory_space=pltpu.SMEM)
    own, rem, rels = partitions.T, remainder.T, relations.T
    edges, lanes = plan.edges, plan.bucket_edges

    targets = [send(own, plan, lambda d: d ^ (plan.bucket_mask(d % plan.rels, 0) * plan.rels))]
    for bucket in range(1, plan.buckets):
        targets.append(send(targets[0], plan, lambda d, b=bucket: d ^ (b * plan.rels)))

    tables = [lhs_rows, lhs_rems, rel_ids, rhs_rows, rhs_rems, neg_rows, neg_rems]
    labels = call(
        functools.partial(lists_kernel, plan),
        [shape((plan.buckets * plan.maxb, 8, LANES), jnp.int32)] * plan.rels,
        tables + [counts.reshape(-1)],
        in_specs=[vmem] * 7 + [smem],
        name="lists",
    )
    labels = [labels[0]] + [
        send(labels[mask], plan, lambda d, m=mask: d ^ m) for mask in range(1, plan.rels)
    ]

    lhs, vec, u_vec, cand_rem = call(
        functools.partial(prep_kernel, plan),
        [
            shape((width, edges), F32),
            shape((width, edges), F32),
            shape((width, edges), F32),
            shape((width, 2 * edges), BF16),
        ],
        labels + [own, rem, rels],
        scratch=[pltpu.VMEM((2 * width, plan.nrels), BF16)],
        name="prep",
    )

    grads, parts = [], []
    for bucket in range(plan.buckets):
        packed = bucket > 0
        one = pl.BlockSpec((width, lanes), lambda i, b=bucket: (0, b))
        two = pl.BlockSpec((width, 2 * lanes), lambda i, b=bucket: (0, b))
        whole = lambda extent: pl.BlockSpec(extent, lambda i: (0,) * len(extent))
        outs = [
            shape((2 * width, lanes), BF16),
            shape((2 * width, lanes), BF16),
            shape((2 * width, 2 * lanes), BF16),
            shape((width + 16, prows), jnp.int16) if packed else shape((width, prows), F32),
        ]
        made = pl.pallas_call(
            functools.partial(bucket_kernel, plan, bucket, packed),
            grid=(1,),
            out_shape=outs,
            in_specs=[whole(label.shape) for label in labels]
            + [whole(own.shape), one, one, one, two],
            out_specs=[whole(out.shape) for out in outs],
            compiler_params=params(),
            name="bucket",
        )(*labels, targets[bucket], lhs, vec, u_vec, cand_rem)
        grads += made[:3]
        parts.append(made[3])

    chunk = (plan.half_chunks, plan.chunk_rows, LANES)
    half_args = labels + grads
    table = [pltpu.VMEM((width, plan.half_lanes), F32)]
    (away,) = call(
        functools.partial(reduce_kernel, plan, True),
        [shape(chunk, jnp.int16)],
        half_args,
        scratch=table,
        name="reduce_away",
    )
    arrived = [send(away, plan, lambda d: d ^ 1)]
    near = [
        send(parts[bucket], plan, lambda d, b=bucket: d ^ (b * plan.rels))
        for bucket in range(1, plan.buckets)
    ]
    (keep,) = call(
        functools.partial(reduce_kernel, plan, False),
        [shape(chunk, F32)],
        half_args,
        scratch=table,
        name="reduce_home",
    )
    (far,) = call(
        add_pack_kernel, [shape((width + 16, prows), jnp.int16)], [parts[0]] + near, name="far"
    )
    far = send(far, plan, lambda d: d ^ (plan.bucket_mask(d % plan.rels, 0) * plan.rels))
    (source,) = call(
        functools.partial(source_kernel, plan),
        [shape((width, prows), F32)],
        labels + grads[0::3],
        name="source",
    )

    count = plan.half_chunks
    for level, masks in enumerate(plan.masks[1:]):
        size = len(masks)
        count //= size
        outs = [shape((count,) + chunk[1:], F32)] + [
            shape((count,) + chunk[1:], jnp.int16)
        ] * (size - 1)
        made = call(
            functools.partial(combine_kernel, 1 + len(arrived), False),
            outs,
            [keep] + arrived,
            name="combine",
        )
        keep = made[0]
        arrived = [
            send(value, plan, lambda d, m=mask: d ^ m)
            for value, mask in zip(made[1:], masks[1:])
        ]
    (total,) = call(
        functools.partial(combine_kernel, 1 + len(arrived), True),
        [shape((1,) + chunk[1:], jnp.int16)],
        [keep] + arrived,
        name="total",
    )

    lanes = plan.part_lanes
    shares = call(
        functools.partial(share_kernel, plan),
        [shape((width, lanes), F32)]
        + [shape((width + 16, lanes), jnp.int16)] * (plan.rels - 1),
        [source, far],
        name="share",
    )
    mine = [shares[0]] + [
        send(value, plan, lambda d, m=mask: d ^ m)
        for mask, value in zip(range(1, plan.rels), shares[1:])
    ]
    (mine,) = call(
        add_pack_kernel, [shape((width + 16, lanes), jnp.int16)], mine, name="mine"
    )

    pieces = [total]
    for masks in reversed(plan.masks[1:]):
        whole_piece = jnp.concatenate(pieces, axis=0)
        pieces = [whole_piece] + [
            send(whole_piece, plan, lambda d, m=mask: d ^ m) for mask in masks[1:]
        ]
    pieces += [send(piece, plan, lambda d: d ^ 1) for piece in pieces]

    owners = [mine] + [
        send(mine, plan, lambda d, m=mask: d ^ m) for mask in range(1, plan.rels)
    ]
    (grad_partitions,) = call(
        functools.partial(part_out_kernel, plan),
        [shape((width, prows), F32)],
        owners,
        name="part_out",
    )
    if lanes % LANES:
        order = jnp.arange(plan.rels) ^ lax.axis_index("rel")
        split_lanes = grad_partitions.reshape(width, plan.rels, lanes)
        grad_partitions = jnp.take(split_lanes, order, axis=1).reshape(width, prows)
    grad_relations, grad_remainder = call(
        functools.partial(spread_kernel, plan, len(pieces)),
        [shape((width, plan.nrels), F32), shape((width, plan.rems), F32)],
        pieces,
        scratch=[pltpu.VMEM((plan.devices,) + chunk[1:], jnp.int16)],
        name="spread",
    )
    return grad_partitions.T, grad_remainder.T, grad_relations.T


def solution(mesh):
    edge = P("dom", None, "rel", None)
    in_specs = (P("dom", None), P(), P(), P("dom", None, "rel")) + (edge,) * 7
    out_specs = (P("dom", None), P(), P())
    return jax.shard_map(body, mesh=mesh, in_specs=in_specs, out_specs=out_specs, check_vma=False)
```

```python
import functools

import jax
import jax.numpy as jnp
from jax import lax
from jax.experimental import pallas as pl
from jax.experimental.pallas import tpu as pltpu
from jax.sharding import PartitionSpec as P

F32 = jnp.float32
BF16 = jnp.bfloat16
LANES = 128
NT = (((1,), (1,)), ((), ()))
NN = (((1,), (0,)), ((), ()))
TN = (((0,), (0,)), ((), ()))


def bits_of(count):
    return count.bit_length() - 1


def reverse_bits(value, count):
    out = 0
    for bit in range(bits_of(count)):
        out = out * 2 + ((value >> bit) & 1)
    return out


def split(value):
    high = value.astype(BF16)
    low = (value - high.astype(F32)).astype(BF16)
    return high, low


def dot(left, right, dims):
    return lax.dot_general(left, right, dims, preferred_element_type=F32)


def dot3(left, right, dims):
    left_high, left_low = split(left)
    right_high, right_low = split(right)
    return (
        dot(left_high, right_high, dims)
        + dot(left_high, right_low, dims)
        + dot(left_low, right_high, dims)
    )


def one_hot(ids, rows, base=0):
    place = lax.broadcasted_iota(jnp.int32, (rows, ids.shape[1]), 0)
    return jnp.where(place == ids - base, 1.0, 0.0).astype(BF16)


def store_split(ref, cols, value):
    high, low = split(value)
    depth = value.shape[0]
    ref[0:depth, cols] = high
    ref[depth : 2 * depth, cols] = low


def folded(value):
    depth = value.shape[0] // 2
    return value[:depth] + value[depth:]


def quantized(value):
    top = jnp.max(jnp.abs(value), axis=0, keepdims=True)
    exponent = jnp.floor(jnp.log2(jnp.maximum(top, 1e-30))) + 1.0
    scaled = jnp.round(value * jnp.exp2(15.0 - exponent))
    return jnp.clip(scaled, -32767.0, 32767.0), exponent


def to_words(value):
    return value.astype(jnp.int32).astype(jnp.int16)


def from_words(words):
    return words.astype(jnp.int32).astype(F32)


def pack_table(value):
    scaled, exponent = quantized(value)
    tail = jnp.broadcast_to(exponent, (16, value.shape[1]))
    return to_words(jnp.concatenate([scaled, tail], axis=0))


def unpack_table(words):
    depth = words.shape[0] - 16
    value = from_words(words)
    return value[:depth] * jnp.exp2(value[depth : depth + 1] - 15.0)


def pack_chunk(value):
    scaled, exponent = quantized(value)
    rows = value.shape[0]
    place = lax.broadcasted_iota(jnp.int32, value.shape, 0)
    return to_words(jnp.where(place >= rows - 8, exponent, scaled))


def unpack_chunk(words):
    value = from_words(words)
    rows = value.shape[0]
    place = lax.broadcasted_iota(jnp.int32, value.shape, 0)
    scale = jnp.exp2(value[rows - 1 : rows] - 15.0)
    return jnp.where(place >= rows - 8, 0.0, value * scale)


class Plan:
    def __init__(self, doms, rels, prows, width, rems, nrels, maxb):
        self.doms, self.rels, self.maxb = doms, rels, maxb
        self.devices = doms * rels
        self.prows, self.width, self.rems, self.nrels = prows, width, rems, nrels
        self.buckets = doms // rels
        self.slots = rels * maxb
        self.bucket_edges = self.slots * LANES
        self.edges = self.buckets * self.bucket_edges
        self.part_lanes = prows // rels
        self.half_rel, self.half_rem = nrels // 2, rems // 2
        self.half_lanes = self.half_rel + self.half_rem
        self.subs = width // 8
        self.units = (self.half_lanes // LANES) * self.subs
        self.half_chunks = self.devices // 2
        self.chunk_units = -(-self.units // self.half_chunks)
        self.chunk_rows = (self.chunk_units + 2) // 2 * 16
        rel_bits = bits_of(rels)
        all_bits = rel_bits + bits_of(doms)
        self.groups = [
            [0],
            list(range(1, rel_bits + 1)),
            list(range(rel_bits + 1, all_bits)),
        ]
        self.masks = [self.group_masks(bits) for bits in self.groups]
        order = [bit for group in self.groups for bit in reversed(group)]
        self.place = {bit: all_bits - 1 - at for at, bit in enumerate(order)}

    @staticmethod
    def group_masks(bits):
        masks = []
        for index in range(2 ** len(bits)):
            masks.append(sum(((index >> at) & 1) << bit for at, bit in enumerate(bits)))
        return masks

    def row(self, labels, bucket, kinds, first, count):
        rows = []
        for slot in range(first, first + count):
            mask, turn = divmod(slot, self.maxb)
            block = bucket * self.maxb + turn
            rows += [labels[mask][block, kind : kind + 1, :] for kind in kinds]
        return jnp.concatenate(rows, axis=1) if len(rows) > 1 else rows[0]

    def whole_row(self, labels, kinds):
        rows = [
            self.row(labels, bucket, kinds, 0, self.slots) for bucket in range(self.buckets)
        ]
        return jnp.concatenate(rows, axis=1) if len(rows) > 1 else rows[0]

    def me(self):
        return lax.axis_index("dom") * self.rels + lax.axis_index("rel")

    def low_chunk(self, device):
        return device >> 1

    def position(self, chunk, me):
        relative = chunk ^ (me >> 1)
        out = 0
        for bit, at in self.place.items():
            if bit:
                out = out + (((relative >> (bit - 1)) & 1) << at)
        return out

    def bucket_mask(self, rel, bucket):
        return reverse_bits(rel, self.rels) * self.buckets + bucket

    def dynamic_mask(self, rel, bucket):
        out = 0
        width = bits_of(self.rels)
        for bit in range(width):
            out = out + (((rel >> bit) & 1) << (width - 1 - bit))
        return out * self.buckets + bucket


def send(value, plan, target):
    pairs = [(device, target(device)) for device in range(plan.devices)]
    return lax.ppermute(value, ("dom", "rel"), pairs)


def lists_kernel(plan, *refs):
    tables, counts, outs = refs[:7], refs[7], refs[8:]
    source = lax.axis_index("dom")
    rel = lax.axis_index("rel")
    for mask, out in enumerate(outs):
        for bucket in range(plan.buckets):
            target = source ^ plan.dynamic_mask(rel ^ mask, bucket)
            stop = lax.rem(source - target + plan.doms, plan.doms)
            for turn in range(plan.maxb):
                block = bucket * plan.maxb + turn
                for at, table in enumerate(tables):
                    out[block, at : at + 1, :] = table[0, stop, turn : turn + 1, :]
                live = jnp.where(turn < counts[stop], 1, 0)
                out[block, 7:8, :] = jnp.full((1, LANES), live, jnp.int32)


def prep_kernel(plan, *refs):
    labels = refs[: plan.rels]
    own, rem, relations, lhs_out, rel_out, rem_out, rel_split = refs[plan.rels :]
    depth = plan.width
    high, low = split(relations[...])
    rel_split[0:depth, :] = high
    rel_split[depth : 2 * depth, :] = low
    for bucket in range(plan.buckets):
        for pair in range(0, plan.slots, 2):
            count = min(2, plan.slots - pair)
            row = lambda at: plan.row(labels, bucket, (at,), pair, count)
            start = bucket * plan.bucket_edges + pair * LANES
            cols = slice(start, start + count * LANES)
            lhs_out[:, cols] = dot(own[...], one_hot(row(0), plan.prows), NN) + dot(
                rem[...], one_hot(row(1), plan.rems), NN
            )
            rel_out[:, cols] = folded(dot(rel_split[...], one_hot(row(2), plan.nrels), NN))
            ids = plan.row(labels, bucket, (4, 6), pair, count)
            rem_out[:, 2 * start : 2 * (start + count * LANES)] = dot(
                rem[...], one_hot(ids, plan.rems), NN
            ).astype(BF16)


def conjugate_parts(grad, other):
    half = grad.shape[0] // 2
    grad_re, grad_im = grad[:half], grad[half:]
    other_re, other_im = other[:half], other[half:]
    return jnp.concatenate(
        [grad_re * other_re + grad_im * other_im, grad_im * other_re - grad_re * other_im], 0
    )


def complex_product(left, right):
    half = left.shape[0] // 2
    left_re, left_im = left[:half], left[half:]
    right_re, right_im = right[:half], right[half:]
    return jnp.concatenate(
        [left_re * right_re - left_im * right_im, left_re * right_im + left_im * right_re], 0
    )


def bucket_grads(plan, bucket, labels, target, lhs_in, rel_in, rem_in, lhs_out, rel_out, cand_out, base):
    total = 2 * LANES
    edge = lax.broadcasted_iota(jnp.int32, (LANES, total), 0)
    column = lax.broadcasted_iota(jnp.int32, (LANES, total), 1)
    keep = jnp.where(edge == column, 0.0, 1.0 / total)
    for slot in range(plan.slots):
        cols = slice(slot * LANES, (slot + 1) * LANES)
        wide = slice(slot * total, (slot + 1) * total)
        ids = plan.row(labels, bucket, (3, 5), slot, 1)
        cand = dot(target[...], one_hot(ids, plan.prows), NN) + rem_in[:, wide].astype(F32)
        rhs = cand[:, :LANES]
        lhs, vec = lhs_in[:, cols], rel_in[:, cols]
        u_vec = complex_product(lhs, vec)
        live = plan.row(labels, bucket, (7,), slot, 1).astype(F32)
        positive = jnp.sum(u_vec * rhs, axis=0, keepdims=True)
        negative = dot3(u_vec, cand, TN)
        grad_pos = -jax.nn.sigmoid(-positive) * live
        grad_neg = jax.nn.sigmoid(negative) * keep * live[0:1, 0:1]
        grad_u = grad_pos * rhs + dot3(cand, grad_neg, NT)
        from_neg = dot3(u_vec, grad_neg, NN)
        grad_cand = jnp.concatenate(
            [from_neg[:, :LANES] + grad_pos * u_vec, from_neg[:, LANES:]], axis=1
        )
        at = base + slot
        cols = slice(at * LANES, (at + 1) * LANES)
        wide = slice(at * total, (at + 1) * total)
        store_split(lhs_out, cols, conjugate_parts(grad_u, vec))
        store_split(rel_out, cols, conjugate_parts(grad_u, lhs))
        store_split(cand_out, wide, grad_cand)


def bucket_kernel(plan, bucket, *refs):
    bucket_grads(plan, bucket, refs[: plan.rels], *refs[plan.rels :], 0)


def last_kernel(plan, *refs):
    labels = refs[: plan.rels]
    before = refs[plan.rels : plan.rels + 3 * (plan.buckets - 1)]
    refs = refs[plan.rels + 3 * (plan.buckets - 1) :]
    target, lhs_in, rel_in, rem_in = refs[:4]
    away, outs, helds, table, sems = refs[4], refs[5:8], refs[8:11], refs[11], refs[12]
    edges = plan.bucket_edges
    loads = []
    for at, ref in enumerate(before):
        wide = edges * (2 if at % 3 == 2 else 1)
        start = (at // 3) * wide
        loads.append(
            pltpu.make_async_copy(ref, helds[at % 3].at[:, start : start + wide], sems.at[at])
        )
        loads[-1].start()
    base = (plan.buckets - 1) * plan.slots
    bucket_grads(plan, plan.buckets - 1, labels, target, lhs_in, rel_in, rem_in, *helds, base)
    for load in loads:
        load.wait()
    stores = [
        pltpu.make_async_copy(held, out, sems.at[len(loads) + at])
        for at, (held, out) in enumerate(zip(helds, outs))
    ]
    for store in stores:
        store.start()
    reduce_half(plan, True, labels, helds, table, away)
    for store in stores:
        store.wait()


def reduce_half(plan, away, labels, grads, table, out):
    lhs_grads, rel_grads, cand_grads = grads
    me = plan.me()
    half = (me & 1) ^ (1 if away else 0)
    step = 2 * LANES if plan.half_rel % (2 * LANES) == 0 else LANES
    ids = plan.whole_row(labels, (2,)) - half * plan.half_rel
    for start in range(0, plan.half_rel, step):
        hot = one_hot(ids, step, start)
        table[:, start : start + step] = folded(dot(rel_grads[...], hot, NT))
    base = half * plan.half_rem
    first = one_hot(plan.whole_row(labels, (1,)), plan.half_rem, base)
    second = one_hot(plan.whole_row(labels, (4, 6)), plan.half_rem, base)
    table[:, plan.half_rel :] = folded(
        dot(lhs_grads[...], first, NT) + dot(cand_grads[...], second, NT)
    )
    for chunk in range(plan.half_chunks):
        parts = []
        for unit in range(chunk * plan.chunk_units, (chunk + 1) * plan.chunk_units):
            if unit < plan.units:
                lane, sub = divmod(unit, plan.subs)
                parts.append(table[8 * sub : 8 * sub + 8, lane * LANES : (lane + 1) * LANES])
            else:
                parts.append(jnp.zeros((8, LANES), F32))
        spare = plan.chunk_rows - 8 * plan.chunk_units
        parts.append(jnp.zeros((spare, LANES), F32))
        value = jnp.concatenate(parts, axis=0)
        out[plan.position(chunk, me)] = pack_chunk(value) if away else value


def part_sum(plan, labels, bucket, grads):
    ids = plan.row(labels, bucket, (3, 5), 0, plan.slots)
    shift = lax.axis_index("rel") * plan.part_lanes
    return folded(dot(grads, one_hot(ids ^ shift, plan.prows), NT))


def near_kernel(plan, bucket, *refs):
    labels = refs[: plan.rels]
    grads, out = refs[plan.rels :]
    out[...] = pack_table(part_sum(plan, labels, bucket, grads[...]))


def home_kernel(plan, after, *refs):
    labels = refs[: plan.rels]
    grads = refs[plan.rels : plan.rels + 3]
    keep, part, source, table = refs[plan.rels + 3 + after :]
    reduce_half(plan, False, labels, grads, table, keep)
    part[...] = part_sum(plan, labels, 0, grads[2][:, : 2 * plan.bucket_edges])
    ids = plan.whole_row(labels, (0,)) ^ (lax.axis_index("rel") * plan.part_lanes)
    source[...] = folded(dot(grads[0][...], one_hot(ids, plan.prows), NT))


def combine(keep, arrived, outs, last=False):
    count = keep.shape[0]
    share = count // len(outs)
    for at in range(count):
        value = keep[at]
        for ref in arrived:
            value = value + unpack_chunk(ref[at])
        which, place = divmod(at, share)
        outs[which][place] = pack_chunk(value) if (which or last) else value


def stage_one_kernel(plan, *refs):
    keep, core, part = refs[:3]
    near = refs[3 : 2 + plan.buckets]
    outs, far = refs[2 + plan.buckets : -1], refs[-1]
    combine(keep, [core], outs)
    value = part[...]
    for ref in near:
        value = value + unpack_table(ref[...])
    far[...] = pack_table(value)


def stage_two_kernel(plan, *refs):
    size, later = len(plan.masks[1]), len(plan.masks[2])
    keep, arrived, (source, far) = refs[0], refs[1:size], refs[size : size + 2]
    outs = refs[size + 2 : size + 2 + later]
    mine, shares = refs[size + 2 + later], refs[size + 3 + later :]
    combine(keep, arrived, outs)
    lanes = plan.part_lanes
    value = source[...] + unpack_table(far[...])
    mine[...] = value[:, :lanes]
    for at, out in enumerate(shares):
        out[...] = pack_table(value[:, (at + 1) * lanes : (at + 2) * lanes])


def stage_three_kernel(plan, *refs):
    size = len(plan.masks[2])
    keep, arrived = refs[0], refs[1:size]
    mine, shares = refs[size], refs[size + 1 : size + plan.rels]
    total, part = refs[size + plan.rels :]
    combine(keep, arrived, [total], True)
    value = mine[...]
    for ref in shares:
        value = value + unpack_table(ref[...])
    part[...] = pack_table(value)


def spread_kernel(plan, other, count, core, *refs):
    pieces, (rel_out, rem_out, held) = refs[:count], refs[-3:]
    at = 0
    for piece in pieces:
        held[at : at + piece.shape[0]] = piece[...]
        at += piece.shape[0]
    me = plan.me()
    for chunk in range(plan.half_chunks):
        value = unpack_chunk(held[plan.position(chunk, me)])
        for index in range(plan.chunk_units):
            unit = chunk * plan.chunk_units + index
            if unit >= plan.units:
                break
            lane, sub = divmod(unit, plan.subs)
            lane = lane * LANES
            rows = slice(8 * sub, 8 * sub + 8)
            block = value[8 * index : 8 * index + 8]
            if lane < plan.half_rel:
                rel_out[rows, lane : lane + LANES] = block
            else:
                lane -= plan.half_rel
                rem_out[rows, lane : lane + LANES] = block


def relay_kernel(*refs):
    pass


def part_out_kernel(plan, *refs):
    out = refs[-1]
    rel = lax.axis_index("rel")
    lanes = plan.part_lanes
    for mask, ref in enumerate(refs[:-1]):
        if lanes % LANES:
            out[:, mask * lanes : (mask + 1) * lanes] = unpack_table(ref[...])
        else:
            start = pl.multiple_of((rel ^ mask) * lanes, lanes)
            out[:, pl.ds(start, lanes)] = unpack_table(ref[...])


def shape(extent, kind):
    return jax.ShapeDtypeStruct(extent, kind)


VMEM = pl.BlockSpec(memory_space=pltpu.VMEM)
ANY = pl.BlockSpec(memory_space=pl.ANY)


def call(kernel, outs, args, name, cost, limit=48, scratch=(), in_specs=None, out_specs=None, **more):
    work = pl.CostEstimate(flops=int(cost * 1e9), bytes_accessed=int(cost * 3e6), transcendentals=0)
    return pl.pallas_call(
        kernel,
        out_shape=outs,
        in_specs=in_specs or [VMEM] * len(args),
        out_specs=out_specs or [VMEM] * len(outs),
        scratch_shapes=list(scratch),
        compiler_params=pltpu.CompilerParams(vmem_limit_bytes=limit * 2**20),
        cost_estimate=work,
        name=name,
        **more,
    )(*args)


def body(
    partitions,
    remainder,
    relations,
    counts,
    lhs_rows,
    lhs_rems,
    rel_ids,
    rhs_rows,
    rhs_rems,
    neg_rows,
    neg_rems,
):
    prows, width = partitions.shape
    plan = Plan(
        lax.axis_size("dom"),
        lax.axis_size("rel"),
        prows,
        width,
        remainder.shape[0],
        relations.shape[0],
        lhs_rows.shape[2],
    )
    smem = pl.BlockSpec(memory_space=pltpu.SMEM)
    own, rem, rels = partitions.T, remainder.T, relations.T
    edges, wide = plan.edges, plan.bucket_edges
    buckets = plan.buckets
    afar = lambda d: d ^ (plan.bucket_mask(d % plan.rels, 0) * plan.rels)
    i16 = jnp.int16

    first = send(own, plan, afar)
    tables = [lhs_rows, lhs_rems, rel_ids, rhs_rows, rhs_rems, neg_rows, neg_rems]
    labels = call(
        functools.partial(lists_kernel, plan),
        [shape((buckets * plan.maxb, 8, LANES), jnp.int32)] * plan.rels,
        tables + [counts.reshape(-1)],
        "lists",
        1.0,
        8,
        in_specs=[VMEM] * 7 + [smem],
    )
    labels = [labels[0]] + [
        send(labels[mask], plan, lambda d, m=mask: d ^ m) for mask in range(1, plan.rels)
    ]
    lhs, vec, cand_rem = call(
        functools.partial(prep_kernel, plan),
        [shape((width, edges), F32), shape((width, edges), F32), shape((width, 2 * edges), BF16)],
        labels + [own, rem, rels],
        "prep",
        10.0,
        scratch=[pltpu.VMEM((2 * width, plan.nrels), BF16)],
    )
    (first,) = call(
        relay_kernel,
        [shape((width, prows), BF16)],
        [first, cand_rem],
        "relay",
        0.1,
        1,
        in_specs=[ANY, ANY],
        out_specs=[ANY],
        input_output_aliases={0: 0},
    )
    targets = [first] + [
        send(first, plan, lambda d, b=bucket: d ^ (b * plan.rels)) for bucket in range(1, buckets)
    ]

    grad_shapes = lambda count: [
        shape((2 * width, count), BF16),
        shape((2 * width, count), BF16),
        shape((2 * width, 2 * count), BF16),
    ]
    one = lambda b: pl.BlockSpec((width, wide), lambda i: (0, b))
    two = lambda b: pl.BlockSpec((width, 2 * wide), lambda i: (0, b))
    whole = lambda extent: pl.BlockSpec(extent, lambda i: (0,) * len(extent))
    label_specs = [whole(label.shape) for label in labels]
    grads = []
    for bucket in range(buckets - 1):
        outs = grad_shapes(wide)
        grads += call(
            functools.partial(bucket_kernel, plan, bucket),
            outs,
            labels + [targets[bucket], lhs, vec, cand_rem],
            "bucket",
            7.0,
            grid=(1,),
            in_specs=label_specs + [whole(own.shape), one(bucket), one(bucket), two(bucket)],
            out_specs=[whole(out.shape) for out in outs],
        )
    last = buckets - 1
    chunk = (plan.half_chunks, plan.chunk_rows, LANES)
    table = [pltpu.VMEM((width, plan.half_lanes), F32)]
    made = call(
        functools.partial(last_kernel, plan),
        [shape(chunk, i16)] + grad_shapes(edges),
        labels + grads + [targets[last], lhs, vec, cand_rem],
        "last",
        14.0,
        grid=(1,),
        in_specs=label_specs
        + [ANY] * len(grads)
        + [whole(own.shape), one(last), one(last), two(last)],
        out_specs=[whole(chunk)] + [ANY] * 3,
        scratch=[pltpu.VMEM(held.shape, BF16) for held in grad_shapes(edges)]
        + table
        + [pltpu.SemaphoreType.DMA((len(grads) + 3,))],
    )
    away, grads = made[0], list(made[1:])
    core = send(away, plan, lambda d: d ^ 1)

    near, packed = [], []
    for bucket in range(1, buckets):
        packed += call(
            functools.partial(near_kernel, plan, bucket),
            [shape((width + 16, prows), i16)],
            labels + [grads[2]],
            "near",
            2.5,
            grid=(1,),
            in_specs=label_specs
            + [pl.BlockSpec((2 * width, 2 * wide), lambda i, b=bucket: (0, b))],
            out_specs=[whole((width + 16, prows))],
        )
        near.append(send(packed[-1], plan, lambda d, b=bucket: d ^ (b * plan.rels)))
    keep, part, source = call(
        functools.partial(home_kernel, plan, len(packed) + 1),
        [shape(chunk, F32), shape((width, prows), F32), shape((width, prows), F32)],
        labels + grads + packed + [away],
        "home",
        11.0,
        in_specs=[VMEM] * (len(labels) + 3) + [ANY] * (len(packed) + 1),
        scratch=table,
    )

    def shares(count, size):
        extent = (count // size,) + chunk[1:]
        return [shape(extent, F32)] + [shape(extent, i16)] * (size - 1)

    def exchanged(values, masks):
        return [
            send(value, plan, lambda d, m=mask: d ^ m) for value, mask in zip(values, masks[1:])
        ]

    size, later = len(plan.masks[1]), len(plan.masks[2])
    made = call(
        functools.partial(stage_one_kernel, plan),
        shares(chunk[0], size) + [shape((width + 16, prows), i16)],
        [keep, core, part] + near,
        "stage_one",
        4.0,
        16,
    )
    keep, arrived = made[0], exchanged(made[1:-1], plan.masks[1])
    far = send(made[-1], plan, afar)

    lanes = plan.part_lanes
    made = call(
        functools.partial(stage_two_kernel, plan),
        shares(chunk[0] // size, later)
        + [shape((width, lanes), F32)]
        + [shape((width + 16, lanes), i16)] * (plan.rels - 1),
        [keep] + arrived + [source, far],
        "stage_two",
        3.0,
        16,
    )
    keep, arrived = made[0], exchanged(made[1:later], plan.masks[2])
    mine = [made[later]] + exchanged(made[later + 1 :], range(plan.rels))

    total, part = call(
        functools.partial(stage_three_kernel, plan),
        [shape((1,) + chunk[1:], i16), shape((width + 16, lanes), i16)],
        [keep] + arrived + mine,
        "stage_three",
        2.0,
        16,
    )
    pieces = [total] + exchanged([total] * (later - 1), plan.masks[2])
    owners = [part] + exchanged([part] * (plan.rels - 1), range(plan.rels))
    block = jnp.concatenate(pieces, axis=0)
    pieces = [block] + exchanged([block] * (size - 1), plan.masks[1])
    (grad_partitions,) = call(
        functools.partial(part_out_kernel, plan),
        [shape((width, prows), F32)],
        owners,
        "part_out",
        2.0,
        16,
    )
    if lanes % LANES:
        order = jnp.arange(plan.rels) ^ lax.axis_index("rel")
        split_lanes = grad_partitions.reshape(width, plan.rels, lanes)
        grad_partitions = jnp.take(split_lanes, order, axis=1).reshape(width, prows)

    others = [send(piece, plan, lambda d: d ^ 1) for piece in pieces]
    side = lax.axis_index("rel") & 1
    outs = [shape((width, plan.nrels), F32), shape((width, plan.rems), F32)]
    held = pltpu.VMEM(chunk, i16)
    for turn, group in enumerate([pieces, others]):
        base = [] if turn == 0 else list(outs_made)
        spec = lambda lanes: pl.BlockSpec((width, lanes), lambda i, half: (0, half[0]))
        work = pl.CostEstimate(flops=int(2e9), bytes_accessed=int(6e6), transcendentals=0)
        outs_made = pl.pallas_call(
            functools.partial(spread_kernel, plan, turn, len(group)),
            out_shape=outs,
            grid_spec=pltpu.PrefetchScalarGridSpec(
                num_scalar_prefetch=1,
                grid=(1,),
                in_specs=[
                    pl.BlockSpec(piece.shape, lambda i, half: (0, 0, 0)) for piece in group
                ]
                + [ANY] * len(base),
                out_specs=[spec(plan.half_rel), spec(plan.half_rem)],
                scratch_shapes=[held],
            ),
            input_output_aliases={1 + len(group) + at: at for at in range(len(base))},
            compiler_params=pltpu.CompilerParams(vmem_limit_bytes=24 * 2**20),
            cost_estimate=work,
            name="spread",
        )((side ^ turn).reshape(1), *group, *base)
    grad_relations, grad_remainder = outs_made
    return grad_partitions.T, grad_remainder.T, grad_relations.T


def solution(mesh):
    edge = P("dom", None, "rel", None)
    in_specs = (P("dom", None), P(), P(), P("dom", None, "rel")) + (edge,) * 7
    out_specs = (P("dom", None), P(), P())
    return jax.shard_map(body, mesh=mesh, in_specs=in_specs, out_specs=out_specs, check_vma=False)
```

```python
import functools

import jax
import jax.numpy as jnp
from jax import lax
from jax.experimental import pallas as pl
from jax.experimental.pallas import tpu as pltpu
from jax.sharding import PartitionSpec as P

F32 = jnp.float32
BF16 = jnp.bfloat16
LANES = 128
REACH = 32766.0
NT = (((1,), (1,)), ((), ()))
NN = (((1,), (0,)), ((), ()))
TN = (((0,), (0,)), ((), ()))


def bits_of(count):
    return count.bit_length() - 1


def reverse_bits(value, count):
    out = 0
    for bit in range(bits_of(count)):
        out = out * 2 + ((value >> bit) & 1)
    return out


def split(value):
    high = value.astype(BF16)
    low = (value - high.astype(F32)).astype(BF16)
    return high, low


def dot(left, right, dims):
    return lax.dot_general(left, right, dims, preferred_element_type=F32)


def dot3(left, right, dims):
    left_high, left_low = split(left)
    right_high, right_low = split(right)
    return (
        dot(left_high, right_high, dims)
        + dot(left_high, right_low, dims)
        + dot(left_low, right_high, dims)
    )


def one_hot(ids, rows, base=0):
    place = lax.broadcasted_iota(jnp.int32, (rows, ids.shape[1]), 0)
    return jnp.where(place == ids - base, 1.0, 0.0).astype(BF16)


def store_split(ref, cols, value):
    high, low = split(value)
    depth = value.shape[0]
    ref[0:depth, cols] = high
    ref[depth : 2 * depth, cols] = low


def folded(value):
    depth = value.shape[0] // 2
    return value[:depth] + value[depth:]


def quantized(value):
    top = jnp.max(jnp.abs(value), axis=0, keepdims=True)
    exponent = jnp.floor(jnp.log2(jnp.maximum(top, 1e-30))) + 1.0
    return jnp.round(value * (REACH * jnp.exp2(-exponent))), exponent


def scale_of(exponent):
    return jnp.exp2(exponent) * (1.0 / REACH)


def to_words(value):
    return value.astype(jnp.int32).astype(jnp.int16)


def from_words(words):
    return words.astype(jnp.int32).astype(F32)


def pack_table(value, rows=None):
    scaled, exponent = quantized(value)
    spare = (rows or value.shape[0] + 16) - value.shape[0]
    tail = jnp.broadcast_to(exponent, (spare, value.shape[1]))
    return to_words(jnp.concatenate([scaled, tail], axis=0))


def unpack_table(words, depth=None):
    depth = depth or words.shape[0] - 16
    value = from_words(words)
    return value[:depth] * scale_of(value[depth : depth + 1])


class Plan:
    def __init__(self, doms, rels, prows, width, rems, nrels, maxb):
        self.doms, self.rels, self.maxb = doms, rels, maxb
        self.devices = doms * rels
        self.prows, self.width, self.rems, self.nrels = prows, width, rems, nrels
        self.buckets = doms // rels
        self.slots = rels * maxb
        self.bucket_edges = self.slots * LANES
        self.edges = self.buckets * self.bucket_edges
        self.part_lanes = prows // rels
        self.half_rel, self.half_rem = nrels // 2, rems // 2
        self.half_lanes = self.half_rel + self.half_rem
        self.subs = width // 8
        self.units = (self.half_lanes // LANES) * self.subs
        self.half_chunks = self.devices // 2
        self.chunk_units = -(-self.units // self.half_chunks)
        self.chunk_rows = (self.chunk_units + 2) // 2 * 16
        rel_bits = bits_of(rels)
        all_bits = rel_bits + bits_of(doms)
        self.groups = [
            [0],
            list(range(1, rel_bits + 1)),
            list(range(rel_bits + 1, all_bits)),
        ]
        self.masks = [self.group_masks(bits) for bits in self.groups]
        order = [bit for group in self.groups for bit in reversed(group)]
        self.place = {bit: all_bits - 1 - at for at, bit in enumerate(order)}

    @staticmethod
    def group_masks(bits):
        masks = []
        for index in range(2 ** len(bits)):
            masks.append(sum(((index >> at) & 1) << bit for at, bit in enumerate(bits)))
        return masks

    def row(self, labels, bucket, kinds, first, count):
        rows = []
        for slot in range(first, first + count):
            mask, turn = divmod(slot, self.maxb)
            block = bucket * self.maxb + turn
            rows += [labels[mask][block, kind : kind + 1, :] for kind in kinds]
        return jnp.concatenate(rows, axis=1) if len(rows) > 1 else rows[0]

    def whole_row(self, labels, kinds):
        rows = [
            self.row(labels, bucket, kinds, 0, self.slots) for bucket in range(self.buckets)
        ]
        return jnp.concatenate(rows, axis=1) if len(rows) > 1 else rows[0]

    def me(self):
        return lax.axis_index("dom") * self.rels + lax.axis_index("rel")

    def low_chunk(self, device):
        return device >> 1

    def position(self, chunk, me):
        relative = chunk ^ (me >> 1)
        out = 0
        for bit, at in self.place.items():
            if bit:
                out = out + (((relative >> (bit - 1)) & 1) << at)
        return out

    def bucket_mask(self, rel, bucket):
        return reverse_bits(rel, self.rels) * self.buckets + bucket

    def dynamic_mask(self, rel, bucket):
        out = 0
        width = bits_of(self.rels)
        for bit in range(width):
            out = out + (((rel >> bit) & 1) << (width - 1 - bit))
        return out * self.buckets + bucket


def send(value, plan, target):
    pairs = [(device, target(device)) for device in range(plan.devices)]
    return lax.ppermute(value, ("dom", "rel"), pairs)


def lists_kernel(plan, *refs):
    tables, counts, outs = refs[:7], refs[7], refs[8:]
    source = lax.axis_index("dom")
    rel = lax.axis_index("rel")
    for mask, out in enumerate(outs):
        for bucket in range(plan.buckets):
            target = source ^ plan.dynamic_mask(rel ^ mask, bucket)
            stop = lax.rem(source - target + plan.doms, plan.doms)
            for turn in range(plan.maxb):
                block = bucket * plan.maxb + turn
                for at, table in enumerate(tables):
                    out[block, at : at + 1, :] = table[0, stop, turn : turn + 1, :]
                live = jnp.where(turn < counts[stop], 1, 0)
                out[block, 7:8, :] = jnp.full((1, LANES), live, jnp.int32)


def relation_kernel(plan, *refs):
    labels = refs[: plan.rels]
    relations, rel_out, rel_split = refs[plan.rels :]
    depth = plan.width
    high, low = split(relations[...])
    rel_split[0:depth, :] = high
    rel_split[depth : 2 * depth, :] = low
    for bucket in range(plan.buckets):
        for pair in range(0, plan.slots, 2):
            count = min(2, plan.slots - pair)
            start = bucket * plan.bucket_edges + pair * LANES
            ids = plan.row(labels, bucket, (2,), pair, count)
            rel_out[:, start : start + count * LANES] = folded(
                dot(rel_split[...], one_hot(ids, plan.nrels), NN)
            )


def source_rows_kernel(plan, *refs):
    labels = refs[: plan.rels]
    own, rem = refs[plan.rels : plan.rels + 2]
    lhs_out, rem_out = refs[-2:]
    for bucket in range(plan.buckets):
        for pair in range(0, plan.slots, 2):
            count = min(2, plan.slots - pair)
            row = lambda *kinds: plan.row(labels, bucket, kinds, pair, count)
            start = bucket * plan.bucket_edges + pair * LANES
            end = start + count * LANES
            lhs_out[:, start:end] = dot(own[...], one_hot(row(0), plan.prows), NN) + dot(
                rem[...], one_hot(row(1), plan.rems), NN
            )
            rem_out[:, 2 * start : 2 * end] = dot(
                rem[...], one_hot(row(4, 6), plan.rems), NN
            ).astype(BF16)


def conjugate_parts(grad, other):
    half = grad.shape[0] // 2
    grad_re, grad_im = grad[:half], grad[half:]
    other_re, other_im = other[:half], other[half:]
    return jnp.concatenate(
        [grad_re * other_re + grad_im * other_im, grad_im * other_re - grad_re * other_im], 0
    )


def complex_product(left, right):
    half = left.shape[0] // 2
    left_re, left_im = left[:half], left[half:]
    right_re, right_im = right[:half], right[half:]
    return jnp.concatenate(
        [left_re * right_re - left_im * right_im, left_re * right_im + left_im * right_re], 0
    )


def bucket_grads(plan, bucket, labels, target, lhs_in, rel_in, rem_in, lhs_out, rel_out, cand_out, base):
    total = 2 * LANES
    edge = lax.broadcasted_iota(jnp.int32, (LANES, total), 0)
    column = lax.broadcasted_iota(jnp.int32, (LANES, total), 1)
    keep = jnp.where(edge == column, 0.0, 1.0 / total)
    for slot in range(plan.slots):
        at = bucket * plan.slots + slot
        cols = slice(at * LANES, (at + 1) * LANES)
        wide = slice(at * total, (at + 1) * total)
        ids = plan.row(labels, bucket, (3, 5), slot, 1)
        cand = dot(target[...], one_hot(ids, plan.prows), NN) + rem_in[:, wide].astype(F32)
        rhs = cand[:, :LANES]
        lhs, vec = lhs_in[:, cols], rel_in[:, cols]
        u_vec = complex_product(lhs, vec)
        live = plan.row(labels, bucket, (7,), slot, 1).astype(F32)
        positive = jnp.sum(u_vec * rhs, axis=0, keepdims=True)
        negative = dot3(u_vec, cand, TN)
        grad_pos = -jax.nn.sigmoid(-positive) * live
        grad_neg = jax.nn.sigmoid(negative) * keep * live[0:1, 0:1]
        grad_u = grad_pos * rhs + dot3(cand, grad_neg, NT)
        from_neg = dot3(u_vec, grad_neg, NN)
        grad_cand = jnp.concatenate(
            [from_neg[:, :LANES] + grad_pos * u_vec, from_neg[:, LANES:]], axis=1
        )
        at = base + slot
        cols = slice(at * LANES, (at + 1) * LANES)
        wide = slice(at * total, (at + 1) * total)
        store_split(lhs_out, cols, conjugate_parts(grad_u, vec))
        store_split(rel_out, cols, conjugate_parts(grad_u, lhs))
        store_split(cand_out, wide, grad_cand)


def bucket_kernel(plan, bucket, *refs):
    bucket_grads(plan, bucket, refs[: plan.rels], *refs[plan.rels :], 0)


def last_kernel(plan, *refs):
    labels = refs[: plan.rels]
    before = refs[plan.rels : plan.rels + 3 * (plan.buckets - 1)]
    refs = refs[plan.rels + 3 * (plan.buckets - 1) :]
    target, lhs_in, rel_in, rem_in = refs[:4]
    away, outs, helds, table, sems = refs[4], refs[5:8], refs[8:11], refs[11], refs[12]
    edges = plan.bucket_edges
    loads = []
    for at, ref in enumerate(before):
        wide = edges * (2 if at % 3 == 2 else 1)
        start = (at // 3) * wide
        loads.append(
            pltpu.make_async_copy(ref, helds[at % 3].at[:, start : start + wide], sems.at[at])
        )
        loads[-1].start()
    base = (plan.buckets - 1) * plan.slots
    bucket_grads(plan, plan.buckets - 1, labels, target, lhs_in, rel_in, rem_in, *helds, base)
    for load in loads:
        load.wait()
    stores = [
        pltpu.make_async_copy(held, out, sems.at[len(loads) + at])
        for at, (held, out) in enumerate(zip(helds, outs))
    ]
    for store in stores:
        store.start()
    reduce_half(plan, True, labels, helds, table, away)
    for store in stores:
        store.wait()


def reduce_half(plan, away, labels, grads, table, out):
    lhs_grads, rel_grads, cand_grads = grads
    me = plan.me()
    half = (me & 1) ^ (1 if away else 0)
    step = 2 * LANES if plan.half_rel % (2 * LANES) == 0 else LANES
    ids = plan.whole_row(labels, (2,)) - half * plan.half_rel
    for start in range(0, plan.half_rel, step):
        hot = one_hot(ids, step, start)
        table[:, start : start + step] = folded(dot(rel_grads[...], hot, NT))
    base = half * plan.half_rem
    first = one_hot(plan.whole_row(labels, (1,)), plan.half_rem, base)
    second = one_hot(plan.whole_row(labels, (4, 6)), plan.half_rem, base)
    table[:, plan.half_rel :] = folded(
        dot(lhs_grads[...], first, NT) + dot(cand_grads[...], second, NT)
    )
    for chunk in range(plan.half_chunks):
        parts = []
        for unit in range(chunk * plan.chunk_units, (chunk + 1) * plan.chunk_units):
            if unit < plan.units:
                lane, sub = divmod(unit, plan.subs)
                parts.append(table[8 * sub : 8 * sub + 8, lane * LANES : (lane + 1) * LANES])
            else:
                parts.append(jnp.zeros((8, LANES), F32))
        value = jnp.concatenate(parts, axis=0)
        out[plan.position(chunk, me)] = pack_table(value, plan.chunk_rows) if away else value


def part_sum(plan, labels, bucket, grads):
    ids = plan.row(labels, bucket, (3, 5), 0, plan.slots)
    shift = lax.axis_index("rel") * plan.part_lanes
    start, wide = 2 * bucket * plan.bucket_edges, 2 * plan.bucket_edges
    return folded(dot(grads[:, start : start + wide], one_hot(ids ^ shift, plan.prows), NT))


def near_kernel(plan, bucket, *refs):
    labels = refs[: plan.rels]
    grads, out = refs[plan.rels], refs[-1]
    out[...] = pack_table(part_sum(plan, labels, bucket, grads))


def home_kernel(plan, after, *refs):
    labels = refs[: plan.rels]
    grads = refs[plan.rels : plan.rels + 3]
    keep, table = refs[plan.rels + 3 + after :]
    reduce_half(plan, False, labels, grads, table, keep)


def far_kernel(plan, *refs):
    labels = refs[: plan.rels]
    grads, near = refs[plan.rels], refs[plan.rels + 1 : plan.rels + plan.buckets]
    out = refs[-1]
    value = part_sum(plan, labels, 0, grads)
    for ref in near:
        value = value + unpack_table(ref[...])
    out[...] = pack_table(value)


def source_kernel(plan, *refs):
    labels = refs[: plan.rels]
    grads, out = refs[plan.rels], refs[-1]
    ids = plan.whole_row(labels, (0,)) ^ (lax.axis_index("rel") * plan.part_lanes)
    out[...] = folded(dot(grads[...], one_hot(ids, plan.prows), NT))


def share_kernel(plan, *refs):
    source, far = refs[:2]
    mine, shares = refs[-plan.rels], refs[len(refs) - plan.rels + 1 :]
    lanes = plan.part_lanes
    value = source[...] + unpack_table(far[...])
    mine[...] = value[:, :lanes]
    for at, out in enumerate(shares):
        out[...] = pack_table(value[:, (at + 1) * lanes : (at + 2) * lanes])


def mine_kernel(plan, *refs):
    value = refs[0][...]
    for ref in refs[1 : plan.rels]:
        value = value + unpack_table(ref[...])
    refs[-1][...] = pack_table(value)


def combine_kernel(plan, group, last, *refs):
    keep, arrived, outs = refs[0], refs[1:group], refs[group:]
    count, depth = keep.shape[0], keep.shape[1]
    share = count // len(outs)
    for at in range(count):
        value = keep[at]
        for ref in arrived:
            value = value + unpack_table(ref[at], depth)
        which, place = divmod(at, share)
        packed = which or last
        outs[which][place] = pack_table(value, plan.chunk_rows) if packed else value


def spread_kernel(plan, count, side, *refs):
    pieces, (rel_out, rem_out, held) = refs[:count], refs[-3:]
    at = 0
    for piece in pieces:
        held[at : at + piece.shape[0]] = piece[...]
        at += piece.shape[0]
    me = plan.me()
    for chunk in range(plan.half_chunks):
        value = unpack_table(held[plan.position(chunk, me)], 8 * plan.chunk_units)
        for index in range(plan.chunk_units):
            unit = chunk * plan.chunk_units + index
            if unit >= plan.units:
                break
            lane, sub = divmod(unit, plan.subs)
            lane = lane * LANES
            rows = slice(8 * sub, 8 * sub + 8)
            block = value[8 * index : 8 * index + 8]
            if lane < plan.half_rel:
                rel_out[rows, lane : lane + LANES] = block
            else:
                lane -= plan.half_rel
                rem_out[rows, lane : lane + LANES] = block


def relay_kernel(*refs):
    pass


def part_out_kernel(plan, *refs):
    out = refs[-1]
    rel = lax.axis_index("rel")
    lanes = plan.part_lanes
    for mask, ref in enumerate(refs[: plan.rels]):
        if lanes % LANES:
            out[:, mask * lanes : (mask + 1) * lanes] = unpack_table(ref[...])
        else:
            start = pl.multiple_of((rel ^ mask) * lanes, lanes)
            out[:, pl.ds(start, lanes)] = unpack_table(ref[...])


def shape(extent, kind):
    return jax.ShapeDtypeStruct(extent, kind)


VMEM = pl.BlockSpec(memory_space=pltpu.VMEM)
ANY = pl.BlockSpec(memory_space=pl.ANY)


def call(kernel, outs, args, name, cost, limit, scratch=(), in_specs=None, out_specs=None, **more):
    work = pl.CostEstimate(flops=int(cost * 1e9), bytes_accessed=int(cost * 3e6), transcendentals=0)
    if "grid_spec" not in more:
        more["in_specs"] = in_specs or [VMEM] * len(args)
        more["out_specs"] = out_specs or [VMEM] * len(outs)
        more["scratch_shapes"] = list(scratch)
    return pl.pallas_call(
        kernel,
        out_shape=outs,
        compiler_params=pltpu.CompilerParams(vmem_limit_bytes=int(limit * 2**20)),
        cost_estimate=work,
        name=name,
        **more,
    )(*args)


def body(
    partitions,
    remainder,
    relations,
    counts,
    lhs_rows,
    lhs_rems,
    rel_ids,
    rhs_rows,
    rhs_rems,
    neg_rows,
    neg_rems,
):
    prows, width = partitions.shape
    plan = Plan(
        lax.axis_size("dom"),
        lax.axis_size("rel"),
        prows,
        width,
        remainder.shape[0],
        relations.shape[0],
        lhs_rows.shape[2],
    )
    smem = pl.BlockSpec(memory_space=pltpu.SMEM)
    own, rem, rels = partitions.T, remainder.T, relations.T
    edges, wide = plan.edges, plan.bucket_edges
    grow = max(1, edges // 1024)
    buckets = plan.buckets
    afar = lambda d: d ^ (plan.bucket_mask(d % plan.rels, 0) * plan.rels)
    i16 = jnp.int16

    first = send(own, plan, afar)
    tables = [lhs_rows, lhs_rems, rel_ids, rhs_rows, rhs_rems, neg_rows, neg_rems]
    labels = call(
        functools.partial(lists_kernel, plan),
        [shape((buckets * plan.maxb, 8, LANES), jnp.int32)] * plan.rels,
        tables + [counts.reshape(-1)],
        "lists",
        1.0,
        60,
        in_specs=[VMEM] * 7 + [smem],
    )
    labels = [labels[0]] + [
        send(labels[mask], plan, lambda d, m=mask: d ^ m) for mask in range(1, plan.rels)
    ]
    (vec,) = call(
        functools.partial(relation_kernel, plan),
        [shape((width, edges), F32)],
        labels + [rels],
        "relation",
        6.0,
        24 * grow,
        scratch=[pltpu.VMEM((2 * width, plan.nrels), BF16)],
    )
    (first,) = call(
        relay_kernel,
        [shape((width, prows), BF16)],
        [first, vec],
        "relay",
        0.1,
        1,
        in_specs=[ANY, ANY],
        out_specs=[ANY],
        input_output_aliases={0: 0},
    )
    targets = [first] + [
        send(first, plan, lambda d, b=bucket: d ^ (b * plan.rels)) for bucket in range(1, buckets)
    ]
    lhs, cand_rem = call(
        functools.partial(source_rows_kernel, plan),
        [shape((width, edges), F32), shape((width, 2 * edges), BF16)],
        labels + [own, rem, first],
        "source_rows",
        1.5,
        12 * grow,
        in_specs=[VMEM] * (len(labels) + 2) + [ANY],
    )

    grad_shapes = lambda count: [
        shape((2 * width, count), BF16),
        shape((2 * width, count), BF16),
        shape((2 * width, 2 * count), BF16),
    ]
    grads = []
    for bucket in range(buckets - 1):
        grads += call(
            functools.partial(bucket_kernel, plan, bucket),
            grad_shapes(wide),
            labels + [targets[bucket], lhs, vec, cand_rem],
            "bucket",
            5.0,
            16 * grow,
        )
    last = buckets - 1
    chunk = (plan.half_chunks, plan.chunk_rows, LANES)
    bare = (plan.half_chunks, 8 * plan.chunk_units, LANES)
    table = [pltpu.VMEM((width, plan.half_lanes), F32)]
    made = call(
        functools.partial(last_kernel, plan),
        [shape(chunk, i16)] + grad_shapes(edges),
        labels + grads + [targets[last], lhs, vec, cand_rem],
        "last",
        12.0,
        24 * grow,
        in_specs=[VMEM] * len(labels) + [ANY] * len(grads) + [VMEM] * 4,
        out_specs=[VMEM] + [ANY] * 3,
        scratch=[pltpu.VMEM(held.shape, BF16) for held in grad_shapes(edges)]
        + table
        + [pltpu.SemaphoreType.DMA((len(grads) + 3,))],
    )
    away, grads = made[0], list(made[1:])
    core = send(away, plan, lambda d: d ^ 1)

    near, packed = [], []
    for bucket in range(1, buckets):
        packed += call(
            functools.partial(near_kernel, plan, bucket),
            [shape((width + 16, prows), i16)],
            labels + [grads[2], away],
            "near",
            1.5,
            12 * grow,
            in_specs=[VMEM] * (len(labels) + 1) + [ANY],
        )
        near.append(send(packed[-1], plan, lambda d, b=bucket: d ^ (b * plan.rels)))
    (keep,) = call(
        functools.partial(home_kernel, plan, len(packed) + 1),
        [shape(bare, F32)],
        labels + grads + packed + [away],
        "home",
        6.0,
        16 * grow,
        in_specs=[VMEM] * (len(labels) + 3) + [ANY] * (len(packed) + 1),
        scratch=table,
    )

    def shares(count, size):
        return [shape((count // size,) + bare[1:], F32)] + [
            shape((count // size,) + chunk[1:], i16)
        ] * (size - 1)

    def exchanged(values, masks):
        return [
            send(value, plan, lambda d, m=mask: d ^ m) for value, mask in zip(values, masks[1:])
        ]

    def after(kernel, outs, args, others, name, cost, limit=12):
        return call(
            kernel,
            outs,
            list(args) + list(others),
            name,
            cost,
            limit,
            in_specs=[VMEM] * len(args) + [ANY] * len(others),
        )

    size, later = len(plan.masks[1]), len(plan.masks[2])
    made = call(
        functools.partial(combine_kernel, plan, 2, False),
        shares(chunk[0], size),
        [keep, core],
        "combine_cores",
        1.0,
        12,
    )
    keep, arrived = made[0], exchanged(made[1:], plan.masks[1])
    (far,) = after(
        functools.partial(far_kernel, plan),
        [shape((width + 16, prows), i16)],
        labels + [grads[2]] + near,
        [keep],
        "far",
        2.0,
        12 * grow,
    )
    (source,) = after(
        functools.partial(source_kernel, plan),
        [shape((width, prows), F32)],
        labels + [grads[0]],
        [far],
        "source",
        1.5,
        12 * grow,
    )
    far = send(far, plan, afar)

    made = after(
        functools.partial(combine_kernel, plan, size, False),
        shares(chunk[0] // size, later),
        [keep] + arrived,
        [],
        "combine_xy",
        1.0,
    )
    keep, arrived = made[0], exchanged(made[1:], plan.masks[2])
    lanes = plan.part_lanes
    made = after(
        functools.partial(share_kernel, plan),
        [shape((width, lanes), F32)] + [shape((width + 16, lanes), i16)] * (plan.rels - 1),
        [source, far],
        [keep],
        "share",
        1.0,
    )
    mine = [made[0]] + exchanged(made[1:], range(plan.rels))

    (total,) = after(
        functools.partial(combine_kernel, plan, later, True),
        [shape((1,) + chunk[1:], i16)],
        [keep] + arrived,
        [],
        "combine_z",
        0.5,
    )
    pieces = [total] + exchanged([total] * (later - 1), plan.masks[2])
    (part,) = after(
        functools.partial(mine_kernel, plan),
        [shape((width + 16, lanes), i16)],
        mine,
        [total],
        "mine",
        0.5,
    )
    owners = [part] + exchanged([part] * (plan.rels - 1), range(plan.rels))
    block = jnp.concatenate(pieces, axis=0)
    pieces = [block] + exchanged([block] * (size - 1), plan.masks[1])
    (grad_partitions,) = after(
        functools.partial(part_out_kernel, plan),
        [shape((width, prows), F32)],
        owners,
        [block],
        "part_out",
        1.0,
    )
    if lanes % LANES:
        order = jnp.arange(plan.rels) ^ lax.axis_index("rel")
        split_lanes = grad_partitions.reshape(width, plan.rels, lanes)
        grad_partitions = jnp.take(split_lanes, order, axis=1).reshape(width, prows)

    others = [send(piece, plan, lambda d: d ^ 1) for piece in pieces]
    side = lax.axis_index("rel") & 1
    outs = [shape((width, plan.nrels), F32), shape((width, plan.rems), F32)]
    spec = lambda lanes: pl.BlockSpec((width, lanes), lambda i, half: (0, half[0]))
    made = []
    for turn, group in enumerate([pieces, others]):
        made = call(
            functools.partial(spread_kernel, plan, len(group)),
            outs,
            [(side ^ turn).reshape(1), *group, *made],
            "spread",
            2.0,
            16,
            grid_spec=pltpu.PrefetchScalarGridSpec(
                num_scalar_prefetch=1,
                grid=(1,),
                in_specs=[pl.BlockSpec(piece.shape, lambda i, half: (0, 0, 0)) for piece in group]
                + [ANY] * len(made),
                out_specs=[spec(plan.half_rel), spec(plan.half_rem)],
                scratch_shapes=[pltpu.VMEM(chunk, i16)],
            ),
            input_output_aliases={1 + len(group) + at: at for at in range(len(made))},
        )
    grad_relations, grad_remainder = made
    return grad_partitions.T, grad_remainder.T, grad_relations.T


def solution(mesh):
    edge = P("dom", None, "rel", None)
    in_specs = (P("dom", None), P(), P(), P("dom", None, "rel")) + (edge,) * 7
    out_specs = (P("dom", None), P(), P())
    return jax.shard_map(body, mesh=mesh, in_specs=in_specs, out_specs=out_specs, check_vma=False)
```

```python
import functools

import jax
import jax.numpy as jnp
from jax import lax
from jax.experimental import pallas as pl
from jax.experimental.pallas import tpu as pltpu
from jax.sharding import PartitionSpec as P

F32 = jnp.float32
BF16 = jnp.bfloat16
LANES = 128
REACH = 32766.0
NT = (((1,), (1,)), ((), ()))
NN = (((1,), (0,)), ((), ()))
TN = (((0,), (0,)), ((), ()))


def bits_of(count):
    return count.bit_length() - 1


def reverse_bits(value, count):
    out = 0
    for bit in range(bits_of(count)):
        out = out * 2 + ((value >> bit) & 1)
    return out


def split(value):
    high = value.astype(BF16)
    low = (value - high.astype(F32)).astype(BF16)
    return high, low


def dot(left, right, dims):
    return lax.dot_general(left, right, dims, preferred_element_type=F32)


def dot3(left, right, dims):
    left_high, left_low = split(left)
    right_high, right_low = split(right)
    return (
        dot(left_high, right_high, dims)
        + dot(left_high, right_low, dims)
        + dot(left_low, right_high, dims)
    )


def one_hot(ids, rows, base=0):
    place = lax.broadcasted_iota(jnp.int32, (rows, ids.shape[1]), 0)
    return jnp.where(place == ids - base, 1.0, 0.0).astype(BF16)


def store_split(ref, cols, value):
    high, low = split(value)
    depth = value.shape[0]
    ref[0:depth, cols] = high
    ref[depth : 2 * depth, cols] = low


def folded(value):
    depth = value.shape[0] // 2
    return value[:depth] + value[depth:]


def quantized(value):
    top = jnp.max(jnp.abs(value), axis=0, keepdims=True)
    exponent = jnp.floor(jnp.log2(jnp.maximum(top, 1e-30))) + 1.0
    return jnp.round(value * (REACH * jnp.exp2(-exponent))), exponent


def scale_of(exponent):
    return jnp.exp2(exponent) * (1.0 / REACH)


def to_words(value):
    return value.astype(jnp.int32).astype(jnp.int16)


def from_words(words):
    return words.astype(jnp.int32).astype(F32)


def pack_table(value, rows=None):
    scaled, exponent = quantized(value)
    spare = (rows or value.shape[0] + 16) - value.shape[0]
    tail = jnp.broadcast_to(exponent, (spare, value.shape[1]))
    return to_words(jnp.concatenate([scaled, tail], axis=0))


def unpack_table(words, depth=None):
    depth = depth or words.shape[0] - 16
    value = from_words(words)
    return value[:depth] * scale_of(value[depth : depth + 1])


class Plan:
    def __init__(self, doms, rels, prows, width, rems, nrels, maxb):
        self.doms, self.rels, self.maxb = doms, rels, maxb
        self.devices = doms * rels
        self.prows, self.width, self.rems, self.nrels = prows, width, rems, nrels
        self.buckets = doms // rels
        self.slots = rels * maxb
        self.bucket_edges = self.slots * LANES
        self.edges = self.buckets * self.bucket_edges
        self.part_lanes = prows // rels
        self.half_rel, self.half_rem = nrels // 2, rems // 2
        self.half_lanes = self.half_rel + self.half_rem
        self.subs = width // 8
        self.units = (self.half_lanes // LANES) * self.subs
        self.half_chunks = self.devices // 2
        self.chunk_units = -(-self.units // self.half_chunks)
        self.chunk_rows = (self.chunk_units + 2) // 2 * 16
        rel_bits = bits_of(rels)
        all_bits = rel_bits + bits_of(doms)
        self.groups = [
            [0],
            list(range(1, rel_bits + 1)),
            list(range(rel_bits + 1, all_bits)),
        ]
        self.masks = [self.group_masks(bits) for bits in self.groups]
        order = [bit for group in self.groups for bit in reversed(group)]
        self.place = {bit: all_bits - 1 - at for at, bit in enumerate(order)}

    @staticmethod
    def group_masks(bits):
        masks = []
        for index in range(2 ** len(bits)):
            masks.append(sum(((index >> at) & 1) << bit for at, bit in enumerate(bits)))
        return masks

    def row(self, labels, bucket, kinds, first, count):
        rows = []
        for slot in range(first, first + count):
            mask, turn = divmod(slot, self.maxb)
            block = labels[bucket * self.rels + mask]
            rows += [block[turn, kind : kind + 1, :] for kind in kinds]
        return jnp.concatenate(rows, axis=1) if len(rows) > 1 else rows[0]

    def whole_row(self, labels, kinds):
        rows = [
            self.row(labels, bucket, kinds, 0, self.slots) for bucket in range(self.buckets)
        ]
        return jnp.concatenate(rows, axis=1) if len(rows) > 1 else rows[0]

    def me(self):
        return lax.axis_index("dom") * self.rels + lax.axis_index("rel")

    def low_chunk(self, device):
        return device >> 1

    def position(self, chunk, me):
        relative = chunk ^ (me >> 1)
        out = 0
        for bit, at in self.place.items():
            if bit:
                out = out + (((relative >> (bit - 1)) & 1) << at)
        return out

    def target_mask(self, rel):
        return reverse_bits(rel, self.rels) * self.buckets

    def dynamic_mask(self, rel):
        out = 0
        width = bits_of(self.rels)
        for bit in range(width):
            out = out + (((rel >> bit) & 1) << (width - 1 - bit))
        return out * self.buckets


def send(value, plan, target):
    pairs = [(device, target(device)) for device in range(plan.devices)]
    return lax.ppermute(value, ("dom", "rel"), pairs)


def lists_kernel(plan, *refs):
    tables, counts, outs = refs[:7], refs[7], refs[8:]
    source = lax.axis_index("dom")
    rel = lax.axis_index("rel")
    for at, out in enumerate(outs):
        bucket, mask = divmod(at, plan.rels)
        target = source ^ bucket ^ plan.dynamic_mask(rel ^ mask)
        stop = lax.rem(source - target + plan.doms, plan.doms)
        for turn in range(plan.maxb):
            for kind, table in enumerate(tables):
                out[turn, kind : kind + 1, :] = table[0, stop, turn : turn + 1, :]
            live = jnp.where(turn < counts[stop], 1, 0)
            out[turn, 7:8, :] = jnp.full((1, LANES), live, jnp.int32)


def split_kernel(relations, out):
    depth = relations.shape[0]
    high, low = split(relations[...])
    out[0:depth, :] = high
    out[depth : 2 * depth, :] = low


def relation_kernel(plan, *refs):
    labels = refs[: plan.rels]
    relations, out = refs[plan.rels], refs[-1]
    for pair in range(0, plan.slots, 2):
        count = min(2, plan.slots - pair)
        start = pair * LANES
        ids = plan.row(labels, 0, (2,), pair, count)
        out[:, start : start + count * LANES] = folded(
            dot(relations[...], one_hot(ids, plan.nrels), NN)
        )


def rows_kernel(plan, *refs):
    labels = refs[: plan.rels]
    own, rem = refs[plan.rels : plan.rels + 2]
    lhs_out, rem_out = refs[-2:]
    for pair in range(0, plan.slots, 2):
        count = min(2, plan.slots - pair)
        row = lambda *kinds: plan.row(labels, 0, kinds, pair, count)
        start = pair * LANES
        end = start + count * LANES
        lhs_out[:, start:end] = dot(own[...], one_hot(row(0), plan.prows), NN) + dot(
            rem[...], one_hot(row(1), plan.rems), NN
        )
        rem_out[:, 2 * start : 2 * end] = dot(
            rem[...], one_hot(row(4, 6), plan.rems), NN
        ).astype(BF16)


def conjugate_parts(grad, other):
    half = grad.shape[0] // 2
    grad_re, grad_im = grad[:half], grad[half:]
    other_re, other_im = other[:half], other[half:]
    return jnp.concatenate(
        [grad_re * other_re + grad_im * other_im, grad_im * other_re - grad_re * other_im], 0
    )


def complex_product(left, right):
    half = left.shape[0] // 2
    left_re, left_im = left[:half], left[half:]
    right_re, right_im = right[:half], right[half:]
    return jnp.concatenate(
        [left_re * right_re - left_im * right_im, left_re * right_im + left_im * right_re], 0
    )


def bucket_grads(plan, labels, target, lhs_in, rel_in, rem_in, lhs_out, rel_out, cand_out, base):
    total = 2 * LANES
    edge = lax.broadcasted_iota(jnp.int32, (LANES, total), 0)
    column = lax.broadcasted_iota(jnp.int32, (LANES, total), 1)
    keep = jnp.where(edge == column, 0.0, 1.0 / total)
    for slot in range(plan.slots):
        cols = slice(slot * LANES, (slot + 1) * LANES)
        wide = slice(slot * total, (slot + 1) * total)
        ids = plan.row(labels, 0, (3, 5), slot, 1)
        cand = dot(target[...], one_hot(ids, plan.prows), NN) + rem_in[:, wide].astype(F32)
        rhs = cand[:, :LANES]
        lhs, vec = lhs_in[:, cols], rel_in[:, cols]
        u_vec = complex_product(lhs, vec)
        live = plan.row(labels, 0, (7,), slot, 1).astype(F32)
        positive = jnp.sum(u_vec * rhs, axis=0, keepdims=True)
        negative = dot3(u_vec, cand, TN)
        grad_pos = -jax.nn.sigmoid(-positive) * live
        grad_neg = jax.nn.sigmoid(negative) * keep * live[0:1, 0:1]
        grad_u = grad_pos * rhs + dot3(cand, grad_neg, NT)
        from_neg = dot3(u_vec, grad_neg, NN)
        grad_cand = jnp.concatenate(
            [from_neg[:, :LANES] + grad_pos * u_vec, from_neg[:, LANES:]], axis=1
        )
        at = base + slot
        cols = slice(at * LANES, (at + 1) * LANES)
        wide = slice(at * total, (at + 1) * total)
        store_split(lhs_out, cols, conjugate_parts(grad_u, vec))
        store_split(rel_out, cols, conjugate_parts(grad_u, lhs))
        store_split(cand_out, wide, grad_cand)


def bucket_kernel(plan, *refs):
    bucket_grads(plan, refs[: plan.rels], *refs[plan.rels :], 0)


def last_kernel(plan, *refs):
    count = plan.rels * plan.buckets
    labels = refs[:count]
    before = refs[count : count + 3 * (plan.buckets - 1)]
    refs = refs[count + 3 * (plan.buckets - 1) :]
    target, lhs_in, rel_in, rem_in = refs[:4]
    away, outs, helds, table, sems = refs[4], refs[5:8], refs[8:11], refs[11], refs[12]
    edges = plan.bucket_edges
    loads = []
    for at, ref in enumerate(before):
        wide = edges * (2 if at % 3 == 2 else 1)
        start = (at // 3) * wide
        loads.append(
            pltpu.make_async_copy(ref, helds[at % 3].at[:, start : start + wide], sems.at[at])
        )
        loads[-1].start()
    base = (plan.buckets - 1) * plan.slots
    own_labels = labels[count - plan.rels :]
    bucket_grads(plan, own_labels, target, lhs_in, rel_in, rem_in, *helds, base)
    for load in loads:
        load.wait()
    stores = [
        pltpu.make_async_copy(held, out, sems.at[len(loads) + at])
        for at, (held, out) in enumerate(zip(helds, outs))
    ]
    for store in stores:
        store.start()
    reduce_half(plan, True, labels, helds, table, away)
    for store in stores:
        store.wait()


def reduce_half(plan, away, labels, grads, table, out):
    lhs_grads, rel_grads, cand_grads = grads
    me = plan.me()
    half = (me & 1) ^ (1 if away else 0)
    step = 2 * LANES if plan.half_rel % (2 * LANES) == 0 else LANES
    ids = plan.whole_row(labels, (2,)) - half * plan.half_rel
    for start in range(0, plan.half_rel, step):
        hot = one_hot(ids, step, start)
        table[:, start : start + step] = folded(dot(rel_grads[...], hot, NT))
    base = half * plan.half_rem
    first = one_hot(plan.whole_row(labels, (1,)), plan.half_rem, base)
    second = one_hot(plan.whole_row(labels, (4, 6)), plan.half_rem, base)
    table[:, plan.half_rel :] = folded(
        dot(lhs_grads[...], first, NT) + dot(cand_grads[...], second, NT)
    )
    for chunk in range(plan.half_chunks):
        parts = []
        for unit in range(chunk * plan.chunk_units, (chunk + 1) * plan.chunk_units):
            if unit < plan.units:
                lane, sub = divmod(unit, plan.subs)
                parts.append(table[8 * sub : 8 * sub + 8, lane * LANES : (lane + 1) * LANES])
            else:
                parts.append(jnp.zeros((8, LANES), F32))
        value = jnp.concatenate(parts, axis=0)
        out[plan.position(chunk, me)] = pack_table(value, plan.chunk_rows) if away else value


def rows_sum(plan, ids, grads):
    shift = lax.axis_index("rel") * plan.part_lanes
    return folded(dot(grads, one_hot(ids ^ shift, plan.prows), NT))


def target_kernel(plan, *refs):
    count = plan.rels * plan.buckets
    ids = plan.whole_row(refs[:count], (3, 5))
    refs[-1][...] = pack_table(rows_sum(plan, ids, refs[count][...]))


def home_kernel(plan, *refs):
    count = plan.rels * plan.buckets
    keep, table = refs[-2:]
    reduce_half(plan, False, refs[:count], refs[count : count + 3], table, keep)


def source_sum(plan, labels, grads, bucket):
    start = bucket * plan.bucket_edges
    ids = plan.row(labels, 0, (0,), 0, plan.slots)
    return rows_sum(plan, ids, grads[:, start : start + plan.bucket_edges])


def to_shares(plan, value, outs):
    lanes = plan.part_lanes
    outs[0][...] = value[:, :lanes]
    for at, out in enumerate(outs[1:], 1):
        out[...] = pack_table(value[:, at * lanes : (at + 1) * lanes])


def source_kernel(plan, bucket, *refs):
    value = source_sum(plan, refs[: plan.rels], refs[plan.rels], bucket)
    to_shares(plan, value, refs[-plan.rels :])


def share_kernel(plan, *refs):
    value = source_sum(plan, refs[: plan.rels], refs[plan.rels], 0)
    to_shares(plan, value + unpack_table(refs[plan.rels + 1][...]), refs[-plan.rels :])


def add_kernel(count, *refs):
    value = refs[0][...]
    for ref in refs[1:count]:
        value = value + unpack_table(ref[...])
    refs[-1][...] = pack_table(value)


def combine_kernel(plan, group, last, after, *refs):
    keep, arrived, outs = refs[0], refs[1:group], refs[group + after :]
    count, depth = keep.shape[0], keep.shape[1]
    share = count // len(outs)
    for at in range(count):
        value = keep[at]
        for ref in arrived:
            value = value + unpack_table(ref[at], depth)
        which, place = divmod(at, share)
        packed = which or last
        outs[which][place] = pack_table(value, plan.chunk_rows) if packed else value


def stack_kernel(*refs):
    out = refs[-1]
    for at in range(out.shape[0]):
        out[at] = refs[at][0]


def spread_kernel(plan, count, side, *refs):
    pieces, (rel_out, rem_out, held) = refs[:count], refs[-3:]
    at = 0
    for piece in pieces:
        held[at : at + piece.shape[0]] = piece[...]
        at += piece.shape[0]
    me = plan.me()
    for chunk in range(plan.half_chunks):
        value = unpack_table(held[plan.position(chunk, me)], 8 * plan.chunk_units)
        for index in range(plan.chunk_units):
            unit = chunk * plan.chunk_units + index
            if unit >= plan.units:
                break
            lane, sub = divmod(unit, plan.subs)
            lane = lane * LANES
            rows = slice(8 * sub, 8 * sub + 8)
            block = value[8 * index : 8 * index + 8]
            if lane < plan.half_rel:
                rel_out[rows, lane : lane + LANES] = block
            else:
                lane -= plan.half_rel
                rem_out[rows, lane : lane + LANES] = block


def relay_kernel(*refs):
    pass


def part_out_kernel(plan, *refs):
    out = refs[-1]
    rel = lax.axis_index("rel")
    lanes = plan.part_lanes
    for mask, ref in enumerate(refs[: plan.rels]):
        if lanes % LANES:
            out[:, mask * lanes : (mask + 1) * lanes] = unpack_table(ref[...])
        else:
            start = pl.multiple_of((rel ^ mask) * lanes, lanes)
            out[:, pl.ds(start, lanes)] = unpack_table(ref[...])


def shape(extent, kind):
    return jax.ShapeDtypeStruct(extent, kind)


VMEM = pl.BlockSpec(memory_space=pltpu.VMEM)
ANY = pl.BlockSpec(memory_space=pl.ANY)


def call(kernel, outs, args, name, cost, limit, scratch=(), in_specs=None, out_specs=None, **more):
    work = pl.CostEstimate(flops=int(cost * 1e9), bytes_accessed=int(cost * 3e6), transcendentals=0)
    if "grid_spec" not in more:
        more["in_specs"] = in_specs or [VMEM] * len(args)
        more["out_specs"] = out_specs or [VMEM] * len(outs)
        more["scratch_shapes"] = list(scratch)
    return pl.pallas_call(
        kernel,
        out_shape=outs,
        compiler_params=pltpu.CompilerParams(vmem_limit_bytes=int(limit * 2**20)),
        cost_estimate=work,
        name=name,
        **more,
    )(*args)


def body(
    partitions,
    remainder,
    relations,
    counts,
    lhs_rows,
    lhs_rems,
    rel_ids,
    rhs_rows,
    rhs_rems,
    neg_rows,
    neg_rems,
):
    prows, width = partitions.shape
    plan = Plan(
        lax.axis_size("dom"),
        lax.axis_size("rel"),
        prows,
        width,
        remainder.shape[0],
        relations.shape[0],
        lhs_rows.shape[2],
    )
    smem = pl.BlockSpec(memory_space=pltpu.SMEM)
    own, rem, rels = partitions.T, remainder.T, relations.T
    edges, wide = plan.edges, plan.bucket_edges
    grow = max(1, edges // 1024)
    buckets = plan.buckets
    afar = lambda d: d ^ (plan.target_mask(d % plan.rels) * plan.rels)
    i16 = jnp.int16

    def after(kernel, outs, args, others, name, cost, limit=12, **more):
        return call(
            kernel,
            outs,
            list(args) + list(others),
            name,
            cost,
            limit,
            in_specs=[VMEM] * len(args) + [ANY] * len(others),
            **more,
        )

    target = send(own, plan, afar)
    sources = [own] + [
        send(own, plan, lambda d, b=bucket: d ^ (b * plan.rels)) for bucket in range(1, buckets)
    ]
    tables = [lhs_rows, lhs_rems, rel_ids, rhs_rows, rhs_rems, neg_rows, neg_rems]
    labels = call(
        functools.partial(lists_kernel, plan),
        [shape((plan.maxb, 8, LANES), jnp.int32)] * (plan.rels * buckets),
        tables + [counts.reshape(-1)],
        "lists",
        0.5,
        60,
        in_specs=[VMEM] * 7 + [smem],
    )
    labels = [labels[0]] + [
        send(labels[mask], plan, lambda d, m=mask: d ^ m) for mask in range(1, len(labels))
    ]
    labels_of = lambda bucket: labels[bucket * plan.rels : (bucket + 1) * plan.rels]
    (rel_split,) = call(
        split_kernel, [shape((2 * width, plan.nrels), BF16)], [rels], "rel_split", 2.0, 50
    )

    grad_shapes = lambda count: [
        shape((2 * width, count), BF16),
        shape((2 * width, count), BF16),
        shape((2 * width, 2 * count), BF16),
    ]
    inputs = []
    for bucket in range(buckets):
        (vec,) = call(
            functools.partial(relation_kernel, plan),
            [shape((width, wide), F32)],
            labels_of(bucket) + [rel_split],
            "relation",
            2.0,
            16 * grow,
        )
        lhs, cand_rem = call(
            functools.partial(rows_kernel, plan),
            [shape((width, wide), F32), shape((width, 2 * wide), BF16)],
            labels_of(bucket) + [sources[bucket], rem],
            "rows",
            0.7,
            12 * grow,
        )
        inputs.append([lhs, vec, cand_rem])
    grads = []
    for bucket in range(buckets - 1):
        grads += call(
            functools.partial(bucket_kernel, plan),
            grad_shapes(wide),
            labels_of(bucket) + [target] + inputs[bucket],
            "bucket",
            4.0,
            16 * grow,
        )
    chunk = (plan.half_chunks, plan.chunk_rows, LANES)
    bare = (plan.half_chunks, 8 * plan.chunk_units, LANES)
    table = [pltpu.VMEM((width, plan.half_lanes), F32)]
    made = call(
        functools.partial(last_kernel, plan),
        [shape(chunk, i16)] + grad_shapes(edges),
        labels + grads + [target] + inputs[-1],
        "last",
        9.0,
        24 * grow,
        in_specs=[VMEM] * len(labels) + [ANY] * len(grads) + [VMEM] * 4,
        out_specs=[VMEM] + [ANY] * 3,
        scratch=[pltpu.VMEM(held.shape, BF16) for held in grad_shapes(edges)]
        + table
        + [pltpu.SemaphoreType.DMA((len(grads) + 3,))],
    )
    away, grads = made[0], list(made[1:])
    core = send(away, plan, lambda d: d ^ 1)

    (far,) = after(
        functools.partial(target_kernel, plan),
        [shape((width + 16, prows), i16)],
        labels + [grads[2]],
        [away],
        "target",
        1.8,
        16 * grow,
    )
    (keep,) = after(
        functools.partial(home_kernel, plan),
        [shape(bare, F32)],
        labels + grads,
        [far],
        "home",
        4.0,
        16 * grow,
        scratch=table,
    )
    far = send(far, plan, afar)

    def shares(count, size):
        return [shape((count // size,) + bare[1:], F32)] + [
            shape((count // size,) + chunk[1:], i16)
        ] * (size - 1)

    def exchanged(values, masks):
        return [
            send(value, plan, lambda d, m=mask: d ^ m) for value, mask in zip(values, masks[1:])
        ]

    size, later = len(plan.masks[1]), len(plan.masks[2])
    made = call(
        functools.partial(combine_kernel, plan, 2, False, 0),
        shares(chunk[0], size),
        [keep, core],
        "combine_cores",
        1.0,
        12,
    )
    keep, arrived = made[0], exchanged(made[1:], plan.masks[1])
    lanes = plan.part_lanes
    share_shapes = [shape((width, lanes), F32)] + [shape((width + 16, lanes), i16)] * (
        plan.rels - 1
    )
    others = []
    for bucket in range(1, buckets):
        made = after(
            functools.partial(source_kernel, plan, bucket),
            share_shapes,
            labels_of(bucket) + [grads[0]],
            [keep],
            "source",
            1.0,
        )
        others.append([made[0]] + exchanged(made[1:], range(plan.rels)))

    made = after(
        functools.partial(combine_kernel, plan, size, False, len(others)),
        shares(chunk[0] // size, later),
        [keep] + arrived,
        [other[0] for other in others],
        "combine_xy",
        1.0,
    )
    keep, arrived = made[0], exchanged(made[1:], plan.masks[2])
    made = after(
        functools.partial(share_kernel, plan),
        share_shapes,
        labels_of(0) + [grads[0], far],
        [keep],
        "share",
        1.0,
    )
    mine = [made[0]] + exchanged(made[1:], range(plan.rels))
    for bucket in range(1, buckets):
        (other,) = after(
            functools.partial(add_kernel, plan.rels),
            [shape((width + 16, lanes), i16)],
            others[bucket - 1],
            [made[0]],
            "other",
            0.3,
        )
        mine.append(send(other, plan, lambda d, b=bucket: d ^ (b * plan.rels)))

    (total,) = after(
        functools.partial(combine_kernel, plan, later, True, 1),
        [shape((1,) + chunk[1:], i16)],
        [keep] + arrived,
        [mine[0]],
        "combine_z",
        0.5,
    )
    pieces = [total] + exchanged([total] * (later - 1), plan.masks[2])
    (part,) = after(
        functools.partial(add_kernel, len(mine)),
        [shape((width + 16, lanes), i16)],
        mine,
        [total],
        "mine",
        0.5,
    )
    owners = [part] + exchanged([part] * (plan.rels - 1), range(plan.rels))
    (block,) = after(
        stack_kernel,
        [shape((len(pieces),) + chunk[1:], i16)],
        pieces,
        [part],
        "stack",
        0.3,
    )
    pieces = [block] + exchanged([block] * (size - 1), plan.masks[1])
    (grad_partitions,) = after(
        functools.partial(part_out_kernel, plan),
        [shape((width, prows), F32)],
        owners,
        [block],
        "part_out",
        1.0,
    )
    if lanes % LANES:
        order = jnp.arange(plan.rels) ^ lax.axis_index("rel")
        split_lanes = grad_partitions.reshape(width, plan.rels, lanes)
        grad_partitions = jnp.take(split_lanes, order, axis=1).reshape(width, prows)

    others = [send(piece, plan, lambda d: d ^ 1) for piece in pieces]
    side = lax.axis_index("rel") & 1
    outs = [shape((width, plan.nrels), F32), shape((width, plan.rems), F32)]
    spec = lambda lanes: pl.BlockSpec((width, lanes), lambda i, half: (0, half[0]))
    made = []
    for turn, group in enumerate([pieces, others]):
        made = call(
            functools.partial(spread_kernel, plan, len(group)),
            outs,
            [(side ^ turn).reshape(1), *group, *made],
            "spread",
            2.0,
            16,
            grid_spec=pltpu.PrefetchScalarGridSpec(
                num_scalar_prefetch=1,
                grid=(1,),
                in_specs=[pl.BlockSpec(piece.shape, lambda i, half: (0, 0, 0)) for piece in group]
                + [ANY] * len(made),
                out_specs=[spec(plan.half_rel), spec(plan.half_rem)],
                scratch_shapes=[pltpu.VMEM(chunk, i16)],
            ),
            input_output_aliases={1 + len(group) + at: at for at in range(len(made))},
        )
    grad_relations, grad_remainder = made
    return grad_partitions.T, grad_remainder.T, grad_relations.T


def solution(mesh):
    edge = P("dom", None, "rel", None)
    in_specs = (P("dom", None), P(), P(), P("dom", None, "rel")) + (edge,) * 7
    out_specs = (P("dom", None), P(), P())
    return jax.shard_map(body, mesh=mesh, in_specs=in_specs, out_specs=out_specs, check_vma=False)
```

```python
import functools

import jax
import jax.numpy as jnp
from jax import lax
from jax.experimental import pallas as pl
from jax.experimental.pallas import tpu as pltpu
from jax.sharding import PartitionSpec as P

F32 = jnp.float32
BF16 = jnp.bfloat16
LANES = 128
REACH = 32766.0
NT = (((1,), (1,)), ((), ()))
NN = (((1,), (0,)), ((), ()))
TN = (((0,), (0,)), ((), ()))


def bits_of(count):
    return count.bit_length() - 1


def reverse_bits(value, count):
    out = 0
    for bit in range(bits_of(count)):
        out = out * 2 + ((value >> bit) & 1)
    return out


def split(value):
    high = value.astype(BF16)
    low = (value - high.astype(F32)).astype(BF16)
    return high, low


def dot(left, right, dims):
    return lax.dot_general(left, right, dims, preferred_element_type=F32)


def dot3(left, right, dims):
    left_high, left_low = split(left)
    right_high, right_low = split(right)
    return (
        dot(left_high, right_high, dims)
        + dot(left_high, right_low, dims)
        + dot(left_low, right_high, dims)
    )


def one_hot(ids, rows, base=0):
    place = lax.broadcasted_iota(jnp.int32, (rows, ids.shape[1]), 0)
    return jnp.where(place == ids - base, 1.0, 0.0).astype(BF16)


def store_split(ref, cols, value):
    high, low = split(value)
    depth = value.shape[0]
    ref[0:depth, cols] = high
    ref[depth : 2 * depth, cols] = low


def folded(value):
    depth = value.shape[0] // 2
    return value[:depth] + value[depth:]


def quantized(value):
    top = jnp.max(jnp.abs(value), axis=0, keepdims=True)
    exponent = jnp.floor(jnp.log2(jnp.maximum(top, 1e-30))) + 1.0
    return jnp.round(value * (REACH * jnp.exp2(-exponent))), exponent


def scale_of(exponent):
    return jnp.exp2(exponent) * (1.0 / REACH)


def to_words(value):
    return value.astype(jnp.int32).astype(jnp.int16)


def from_words(words):
    return words.astype(jnp.int32).astype(F32)


def pack_table(value, rows=None):
    scaled, exponent = quantized(value)
    spare = (rows or value.shape[0] + 16) - value.shape[0]
    tail = jnp.broadcast_to(exponent, (spare, value.shape[1]))
    return to_words(jnp.concatenate([scaled, tail], axis=0))


def unpack_table(words, depth=None):
    depth = depth or words.shape[0] - 16
    value = from_words(words)
    return value[:depth] * scale_of(value[depth : depth + 1])


class Part:
    def __init__(self, plan, units, groups):
        self.units = units
        self.rows = (units + 2) // 2 * 16
        self.masks = [self.group_masks(bits) for bits in groups]
        order = [bit for group in groups for bit in reversed(group)]
        self.place = {bit: len(order) - 1 - at for at, bit in enumerate(order)}
        self.packed = (plan.half_chunks, self.rows, LANES)
        self.bare = (plan.half_chunks, 8 * units, LANES)

    @staticmethod
    def group_masks(bits):
        masks = []
        for index in range(2 ** len(bits)):
            masks.append(sum(((index >> at) & 1) << bit for at, bit in enumerate(bits)))
        return masks

    def position(self, chunk, me):
        relative = chunk ^ (me >> 1)
        out = 0
        for bit, at in self.place.items():
            out = out + (((relative >> (bit - 1)) & 1) << at)
        return out

    def shares(self, count, size):
        count = count // size
        return [shape((count,) + self.bare[1:], F32)] + [
            shape((count,) + self.packed[1:], jnp.int16)
        ] * (size - 1)


class Plan:
    def __init__(self, doms, rels, prows, width, rems, nrels, maxb):
        self.doms, self.rels, self.maxb = doms, rels, maxb
        self.devices = doms * rels
        self.prows, self.width, self.rems, self.nrels = prows, width, rems, nrels
        self.buckets = doms // rels
        self.slots = rels * maxb
        self.bucket_edges = self.slots * LANES
        self.edges = self.buckets * self.bucket_edges
        self.part_lanes = prows // rels
        self.half_rel, self.half_rem = nrels // 2, rems // 2
        self.half_lanes = self.half_rel + self.half_rem
        self.subs = width // 8
        self.units = (self.half_lanes // LANES) * self.subs
        self.half_chunks = self.devices // 2
        self.chunk_units = -(-self.units // self.half_chunks)
        rel_bits = bits_of(rels)
        all_bits = rel_bits + bits_of(doms)
        near = list(range(1, rel_bits + 1))
        far = list(range(rel_bits + 1, all_bits))
        self.parts = [Part(self, self.chunk_units, [near, far])]

    def chunk_blocks(self, chunk, part):
        first = chunk * self.chunk_units + (self.parts[0].units if part else 0)
        blocks = []
        for unit in range(first, first + self.parts[part].units):
            lane, sub = divmod(unit, self.subs)
            blocks.append((lane * LANES, 8 * sub) if unit < self.units else None)
        return blocks

    def row(self, labels, bucket, kinds, first, count):
        rows = []
        for slot in range(first, first + count):
            rows += [labels[bucket][slot, kind : kind + 1, :] for kind in kinds]
        return jnp.concatenate(rows, axis=1) if len(rows) > 1 else rows[0]

    def whole_row(self, labels, kinds):
        rows = [
            self.row(labels, bucket, kinds, 0, self.slots) for bucket in range(self.buckets)
        ]
        return jnp.concatenate(rows, axis=1) if len(rows) > 1 else rows[0]

    def me(self):
        return lax.axis_index("dom") * self.rels + lax.axis_index("rel")

    def target_mask(self, rel):
        return reverse_bits(rel, self.rels) * self.buckets

    def dynamic_mask(self, rel):
        out = 0
        width = bits_of(self.rels)
        for bit in range(width):
            out = out + (((rel >> bit) & 1) << (width - 1 - bit))
        return out * self.buckets


def send(value, plan, target):
    pairs = [(device, target(device)) for device in range(plan.devices)]
    return lax.ppermute(value, ("dom", "rel"), pairs)


def lists_kernel(plan, *refs):
    tables, counts, outs = refs[:7], refs[7], refs[8:]
    source = lax.axis_index("dom")
    rel = lax.axis_index("rel")
    for mask, out in enumerate(outs):
        for bucket in range(plan.buckets):
            target = source ^ bucket ^ plan.dynamic_mask(rel ^ mask)
            stop = lax.rem(source - target + plan.doms, plan.doms)
            for turn in range(plan.maxb):
                at = bucket * plan.maxb + turn
                for kind, table in enumerate(tables):
                    out[at, kind : kind + 1, :] = table[0, stop, turn : turn + 1, :]
                live = jnp.where(turn < counts[stop], 1, 0)
                out[at, 7:8, :] = jnp.full((1, LANES), live, jnp.int32)


def forward_kernel(plan, *refs):
    lists, outs = refs[: plan.rels], refs[plan.rels :]
    for bucket, out in enumerate(outs):
        for mask, ref in enumerate(lists):
            for turn in range(plan.maxb):
                out[mask * plan.maxb + turn] = ref[bucket * plan.maxb + turn]


def split_kernel(relations, out):
    depth = relations.shape[0]
    high, low = split(relations[...])
    out[0:depth, :] = high
    out[depth : 2 * depth, :] = low


def relation_kernel(plan, *refs):
    labels, relations, out = refs[:1], refs[1], refs[-1]
    for pair in range(0, plan.slots, 2):
        count = min(2, plan.slots - pair)
        start = pair * LANES
        ids = plan.row(labels, 0, (2,), pair, count)
        out[:, start : start + count * LANES] = folded(
            dot(relations[...], one_hot(ids, plan.nrels), NN)
        )


def rows_kernel(plan, *refs):
    labels, (own, rem) = refs[:1], refs[1:3]
    lhs_out, rem_out = refs[-2:]
    for pair in range(0, plan.slots, 2):
        count = min(2, plan.slots - pair)
        row = lambda *kinds: plan.row(labels, 0, kinds, pair, count)
        start = pair * LANES
        end = start + count * LANES
        lhs_out[:, start:end] = dot(own[...], one_hot(row(0), plan.prows), NN) + dot(
            rem[...], one_hot(row(1), plan.rems), NN
        )
        rem_out[:, 2 * start : 2 * end] = dot(
            rem[...], one_hot(row(4, 6), plan.rems), NN
        ).astype(BF16)


def conjugate_parts(grad, other):
    half = grad.shape[0] // 2
    grad_re, grad_im = grad[:half], grad[half:]
    other_re, other_im = other[:half], other[half:]
    return jnp.concatenate(
        [grad_re * other_re + grad_im * other_im, grad_im * other_re - grad_re * other_im], 0
    )


def complex_product(left, right):
    half = left.shape[0] // 2
    left_re, left_im = left[:half], left[half:]
    right_re, right_im = right[:half], right[half:]
    return jnp.concatenate(
        [left_re * right_re - left_im * right_im, left_re * right_im + left_im * right_re], 0
    )


def bucket_grads(plan, labels, target, lhs_in, rel_in, rem_in, lhs_out, rel_out, cand_out, base):
    total = 2 * LANES
    edge = lax.broadcasted_iota(jnp.int32, (LANES, total), 0)
    column = lax.broadcasted_iota(jnp.int32, (LANES, total), 1)
    keep = jnp.where(edge == column, 0.0, 1.0 / total)
    for slot in range(plan.slots):
        cols = slice(slot * LANES, (slot + 1) * LANES)
        wide = slice(slot * total, (slot + 1) * total)
        ids = plan.row(labels, 0, (3, 5), slot, 1)
        cand = dot(target[...], one_hot(ids, plan.prows), NN) + rem_in[:, wide].astype(F32)
        rhs = cand[:, :LANES]
        lhs, vec = lhs_in[:, cols], rel_in[:, cols]
        u_vec = complex_product(lhs, vec)
        live = plan.row(labels, 0, (7,), slot, 1).astype(F32)
        positive = jnp.sum(u_vec * rhs, axis=0, keepdims=True)
        negative = dot3(u_vec, cand, TN)
        grad_pos = -jax.nn.sigmoid(-positive) * live
        grad_neg = jax.nn.sigmoid(negative) * keep * live[0:1, 0:1]
        grad_u = grad_pos * rhs + dot3(cand, grad_neg, NT)
        from_neg = dot3(u_vec, grad_neg, NN)
        grad_cand = jnp.concatenate(
            [from_neg[:, :LANES] + grad_pos * u_vec, from_neg[:, LANES:]], axis=1
        )
        at = base + slot
        cols = slice(at * LANES, (at + 1) * LANES)
        wide = slice(at * total, (at + 1) * total)
        store_split(lhs_out, cols, conjugate_parts(grad_u, vec))
        store_split(rel_out, cols, conjugate_parts(grad_u, lhs))
        store_split(cand_out, wide, grad_cand)


def bucket_kernel(plan, *refs):
    bucket_grads(plan, refs[:1], *refs[1:], 0)


def last_kernel(plan, *refs):
    count = plan.buckets
    labels = refs[:count]
    before = refs[count : count + 3 * (plan.buckets - 1)]
    refs = refs[count + 3 * (plan.buckets - 1) :]
    target, lhs_in, rel_in, rem_in = refs[:4]
    away, refs = refs[4 : 4 + len(plan.parts)], refs[4 + len(plan.parts) :]
    outs, helds, table, sems = refs[:3], refs[3:6], refs[6], refs[7]
    edges = plan.bucket_edges
    loads = []
    for at, ref in enumerate(before):
        wide = edges * (2 if at % 3 == 2 else 1)
        start = (at // 3) * wide
        loads.append(
            pltpu.make_async_copy(ref, helds[at % 3].at[:, start : start + wide], sems.at[at])
        )
        loads[-1].start()
    base = (plan.buckets - 1) * plan.slots
    own_labels = labels[-1:]
    bucket_grads(plan, own_labels, target, lhs_in, rel_in, rem_in, *helds, base)
    for load in loads:
        load.wait()
    stores = [
        pltpu.make_async_copy(held, out, sems.at[len(loads) + at])
        for at, (held, out) in enumerate(zip(helds, outs))
    ]
    for store in stores:
        store.start()
    reduce_half(plan, True, labels, helds, table, away)
    for store in stores:
        store.wait()


def reduce_half(plan, away, labels, grads, table, outs):
    lhs_grads, rel_grads, cand_grads = grads
    me = plan.me()
    half = (me & 1) ^ (1 if away else 0)
    step = 2 * LANES if plan.half_rel % (2 * LANES) == 0 else LANES
    ids = plan.whole_row(labels, (2,)) - half * plan.half_rel
    for start in range(0, plan.half_rel, step):
        hot = one_hot(ids, step, start)
        table[:, start : start + step] = folded(dot(rel_grads[...], hot, NT))
    base = half * plan.half_rem
    first = one_hot(plan.whole_row(labels, (1,)), plan.half_rem, base)
    second = one_hot(plan.whole_row(labels, (4, 6)), plan.half_rem, base)
    table[:, plan.half_rel :] = folded(
        dot(lhs_grads[...], first, NT) + dot(cand_grads[...], second, NT)
    )
    for chunk in range(plan.half_chunks):
        for which, (part, out) in enumerate(zip(plan.parts, outs)):
            value = jnp.concatenate(
                [
                    table[block[1] : block[1] + 8, block[0] : block[0] + LANES]
                    if block
                    else jnp.zeros((8, LANES), F32)
                    for block in plan.chunk_blocks(chunk, which)
                ],
                axis=0,
            )
            out[part.position(chunk, me)] = pack_table(value, part.rows) if away else value


def rows_sum(plan, ids, grads):
    shift = lax.axis_index("rel") * plan.part_lanes
    return folded(dot(grads, one_hot(ids ^ shift, plan.prows), NT))


def target_kernel(plan, *refs):
    count = plan.buckets
    ids = plan.whole_row(refs[:count], (3, 5))
    refs[-1][...] = pack_table(rows_sum(plan, ids, refs[count][...]))


def home_kernel(plan, *refs):
    count = plan.buckets
    reduce_half(plan, False, refs[:count], refs[count : count + 3], refs[-1], refs[-1 - len(plan.parts) : -1])


def source_sum(plan, labels, grads, bucket):
    start = bucket * plan.bucket_edges
    ids = plan.row(labels, 0, (0,), 0, plan.slots)
    return rows_sum(plan, ids, grads[:, start : start + plan.bucket_edges])


def to_shares(plan, value, outs):
    lanes = plan.part_lanes
    outs[0][...] = value[:, :lanes]
    for at, out in enumerate(outs[1:], 1):
        out[...] = pack_table(value[:, at * lanes : (at + 1) * lanes])


def source_kernel(plan, bucket, *refs):
    value = source_sum(plan, refs[:1], refs[1], bucket)
    to_shares(plan, value, refs[-plan.rels :])


def share_kernel(plan, *refs):
    value = source_sum(plan, refs[:1], refs[1], 0)
    to_shares(plan, value + unpack_table(refs[2][...]), refs[-plan.rels :])


def add_kernel(count, *refs):
    value = refs[0][...]
    for ref in refs[1:count]:
        value = value + unpack_table(ref[...])
    refs[-1][...] = pack_table(value)


def combine_kernel(plan, arrivals, sizes, after, *refs):
    at, out_at = 0, sum(arrivals) + len(arrivals) + after
    for part, count, size in zip(plan.parts, arrivals, sizes):
        keep, arrived = refs[at], refs[at + 1 : at + 1 + count]
        outs = refs[out_at : out_at + size]
        at, out_at = at + 1 + count, out_at + size
        share = keep.shape[0] // size
        for place in range(keep.shape[0]):
            value = keep[place]
            for ref in arrived:
                value = value + unpack_table(ref[place], 8 * part.units)
            which, inner = divmod(place, share)
            packed = which or size == 1
            outs[which][inner] = pack_table(value, part.rows) if packed else value


def stack_kernel(plan, counts, *refs):
    outs = refs[-len(counts) :]
    first = 0
    for count, out in zip(counts, outs):
        for at in range(count):
            out[at] = refs[first + at][0]
        first += count


def spread_kernel(plan, counts, side, *refs):
    helds = refs[len(refs) - len(counts) :]
    rel_out, rem_out = refs[-2 - len(counts) : len(refs) - len(counts)]
    me = plan.me()
    first = 0
    for count, held in zip(counts, helds):
        at = 0
        for piece in refs[first : first + count]:
            held[at : at + piece.shape[0]] = piece[...]
            at += piece.shape[0]
        first += count
    for chunk in range(plan.half_chunks):
        for which, (part, held) in enumerate(zip(plan.parts, helds)):
            value = unpack_table(held[part.position(chunk, me)], 8 * part.units)
            for index, block in enumerate(plan.chunk_blocks(chunk, which)):
                if block is None:
                    break
                lane, sub = block
                rows = slice(sub, sub + 8)
                piece = value[8 * index : 8 * index + 8]
                if lane < plan.half_rel:
                    rel_out[rows, lane : lane + LANES] = piece
                else:
                    lane -= plan.half_rel
                    rem_out[rows, lane : lane + LANES] = piece


def copy_kernel(*refs):
    refs[-1][...] = refs[0][...]


def part_out_kernel(plan, *refs):
    out = refs[-1]
    rel = lax.axis_index("rel")
    lanes = plan.part_lanes
    for mask, ref in enumerate(refs[: plan.rels]):
        if lanes % LANES:
            out[:, mask * lanes : (mask + 1) * lanes] = unpack_table(ref[...])
        else:
            start = pl.multiple_of((rel ^ mask) * lanes, lanes)
            out[:, pl.ds(start, lanes)] = unpack_table(ref[...])


def shape(extent, kind):
    return jax.ShapeDtypeStruct(extent, kind)


VMEM = pl.BlockSpec(memory_space=pltpu.VMEM)
ANY = pl.BlockSpec(memory_space=pl.ANY)


def call(kernel, outs, args, name, cost, limit, scratch=(), in_specs=None, out_specs=None, **more):
    work = pl.CostEstimate(flops=int(cost * 1e9), bytes_accessed=int(cost * 3e6), transcendentals=0)
    if "grid_spec" not in more:
        more["in_specs"] = in_specs or [VMEM] * len(args)
        more["out_specs"] = out_specs or [VMEM] * len(outs)
        more["scratch_shapes"] = list(scratch)
    return pl.pallas_call(
        kernel,
        out_shape=outs,
        compiler_params=pltpu.CompilerParams(vmem_limit_bytes=int(limit * 2**20)),
        cost_estimate=work,
        name=name,
        **more,
    )(*args)


def body(
    partitions,
    remainder,
    relations,
    counts,
    lhs_rows,
    lhs_rems,
    rel_ids,
    rhs_rows,
    rhs_rems,
    neg_rows,
    neg_rems,
):
    prows, width = partitions.shape
    plan = Plan(
        lax.axis_size("dom"),
        lax.axis_size("rel"),
        prows,
        width,
        remainder.shape[0],
        relations.shape[0],
        lhs_rows.shape[2],
    )
    smem = pl.BlockSpec(memory_space=pltpu.SMEM)
    own, rem, rels = partitions.T, remainder.T, relations.T
    edges, wide = plan.edges, plan.bucket_edges
    grow = max(1, edges // 1024)
    buckets = plan.buckets
    afar = lambda d: d ^ (plan.target_mask(d % plan.rels) * plan.rels)
    i16 = jnp.int16

    def exchanged(values, masks):
        return [
            send(value, plan, lambda d, m=mask: d ^ m) for value, mask in zip(values, masks[1:])
        ]

    def after(kernel, outs, args, others, name, cost, limit=12, **more):
        return call(
            kernel,
            outs,
            list(args) + list(others),
            name,
            cost,
            limit,
            in_specs=[VMEM] * len(args) + [ANY] * len(others),
            **more,
        )

    tables = [lhs_rows, lhs_rems, rel_ids, rhs_rows, rhs_rems, neg_rows, neg_rems]
    lists = call(
        functools.partial(lists_kernel, plan),
        [shape((buckets * plan.maxb, 8, LANES), jnp.int32)] * plan.rels,
        tables + [counts.reshape(-1)],
        "lists",
        0.5,
        60,
        in_specs=[VMEM] * 7 + [smem],
    )
    lists = [lists[0]] + exchanged(lists[1:], range(plan.rels))
    (own,) = after(
        copy_kernel, [shape(own.shape, own.dtype)], [own], lists[1:], "own", 0.3, 4
    )
    target = send(own, plan, afar)
    sources = [own] + [
        send(own, plan, lambda d, b=bucket: d ^ (b * plan.rels)) for bucket in range(1, buckets)
    ]
    labels = call(
        functools.partial(forward_kernel, plan),
        [shape((plan.slots, 8, LANES), jnp.int32)] * buckets,
        lists,
        "forward",
        0.2,
        8,
    )
    labels = [labels[0]] + [
        send(labels[bucket], plan, lambda d, b=bucket: d ^ (b * plan.rels))
        for bucket in range(1, buckets)
    ]
    labels_of = lambda bucket: [labels[bucket]]
    (rel_split,) = call(
        split_kernel, [shape((2 * width, plan.nrels), BF16)], [rels], "rel_split", 2.0, 50
    )

    grad_shapes = lambda count: [
        shape((2 * width, count), BF16),
        shape((2 * width, count), BF16),
        shape((2 * width, 2 * count), BF16),
    ]
    inputs = []
    for bucket in range(buckets):
        (vec,) = call(
            functools.partial(relation_kernel, plan),
            [shape((width, wide), F32)],
            labels_of(bucket) + [rel_split],
            "relation",
            2.0,
            16 * grow,
        )
        lhs, cand_rem = call(
            functools.partial(rows_kernel, plan),
            [shape((width, wide), F32), shape((width, 2 * wide), BF16)],
            labels_of(bucket) + [sources[bucket], rem],
            "rows",
            0.7,
            12 * grow,
        )
        inputs.append([lhs, vec, cand_rem])
    grads = []
    for bucket in range(buckets - 1):
        grads += call(
            functools.partial(bucket_kernel, plan),
            grad_shapes(wide),
            labels_of(bucket) + [target] + inputs[bucket],
            "bucket",
            4.0,
            16 * grow,
        )
    table = [pltpu.VMEM((width, plan.half_lanes), F32)]
    made = call(
        functools.partial(last_kernel, plan),
        [shape(part.packed, i16) for part in plan.parts] + grad_shapes(edges),
        labels + grads + [target] + inputs[-1],
        "last",
        9.0,
        24 * grow,
        in_specs=[VMEM] * len(labels) + [ANY] * len(grads) + [VMEM] * 4,
        out_specs=[VMEM] * len(plan.parts) + [ANY] * 3,
        scratch=[pltpu.VMEM(held.shape, BF16) for held in grad_shapes(edges)]
        + table
        + [pltpu.SemaphoreType.DMA((len(grads) + 3,))],
    )
    away, grads = made[: len(plan.parts)], list(made[len(plan.parts) :])
    cores = [send(value, plan, lambda d: d ^ 1) for value in away]

    lanes = plan.part_lanes
    share_shapes = [shape((width, lanes), F32)] + [shape((width + 16, lanes), i16)] * (
        plan.rels - 1
    )
    others, order = [], away[0]
    for bucket in range(1, buckets):
        made = after(
            functools.partial(source_kernel, plan, bucket),
            share_shapes,
            labels_of(bucket) + [grads[0]],
            [order],
            "source",
            0.8,
        )
        others.append([made[0]] + exchanged(made[1:], range(plan.rels)))
        order = made[0]
    (far,) = after(
        functools.partial(target_kernel, plan),
        [shape((width + 16, prows), i16)],
        labels + [grads[2]],
        [order],
        "target",
        1.8,
        16 * grow,
    )
    keeps = after(
        functools.partial(home_kernel, plan),
        [shape(part.bare, F32) for part in plan.parts],
        labels + grads,
        [far],
        "home",
        4.0,
        16 * grow,
        scratch=table,
    )
    far = send(far, plan, afar)

    def combine(keeps, arrived, order, level, name):
        sizes = [len(part.masks[level]) if level < 2 else 1 for part in plan.parts]
        outs, args = [], []
        for part, keep, pieces, size in zip(plan.parts, keeps, arrived, sizes):
            args += [keep] + pieces
            if level < 2:
                outs += part.shares(keep.shape[0], size)
            else:
                outs.append(shape((1,) + part.packed[1:], i16))
        made = after(
            functools.partial(
                combine_kernel, plan, [len(pieces) for pieces in arrived], sizes, len(order)
            ),
            outs,
            args,
            order,
            name,
            0.5,
        )
        if level == 2:
            return made, []
        keeps, arrived = [], []
        for part, size in zip(plan.parts, sizes):
            group, made = made[:size], made[size:]
            keeps.append(group[0])
            arrived.append(exchanged(group[1:], part.masks[level]))
        return keeps, arrived

    order, crossing = keeps[0], []
    for bucket in range(1, buckets):
        (order,) = after(
            functools.partial(add_kernel, plan.rels),
            [shape((width + 16, lanes), i16)],
            others[bucket - 1],
            [order],
            "other",
            0.3,
        )
        crossing.append(send(order, plan, lambda d, b=bucket: d ^ (b * plan.rels)))
    keeps, arrived = combine(keeps, [[core] for core in cores], [order], 0, "combine_cores")
    keeps, arrived = combine(keeps, arrived, [], 1, "combine_first")
    made = after(
        functools.partial(share_kernel, plan),
        share_shapes,
        labels_of(0) + [grads[0], far],
        [keeps[0]],
        "share",
        0.8,
    )
    mine, order = [made[0]] + exchanged(made[1:], range(plan.rels)) + crossing, made[0]
    totals, _ = combine(keeps, arrived, [order], 2, "combine_last")

    pieces = [
        [total] + exchanged([total] * (len(part.masks[1]) - 1), part.masks[1])
        for part, total in zip(plan.parts, totals)
    ]
    (owner,) = after(
        functools.partial(add_kernel, len(mine)),
        [shape((width + 16, lanes), i16)],
        mine,
        [totals[0]],
        "mine",
        0.3,
    )
    owners = [owner] + exchanged([owner] * (plan.rels - 1), range(plan.rels))
    (grad_partitions,) = after(
        functools.partial(part_out_kernel, plan),
        [shape((width, prows), F32)],
        owners,
        [],
        "part_out",
        1.0,
    )
    blocks = after(
        functools.partial(stack_kernel, plan, [len(group) for group in pieces]),
        [
            shape((len(group),) + part.packed[1:], i16)
            for part, group in zip(plan.parts, pieces)
        ],
        sum(pieces, []),
        [grad_partitions],
        "stack",
        0.3,
    )
    pieces = [
        [block] + exchanged([block] * (len(part.masks[0]) - 1), part.masks[0])
        for part, block in zip(plan.parts, blocks)
    ]
    if lanes % LANES:
        order = jnp.arange(plan.rels) ^ lax.axis_index("rel")
        split_lanes = grad_partitions.reshape(width, plan.rels, lanes)
        grad_partitions = jnp.take(split_lanes, order, axis=1).reshape(width, prows)

    crossed = [[send(piece, plan, lambda d: d ^ 1) for piece in group] for group in pieces]
    side = lax.axis_index("rel") & 1
    outs = [shape((width, plan.nrels), F32), shape((width, plan.rems), F32)]
    spec = lambda lanes: pl.BlockSpec((width, lanes), lambda i, half: (0, half[0]))
    made = []
    for turn, groups in enumerate([pieces, crossed]):
        flat = sum(groups, [])
        made = call(
            functools.partial(spread_kernel, plan, [len(group) for group in groups]),
            outs,
            [(side ^ turn).reshape(1), *flat, *made],
            "spread",
            2.0,
            16,
            grid_spec=pltpu.PrefetchScalarGridSpec(
                num_scalar_prefetch=1,
                grid=(1,),
                in_specs=[pl.BlockSpec(piece.shape, lambda i, half: (0, 0, 0)) for piece in flat]
                + [ANY] * len(made),
                out_specs=[spec(plan.half_rel), spec(plan.half_rem)],
                scratch_shapes=[pltpu.VMEM(part.packed, i16) for part in plan.parts],
            ),
            input_output_aliases={1 + len(flat) + at: at for at in range(len(made))},
        )
    grad_relations, grad_remainder = made
    return grad_partitions.T, grad_remainder.T, grad_relations.T


def solution(mesh):
    edge = P("dom", None, "rel", None)
    in_specs = (P("dom", None), P(), P(), P("dom", None, "rel")) + (edge,) * 7
    out_specs = (P("dom", None), P(), P())
    return jax.shard_map(body, mesh=mesh, in_specs=in_specs, out_specs=out_specs, check_vma=False)
```

```python
import functools

import jax
import jax.numpy as jnp
from jax import lax
from jax.experimental import pallas as pl
from jax.experimental.pallas import tpu as pltpu
from jax.sharding import PartitionSpec as P

F32 = jnp.float32
BF16 = jnp.bfloat16
LANES = 128
REACH = 32766.0
NT = (((1,), (1,)), ((), ()))
NN = (((1,), (0,)), ((), ()))
TN = (((0,), (0,)), ((), ()))


def bits_of(count):
    return count.bit_length() - 1


def reverse_bits(value, count):
    out = 0
    for bit in range(bits_of(count)):
        out = out * 2 + ((value >> bit) & 1)
    return out


def split(value):
    high = value.astype(BF16)
    low = (value - high.astype(F32)).astype(BF16)
    return high, low


def dot(left, right, dims):
    return lax.dot_general(left, right, dims, preferred_element_type=F32)


def dot3(left, right, dims):
    left_high, left_low = split(left)
    right_high, right_low = split(right)
    return (
        dot(left_high, right_high, dims)
        + dot(left_high, right_low, dims)
        + dot(left_low, right_high, dims)
    )


def one_hot(ids, rows, base=0):
    place = lax.broadcasted_iota(jnp.int32, (rows, ids.shape[1]), 0)
    return jnp.where(place == ids - base, 1.0, 0.0).astype(BF16)


def store_split(ref, cols, value):
    high, low = split(value)
    depth = value.shape[0]
    ref[0:depth, cols] = high
    ref[depth : 2 * depth, cols] = low


def folded(value):
    depth = value.shape[0] // 2
    return value[:depth] + value[depth:]


def quantized(value):
    top = jnp.max(jnp.abs(value), axis=0, keepdims=True)
    exponent = jnp.floor(jnp.log2(jnp.maximum(top, 1e-30))) + 1.0
    return jnp.round(value * (REACH * jnp.exp2(-exponent))), exponent


def scale_of(exponent):
    return jnp.exp2(exponent) * (1.0 / REACH)


def to_words(value):
    return value.astype(jnp.int32).astype(jnp.int16)


def from_words(words):
    return words.astype(jnp.int32).astype(F32)


def pack_table(value, rows=None):
    scaled, exponent = quantized(value)
    spare = (rows or value.shape[0] + 16) - value.shape[0]
    tail = jnp.broadcast_to(exponent, (spare, value.shape[1]))
    return to_words(jnp.concatenate([scaled, tail], axis=0))


def unpack_table(words, depth=None):
    depth = depth or words.shape[0] - 16
    value = from_words(words)
    return value[:depth] * scale_of(value[depth : depth + 1])


class Part:
    def __init__(self, plan, units, groups):
        self.units = units
        self.rows = (units + 2) // 2 * 16
        self.masks = [self.group_masks(bits) for bits in groups]
        order = [bit for group in groups for bit in reversed(group)]
        self.place = {bit: len(order) - 1 - at for at, bit in enumerate(order)}
        self.packed = (plan.half_chunks, self.rows, LANES)
        self.bare = (plan.half_chunks, 8 * units, LANES)

    @staticmethod
    def group_masks(bits):
        masks = []
        for index in range(2 ** len(bits)):
            masks.append(sum(((index >> at) & 1) << bit for at, bit in enumerate(bits)))
        return masks

    def position(self, chunk, me):
        relative = chunk ^ (me >> 1)
        out = 0
        for bit, at in self.place.items():
            out = out + (((relative >> (bit - 1)) & 1) << at)
        return out

    def shares(self, count, size):
        count = count // size
        return [shape((count,) + self.bare[1:], F32)] + [
            shape((count,) + self.packed[1:], jnp.int16)
        ] * (size - 1)


class Plan:
    def __init__(self, doms, rels, prows, width, rems, nrels, maxb):
        self.doms, self.rels, self.maxb = doms, rels, maxb
        self.devices = doms * rels
        self.prows, self.width, self.rems, self.nrels = prows, width, rems, nrels
        self.buckets = doms // rels
        self.slots = rels * maxb
        self.bucket_edges = self.slots * LANES
        self.edges = self.buckets * self.bucket_edges
        self.part_lanes = prows // rels
        self.half_rel, self.half_rem = nrels // 2, rems // 2
        self.half_lanes = self.half_rel + self.half_rem
        self.subs = width // 8
        self.units = (self.half_lanes // LANES) * self.subs
        self.half_chunks = self.devices // 2
        self.chunk_units = -(-self.units // self.half_chunks)
        rel_bits = bits_of(rels)
        all_bits = rel_bits + bits_of(doms)
        near = list(range(1, rel_bits + 1))
        far = list(range(rel_bits + 1, all_bits))
        self.parts = [Part(self, self.chunk_units, [near, far])]

    def chunk_blocks(self, chunk, part):
        first = chunk * self.chunk_units + (self.parts[0].units if part else 0)
        blocks = []
        for unit in range(first, first + self.parts[part].units):
            lane, sub = divmod(unit, self.subs)
            blocks.append((lane * LANES, 8 * sub) if unit < self.units else None)
        return blocks

    def row(self, labels, bucket, kinds, first, count):
        rows = []
        for slot in range(first, first + count):
            rows += [labels[bucket][slot, kind : kind + 1, :] for kind in kinds]
        return jnp.concatenate(rows, axis=1) if len(rows) > 1 else rows[0]

    def whole_row(self, labels, kinds):
        rows = [
            self.row(labels, bucket, kinds, 0, self.slots) for bucket in range(self.buckets)
        ]
        return jnp.concatenate(rows, axis=1) if len(rows) > 1 else rows[0]

    def me(self):
        return lax.axis_index("dom") * self.rels + lax.axis_index("rel")

    def target_mask(self, rel):
        return reverse_bits(rel, self.rels) * self.buckets

    def dynamic_mask(self, rel):
        out = 0
        width = bits_of(self.rels)
        for bit in range(width):
            out = out + (((rel >> bit) & 1) << (width - 1 - bit))
        return out * self.buckets


def send(value, plan, target):
    pairs = [(device, target(device)) for device in range(plan.devices)]
    return lax.ppermute(value, ("dom", "rel"), pairs)


def lists_kernel(plan, *refs):
    tables, counts, outs = refs[:7], refs[7], refs[8:]
    source = lax.axis_index("dom")
    rel = lax.axis_index("rel")
    for mask, out in enumerate(outs):
        for bucket in range(plan.buckets):
            target = source ^ bucket ^ plan.dynamic_mask(rel ^ mask)
            stop = lax.rem(source - target + plan.doms, plan.doms)
            for turn in range(plan.maxb):
                at = bucket * plan.maxb + turn
                for kind, table in enumerate(tables):
                    out[at, kind : kind + 1, :] = table[0, stop, turn : turn + 1, :]
                live = jnp.where(turn < counts[stop], 1, 0)
                out[at, 7:8, :] = jnp.full((1, LANES), live, jnp.int32)


def forward_kernel(plan, *refs):
    lists, outs = refs[: plan.rels], refs[plan.rels :]
    for bucket, out in enumerate(outs):
        for mask, ref in enumerate(lists):
            for turn in range(plan.maxb):
                out[mask * plan.maxb + turn] = ref[bucket * plan.maxb + turn]


def split_kernel(relations, out):
    depth = relations.shape[0]
    high, low = split(relations[...])
    out[0:depth, :] = high
    out[depth : 2 * depth, :] = low


def relation_kernel(plan, *refs):
    labels, relations, out = refs[:1], refs[1], refs[-1]
    for pair in range(0, plan.slots, 2):
        count = min(2, plan.slots - pair)
        start = pair * LANES
        ids = plan.row(labels, 0, (2,), pair, count)
        out[:, start : start + count * LANES] = folded(
            dot(relations[...], one_hot(ids, plan.nrels), NN)
        )


def rows_kernel(plan, *refs):
    labels, (own, rem) = refs[:1], refs[1:3]
    lhs_out, rem_out = refs[-2:]
    for pair in range(0, plan.slots, 2):
        count = min(2, plan.slots - pair)
        row = lambda *kinds: plan.row(labels, 0, kinds, pair, count)
        start = pair * LANES
        end = start + count * LANES
        lhs_out[:, start:end] = dot(own[...], one_hot(row(0), plan.prows), NN) + dot(
            rem[...], one_hot(row(1), plan.rems), NN
        )
        rem_out[:, 2 * start : 2 * end] = dot(
            rem[...], one_hot(row(4, 6), plan.rems), NN
        ).astype(BF16)


def conjugate_parts(grad, other):
    half = grad.shape[0] // 2
    grad_re, grad_im = grad[:half], grad[half:]
    other_re, other_im = other[:half], other[half:]
    return jnp.concatenate(
        [grad_re * other_re + grad_im * other_im, grad_im * other_re - grad_re * other_im], 0
    )


def complex_product(left, right):
    half = left.shape[0] // 2
    left_re, left_im = left[:half], left[half:]
    right_re, right_im = right[:half], right[half:]
    return jnp.concatenate(
        [left_re * right_re - left_im * right_im, left_re * right_im + left_im * right_re], 0
    )


def bucket_grads(plan, labels, target, lhs_in, rel_in, rem_in, lhs_out, rel_out, cand_out, base):
    total = 2 * LANES
    edge = lax.broadcasted_iota(jnp.int32, (LANES, total), 0)
    column = lax.broadcasted_iota(jnp.int32, (LANES, total), 1)
    keep = jnp.where(edge == column, 0.0, 1.0 / total)
    for slot in range(plan.slots):
        cols = slice(slot * LANES, (slot + 1) * LANES)
        wide = slice(slot * total, (slot + 1) * total)
        ids = plan.row(labels, 0, (3, 5), slot, 1)
        cand = dot(target[...], one_hot(ids, plan.prows), NN) + rem_in[:, wide].astype(F32)
        rhs = cand[:, :LANES]
        lhs, vec = lhs_in[:, cols], rel_in[:, cols]
        u_vec = complex_product(lhs, vec)
        live = plan.row(labels, 0, (7,), slot, 1).astype(F32)
        positive = jnp.sum(u_vec * rhs, axis=0, keepdims=True)
        negative = dot3(u_vec, cand, TN)
        grad_pos = -jax.nn.sigmoid(-positive) * live
        grad_neg = jax.nn.sigmoid(negative) * keep * live[0:1, 0:1]
        grad_u = grad_pos * rhs + dot3(cand, grad_neg, NT)
        from_neg = dot3(u_vec, grad_neg, NN)
        grad_cand = jnp.concatenate(
            [from_neg[:, :LANES] + grad_pos * u_vec, from_neg[:, LANES:]], axis=1
        )
        at = base + slot
        cols = slice(at * LANES, (at + 1) * LANES)
        wide = slice(at * total, (at + 1) * total)
        store_split(lhs_out, cols, conjugate_parts(grad_u, vec))
        store_split(rel_out, cols, conjugate_parts(grad_u, lhs))
        store_split(cand_out, wide, grad_cand)


def bucket_kernel(plan, *refs):
    bucket_grads(plan, refs[:1], *refs[1:], 0)


def last_kernel(plan, *refs):
    count = plan.buckets
    labels = refs[:count]
    before = refs[count : count + 3 * (plan.buckets - 1)]
    refs = refs[count + 3 * (plan.buckets - 1) :]
    target, lhs_in, rel_in, rem_in = refs[:4]
    away, refs = refs[4 : 4 + len(plan.parts)], refs[4 + len(plan.parts) :]
    outs, helds, table, sems = refs[:3], refs[3:6], refs[6], refs[7]
    edges = plan.bucket_edges
    loads = []
    for at, ref in enumerate(before):
        wide = edges * (2 if at % 3 == 2 else 1)
        start = (at // 3) * wide
        loads.append(
            pltpu.make_async_copy(ref, helds[at % 3].at[:, start : start + wide], sems.at[at])
        )
        loads[-1].start()
    base = (plan.buckets - 1) * plan.slots
    own_labels = labels[-1:]
    bucket_grads(plan, own_labels, target, lhs_in, rel_in, rem_in, *helds, base)
    for load in loads:
        load.wait()
    stores = [
        pltpu.make_async_copy(held, out, sems.at[len(loads) + at])
        for at, (held, out) in enumerate(zip(helds, outs))
    ]
    for store in stores:
        store.start()
    reduce_half(plan, True, labels, helds, table, away)
    for store in stores:
        store.wait()


def reduce_half(plan, away, labels, grads, table, outs):
    lhs_grads, rel_grads, cand_grads = grads
    me = plan.me()
    half = (me & 1) ^ (1 if away else 0)
    step = 2 * LANES if plan.half_rel % (2 * LANES) == 0 else LANES
    ids = plan.whole_row(labels, (2,)) - half * plan.half_rel
    for start in range(0, plan.half_rel, step):
        hot = one_hot(ids, step, start)
        table[:, start : start + step] = folded(dot(rel_grads[...], hot, NT))
    base = half * plan.half_rem
    first = one_hot(plan.whole_row(labels, (1,)), plan.half_rem, base)
    second = one_hot(plan.whole_row(labels, (4, 6)), plan.half_rem, base)
    table[:, plan.half_rel :] = folded(
        dot(lhs_grads[...], first, NT) + dot(cand_grads[...], second, NT)
    )
    for chunk in range(plan.half_chunks):
        for which, (part, out) in enumerate(zip(plan.parts, outs)):
            value = jnp.concatenate(
                [
                    table[block[1] : block[1] + 8, block[0] : block[0] + LANES]
                    if block
                    else jnp.zeros((8, LANES), F32)
                    for block in plan.chunk_blocks(chunk, which)
                ],
                axis=0,
            )
            out[part.position(chunk, me)] = pack_table(value, part.rows) if away else value


def rows_sum(plan, ids, grads):
    shift = lax.axis_index("rel") * plan.part_lanes
    return folded(dot(grads, one_hot(ids ^ shift, plan.prows), NT))


def target_kernel(plan, *refs):
    count = plan.buckets
    ids = plan.whole_row(refs[:count], (3, 5))
    value = pack_table(rows_sum(plan, ids, refs[count][...]))
    for at, out in enumerate(refs[-2:]):
        lanes = out.shape[1]
        out[...] = value[:, at * lanes : (at + 1) * lanes]


def home_kernel(plan, *refs):
    count = plan.buckets
    reduce_half(plan, False, refs[:count], refs[count : count + 3], refs[-1], refs[-1 - len(plan.parts) : -1])


def source_sum(plan, labels, grads, bucket):
    start = bucket * plan.bucket_edges
    ids = plan.row(labels, bucket, (0,), 0, plan.slots)
    return rows_sum(plan, ids, grads[:, start : start + plan.bucket_edges])


def deal(plan, value, bucket, outs):
    keep, away = outs
    lanes = plan.part_lanes
    for at in range(value.shape[1] // lanes):
        share = value[:, at * lanes : (at + 1) * lanes]
        to = slice(at // 2 * lanes, (at // 2 + 1) * lanes)
        if at % 2:
            away[bucket, :, to] = pack_table(share)
        else:
            keep[bucket, :, to] = share


def sources_kernel(plan, *refs):
    out = refs[-1]
    for bucket in range(plan.buckets):
        out[bucket] = source_sum(plan, refs[: plan.buckets], refs[plan.buckets], bucket)


def share(plan, sources, *refs):
    far, outs = refs[:-2], refs[-2:]
    for bucket in range(plan.buckets):
        value = sources[bucket]
        if bucket == 0:
            value = value + jnp.concatenate([unpack_table(ref[...]) for ref in far], axis=1)
        deal(plan, value, bucket, outs)


def deal_again(plan, keep, came, *outs):
    for bucket in range(plan.buckets):
        deal(plan, keep[bucket] + unpack_table(came[bucket]), bucket, outs)


def deal_kernel(plan, *refs):
    deal_again(plan, *refs)


def settle(plan, keep, came, *outs):
    for bucket, out in enumerate(outs):
        value = keep[bucket] + unpack_table(came[bucket])
        out[...] = pack_table(value) if bucket else value


def mine_kernel(plan, *refs):
    value = refs[0][...]
    for ref in refs[1 : plan.buckets]:
        value = value + unpack_table(ref[...])
    refs[-1][...] = pack_table(value)


def combine_kernel(plan, arrivals, sizes, beside, *refs):
    at, out_at = 0, sum(arrivals) + len(arrivals)
    if beside:
        step, ins, outs = beside
        step(plan, *refs[out_at : out_at + ins], *refs[len(refs) - outs :])
        out_at += ins
    for part, count, size in zip(plan.parts, arrivals, sizes):
        keep, arrived = refs[at], refs[at + 1 : at + 1 + count]
        outs = refs[out_at : out_at + size]
        at, out_at = at + 1 + count, out_at + size
        share = keep.shape[0] // size
        for place in range(keep.shape[0]):
            value = keep[place]
            for ref in arrived:
                value = value + unpack_table(ref[place], 8 * part.units)
            which, inner = divmod(place, share)
            packed = which or size == 1
            outs[which][inner] = pack_table(value, part.rows) if packed else value


def stack_kernel(plan, counts, *refs):
    total = sum(counts)
    outs, refs = refs[total + 2 : total + 2 + len(counts)], refs[: total + 2] + refs[total + 2 + len(counts) :]
    settle(plan, *refs[total:])
    first = 0
    for count, out in zip(counts, outs):
        for at in range(count):
            out[at] = refs[first + at][0]
        first += count


def spread_kernel(plan, counts, side, *refs):
    helds = refs[len(refs) - len(counts) :]
    rel_out, rem_out = refs[-2 - len(counts) : len(refs) - len(counts)]
    me = plan.me()
    first = 0
    for count, held in zip(counts, helds):
        at = 0
        for piece in refs[first : first + count]:
            held[at : at + piece.shape[0]] = piece[...]
            at += piece.shape[0]
        first += count
    for chunk in range(plan.half_chunks):
        for which, (part, held) in enumerate(zip(plan.parts, helds)):
            value = unpack_table(held[part.position(chunk, me)], 8 * part.units)
            for index, block in enumerate(plan.chunk_blocks(chunk, which)):
                if block is None:
                    break
                lane, sub = block
                rows = slice(sub, sub + 8)
                piece = value[8 * index : 8 * index + 8]
                if lane < plan.half_rel:
                    rel_out[rows, lane : lane + LANES] = piece
                else:
                    lane -= plan.half_rel
                    rem_out[rows, lane : lane + LANES] = piece


def part_out_kernel(plan, *refs):
    out = refs[-1]
    rel = lax.axis_index("rel")
    lanes = plan.part_lanes
    for mask, ref in enumerate(refs[: plan.rels]):
        if lanes % LANES:
            out[:, mask * lanes : (mask + 1) * lanes] = unpack_table(ref[...])
        else:
            start = pl.multiple_of((rel ^ mask) * lanes, lanes)
            out[:, pl.ds(start, lanes)] = unpack_table(ref[...])


def shape(extent, kind):
    return jax.ShapeDtypeStruct(extent, kind)


VMEM = pl.BlockSpec(memory_space=pltpu.VMEM)
ANY = pl.BlockSpec(memory_space=pl.ANY)


def call(kernel, outs, args, name, cost, limit, scratch=(), in_specs=None, out_specs=None, **more):
    work = pl.CostEstimate(flops=int(cost * 1e9), bytes_accessed=int(cost * 3e6), transcendentals=0)
    if "grid_spec" not in more:
        more["in_specs"] = in_specs or [VMEM] * len(args)
        more["out_specs"] = out_specs or [VMEM] * len(outs)
        more["scratch_shapes"] = list(scratch)
    return pl.pallas_call(
        kernel,
        out_shape=outs,
        compiler_params=pltpu.CompilerParams(vmem_limit_bytes=int(limit * 2**20)),
        cost_estimate=work,
        name=name,
        **more,
    )(*args)


def body(
    partitions,
    remainder,
    relations,
    counts,
    lhs_rows,
    lhs_rems,
    rel_ids,
    rhs_rows,
    rhs_rems,
    neg_rows,
    neg_rems,
):
    prows, width = partitions.shape
    plan = Plan(
        lax.axis_size("dom"),
        lax.axis_size("rel"),
        prows,
        width,
        remainder.shape[0],
        relations.shape[0],
        lhs_rows.shape[2],
    )
    smem = pl.BlockSpec(memory_space=pltpu.SMEM)
    own, rem, rels = partitions.T, remainder.T, relations.T
    edges, wide = plan.edges, plan.bucket_edges
    grow = max(1, edges // 1024)
    buckets = plan.buckets
    afar = lambda d: d ^ (plan.target_mask(d % plan.rels) * plan.rels)
    i16 = jnp.int16

    def exchanged(values, masks):
        return [
            send(value, plan, lambda d, m=mask: d ^ m) for value, mask in zip(values, masks[1:])
        ]

    def after(kernel, outs, args, others, name, cost, limit=12, **more):
        return call(
            kernel,
            outs,
            list(args) + list(others),
            name,
            cost,
            limit,
            in_specs=[VMEM] * len(args) + [ANY] * len(others),
            **more,
        )

    target = send(own, plan, afar)
    sources = [own] + [
        send(own, plan, lambda d, b=bucket: d ^ (b * plan.rels)) for bucket in range(1, buckets)
    ]
    tables = [lhs_rows, lhs_rems, rel_ids, rhs_rows, rhs_rems, neg_rows, neg_rems]
    lists = call(
        functools.partial(lists_kernel, plan),
        [shape((buckets * plan.maxb, 8, LANES), jnp.int32)] * plan.rels,
        tables + [counts.reshape(-1)],
        "lists",
        0.5,
        60,
        in_specs=[VMEM] * 7 + [smem],
    )
    lists = [lists[0]] + exchanged(lists[1:], range(plan.rels))
    labels = call(
        functools.partial(forward_kernel, plan),
        [shape((plan.slots, 8, LANES), jnp.int32)] * buckets,
        lists,
        "forward",
        0.2,
        8,
    )
    labels = [labels[0]] + [
        send(labels[bucket], plan, lambda d, b=bucket: d ^ (b * plan.rels))
        for bucket in range(1, buckets)
    ]
    labels_of = lambda bucket: [labels[bucket]]
    (rel_split,) = call(
        split_kernel, [shape((2 * width, plan.nrels), BF16)], [rels], "rel_split", 2.0, 50
    )

    grad_shapes = lambda count: [
        shape((2 * width, count), BF16),
        shape((2 * width, count), BF16),
        shape((2 * width, 2 * count), BF16),
    ]
    inputs = []
    for bucket in range(buckets):
        (vec,) = call(
            functools.partial(relation_kernel, plan),
            [shape((width, wide), F32)],
            labels_of(bucket) + [rel_split],
            "relation",
            2.0,
            16 * grow,
        )
        lhs, cand_rem = call(
            functools.partial(rows_kernel, plan),
            [shape((width, wide), F32), shape((width, 2 * wide), BF16)],
            labels_of(bucket) + [sources[bucket], rem],
            "rows",
            0.7,
            12 * grow,
        )
        inputs.append([lhs, vec, cand_rem])
    grads = []
    for bucket in range(buckets - 1):
        grads += call(
            functools.partial(bucket_kernel, plan),
            grad_shapes(wide),
            labels_of(bucket) + [target] + inputs[bucket],
            "bucket",
            4.0,
            16 * grow,
        )
    table = [pltpu.VMEM((width, plan.half_lanes), F32)]
    made = call(
        functools.partial(last_kernel, plan),
        [shape(part.packed, i16) for part in plan.parts] + grad_shapes(edges),
        labels + grads + [target] + inputs[-1],
        "last",
        9.0,
        24 * grow,
        in_specs=[VMEM] * len(labels) + [ANY] * len(grads) + [VMEM] * 4,
        out_specs=[VMEM] * len(plan.parts) + [ANY] * 3,
        scratch=[pltpu.VMEM(held.shape, BF16) for held in grad_shapes(edges)]
        + table
        + [pltpu.SemaphoreType.DMA((len(grads) + 3,))],
    )
    away, grads = made[: len(plan.parts)], list(made[len(plan.parts) :])
    cores = [send(value, plan, lambda d: d ^ 1) for value in away]

    keeps = after(
        functools.partial(home_kernel, plan),
        [shape(part.bare, F32) for part in plan.parts],
        labels + grads,
        away,
        "home",
        4.0,
        16 * grow,
        scratch=table,
    )

    def combine(keeps, arrived, level, name, step=None, step_args=(), step_outs=()):
        sizes = [len(part.masks[level]) if level < 2 else 1 for part in plan.parts]
        outs, args = [], []
        for part, keep, pieces, size in zip(plan.parts, keeps, arrived, sizes):
            args += [keep] + pieces
            if level < 2:
                outs += part.shares(keep.shape[0], size)
            else:
                outs.append(shape((1,) + part.packed[1:], i16))
        beside = (step, len(step_args), len(step_outs)) if step else None
        count = [len(pieces) for pieces in arrived]
        made = after(
            functools.partial(combine_kernel, plan, count, sizes, beside),
            outs + list(step_outs),
            args + list(step_args),
            [],
            name,
            0.6,
        )
        made, beside = made[: len(outs)], made[len(outs) :]
        if level == 2:
            return made, [], beside
        keeps, arrived = [], []
        for part, size in zip(plan.parts, sizes):
            group, made = made[:size], made[size:]
            keeps.append(group[0])
            arrived.append(exchanged(group[1:], part.masks[level]))
        return keeps, arrived, beside

    keeps, arrived, _ = combine(keeps, [[core] for core in cores], 0, "combine_cores")
    far = after(
        functools.partial(target_kernel, plan),
        [shape((width + 16, prows // 2), i16)] * 2,
        labels + [grads[2]],
        [keeps[0]],
        "target",
        1.8,
        16 * grow,
    )
    (sources,) = after(
        functools.partial(sources_kernel, plan),
        [shape((buckets, width, prows), F32)],
        labels + [grads[0]],
        [far[0]],
        "sources",
        1.5,
        16 * grow,
    )
    far = [send(value, plan, afar) for value in far]
    lanes = plan.part_lanes
    count, bit = plan.rels // 2, 1
    dealt = lambda count: [
        shape((buckets, width, count * lanes), F32),
        shape((buckets, width + 16, count * lanes), i16),
    ]
    keeps, arrived, (mine, away) = combine(
        keeps, arrived, 1, "combine_first", share, [sources] + far, dealt(count)
    )
    came = send(away, plan, lambda d: d ^ 1)
    while count > 2:
        count, bit = count // 2, bit * 2
        mine, away = after(
            functools.partial(deal_kernel, plan), dealt(count), [mine, came], [], "deal", 0.3
        )
        came = send(away, plan, lambda d, m=bit: d ^ m)
    count, bit = count // 2, bit * 2
    totals, _, (mine, away) = combine(
        keeps, arrived, 2, "combine_last", deal_again, [mine, came], dealt(count)
    )
    came = send(away, plan, lambda d: d ^ bit)
    pieces = [
        [total] + exchanged([total] * (len(part.masks[1]) - 1), part.masks[1])
        for part, total in zip(plan.parts, totals)
    ]
    flat = sum(pieces, [])
    made = after(
        functools.partial(stack_kernel, plan, [len(group) for group in pieces]),
        [
            shape((len(group),) + part.packed[1:], i16)
            for part, group in zip(plan.parts, pieces)
        ]
        + [shape((width, lanes), F32)]
        + [shape((width + 16, lanes), i16)] * (buckets - 1),
        flat + [mine, came],
        [],
        "stack",
        0.5,
    )
    blocks, made = made[: len(plan.parts)], made[len(plan.parts) :]
    pieces = [
        [block] + exchanged([block] * (len(part.masks[0]) - 1), part.masks[0])
        for part, block in zip(plan.parts, blocks)
    ]
    mine = [made[0]] + exchanged(made[1:], range(0, plan.rels * buckets, plan.rels))
    (owner,) = call(
        functools.partial(mine_kernel, plan),
        [shape((width + 16, lanes), i16)],
        mine,
        "mine",
        0.3,
        12,
    )
    owners = {0: owner}
    while bit:
        for mask in sorted(owners):
            owners[mask | bit] = send(owners[mask], plan, lambda d, m=bit: d ^ m)
        bit //= 2
    (grad_partitions,) = after(
        functools.partial(part_out_kernel, plan),
        [shape((width, prows), F32)],
        [owners[mask] for mask in range(plan.rels)],
        [],
        "part_out",
        1.0,
    )
    if lanes % LANES:
        order = jnp.arange(plan.rels) ^ lax.axis_index("rel")
        split_lanes = grad_partitions.reshape(width, plan.rels, lanes)
        grad_partitions = jnp.take(split_lanes, order, axis=1).reshape(width, prows)

    crossed = [[send(piece, plan, lambda d: d ^ 1) for piece in group] for group in pieces]
    side = lax.axis_index("rel") & 1
    outs = [shape((width, plan.nrels), F32), shape((width, plan.rems), F32)]
    spec = lambda lanes: pl.BlockSpec((width, lanes), lambda i, half: (0, half[0]))
    made = []
    for turn, groups in enumerate([pieces, crossed]):
        flat = sum(groups, [])
        made = call(
            functools.partial(spread_kernel, plan, [len(group) for group in groups]),
            outs,
            [(side ^ turn).reshape(1), *flat, *made],
            "spread",
            2.0,
            16,
            grid_spec=pltpu.PrefetchScalarGridSpec(
                num_scalar_prefetch=1,
                grid=(1,),
                in_specs=[pl.BlockSpec(piece.shape, lambda i, half: (0, 0, 0)) for piece in flat]
                + [ANY] * len(made),
                out_specs=[spec(plan.half_rel), spec(plan.half_rem)],
                scratch_shapes=[pltpu.VMEM(part.packed, i16) for part in plan.parts],
            ),
            input_output_aliases={1 + len(flat) + at: at for at in range(len(made))},
        )
    grad_relations, grad_remainder = made
    return grad_partitions.T, grad_remainder.T, grad_relations.T


def solution(mesh):
    edge = P("dom", None, "rel", None)
    in_specs = (P("dom", None), P(), P(), P("dom", None, "rel")) + (edge,) * 7
    out_specs = (P("dom", None), P(), P())
    return jax.shard_map(body, mesh=mesh, in_specs=in_specs, out_specs=out_specs, check_vma=False)
```

```python
import functools

import jax
import jax.numpy as jnp
from jax import lax
from jax.experimental import pallas as pl
from jax.experimental.pallas import tpu as pltpu
from jax.sharding import PartitionSpec as P

F32 = jnp.float32
BF16 = jnp.bfloat16
LANES = 128
REACH = 32766.0
NT = (((1,), (1,)), ((), ()))
NN = (((1,), (0,)), ((), ()))
TN = (((0,), (0,)), ((), ()))


def bits_of(count):
    return count.bit_length() - 1


def reverse_bits(value, count):
    out = 0
    for bit in range(bits_of(count)):
        out = out * 2 + ((value >> bit) & 1)
    return out


def split(value):
    high = value.astype(BF16)
    low = (value - high.astype(F32)).astype(BF16)
    return high, low


def dot(left, right, dims):
    return lax.dot_general(left, right, dims, preferred_element_type=F32)


def dot3(left, right, dims):
    left_high, left_low = split(left)
    right_high, right_low = split(right)
    return (
        dot(left_high, right_high, dims)
        + dot(left_high, right_low, dims)
        + dot(left_low, right_high, dims)
    )


def one_hot(ids, rows, base=0):
    place = lax.broadcasted_iota(jnp.int32, (rows, ids.shape[1]), 0)
    return jnp.where(place == ids - base, 1.0, 0.0).astype(BF16)


def store_split(ref, cols, value):
    high, low = split(value)
    depth = value.shape[0]
    ref[0:depth, cols] = high
    ref[depth : 2 * depth, cols] = low


def folded(value):
    depth = value.shape[0] // 2
    return value[:depth] + value[depth:]


def quantized(value):
    top = jnp.max(jnp.abs(value), axis=0, keepdims=True)
    exponent = jnp.floor(jnp.log2(jnp.maximum(top, 1e-30))) + 1.0
    return jnp.round(value * (REACH * jnp.exp2(-exponent))), exponent


def scale_of(exponent):
    return jnp.exp2(exponent) * (1.0 / REACH)


def to_words(value):
    return value.astype(jnp.int32).astype(jnp.int16)


def from_words(words):
    return words.astype(jnp.int32).astype(F32)


def pack_table(value, rows=None):
    scaled, exponent = quantized(value)
    spare = (rows or value.shape[0] + 16) - value.shape[0]
    tail = jnp.broadcast_to(exponent, (spare, value.shape[1]))
    return to_words(jnp.concatenate([scaled, tail], axis=0))


def unpack_table(words, depth=None):
    depth = depth or words.shape[0] - 16
    value = from_words(words)
    return value[:depth] * scale_of(value[depth : depth + 1])


class Part:
    def __init__(self, plan, units, groups):
        self.units = units
        self.rows = (units + 2) // 2 * 16
        self.masks = [self.group_masks(bits) for bits in groups]
        order = [bit for group in groups for bit in reversed(group)]
        self.place = {bit: len(order) - 1 - at for at, bit in enumerate(order)}
        self.packed = (plan.half_chunks, self.rows, LANES)
        self.bare = (plan.half_chunks, 8 * units, LANES)

    @staticmethod
    def group_masks(bits):
        masks = []
        for index in range(2 ** len(bits)):
            masks.append(sum(((index >> at) & 1) << bit for at, bit in enumerate(bits)))
        return masks

    def position(self, chunk, me):
        relative = chunk ^ (me >> 1)
        out = 0
        for bit, at in self.place.items():
            out = out + (((relative >> (bit - 1)) & 1) << at)
        return out

    def shares(self, count, size):
        count = count // size
        return [shape((count,) + self.bare[1:], F32)] + [
            shape((count,) + self.packed[1:], jnp.int16)
        ] * (size - 1)


class Plan:
    def __init__(self, doms, rels, prows, width, rems, nrels, maxb):
        self.doms, self.rels, self.maxb = doms, rels, maxb
        self.devices = doms * rels
        self.prows, self.width, self.rems, self.nrels = prows, width, rems, nrels
        self.buckets = doms // rels
        self.slots = rels * maxb
        self.bucket_edges = self.slots * LANES
        self.edges = self.buckets * self.bucket_edges
        self.part_lanes = prows // rels
        self.half_rel, self.half_rem = nrels // 2, rems // 2
        self.half_lanes = self.half_rel + self.half_rem
        self.subs = width // 8
        self.units = (self.half_lanes // LANES) * self.subs
        self.half_chunks = self.devices // 2
        self.chunk_units = -(-self.units // self.half_chunks)
        rel_bits = bits_of(rels)
        all_bits = rel_bits + bits_of(doms)
        near = list(range(1, rel_bits + 1))
        far = list(range(rel_bits + 1, all_bits))
        self.parts = [Part(self, self.chunk_units, [near, far])]

    def chunk_blocks(self, chunk, part):
        first = chunk * self.chunk_units + (self.parts[0].units if part else 0)
        blocks = []
        for unit in range(first, first + self.parts[part].units):
            lane, sub = divmod(unit, self.subs)
            blocks.append((lane * LANES, 8 * sub) if unit < self.units else None)
        return blocks

    def row(self, labels, bucket, kinds, first, count):
        rows = []
        for slot in range(first, first + count):
            rows += [labels[bucket][slot, kind : kind + 1, :] for kind in kinds]
        return jnp.concatenate(rows, axis=1) if len(rows) > 1 else rows[0]

    def whole_row(self, labels, kinds):
        rows = [
            self.row(labels, bucket, kinds, 0, self.slots) for bucket in range(self.buckets)
        ]
        return jnp.concatenate(rows, axis=1) if len(rows) > 1 else rows[0]

    def me(self):
        return lax.axis_index("dom") * self.rels + lax.axis_index("rel")

    def target_mask(self, rel):
        return reverse_bits(rel, self.rels) * self.buckets

    def dynamic_mask(self, rel):
        out = 0
        width = bits_of(self.rels)
        for bit in range(width):
            out = out + (((rel >> bit) & 1) << (width - 1 - bit))
        return out * self.buckets


def send(value, plan, target):
    pairs = [(device, target(device)) for device in range(plan.devices)]
    return lax.ppermute(value, ("dom", "rel"), pairs)


def lists_kernel(plan, *refs):
    tables, counts, outs = refs[:7], refs[7], refs[8:]
    source = lax.axis_index("dom")
    rel = lax.axis_index("rel")
    for mask, out in enumerate(outs):
        for bucket in range(plan.buckets):
            target = source ^ bucket ^ plan.dynamic_mask(rel ^ mask)
            stop = lax.rem(source - target + plan.doms, plan.doms)
            for turn in range(plan.maxb):
                at = bucket * plan.maxb + turn
                for kind, table in enumerate(tables):
                    out[at, kind : kind + 1, :] = table[0, stop, turn : turn + 1, :]
                live = jnp.where(turn < counts[stop], 1, 0)
                out[at, 7:8, :] = jnp.full((1, LANES), live, jnp.int32)


def forward_kernel(plan, *refs):
    lists, outs = refs[: plan.rels], refs[plan.rels :]
    for bucket, out in enumerate(outs):
        for mask, ref in enumerate(lists):
            for turn in range(plan.maxb):
                out[mask * plan.maxb + turn] = ref[bucket * plan.maxb + turn]


def split_kernel(relations, out):
    depth = relations.shape[0]
    high, low = split(relations[...])
    out[0:depth, :] = high
    out[depth : 2 * depth, :] = low


def relation_kernel(plan, *refs):
    labels, relations, out = refs[:1], refs[1], refs[-1]
    for pair in range(0, plan.slots, 2):
        count = min(2, plan.slots - pair)
        start = pair * LANES
        ids = plan.row(labels, 0, (2,), pair, count)
        out[:, start : start + count * LANES] = folded(
            dot(relations[...], one_hot(ids, plan.nrels), NN)
        )


def rows_kernel(plan, *refs):
    labels, (own, rem) = refs[:1], refs[1:3]
    lhs_out, rem_out = refs[-2:]
    for pair in range(0, plan.slots, 2):
        count = min(2, plan.slots - pair)
        row = lambda *kinds: plan.row(labels, 0, kinds, pair, count)
        start = pair * LANES
        end = start + count * LANES
        lhs_out[:, start:end] = dot(own[...], one_hot(row(0), plan.prows), NN) + dot(
            rem[...], one_hot(row(1), plan.rems), NN
        )
        rem_out[:, 2 * start : 2 * end] = dot(
            rem[...], one_hot(row(4, 6), plan.rems), NN
        ).astype(BF16)


def conjugate_parts(grad, other):
    half = grad.shape[0] // 2
    grad_re, grad_im = grad[:half], grad[half:]
    other_re, other_im = other[:half], other[half:]
    return jnp.concatenate(
        [grad_re * other_re + grad_im * other_im, grad_im * other_re - grad_re * other_im], 0
    )


def complex_product(left, right):
    half = left.shape[0] // 2
    left_re, left_im = left[:half], left[half:]
    right_re, right_im = right[:half], right[half:]
    return jnp.concatenate(
        [left_re * right_re - left_im * right_im, left_re * right_im + left_im * right_re], 0
    )


def bucket_grads(plan, labels, target, lhs_in, rel_in, rem_in, lhs_out, rel_out, cand_out, base):
    total = 2 * LANES
    edge = lax.broadcasted_iota(jnp.int32, (LANES, total), 0)
    column = lax.broadcasted_iota(jnp.int32, (LANES, total), 1)
    keep = jnp.where(edge == column, 0.0, 1.0 / total)
    for slot in range(plan.slots):
        cols = slice(slot * LANES, (slot + 1) * LANES)
        wide = slice(slot * total, (slot + 1) * total)
        ids = plan.row(labels, 0, (3, 5), slot, 1)
        cand = dot(target[...], one_hot(ids, plan.prows), NN) + rem_in[:, wide].astype(F32)
        rhs = cand[:, :LANES]
        lhs, vec = lhs_in[:, cols], rel_in[:, cols]
        u_vec = complex_product(lhs, vec)
        live = plan.row(labels, 0, (7,), slot, 1).astype(F32)
        positive = jnp.sum(u_vec * rhs, axis=0, keepdims=True)
        negative = dot3(u_vec, cand, TN)
        grad_pos = -jax.nn.sigmoid(-positive) * live
        grad_neg = jax.nn.sigmoid(negative) * keep * live[0:1, 0:1]
        grad_u = grad_pos * rhs + dot3(cand, grad_neg, NT)
        from_neg = dot3(u_vec, grad_neg, NN)
        grad_cand = jnp.concatenate(
            [from_neg[:, :LANES] + grad_pos * u_vec, from_neg[:, LANES:]], axis=1
        )
        at = base + slot
        cols = slice(at * LANES, (at + 1) * LANES)
        wide = slice(at * total, (at + 1) * total)
        store_split(lhs_out, cols, conjugate_parts(grad_u, vec))
        store_split(rel_out, cols, conjugate_parts(grad_u, lhs))
        store_split(cand_out, wide, grad_cand)


def bucket_kernel(plan, *refs):
    bucket_grads(plan, refs[:1], *refs[1:], 0)


def last_kernel(plan, after, *refs):
    labels, refs = refs[: plan.buckets], refs[plan.buckets :]
    before, refs = refs[: 3 * (plan.buckets - 1)], refs[3 * (plan.buckets - 1) :]
    inputs, refs = refs[:4], refs[4 + after :]
    away, outs, table = refs[: len(plan.parts)], refs[-4:-1], refs[-1]
    bucket_grads(plan, labels[:1], *inputs, *outs, 0)
    for at, ref in enumerate(before):
        wide = ref.shape[1]
        start = (at // 3 + 1) * wide
        outs[at % 3][:, start : start + wide] = ref[...]
    reduce_half(plan, True, labels, outs, table, away)


def reduce_half(plan, away, labels, grads, table, outs):
    lhs_grads, rel_grads, cand_grads = grads
    me = plan.me()
    half = (me & 1) ^ (1 if away else 0)
    step = 2 * LANES if plan.half_rel % (2 * LANES) == 0 else LANES
    ids = plan.whole_row(labels, (2,)) - half * plan.half_rel
    for start in range(0, plan.half_rel, step):
        hot = one_hot(ids, step, start)
        table[:, start : start + step] = folded(dot(rel_grads[...], hot, NT))
    base = half * plan.half_rem
    first = one_hot(plan.whole_row(labels, (1,)), plan.half_rem, base)
    second = one_hot(plan.whole_row(labels, (4, 6)), plan.half_rem, base)
    table[:, plan.half_rel :] = folded(
        dot(lhs_grads[...], first, NT) + dot(cand_grads[...], second, NT)
    )
    for chunk in range(plan.half_chunks):
        for which, (part, out) in enumerate(zip(plan.parts, outs)):
            value = jnp.concatenate(
                [
                    table[block[1] : block[1] + 8, block[0] : block[0] + LANES]
                    if block
                    else jnp.zeros((8, LANES), F32)
                    for block in plan.chunk_blocks(chunk, which)
                ],
                axis=0,
            )
            out[part.position(chunk, me)] = pack_table(value, part.rows) if away else value


def rows_sum(plan, ids, grads):
    shift = lax.axis_index("rel") * plan.part_lanes
    return folded(dot(grads, one_hot(ids ^ shift, plan.prows), NT))


def target_kernel(plan, *refs):
    count = plan.buckets
    ids = plan.whole_row(refs[:count], (3, 5))
    value = pack_table(rows_sum(plan, ids, refs[count][...]))
    for at, out in enumerate(refs[-2:]):
        lanes = out.shape[1]
        out[...] = value[:, at * lanes : (at + 1) * lanes]


def home_kernel(plan, *refs):
    count = plan.buckets
    reduce_half(plan, False, refs[:count], refs[count : count + 3], refs[-1], refs[-1 - len(plan.parts) : -1])


def source_sum(plan, labels, grads):
    return rows_sum(plan, plan.row([labels], 0, (0,), 0, plan.slots), grads)


def deal(plan, value, keep, away):
    lanes = plan.part_lanes
    for at in range(value.shape[1] // lanes):
        share = value[:, at * lanes : (at + 1) * lanes]
        to = slice(at // 2 * lanes, (at // 2 + 1) * lanes)
        if at % 2:
            away[:, to] = pack_table(share)
        else:
            keep[:, to] = share


def source_kernel(plan, labels, grads, *outs):
    deal(plan, source_sum(plan, labels, grads[...]), *outs)


def own_source_kernel(plan, *refs):
    refs[-1][...] = source_sum(plan, refs[0], refs[1][:, : plan.bucket_edges])


def share(plan, count, *refs):
    source, fars, others = refs[0], refs[1:3], refs[3 : 3 + 2 * count]
    outs = refs[3 + 2 * count :]
    far = jnp.concatenate([unpack_table(ref[...]) for ref in fars], axis=1)
    deal(plan, source[...] + far, *outs[:2])
    for at in range(0, 2 * count, 2):
        deal_again(plan, *others[at : at + 2], *outs[at + 2 : at + 4])


def deal_again(plan, keep, came, *outs):
    deal(plan, keep[...] + unpack_table(came[...]), *outs)


def deal_and_settle(plan, count, *refs):
    ins, outs = refs[: 2 + 2 * count], refs[2 + 2 * count :]
    deal_again(plan, *ins[:2], *outs[:2])
    for at in range(count):
        add_kernel(2, *ins[2 + 2 * at : 4 + 2 * at], outs[2 + at])


def deal_kernel(plan, *refs):
    deal_again(plan, *refs)


def add_kernel(count, *refs):
    value = refs[0][...]
    for ref in refs[1:count]:
        value = value + unpack_table(ref[...])
    refs[-1][...] = pack_table(value)


def combine_kernel(plan, arrivals, sizes, beside, after, *refs):
    at, out_at = 0, sum(arrivals) + len(arrivals) + after
    if beside:
        step, ins, outs = beside
        step(plan, *refs[out_at : out_at + ins], *refs[len(refs) - outs :])
        out_at += ins
    for part, count, size in zip(plan.parts, arrivals, sizes):
        keep, arrived = refs[at], refs[at + 1 : at + 1 + count]
        outs = refs[out_at : out_at + size]
        at, out_at = at + 1 + count, out_at + size
        share = keep.shape[0] // size
        for place in range(keep.shape[0]):
            value = keep[place]
            for ref in arrived:
                value = value + unpack_table(ref[place], 8 * part.units)
            which, inner = divmod(place, share)
            packed = which or size == 1
            outs[which][inner] = pack_table(value, part.rows) if packed else value


def stack_kernel(plan, counts, *refs):
    outs = refs[-1 - len(counts) : -1]
    add = refs[sum(counts) : -1 - len(counts)]
    add_kernel(len(add), *add, refs[-1])
    first = 0
    for count, out in zip(counts, outs):
        for at in range(count):
            out[at] = refs[first + at][0]
        first += count


def spread_kernel(plan, counts, side, *refs):
    helds = refs[len(refs) - len(counts) :]
    rel_out, rem_out = refs[-2 - len(counts) : len(refs) - len(counts)]
    me = plan.me()
    first = 0
    for count, held in zip(counts, helds):
        at = 0
        for piece in refs[first : first + count]:
            held[at : at + piece.shape[0]] = piece[...]
            at += piece.shape[0]
        first += count
    for chunk in range(plan.half_chunks):
        for which, (part, held) in enumerate(zip(plan.parts, helds)):
            value = unpack_table(held[part.position(chunk, me)], 8 * part.units)
            for index, block in enumerate(plan.chunk_blocks(chunk, which)):
                if block is None:
                    break
                lane, sub = block
                rows = slice(sub, sub + 8)
                piece = value[8 * index : 8 * index + 8]
                if lane < plan.half_rel:
                    rel_out[rows, lane : lane + LANES] = piece
                else:
                    lane -= plan.half_rel
                    rem_out[rows, lane : lane + LANES] = piece


def part_out_kernel(plan, *refs):
    out = refs[-1]
    rel = lax.axis_index("rel")
    lanes = plan.part_lanes
    for mask, ref in enumerate(refs[: plan.rels]):
        if lanes % LANES:
            out[:, mask * lanes : (mask + 1) * lanes] = unpack_table(ref[...])
        else:
            start = pl.multiple_of((rel ^ mask) * lanes, lanes)
            out[:, pl.ds(start, lanes)] = unpack_table(ref[...])


def shape(extent, kind):
    return jax.ShapeDtypeStruct(extent, kind)


VMEM = pl.BlockSpec(memory_space=pltpu.VMEM)
ANY = pl.BlockSpec(memory_space=pl.ANY)


def call(kernel, outs, args, name, cost, limit, scratch=(), in_specs=None, out_specs=None, **more):
    work = pl.CostEstimate(flops=int(cost * 1e9), bytes_accessed=int(cost * 3e6), transcendentals=0)
    if "grid_spec" not in more:
        more["in_specs"] = in_specs or [VMEM] * len(args)
        more["out_specs"] = out_specs or [VMEM] * len(outs)
        more["scratch_shapes"] = list(scratch)
    return pl.pallas_call(
        kernel,
        out_shape=outs,
        compiler_params=pltpu.CompilerParams(vmem_limit_bytes=int(limit * 2**20)),
        cost_estimate=work,
        name=name,
        **more,
    )(*args)


def body(
    partitions,
    remainder,
    relations,
    counts,
    lhs_rows,
    lhs_rems,
    rel_ids,
    rhs_rows,
    rhs_rems,
    neg_rows,
    neg_rems,
):
    prows, width = partitions.shape
    plan = Plan(
        lax.axis_size("dom"),
        lax.axis_size("rel"),
        prows,
        width,
        remainder.shape[0],
        relations.shape[0],
        lhs_rows.shape[2],
    )
    smem = pl.BlockSpec(memory_space=pltpu.SMEM)
    own, rem, rels = partitions.T, remainder.T, relations.T
    edges, wide = plan.edges, plan.bucket_edges
    grow = max(1, edges // 1024)
    buckets = plan.buckets
    afar = lambda d: d ^ (plan.target_mask(d % plan.rels) * plan.rels)
    i16 = jnp.int16

    def exchanged(values, masks):
        return [
            send(value, plan, lambda d, m=mask: d ^ m) for value, mask in zip(values, masks[1:])
        ]

    def after(kernel, outs, args, others, name, cost, limit=12, **more):
        return call(
            kernel,
            outs,
            list(args) + list(others),
            name,
            cost,
            limit,
            in_specs=[VMEM] * len(args) + [ANY] * len(others),
            **more,
        )

    target = send(own, plan, afar)
    sources = [own] + [
        send(own, plan, lambda d, b=bucket: d ^ (b * plan.rels)) for bucket in range(1, buckets)
    ]
    tables = [lhs_rows, lhs_rems, rel_ids, rhs_rows, rhs_rems, neg_rows, neg_rems]
    lists = call(
        functools.partial(lists_kernel, plan),
        [shape((buckets * plan.maxb, 8, LANES), jnp.int32)] * plan.rels,
        tables + [counts.reshape(-1)],
        "lists",
        0.5,
        60,
        in_specs=[VMEM] * 7 + [smem],
    )
    lists = [lists[0]] + exchanged(lists[1:], range(plan.rels))
    labels = call(
        functools.partial(forward_kernel, plan),
        [shape((plan.slots, 8, LANES), jnp.int32)] * buckets,
        lists,
        "forward",
        0.2,
        8,
    )
    labels = [labels[0]] + [
        send(labels[bucket], plan, lambda d, b=bucket: d ^ (b * plan.rels))
        for bucket in range(1, buckets)
    ]
    labels_of = lambda bucket: [labels[bucket]]
    (rel_split,) = call(
        split_kernel,
        [shape((2 * width, plan.nrels), BF16)],
        [rels],
        "rel_split",
        2.0,
        50,
        in_specs=[pl.BlockSpec((width, 4 * LANES), lambda i: (0, i))],
        out_specs=[pl.BlockSpec((2 * width, 4 * LANES), lambda i: (0, i))],
        grid=(plan.nrels // (4 * LANES),),
    )

    grad_shapes = lambda count: [
        shape((2 * width, count), BF16),
        shape((2 * width, count), BF16),
        shape((2 * width, 2 * count), BF16),
    ]
    inputs = []
    for bucket in range(buckets):
        (vec,) = call(
            functools.partial(relation_kernel, plan),
            [shape((width, wide), F32)],
            labels_of(bucket) + [rel_split],
            "relation",
            2.0,
            16 * grow,
        )
        lhs, cand_rem = call(
            functools.partial(rows_kernel, plan),
            [shape((width, wide), F32), shape((width, 2 * wide), BF16)],
            labels_of(bucket) + [sources[bucket], rem],
            "rows",
            0.7,
            12 * grow,
        )
        inputs.append([lhs, vec, cand_rem])
    lanes = plan.part_lanes
    dealt = lambda count: [
        shape((width, count * lanes), F32),
        shape((width + 16, count * lanes), i16),
    ]
    grads, others = [], []
    for bucket in range(1, buckets):
        made = call(
            functools.partial(bucket_kernel, plan),
            grad_shapes(wide),
            labels_of(bucket) + [target] + inputs[bucket],
            "bucket",
            4.0,
            16 * grow,
        )
        grads += made
        others.append(
            call(
                functools.partial(source_kernel, plan),
                dealt(plan.rels // 2),
                labels_of(bucket) + [made[0]],
                "source",
                0.8,
                12 * grow,
            )
        )
    table = [pltpu.VMEM((width, plan.half_lanes), F32)]
    made = after(
        functools.partial(last_kernel, plan, len(others)),
        [shape(part.packed, i16) for part in plan.parts] + grad_shapes(edges),
        labels + grads + [target] + inputs[0],
        [other[0] for other in others],
        "last",
        9.0,
        20 * grow,
        scratch=table,
    )
    away, grads = list(made[: len(plan.parts)]), list(made[len(plan.parts) :])
    cores = [send(value, plan, lambda d: d ^ 1) for value in away]

    others = [[keep, send(value, plan, lambda d: d ^ 1)] for keep, value in others]
    keeps = after(
        functools.partial(home_kernel, plan),
        [shape(part.bare, F32) for part in plan.parts],
        labels + grads,
        away,
        "home",
        4.0,
        16 * grow,
        scratch=table,
    )

    def combine(keeps, arrived, level, name, step=None, step_args=(), step_outs=(), order=()):
        sizes = [len(part.masks[level]) if level < 2 else 1 for part in plan.parts]
        outs, args = [], []
        for part, keep, pieces, size in zip(plan.parts, keeps, arrived, sizes):
            args += [keep] + pieces
            if level < 2:
                outs += part.shares(keep.shape[0], size)
            else:
                outs.append(shape((1,) + part.packed[1:], i16))
        beside = (step, len(step_args), len(step_outs)) if step else None
        count = [len(pieces) for pieces in arrived]
        made = after(
            functools.partial(combine_kernel, plan, count, sizes, beside, len(order)),
            outs + list(step_outs),
            args + list(step_args),
            order,
            name,
            0.6,
        )
        made, beside = made[: len(outs)], made[len(outs) :]
        if level == 2:
            return made, [], beside
        keeps, arrived = [], []
        for part, size in zip(plan.parts, sizes):
            group, made = made[:size], made[size:]
            keeps.append(group[0])
            arrived.append(exchanged(group[1:], part.masks[level]))
        return keeps, arrived, beside

    keeps, arrived, _ = combine(
        keeps, [[core] for core in cores], 0, "combine_cores", order=[other[1] for other in others]
    )
    far = after(
        functools.partial(target_kernel, plan),
        [shape((width + 16, prows // 2), i16)] * 2,
        labels + [grads[2]],
        [keeps[0]],
        "target",
        1.8,
        16 * grow,
    )
    (source,) = after(
        functools.partial(own_source_kernel, plan),
        [shape((width, prows), F32)],
        labels_of(0) + [grads[0]],
        [far[0]],
        "own_source",
        0.8,
        16 * grow,
    )
    far = [send(value, plan, afar) for value in far]
    def deal_on(pairs, count, bit):
        while count > 2:
            count, bit = count // 2, bit * 2
            made = [
                after(functools.partial(deal_kernel, plan), dealt(count), pair, [], "deal", 0.3)
                for pair in pairs
            ]
            pairs = [[keep, send(value, plan, lambda d, m=bit: d ^ m)] for keep, value in made]
        return pairs, count // 2, bit * 2

    others, count, bit = deal_on(others, plan.rels // 2, 1)
    keeps, arrived, made = combine(
        keeps,
        arrived,
        1,
        "combine_first",
        lambda plan, *refs: share(plan, len(others), *refs),
        [source] + far + sum(others, []),
        dealt(plan.rels // 2) + dealt(count) * len(others),
    )
    mine = [[made[0], send(made[1], plan, lambda d: d ^ 1)]]
    others = [
        [made[at], send(made[at + 1], plan, lambda d: d ^ bit)] for at in range(2, len(made), 2)
    ]
    (mine,), count, bit = deal_on(mine, plan.rels // 2, 1)
    totals, _, made = combine(
        keeps,
        arrived,
        2,
        "combine_last",
        lambda plan, *refs: deal_and_settle(plan, len(others), *refs),
        mine + sum(others, []),
        dealt(count) + [shape((width + 16, lanes), i16)] * len(others),
    )
    mine, came = made[0], send(made[1], plan, lambda d: d ^ bit)
    crossing = exchanged(made[2:], range(0, plan.rels * buckets, plan.rels))
    pieces = [
        [total] + exchanged([total] * (len(part.masks[1]) - 1), part.masks[1])
        for part, total in zip(plan.parts, totals)
    ]
    flat = sum(pieces, [])
    made = after(
        functools.partial(stack_kernel, plan, [len(group) for group in pieces]),
        [
            shape((len(group),) + part.packed[1:], i16)
            for part, group in zip(plan.parts, pieces)
        ]
        + [shape((width + 16, lanes), i16)],
        flat + [mine, came] + crossing,
        [],
        "stack",
        0.5,
    )
    blocks, owners = made[:-1], {0: made[-1]}
    pieces = [
        [block] + exchanged([block] * (len(part.masks[0]) - 1), part.masks[0])
        for part, block in zip(plan.parts, blocks)
    ]
    while bit:
        for mask in sorted(owners):
            owners[mask | bit] = send(owners[mask], plan, lambda d, m=bit: d ^ m)
        bit //= 2
    (grad_partitions,) = after(
        functools.partial(part_out_kernel, plan),
        [shape((width, prows), F32)],
        [owners[mask] for mask in range(plan.rels)],
        [],
        "part_out",
        1.0,
    )
    if lanes % LANES:
        order = jnp.arange(plan.rels) ^ lax.axis_index("rel")
        split_lanes = grad_partitions.reshape(width, plan.rels, lanes)
        grad_partitions = jnp.take(split_lanes, order, axis=1).reshape(width, prows)

    crossed = [[send(piece, plan, lambda d: d ^ 1) for piece in group] for group in pieces]
    side = lax.axis_index("rel") & 1
    outs = [shape((width, plan.nrels), F32), shape((width, plan.rems), F32)]
    spec = lambda lanes: pl.BlockSpec((width, lanes), lambda i, half: (0, half[0]))
    made = []
    for turn, groups in enumerate([pieces, crossed]):
        flat = sum(groups, [])
        made = call(
            functools.partial(spread_kernel, plan, [len(group) for group in groups]),
            outs,
            [(side ^ turn).reshape(1), *flat, *made],
            "spread",
            2.0,
            16,
            grid_spec=pltpu.PrefetchScalarGridSpec(
                num_scalar_prefetch=1,
                grid=(1,),
                in_specs=[pl.BlockSpec(piece.shape, lambda i, half: (0, 0, 0)) for piece in flat]
                + [ANY] * len(made),
                out_specs=[spec(plan.half_rel), spec(plan.half_rem)],
                scratch_shapes=[pltpu.VMEM(part.packed, i16) for part in plan.parts],
            ),
            input_output_aliases={1 + len(flat) + at: at for at in range(len(made))},
        )
    grad_relations, grad_remainder = made
    return grad_partitions.T, grad_remainder.T, grad_relations.T


def solution(mesh):
    edge = P("dom", None, "rel", None)
    in_specs = (P("dom", None), P(), P(), P("dom", None, "rel")) + (edge,) * 7
    out_specs = (P("dom", None), P(), P())
    return jax.shard_map(body, mesh=mesh, in_specs=in_specs, out_specs=out_specs, check_vma=False)
```

```python
import functools

import jax
import jax.numpy as jnp
from jax import lax
from jax.experimental import pallas as pl
from jax.experimental.pallas import tpu as pltpu
from jax.sharding import PartitionSpec as P

F32 = jnp.float32
BF16 = jnp.bfloat16
LANES = 128
REACH = 32766.0
NT = (((1,), (1,)), ((), ()))
NN = (((1,), (0,)), ((), ()))
TN = (((0,), (0,)), ((), ()))


def bits_of(count):
    return count.bit_length() - 1


def reverse_bits(value, count):
    out = 0
    for bit in range(bits_of(count)):
        out = out * 2 + ((value >> bit) & 1)
    return out


def split(value):
    high = value.astype(BF16)
    low = (value - high.astype(F32)).astype(BF16)
    return high, low


def dot(left, right, dims):
    return lax.dot_general(left, right, dims, preferred_element_type=F32)


def stacked(parts, axis):
    return jnp.concatenate(parts, axis=axis)


def one_hot(ids, rows, base=0):
    place = lax.broadcasted_iota(jnp.int32, (rows, ids.shape[1]), 0)
    return jnp.where(place == ids - base, 1.0, 0.0).astype(BF16)


def store_split(ref, cols, value):
    high, low = split(value)
    depth = value.shape[0]
    ref[0:depth, cols] = high
    ref[depth : 2 * depth, cols] = low


def folded(value):
    depth = value.shape[0] // 2
    return value[:depth] + value[depth:]


def quantized(value):
    top = jnp.max(jnp.abs(value), axis=0, keepdims=True)
    exponent = jnp.floor(jnp.log2(jnp.maximum(top, 1e-30))) + 1.0
    return jnp.round(value * (REACH * jnp.exp2(-exponent))), exponent


def scale_of(exponent):
    return jnp.exp2(exponent) * (1.0 / REACH)


def to_words(value):
    return value.astype(jnp.int32).astype(jnp.int16)


def from_words(words):
    return words.astype(jnp.int32).astype(F32)


def pack_table(value, rows=None):
    scaled, exponent = quantized(value)
    spare = (rows or value.shape[0] + 16) - value.shape[0]
    tail = jnp.broadcast_to(exponent, (spare, value.shape[1]))
    return to_words(jnp.concatenate([scaled, tail], axis=0))


def unpack_table(words, depth=None):
    depth = depth or words.shape[0] - 16
    value = from_words(words)
    return value[:depth] * scale_of(value[depth : depth + 1])


class Part:
    def __init__(self, plan, units, groups):
        self.units = units
        self.rows = (units + 2) // 2 * 16
        self.masks = [self.group_masks(bits) for bits in groups]
        order = [bit for group in groups for bit in reversed(group)]
        self.place = {bit: len(order) - 1 - at for at, bit in enumerate(order)}
        self.packed = (plan.half_chunks, self.rows, LANES)
        self.bare = (plan.half_chunks, 8 * units, LANES)

    @staticmethod
    def group_masks(bits):
        masks = []
        for index in range(2 ** len(bits)):
            masks.append(sum(((index >> at) & 1) << bit for at, bit in enumerate(bits)))
        return masks

    def position(self, chunk, me):
        relative = chunk ^ (me >> 1)
        out = 0
        for bit, at in self.place.items():
            out = out + (((relative >> (bit - 1)) & 1) << at)
        return out

    def shares(self, count, size):
        count = count // size
        return [shape((count,) + self.bare[1:], F32)] + [
            shape((count,) + self.packed[1:], jnp.int16)
        ] * (size - 1)


class Plan:
    def __init__(self, doms, rels, prows, width, rems, nrels, maxb):
        self.doms, self.rels, self.maxb = doms, rels, maxb
        self.devices = doms * rels
        self.prows, self.width, self.rems, self.nrels = prows, width, rems, nrels
        self.buckets = doms // rels
        self.slots = rels * maxb
        self.bucket_edges = self.slots * LANES
        self.edges = self.buckets * self.bucket_edges
        self.part_lanes = prows // rels
        self.half_rel, self.half_rem = nrels // 2, rems // 2
        self.half_lanes = self.half_rel + self.half_rem
        self.subs = width // 8
        self.units = (self.half_lanes // LANES) * self.subs
        self.half_chunks = self.devices // 2
        self.chunk_units = -(-self.units // self.half_chunks)
        rel_bits = bits_of(rels)
        all_bits = rel_bits + bits_of(doms)
        near = list(range(1, rel_bits + 1))
        far = list(range(rel_bits + 1, all_bits))
        self.parts = [Part(self, self.chunk_units, [near, far])]

    def chunk_blocks(self, chunk, part):
        first = chunk * self.chunk_units + (self.parts[0].units if part else 0)
        blocks = []
        for unit in range(first, first + self.parts[part].units):
            lane, sub = divmod(unit, self.subs)
            blocks.append((lane * LANES, 8 * sub) if unit < self.units else None)
        return blocks

    def row(self, labels, bucket, kinds, first, count):
        rows = []
        for slot in range(first, first + count):
            rows += [labels[bucket][slot, kind : kind + 1, :] for kind in kinds]
        return jnp.concatenate(rows, axis=1) if len(rows) > 1 else rows[0]

    def whole_row(self, labels, kinds):
        rows = [
            self.row(labels, bucket, kinds, 0, self.slots) for bucket in range(self.buckets)
        ]
        return jnp.concatenate(rows, axis=1) if len(rows) > 1 else rows[0]

    def me(self):
        return lax.axis_index("dom") * self.rels + lax.axis_index("rel")

    def target_mask(self, rel):
        return reverse_bits(rel, self.rels) * self.buckets

    def dynamic_mask(self, rel):
        out = 0
        width = bits_of(self.rels)
        for bit in range(width):
            out = out + (((rel >> bit) & 1) << (width - 1 - bit))
        return out * self.buckets


def send(value, plan, target):
    pairs = [(device, target(device)) for device in range(plan.devices)]
    return lax.ppermute(value, ("dom", "rel"), pairs)


def lists_kernel(plan, *refs):
    tables, counts, own, outs = refs[:7], refs[7], refs[8], refs[10:-1]
    refs[-1][...] = own[...]
    source = lax.axis_index("dom")
    rel = lax.axis_index("rel")
    for mask, out in enumerate(outs):
        for bucket in range(plan.buckets):
            target = source ^ bucket ^ plan.dynamic_mask(rel ^ mask)
            stop = lax.rem(source - target + plan.doms, plan.doms)
            for turn in range(plan.maxb):
                at = bucket * plan.maxb + turn
                for kind, table in enumerate(tables):
                    out[at, kind : kind + 1, :] = table[0, stop, turn : turn + 1, :]
                live = jnp.where(turn < counts[stop], 1, 0)
                out[at, 7:8, :] = jnp.full((1, LANES), live, jnp.int32)


def forward_kernel(plan, *refs):
    lists, outs = refs[: plan.rels], refs[plan.rels :]
    for bucket, out in enumerate(outs):
        for mask, ref in enumerate(lists):
            for turn in range(plan.maxb):
                out[mask * plan.maxb + turn] = ref[bucket * plan.maxb + turn]


def split_kernel(relations, out):
    depth = relations.shape[0]
    high, low = split(relations[...])
    out[0:depth, :] = high
    out[depth : 2 * depth, :] = low


def relation_kernel(plan, *refs):
    labels, relations, out = refs[:1], refs[1], refs[-1]
    for pair in range(0, plan.slots, 2):
        count = min(2, plan.slots - pair)
        start = pair * LANES
        ids = plan.row(labels, 0, (2,), pair, count)
        out[:, start : start + count * LANES] = folded(
            dot(relations[...], one_hot(ids, plan.nrels), NN)
        )


def rows_kernel(plan, *refs):
    labels, (own, rem) = refs[:1], refs[1:3]
    lhs_out, rem_out = refs[-2:]
    for pair in range(0, plan.slots, 2):
        count = min(2, plan.slots - pair)
        row = lambda *kinds: plan.row(labels, 0, kinds, pair, count)
        start = pair * LANES
        end = start + count * LANES
        lhs_out[:, start:end] = dot(own[...], one_hot(row(0), plan.prows), NN) + dot(
            rem[...], one_hot(row(1), plan.rems), NN
        )
        rem_out[:, 2 * start : 2 * end] = dot(
            rem[...], one_hot(row(4, 6), plan.rems), NN
        ).astype(BF16)


def conjugate_parts(grad, other):
    half = grad.shape[0] // 2
    grad_re, grad_im = grad[:half], grad[half:]
    other_re, other_im = other[:half], other[half:]
    return jnp.concatenate(
        [grad_re * other_re + grad_im * other_im, grad_im * other_re - grad_re * other_im], 0
    )


def complex_product(left, right):
    half = left.shape[0] // 2
    left_re, left_im = left[:half], left[half:]
    right_re, right_im = right[:half], right[half:]
    return jnp.concatenate(
        [left_re * right_re - left_im * right_im, left_re * right_im + left_im * right_re], 0
    )


def bucket_grads(plan, labels, target, lhs_in, rel_in, rem_in, lhs_out, rel_out, cand_out, base):
    total = 2 * LANES
    edge = lax.broadcasted_iota(jnp.int32, (LANES, total), 0)
    column = lax.broadcasted_iota(jnp.int32, (LANES, total), 1)
    keep = jnp.where(edge == column, 0.0, 1.0 / total)
    for slot in range(plan.slots):
        cols = slice(slot * LANES, (slot + 1) * LANES)
        wide = slice(slot * total, (slot + 1) * total)
        ids = plan.row(labels, 0, (3, 5), slot, 1)
        cand = dot(target[...], one_hot(ids, plan.prows), NN) + rem_in[:, wide].astype(F32)
        rhs = cand[:, :LANES]
        lhs, vec = lhs_in[:, cols], rel_in[:, cols]
        u_vec = complex_product(lhs, vec)
        live = plan.row(labels, 0, (7,), slot, 1).astype(F32)
        positive = jnp.sum(u_vec * rhs, axis=0, keepdims=True)
        u_high, u_low = split(u_vec)
        cand_high, cand_low = split(cand)
        u_both, cand_both = stacked([u_high, u_low], 1), stacked([cand_high, cand_low], 0)
        negative = dot(u_both, cand_high, TN)
        negative = negative[:LANES] + negative[LANES:] + dot(u_high, cand_low, TN)
        grad_pos = -jax.nn.sigmoid(-positive) * live
        grad_neg = jax.nn.sigmoid(negative) * keep * live[0:1, 0:1]
        neg_high, neg_low = split(grad_neg)
        grad_u = folded(dot(cand_both, neg_high, NT)) + dot(cand_high, neg_low, NT)
        grad_u = grad_pos * rhs + grad_u
        from_neg = folded(dot(stacked([u_high, u_low], 0), neg_high, NN))
        from_neg = from_neg + dot(u_high, neg_low, NN)
        grad_cand = jnp.concatenate(
            [from_neg[:, :LANES] + grad_pos * u_vec, from_neg[:, LANES:]], axis=1
        )
        at = base + slot
        cols = slice(at * LANES, (at + 1) * LANES)
        wide = slice(at * total, (at + 1) * total)
        store_split(lhs_out, cols, conjugate_parts(grad_u, vec))
        store_split(rel_out, cols, conjugate_parts(grad_u, lhs))
        store_split(cand_out, wide, grad_cand)


def bucket_kernel(plan, *refs):
    bucket_grads(plan, refs[:1], *refs[1:], 0)


def last_kernel(plan, *refs):
    labels, refs = refs[: plan.buckets], refs[plan.buckets :]
    before, refs = refs[: 3 * (plan.buckets - 1)], refs[3 * (plan.buckets - 1) :]
    inputs, refs = refs[:4], refs[4:]
    away, rem_part, outs, table = refs[: len(plan.parts)], refs[-5], refs[-4:-1], refs[-1]
    base = (plan.buckets - 1) * plan.slots
    bucket_grads(plan, labels[-1:], *inputs, *outs, base)
    for at, ref in enumerate(before):
        wide = ref.shape[1]
        start = at // 3 * wide
        outs[at % 3][:, start : start + wide] = ref[...]
    lhs_grads, rel_grads, cand_grads = outs
    first = one_hot(plan.whole_row(labels, (1,)), plan.rems)
    second = one_hot(plan.whole_row(labels, (4, 6)), plan.rems)
    rem = folded(dot(lhs_grads[...], first, NT) + dot(cand_grads[...], second, NT))
    low, high = rem[:, : plan.half_rem], rem[:, plan.half_rem :]
    core = lax.axis_index("rel") & 1
    rem_part[...] = jnp.where(core == 0, low, high)
    table[:, plan.half_rel :] = jnp.where(core == 0, high, low)
    reduce_half(plan, True, labels, rel_grads, table, away)


def home_kernel(plan, *refs):
    count = plan.buckets
    outs, table = refs[-1 - len(plan.parts) : -1], refs[-1]
    table[:, plan.half_rel :] = refs[count + 1][...]
    reduce_half(plan, False, refs[:count], refs[count], table, outs)


def reduce_half(plan, away, labels, rel_grads, table, outs):
    me = plan.me()
    half = (me & 1) ^ (1 if away else 0)
    step = 2 * LANES if plan.half_rel % (2 * LANES) == 0 else LANES
    ids = plan.whole_row(labels, (2,)) - half * plan.half_rel
    for start in range(0, plan.half_rel, step):
        hot = one_hot(ids, step, start)
        table[:, start : start + step] = folded(dot(rel_grads[...], hot, NT))
    for chunk in range(plan.half_chunks):
        for which, (part, out) in enumerate(zip(plan.parts, outs)):
            value = jnp.concatenate(
                [
                    table[block[1] : block[1] + 8, block[0] : block[0] + LANES]
                    if block
                    else jnp.zeros((8, LANES), F32)
                    for block in plan.chunk_blocks(chunk, which)
                ],
                axis=0,
            )
            out[part.position(chunk, me)] = pack_table(value, part.rows) if away else value


def rows_sum(plan, ids, grads):
    shift = lax.axis_index("rel") * plan.part_lanes
    return folded(dot(grads, one_hot(ids ^ shift, plan.prows), NT))


def target_kernel(plan, *refs):
    count = plan.buckets
    ids = plan.whole_row(refs[:count], (3, 5))
    value = pack_table(rows_sum(plan, ids, refs[count][...]))
    for at, out in enumerate(refs[-2:]):
        lanes = out.shape[1]
        out[...] = value[:, at * lanes : (at + 1) * lanes]


def source_sum(plan, labels, grads):
    return rows_sum(plan, plan.row([labels], 0, (0,), 0, plan.slots), grads)


def deal(plan, value, keep, away):
    lanes = plan.part_lanes
    for at in range(value.shape[1] // lanes):
        share = value[:, at * lanes : (at + 1) * lanes]
        to = slice(at // 2 * lanes, (at // 2 + 1) * lanes)
        if at % 2:
            away[:, to] = pack_table(share)
        else:
            keep[:, to] = share


def source_kernel(plan, bucket, *refs):
    start = bucket * plan.bucket_edges
    grads = refs[1][:, start : start + plan.bucket_edges]
    deal(plan, source_sum(plan, refs[0], grads), *refs[-2:])


def own_source_kernel(plan, *refs):
    refs[-1][...] = source_sum(plan, refs[0], refs[1][:, : plan.bucket_edges])


def share(plan, count, *refs):
    source, fars, others = refs[0], refs[1:3], refs[3 : 3 + 2 * count]
    outs = refs[3 + 2 * count :]
    far = jnp.concatenate([unpack_table(ref[...]) for ref in fars], axis=1)
    deal(plan, source[...] + far, *outs[:2])
    for at in range(0, 2 * count, 2):
        deal_again(plan, *others[at : at + 2], *outs[at + 2 : at + 4])


def deal_again(plan, keep, came, *outs):
    deal(plan, keep[...] + unpack_table(came[...]), *outs)


def deal_and_settle(plan, count, *refs):
    ins, outs = refs[: 2 + 2 * count], refs[2 + 2 * count :]
    deal_again(plan, *ins[:2], *outs[:2])
    for at in range(count):
        add_kernel(2, *ins[2 + 2 * at : 4 + 2 * at], outs[2 + at])


def deal_kernel(plan, *refs):
    deal_again(plan, *refs)


def add_kernel(count, *refs):
    value = refs[0][...]
    for ref in refs[1:count]:
        value = value + unpack_table(ref[...])
    refs[-1][...] = pack_table(value)


def combine_kernel(plan, arrivals, sizes, beside, after, *refs):
    at, out_at = 0, sum(arrivals) + len(arrivals) + after
    if beside:
        step, ins, outs = beside
        step(plan, *refs[out_at : out_at + ins], *refs[len(refs) - outs :])
        out_at += ins
    for part, count, size in zip(plan.parts, arrivals, sizes):
        keep, arrived = refs[at], refs[at + 1 : at + 1 + count]
        outs = refs[out_at : out_at + size]
        at, out_at = at + 1 + count, out_at + size
        share = keep.shape[0] // size
        for place in range(keep.shape[0]):
            value = keep[place]
            for ref in arrived:
                value = value + unpack_table(ref[place], 8 * part.units)
            which, inner = divmod(place, share)
            packed = which or size == 1
            outs[which][inner] = pack_table(value, part.rows) if packed else value


def stack_kernel(plan, counts, *refs):
    outs = refs[-1 - len(counts) : -1]
    add = refs[sum(counts) : -1 - len(counts)]
    add_kernel(len(add), *add, refs[-1])
    first = 0
    for count, out in zip(counts, outs):
        for at in range(count):
            out[at] = refs[first + at][0]
        first += count


def spread_kernel(plan, counts, side, *refs):
    helds = refs[len(refs) - len(counts) :]
    rel_out, rem_out = refs[-2 - len(counts) : len(refs) - len(counts)]
    me = plan.me()
    first = 0
    for count, held in zip(counts, helds):
        at = 0
        for piece in refs[first : first + count]:
            held[at : at + piece.shape[0]] = piece[...]
            at += piece.shape[0]
        first += count
    for chunk in range(plan.half_chunks):
        for which, (part, held) in enumerate(zip(plan.parts, helds)):
            value = unpack_table(held[part.position(chunk, me)], 8 * part.units)
            for index, block in enumerate(plan.chunk_blocks(chunk, which)):
                if block is None:
                    break
                lane, sub = block
                rows = slice(sub, sub + 8)
                piece = value[8 * index : 8 * index + 8]
                if lane < plan.half_rel:
                    rel_out[rows, lane : lane + LANES] = piece
                else:
                    lane -= plan.half_rel
                    rem_out[rows, lane : lane + LANES] = piece


def part_out_kernel(plan, *refs):
    out = refs[-1]
    rel = lax.axis_index("rel")
    lanes = plan.part_lanes
    for mask, ref in enumerate(refs[: plan.rels]):
        if lanes % LANES:
            out[:, mask * lanes : (mask + 1) * lanes] = unpack_table(ref[...])
        else:
            start = pl.multiple_of((rel ^ mask) * lanes, lanes)
            out[:, pl.ds(start, lanes)] = unpack_table(ref[...])


def shape(extent, kind):
    return jax.ShapeDtypeStruct(extent, kind)


VMEM = pl.BlockSpec(memory_space=pltpu.VMEM)
ANY = pl.BlockSpec(memory_space=pl.ANY)


def call(kernel, outs, args, name, cost, limit, scratch=(), in_specs=None, out_specs=None, **more):
    work = pl.CostEstimate(flops=int(cost * 1e9), bytes_accessed=int(cost * 3e6), transcendentals=0)
    if "grid_spec" not in more:
        more["in_specs"] = in_specs or [VMEM] * len(args)
        more["out_specs"] = out_specs or [VMEM] * len(outs)
        more["scratch_shapes"] = list(scratch)
    return pl.pallas_call(
        kernel,
        out_shape=outs,
        compiler_params=pltpu.CompilerParams(vmem_limit_bytes=int(limit * 2**20)),
        cost_estimate=work,
        name=name,
        **more,
    )(*args)


def body(
    partitions,
    remainder,
    relations,
    counts,
    lhs_rows,
    lhs_rems,
    rel_ids,
    rhs_rows,
    rhs_rems,
    neg_rows,
    neg_rems,
):
    prows, width = partitions.shape
    plan = Plan(
        lax.axis_size("dom"),
        lax.axis_size("rel"),
        prows,
        width,
        remainder.shape[0],
        relations.shape[0],
        lhs_rows.shape[2],
    )
    smem = pl.BlockSpec(memory_space=pltpu.SMEM)
    own, rem, rels = partitions.T, remainder.T, relations.T
    edges, wide = plan.edges, plan.bucket_edges
    grow = max(1, edges // 1024)
    buckets = plan.buckets
    afar = lambda d: d ^ (plan.target_mask(d % plan.rels) * plan.rels)
    i16 = jnp.int16

    def exchanged(values, masks):
        return [
            send(value, plan, lambda d, m=mask: d ^ m) for value, mask in zip(values, masks[1:])
        ]

    def after(kernel, outs, args, others, name, cost, limit=12, **more):
        return call(
            kernel,
            outs,
            list(args) + list(others),
            name,
            cost,
            limit,
            in_specs=[VMEM] * len(args) + [ANY] * len(others),
            **more,
        )

    (rel_split,) = call(
        split_kernel,
        [shape((2 * width, plan.nrels), BF16)],
        [rels],
        "rel_split",
        2.0,
        50,
    )
    tables = [lhs_rows, lhs_rems, rel_ids, rhs_rows, rhs_rems, neg_rows, neg_rems]
    *lists, own = call(
        functools.partial(lists_kernel, plan),
        [shape((buckets * plan.maxb, 8, LANES), jnp.int32)] * plan.rels
        + [shape(own.shape, own.dtype)],
        tables + [counts.reshape(-1), own, rel_split],
        "lists",
        0.5,
        8,
        in_specs=[VMEM] * 7 + [smem, VMEM, ANY],
    )
    lists = [lists[0]] + exchanged(lists[1:], range(plan.rels))
    target = send(own, plan, afar)
    sources = [own] + [
        send(own, plan, lambda d, b=bucket: d ^ (b * plan.rels)) for bucket in range(1, buckets)
    ]
    labels = call(
        functools.partial(forward_kernel, plan),
        [shape((plan.slots, 8, LANES), jnp.int32)] * buckets,
        lists,
        "forward",
        0.2,
        8,
    )
    labels = [labels[0]] + [
        send(labels[bucket], plan, lambda d, b=bucket: d ^ (b * plan.rels))
        for bucket in range(1, buckets)
    ]
    labels_of = lambda bucket: [labels[bucket]]
    grad_shapes = lambda count: [
        shape((2 * width, count), BF16),
        shape((2 * width, count), BF16),
        shape((2 * width, 2 * count), BF16),
    ]
    inputs = []
    for bucket in range(buckets):
        (vec,) = call(
            functools.partial(relation_kernel, plan),
            [shape((width, wide), F32)],
            labels_of(bucket) + [rel_split],
            "relation",
            2.0,
            16 * grow,
        )
        lhs, cand_rem = call(
            functools.partial(rows_kernel, plan),
            [shape((width, wide), F32), shape((width, 2 * wide), BF16)],
            labels_of(bucket) + [sources[bucket], rem],
            "rows",
            0.7,
            12 * grow,
        )
        inputs.append([lhs, vec, cand_rem])
    lanes = plan.part_lanes
    dealt = lambda count: [
        shape((width, count * lanes), F32),
        shape((width + 16, count * lanes), i16),
    ]
    grads = []
    for bucket in range(buckets - 1):
        grads += call(
            functools.partial(bucket_kernel, plan),
            grad_shapes(wide),
            labels_of(bucket) + [target] + inputs[bucket],
            "bucket",
            4.0,
            16 * grow,
        )
    table = [pltpu.VMEM((width, plan.half_lanes), F32)]
    made = call(
        functools.partial(last_kernel, plan),
        [shape(part.packed, i16) for part in plan.parts]
        + [shape((width, plan.half_rem), F32)]
        + grad_shapes(edges),
        labels + grads + [target] + inputs[-1],
        "last",
        9.0,
        20 * grow,
        scratch=table,
    )
    made, grads = list(made[:-3]), list(made[-3:])
    away, rem_part = made[:-1], made[-1]
    cores = [send(value, plan, lambda d: d ^ 1) for value in away]

    others, order = [], list(away)
    for bucket in range(1, buckets):
        keep, value = after(
            functools.partial(source_kernel, plan, bucket),
            dealt(plan.rels // 2),
            labels_of(bucket) + [grads[0]],
            order,
            "source",
            0.8,
            12 * grow,
        )
        others.append([keep, send(value, plan, lambda d: d ^ 1)])
        order = [keep]
    keeps = after(
        functools.partial(home_kernel, plan),
        [shape(part.bare, F32) for part in plan.parts],
        labels + [grads[1], rem_part],
        order,
        "home",
        3.0,
        16 * grow,
        scratch=table,
    )

    def combine(keeps, arrived, level, name, step=None, step_args=(), step_outs=(), order=()):
        sizes = [len(part.masks[level]) if level < 2 else 1 for part in plan.parts]
        outs, args = [], []
        for part, keep, pieces, size in zip(plan.parts, keeps, arrived, sizes):
            args += [keep] + pieces
            if level < 2:
                outs += part.shares(keep.shape[0], size)
            else:
                outs.append(shape((1,) + part.packed[1:], i16))
        beside = (step, len(step_args), len(step_outs)) if step else None
        count = [len(pieces) for pieces in arrived]
        made = after(
            functools.partial(combine_kernel, plan, count, sizes, beside, len(order)),
            outs + list(step_outs),
            args + list(step_args),
            order,
            name,
            0.6,
        )
        made, beside = made[: len(outs)], made[len(outs) :]
        if level == 2:
            return made, [], beside
        keeps, arrived = [], []
        for part, size in zip(plan.parts, sizes):
            group, made = made[:size], made[size:]
            keeps.append(group[0])
            arrived.append(exchanged(group[1:], part.masks[level]))
        return keeps, arrived, beside

    keeps, arrived, _ = combine(
        keeps, [[core] for core in cores], 0, "combine_cores", order=[other[1] for other in others]
    )
    far = after(
        functools.partial(target_kernel, plan),
        [shape((width + 16, prows // 2), i16)] * 2,
        labels + [grads[2]],
        [keeps[0]],
        "target",
        1.8,
        16 * grow,
    )
    (source,) = after(
        functools.partial(own_source_kernel, plan),
        [shape((width, prows), F32)],
        labels_of(0) + [grads[0]],
        [far[0]],
        "own_source",
        0.8,
        16 * grow,
    )
    far = [send(value, plan, afar) for value in far]
    def deal_on(pairs, count, bit):
        while count > 2:
            count, bit = count // 2, bit * 2
            made = [
                after(functools.partial(deal_kernel, plan), dealt(count), pair, [], "deal", 0.3)
                for pair in pairs
            ]
            pairs = [[keep, send(value, plan, lambda d, m=bit: d ^ m)] for keep, value in made]
        return pairs, count // 2, bit * 2

    others, count, bit = deal_on(others, plan.rels // 2, 1)
    keeps, arrived, made = combine(
        keeps,
        arrived,
        1,
        "combine_first",
        lambda plan, *refs: share(plan, len(others), *refs),
        [source] + far + sum(others, []),
        dealt(plan.rels // 2) + dealt(count) * len(others),
    )
    mine = [[made[0], send(made[1], plan, lambda d: d ^ 1)]]
    others = [
        [made[at], send(made[at + 1], plan, lambda d: d ^ bit)] for at in range(2, len(made), 2)
    ]
    (mine,), count, bit = deal_on(mine, plan.rels // 2, 1)
    totals, _, made = combine(
        keeps,
        arrived,
        2,
        "combine_last",
        lambda plan, *refs: deal_and_settle(plan, len(others), *refs),
        mine + sum(others, []),
        dealt(count) + [shape((width + 16, lanes), i16)] * len(others),
    )
    mine, came = made[0], send(made[1], plan, lambda d: d ^ bit)
    crossing = exchanged(made[2:], range(0, plan.rels * buckets, plan.rels))
    pieces = [
        [total] + exchanged([total] * (len(part.masks[1]) - 1), part.masks[1])
        for part, total in zip(plan.parts, totals)
    ]
    flat = sum(pieces, [])
    made = after(
        functools.partial(stack_kernel, plan, [len(group) for group in pieces]),
        [
            shape((len(group),) + part.packed[1:], i16)
            for part, group in zip(plan.parts, pieces)
        ]
        + [shape((width + 16, lanes), i16)],
        flat + [mine, came] + crossing,
        [],
        "stack",
        0.5,
    )
    blocks, owners = made[:-1], {0: made[-1]}
    pieces = [
        [block] + exchanged([block] * (len(part.masks[0]) - 1), part.masks[0])
        for part, block in zip(plan.parts, blocks)
    ]
    while bit:
        for mask in sorted(owners):
            owners[mask | bit] = send(owners[mask], plan, lambda d, m=bit: d ^ m)
        bit //= 2
    (grad_partitions,) = after(
        functools.partial(part_out_kernel, plan),
        [shape((width, prows), F32)],
        [owners[mask] for mask in range(plan.rels)],
        [],
        "part_out",
        1.0,
    )
    if lanes % LANES:
        order = jnp.arange(plan.rels) ^ lax.axis_index("rel")
        split_lanes = grad_partitions.reshape(width, plan.rels, lanes)
        grad_partitions = jnp.take(split_lanes, order, axis=1).reshape(width, prows)

    crossed = [[send(piece, plan, lambda d: d ^ 1) for piece in group] for group in pieces]
    side = lax.axis_index("rel") & 1
    outs = [shape((width, plan.nrels), F32), shape((width, plan.rems), F32)]
    spec = lambda lanes: pl.BlockSpec((width, lanes), lambda i, half: (0, half[0]))
    made = []
    for turn, groups in enumerate([pieces, crossed]):
        flat = sum(groups, [])
        made = call(
            functools.partial(spread_kernel, plan, [len(group) for group in groups]),
            outs,
            [(side ^ turn).reshape(1), *flat, *made],
            "spread",
            2.0,
            16,
            grid_spec=pltpu.PrefetchScalarGridSpec(
                num_scalar_prefetch=1,
                grid=(1,),
                in_specs=[pl.BlockSpec(piece.shape, lambda i, half: (0, 0, 0)) for piece in flat]
                + [ANY] * len(made),
                out_specs=[spec(plan.half_rel), spec(plan.half_rem)],
                scratch_shapes=[pltpu.VMEM(part.packed, i16) for part in plan.parts],
            ),
            input_output_aliases={1 + len(flat) + at: at for at in range(len(made))},
        )
    grad_relations, grad_remainder = made
    return grad_partitions.T, grad_remainder.T, grad_relations.T


def solution(mesh):
    edge = P("dom", None, "rel", None)
    in_specs = (P("dom", None), P(), P(), P("dom", None, "rel")) + (edge,) * 7
    out_specs = (P("dom", None), P(), P())
    return jax.shard_map(body, mesh=mesh, in_specs=in_specs, out_specs=out_specs, check_vma=False)
```

```python
import functools

import jax
import jax.numpy as jnp
from jax import lax
from jax.experimental import pallas as pl
from jax.experimental.pallas import tpu as pltpu
from jax.sharding import PartitionSpec as P

F32 = jnp.float32
BF16 = jnp.bfloat16
LANES = 128
REACH = 32766.0
NT = (((1,), (1,)), ((), ()))
NN = (((1,), (0,)), ((), ()))
TN = (((0,), (0,)), ((), ()))


def bits_of(count):
    return count.bit_length() - 1


def reverse_bits(value, count):
    out = 0
    for bit in range(bits_of(count)):
        out = out * 2 + ((value >> bit) & 1)
    return out


def split(value):
    high = value.astype(BF16)
    low = (value - high.astype(F32)).astype(BF16)
    return high, low


def dot(left, right, dims):
    return lax.dot_general(left, right, dims, preferred_element_type=F32)


def dot3(left, right, dims):
    left_high, left_low = split(left)
    right_high, right_low = split(right)
    return (
        dot(left_high, right_high, dims)
        + dot(left_high, right_low, dims)
        + dot(left_low, right_high, dims)
    )


def one_hot(ids, rows, base=0):
    place = lax.broadcasted_iota(jnp.int32, (rows, ids.shape[1]), 0)
    return jnp.where(place == ids - base, 1.0, 0.0).astype(BF16)


def store_split(ref, cols, value):
    high, low = split(value)
    depth = value.shape[0]
    ref[0:depth, cols] = high
    ref[depth : 2 * depth, cols] = low


def folded(value):
    depth = value.shape[0] // 2
    return value[:depth] + value[depth:]


def quantized(value):
    top = jnp.max(jnp.abs(value), axis=0, keepdims=True)
    exponent = jnp.floor(jnp.log2(jnp.maximum(top, 1e-30))) + 1.0
    return jnp.round(value * (REACH * jnp.exp2(-exponent))), exponent


def scale_of(exponent):
    return jnp.exp2(exponent) * (1.0 / REACH)


def to_words(value):
    return value.astype(jnp.int32).astype(jnp.int16)


def from_words(words):
    return words.astype(jnp.int32).astype(F32)


def pack_table(value, rows=None):
    scaled, exponent = quantized(value)
    spare = (rows or value.shape[0] + 16) - value.shape[0]
    tail = jnp.broadcast_to(exponent, (spare, value.shape[1]))
    return to_words(jnp.concatenate([scaled, tail], axis=0))


def unpack_table(words, depth=None):
    depth = depth or words.shape[0] - 16
    value = from_words(words)
    return value[:depth] * scale_of(value[depth : depth + 1])


class Part:
    def __init__(self, plan, units, groups):
        self.units = units
        self.rows = (units + 2) // 2 * 16
        self.masks = [self.group_masks(bits) for bits in groups]
        order = [bit for group in groups for bit in reversed(group)]
        self.place = {bit: len(order) - 1 - at for at, bit in enumerate(order)}
        self.packed = (plan.half_chunks, self.rows, LANES)
        self.bare = (plan.half_chunks, 8 * units, LANES)

    @staticmethod
    def group_masks(bits):
        masks = []
        for index in range(2 ** len(bits)):
            masks.append(sum(((index >> at) & 1) << bit for at, bit in enumerate(bits)))
        return masks

    def position(self, chunk, me):
        relative = chunk ^ (me >> 1)
        out = 0
        for bit, at in self.place.items():
            out = out + (((relative >> (bit - 1)) & 1) << at)
        return out

    def shares(self, count, size):
        count = count // size
        return [shape((count,) + self.bare[1:], F32)] + [
            shape((count,) + self.packed[1:], jnp.int16)
        ] * (size - 1)


class Plan:
    def __init__(self, doms, rels, prows, width, rems, nrels, maxb):
        self.doms, self.rels, self.maxb = doms, rels, maxb
        self.devices = doms * rels
        self.prows, self.width, self.rems, self.nrels = prows, width, rems, nrels
        self.buckets = doms // rels
        self.slots = rels * maxb
        self.bucket_edges = self.slots * LANES
        self.edges = self.buckets * self.bucket_edges
        self.part_lanes = prows // rels
        self.half_rel, self.half_rem = nrels // 2, rems // 2
        self.half_lanes = self.half_rel + self.half_rem
        self.subs = width // 8
        self.units = (self.half_lanes // LANES) * self.subs
        self.half_chunks = self.devices // 2
        self.chunk_units = -(-self.units // self.half_chunks)
        rel_bits = bits_of(rels)
        all_bits = rel_bits + bits_of(doms)
        near = list(range(1, rel_bits + 1))
        far = list(range(rel_bits + 1, all_bits))
        self.parts = [Part(self, self.chunk_units, [near, far])]

    def chunk_blocks(self, chunk, part):
        first = chunk * self.chunk_units + (self.parts[0].units if part else 0)
        blocks = []
        for unit in range(first, first + self.parts[part].units):
            lane, sub = divmod(unit, self.subs)
            blocks.append((lane * LANES, 8 * sub) if unit < self.units else None)
        return blocks

    def row(self, labels, bucket, kinds, first, count):
        rows = []
        for slot in range(first, first + count):
            rows += [labels[bucket][slot, kind : kind + 1, :] for kind in kinds]
        return jnp.concatenate(rows, axis=1) if len(rows) > 1 else rows[0]

    def whole_row(self, labels, kinds):
        rows = [
            self.row(labels, bucket, kinds, 0, self.slots) for bucket in range(self.buckets)
        ]
        return jnp.concatenate(rows, axis=1) if len(rows) > 1 else rows[0]

    def me(self):
        return lax.axis_index("dom") * self.rels + lax.axis_index("rel")

    def target_mask(self, rel):
        return reverse_bits(rel, self.rels) * self.buckets

    def dynamic_mask(self, rel):
        out = 0
        width = bits_of(self.rels)
        for bit in range(width):
            out = out + (((rel >> bit) & 1) << (width - 1 - bit))
        return out * self.buckets


def send(value, plan, target):
    pairs = [(device, target(device)) for device in range(plan.devices)]
    return lax.ppermute(value, ("dom", "rel"), pairs)


def lists_kernel(plan, *refs):
    tables, counts, outs = refs[:7], refs[7], refs[8:]
    source = lax.axis_index("dom")
    rel = lax.axis_index("rel")
    for mask, out in enumerate(outs):
        for bucket in range(plan.buckets):
            target = source ^ bucket ^ plan.dynamic_mask(rel ^ mask)
            stop = lax.rem(source - target + plan.doms, plan.doms)
            for turn in range(plan.maxb):
                at = bucket * plan.maxb + turn
                for kind, table in enumerate(tables):
                    out[at, kind : kind + 1, :] = table[0, stop, turn : turn + 1, :]
                live = jnp.where(turn < counts[stop], 1, 0)
                out[at, 7:8, :] = jnp.full((1, LANES), live, jnp.int32)


def forward_kernel(plan, *refs):
    lists, outs = refs[: plan.rels], refs[plan.rels :]
    for bucket, out in enumerate(outs):
        for mask, ref in enumerate(lists):
            for turn in range(plan.maxb):
                out[mask * plan.maxb + turn] = ref[bucket * plan.maxb + turn]


def split_kernel(relations, out):
    depth = relations.shape[0]
    high, low = split(relations[...])
    out[0:depth, :] = high
    out[depth : 2 * depth, :] = low


def relation_kernel(plan, *refs):
    labels, relations, out = refs[:1], refs[1], refs[-1]
    for pair in range(0, plan.slots, 2):
        count = min(2, plan.slots - pair)
        start = pair * LANES
        ids = plan.row(labels, 0, (2,), pair, count)
        out[:, start : start + count * LANES] = folded(
            dot(relations[...], one_hot(ids, plan.nrels), NN)
        )


def rows_kernel(plan, *refs):
    labels, (own, rem) = refs[:1], refs[1:3]
    lhs_out, rem_out = refs[-2:]
    for pair in range(0, plan.slots, 2):
        count = min(2, plan.slots - pair)
        row = lambda *kinds: plan.row(labels, 0, kinds, pair, count)
        start = pair * LANES
        end = start + count * LANES
        lhs_out[:, start:end] = dot(own[...], one_hot(row(0), plan.prows), NN) + dot(
            rem[...], one_hot(row(1), plan.rems), NN
        )
        rem_out[:, 2 * start : 2 * end] = dot(
            rem[...], one_hot(row(4, 6), plan.rems), NN
        ).astype(BF16)


def conjugate_parts(grad, other):
    half = grad.shape[0] // 2
    grad_re, grad_im = grad[:half], grad[half:]
    other_re, other_im = other[:half], other[half:]
    return jnp.concatenate(
        [grad_re * other_re + grad_im * other_im, grad_im * other_re - grad_re * other_im], 0
    )


def complex_product(left, right):
    half = left.shape[0] // 2
    left_re, left_im = left[:half], left[half:]
    right_re, right_im = right[:half], right[half:]
    return jnp.concatenate(
        [left_re * right_re - left_im * right_im, left_re * right_im + left_im * right_re], 0
    )


def bucket_grads(plan, labels, target, lhs_in, rel_in, rem_in, lhs_out, rel_out, cand_out, base):
    total = 2 * LANES
    edge = lax.broadcasted_iota(jnp.int32, (LANES, total), 0)
    column = lax.broadcasted_iota(jnp.int32, (LANES, total), 1)
    keep = jnp.where(edge == column, 0.0, 1.0 / total)
    for slot in range(plan.slots):
        cols = slice(slot * LANES, (slot + 1) * LANES)
        wide = slice(slot * total, (slot + 1) * total)
        ids = plan.row(labels, 0, (3, 5), slot, 1)
        cand = dot(target[...], one_hot(ids, plan.prows), NN) + rem_in[:, wide].astype(F32)
        rhs = cand[:, :LANES]
        lhs, vec = lhs_in[:, cols], rel_in[:, cols]
        u_vec = complex_product(lhs, vec)
        live = plan.row(labels, 0, (7,), slot, 1).astype(F32)
        positive = jnp.sum(u_vec * rhs, axis=0, keepdims=True)
        negative = dot3(u_vec, cand, TN)
        grad_pos = -jax.nn.sigmoid(-positive) * live
        grad_neg = jax.nn.sigmoid(negative) * keep * live[0:1, 0:1]
        grad_u = grad_pos * rhs + dot3(cand, grad_neg, NT)
        from_neg = dot3(u_vec, grad_neg, NN)
        grad_cand = jnp.concatenate(
            [from_neg[:, :LANES] + grad_pos * u_vec, from_neg[:, LANES:]], axis=1
        )
        at = base + slot
        cols = slice(at * LANES, (at + 1) * LANES)
        wide = slice(at * total, (at + 1) * total)
        store_split(lhs_out, cols, conjugate_parts(grad_u, vec))
        store_split(rel_out, cols, conjugate_parts(grad_u, lhs))
        store_split(cand_out, wide, grad_cand)


def bucket_kernel(plan, *refs):
    bucket_grads(plan, refs[:1], *refs[1:], 0)


def last_kernel(plan, *refs):
    labels, refs = refs[: plan.buckets], refs[plan.buckets :]
    before, refs = refs[: 3 * (plan.buckets - 1)], refs[3 * (plan.buckets - 1) :]
    inputs, refs = refs[:4], refs[4:]
    away, rem_part, outs, table = refs[: len(plan.parts)], refs[-5], refs[-4:-1], refs[-1]
    base = (plan.buckets - 1) * plan.slots
    bucket_grads(plan, labels[-1:], *inputs, *outs, base)
    for at, ref in enumerate(before):
        wide = ref.shape[1]
        start = at // 3 * wide
        outs[at % 3][:, start : start + wide] = ref[...]
    lhs_grads, rel_grads, cand_grads = outs
    first = one_hot(plan.whole_row(labels, (1,)), plan.rems)
    second = one_hot(plan.whole_row(labels, (4, 6)), plan.rems)
    rem = folded(dot(lhs_grads[...], first, NT) + dot(cand_grads[...], second, NT))
    low, high = rem[:, : plan.half_rem], rem[:, plan.half_rem :]
    core = lax.axis_index("rel") & 1
    rem_part[...] = jnp.where(core == 0, low, high)
    table[:, plan.half_rel :] = jnp.where(core == 0, high, low)
    reduce_half(plan, True, labels, rel_grads, table, away)


def home_kernel(plan, *refs):
    count = plan.buckets
    outs, table = refs[-1 - len(plan.parts) : -1], refs[-1]
    table[:, plan.half_rel :] = refs[count + 1][...]
    reduce_half(plan, False, refs[:count], refs[count], table, outs)


def reduce_half(plan, away, labels, rel_grads, table, outs):
    me = plan.me()
    half = (me & 1) ^ (1 if away else 0)
    step = 2 * LANES if plan.half_rel % (2 * LANES) == 0 else LANES
    ids = plan.whole_row(labels, (2,)) - half * plan.half_rel
    for start in range(0, plan.half_rel, step):
        hot = one_hot(ids, step, start)
        table[:, start : start + step] = folded(dot(rel_grads[...], hot, NT))
    for chunk in range(plan.half_chunks):
        for which, (part, out) in enumerate(zip(plan.parts, outs)):
            value = jnp.concatenate(
                [
                    table[block[1] : block[1] + 8, block[0] : block[0] + LANES]
                    if block
                    else jnp.zeros((8, LANES), F32)
                    for block in plan.chunk_blocks(chunk, which)
                ],
                axis=0,
            )
            out[part.position(chunk, me)] = pack_table(value, part.rows) if away else value


def rows_sum(plan, ids, grads):
    shift = lax.axis_index("rel") * plan.part_lanes
    return folded(dot(grads, one_hot(ids ^ shift, plan.prows), NT))


def target_kernel(plan, *refs):
    count = plan.buckets
    ids = plan.whole_row(refs[:count], (3, 5))
    value = pack_table(rows_sum(plan, ids, refs[count][...]))
    for at, out in enumerate(refs[-2:]):
        lanes = out.shape[1]
        out[...] = value[:, at * lanes : (at + 1) * lanes]


def source_sum(plan, labels, grads):
    return rows_sum(plan, plan.row([labels], 0, (0,), 0, plan.slots), grads)


def deal(plan, value, keep, away):
    lanes = plan.part_lanes
    for at in range(value.shape[1] // lanes):
        share = value[:, at * lanes : (at + 1) * lanes]
        to = slice(at // 2 * lanes, (at // 2 + 1) * lanes)
        if at % 2:
            away[:, to] = pack_table(share)
        else:
            keep[:, to] = share


def source_kernel(plan, bucket, *refs):
    start = bucket * plan.bucket_edges
    grads = refs[1][:, start : start + plan.bucket_edges]
    deal(plan, source_sum(plan, refs[0], grads), *refs[-2:])


def own_source_kernel(plan, *refs):
    refs[-1][...] = source_sum(plan, refs[0], refs[1][:, : plan.bucket_edges])


def share(plan, count, *refs):
    source, fars, others = refs[0], refs[1:3], refs[3 : 3 + 2 * count]
    outs = refs[3 + 2 * count :]
    far = jnp.concatenate([unpack_table(ref[...]) for ref in fars], axis=1)
    deal(plan, source[...] + far, *outs[:2])
    for at in range(0, 2 * count, 2):
        deal_again(plan, *others[at : at + 2], *outs[at + 2 : at + 4])


def deal_again(plan, keep, came, *outs):
    deal(plan, keep[...] + unpack_table(came[...]), *outs)


def deal_and_settle(plan, count, *refs):
    ins, outs = refs[: 2 + 2 * count], refs[2 + 2 * count :]
    deal_again(plan, *ins[:2], *outs[:2])
    for at in range(count):
        add_kernel(2, *ins[2 + 2 * at : 4 + 2 * at], outs[2 + at])


def deal_kernel(plan, *refs):
    deal_again(plan, *refs)


def add_kernel(count, *refs):
    value = refs[0][...]
    for ref in refs[1:count]:
        value = value + unpack_table(ref[...])
    refs[-1][...] = pack_table(value)


def combine_kernel(plan, arrivals, sizes, beside, after, *refs):
    at, out_at = 0, sum(arrivals) + len(arrivals) + after
    if beside:
        step, ins, outs = beside
        step(plan, *refs[out_at : out_at + ins], *refs[len(refs) - outs :])
        out_at += ins
    for part, count, size in zip(plan.parts, arrivals, sizes):
        keep, arrived = refs[at], refs[at + 1 : at + 1 + count]
        outs = refs[out_at : out_at + size]
        at, out_at = at + 1 + count, out_at + size
        share = keep.shape[0] // size
        for place in range(keep.shape[0]):
            value = keep[place]
            for ref in arrived:
                value = value + unpack_table(ref[place], 8 * part.units)
            which, inner = divmod(place, share)
            packed = which or size == 1
            outs[which][inner] = pack_table(value, part.rows) if packed else value


def stack_kernel(plan, counts, *refs):
    outs = refs[-1 - len(counts) : -1]
    add = refs[sum(counts) : -1 - len(counts)]
    add_kernel(len(add), *add, refs[-1])
    first = 0
    for count, out in zip(counts, outs):
        for at in range(count):
            out[at] = refs[first + at][0]
        first += count


def spread_kernel(plan, counts, side, *refs):
    helds = refs[len(refs) - len(counts) :]
    rel_out, rem_out = refs[-2 - len(counts) : len(refs) - len(counts)]
    me = plan.me()
    first = 0
    for count, held in zip(counts, helds):
        at = 0
        for piece in refs[first : first + count]:
            held[at : at + piece.shape[0]] = piece[...]
            at += piece.shape[0]
        first += count
    for chunk in range(plan.half_chunks):
        for which, (part, held) in enumerate(zip(plan.parts, helds)):
            value = unpack_table(held[part.position(chunk, me)], 8 * part.units)
            for index, block in enumerate(plan.chunk_blocks(chunk, which)):
                if block is None:
                    break
                lane, sub = block
                rows = slice(sub, sub + 8)
                piece = value[8 * index : 8 * index + 8]
                if lane < plan.half_rel:
                    rel_out[rows, lane : lane + LANES] = piece
                else:
                    lane -= plan.half_rel
                    rem_out[rows, lane : lane + LANES] = piece


def part_out_kernel(plan, *refs):
    out = refs[-1]
    rel = lax.axis_index("rel")
    lanes = plan.part_lanes
    for mask, ref in enumerate(refs[: plan.rels]):
        if lanes % LANES:
            out[:, mask * lanes : (mask + 1) * lanes] = unpack_table(ref[...])
        else:
            start = pl.multiple_of((rel ^ mask) * lanes, lanes)
            out[:, pl.ds(start, lanes)] = unpack_table(ref[...])


def shape(extent, kind):
    return jax.ShapeDtypeStruct(extent, kind)


VMEM = pl.BlockSpec(memory_space=pltpu.VMEM)
ANY = pl.BlockSpec(memory_space=pl.ANY)


def call(kernel, outs, args, name, cost, limit, scratch=(), in_specs=None, out_specs=None, **more):
    work = pl.CostEstimate(flops=int(cost * 1e9), bytes_accessed=int(cost * 3e6), transcendentals=0)
    if "grid_spec" not in more:
        more["in_specs"] = in_specs or [VMEM] * len(args)
        more["out_specs"] = out_specs or [VMEM] * len(outs)
        more["scratch_shapes"] = list(scratch)
    return pl.pallas_call(
        kernel,
        out_shape=outs,
        compiler_params=pltpu.CompilerParams(vmem_limit_bytes=int(limit * 2**20)),
        cost_estimate=work,
        name=name,
        **more,
    )(*args)


def body(
    partitions,
    remainder,
    relations,
    counts,
    lhs_rows,
    lhs_rems,
    rel_ids,
    rhs_rows,
    rhs_rems,
    neg_rows,
    neg_rems,
):
    prows, width = partitions.shape
    plan = Plan(
        lax.axis_size("dom"),
        lax.axis_size("rel"),
        prows,
        width,
        remainder.shape[0],
        relations.shape[0],
        lhs_rows.shape[2],
    )
    smem = pl.BlockSpec(memory_space=pltpu.SMEM)
    own, rem, rels = partitions.T, remainder.T, relations.T
    edges, wide = plan.edges, plan.bucket_edges
    grow = max(1, edges // 1024)
    buckets = plan.buckets
    afar = lambda d: d ^ (plan.target_mask(d % plan.rels) * plan.rels)
    i16 = jnp.int16

    def exchanged(values, masks):
        return [
            send(value, plan, lambda d, m=mask: d ^ m) for value, mask in zip(values, masks[1:])
        ]

    def after(kernel, outs, args, others, name, cost, limit=12, **more):
        return call(
            kernel,
            outs,
            list(args) + list(others),
            name,
            cost,
            limit,
            in_specs=[VMEM] * len(args) + [ANY] * len(others),
            **more,
        )

    tables = [lhs_rows, lhs_rems, rel_ids, rhs_rows, rhs_rems, neg_rows, neg_rems]
    target = send(own, plan, afar)
    sources = [own] + [
        send(own, plan, lambda d, b=bucket: d ^ (b * plan.rels)) for bucket in range(1, buckets)
    ]
    lists = call(
        functools.partial(lists_kernel, plan),
        [shape((buckets * plan.maxb, 8, LANES), jnp.int32)] * plan.rels,
        tables + [counts.reshape(-1)],
        "lists",
        0.5,
        60,
        in_specs=[VMEM] * 7 + [smem],
    )
    lists = [lists[0]] + exchanged(lists[1:], range(plan.rels))
    (rel_split,) = call(
        split_kernel,
        [shape((2 * width, plan.nrels), BF16)],
        [rels],
        "rel_split",
        2.0,
        50,
    )
    labels = call(
        functools.partial(forward_kernel, plan),
        [shape((plan.slots, 8, LANES), jnp.int32)] * buckets,
        lists,
        "forward",
        0.2,
        8,
    )
    labels = [labels[0]] + [
        send(labels[bucket], plan, lambda d, b=bucket: d ^ (b * plan.rels))
        for bucket in range(1, buckets)
    ]
    labels_of = lambda bucket: [labels[bucket]]
    grad_shapes = lambda count: [
        shape((2 * width, count), BF16),
        shape((2 * width, count), BF16),
        shape((2 * width, 2 * count), BF16),
    ]
    inputs = []
    for bucket in range(buckets):
        (vec,) = call(
            functools.partial(relation_kernel, plan),
            [shape((width, wide), F32)],
            labels_of(bucket) + [rel_split],
            "relation",
            2.0,
            16 * grow,
        )
        lhs, cand_rem = call(
            functools.partial(rows_kernel, plan),
            [shape((width, wide), F32), shape((width, 2 * wide), BF16)],
            labels_of(bucket) + [sources[bucket], rem],
            "rows",
            0.7,
            12 * grow,
        )
        inputs.append([lhs, vec, cand_rem])
    lanes = plan.part_lanes
    dealt = lambda count: [
        shape((width, count * lanes), F32),
        shape((width + 16, count * lanes), i16),
    ]
    grads = []
    for bucket in range(buckets - 1):
        grads += call(
            functools.partial(bucket_kernel, plan),
            grad_shapes(wide),
            labels_of(bucket) + [target] + inputs[bucket],
            "bucket",
            4.0,
            16 * grow,
        )
    table = [pltpu.VMEM((width, plan.half_lanes), F32)]
    made = call(
        functools.partial(last_kernel, plan),
        [shape(part.packed, i16) for part in plan.parts]
        + [shape((width, plan.half_rem), F32)]
        + grad_shapes(edges),
        labels + grads + [target] + inputs[-1],
        "last",
        9.0,
        20 * grow,
        scratch=table,
    )
    made, grads = list(made[:-3]), list(made[-3:])
    away, rem_part = made[:-1], made[-1]
    cores = [send(value, plan, lambda d: d ^ 1) for value in away]

    others, order = [], list(away)
    for bucket in range(1, buckets):
        keep, value = after(
            functools.partial(source_kernel, plan, bucket),
            dealt(plan.rels // 2),
            labels_of(bucket) + [grads[0]],
            order,
            "source",
            0.8,
            12 * grow,
        )
        others.append([keep, send(value, plan, lambda d: d ^ 1)])
        order = [keep]
    keeps = after(
        functools.partial(home_kernel, plan),
        [shape(part.bare, F32) for part in plan.parts],
        labels + [grads[1], rem_part],
        order,
        "home",
        3.0,
        16 * grow,
        scratch=table,
    )

    def combine(keeps, arrived, level, name, step=None, step_args=(), step_outs=(), order=()):
        sizes = [len(part.masks[level]) if level < 2 else 1 for part in plan.parts]
        outs, args = [], []
        for part, keep, pieces, size in zip(plan.parts, keeps, arrived, sizes):
            args += [keep] + pieces
            if level < 2:
                outs += part.shares(keep.shape[0], size)
            else:
                outs.append(shape((1,) + part.packed[1:], i16))
        beside = (step, len(step_args), len(step_outs)) if step else None
        count = [len(pieces) for pieces in arrived]
        made = after(
            functools.partial(combine_kernel, plan, count, sizes, beside, len(order)),
            outs + list(step_outs),
            args + list(step_args),
            order,
            name,
            0.6,
        )
        made, beside = made[: len(outs)], made[len(outs) :]
        if level == 2:
            return made, [], beside
        keeps, arrived = [], []
        for part, size in zip(plan.parts, sizes):
            group, made = made[:size], made[size:]
            keeps.append(group[0])
            arrived.append(exchanged(group[1:], part.masks[level]))
        return keeps, arrived, beside

    keeps, arrived, _ = combine(
        keeps, [[core] for core in cores], 0, "combine_cores", order=[other[1] for other in others]
    )
    far = after(
        functools.partial(target_kernel, plan),
        [shape((width + 16, prows // 2), i16)] * 2,
        labels + [grads[2]],
        [keeps[0]],
        "target",
        1.8,
        16 * grow,
    )
    (source,) = after(
        functools.partial(own_source_kernel, plan),
        [shape((width, prows), F32)],
        labels_of(0) + [grads[0]],
        [far[0]],
        "own_source",
        0.8,
        16 * grow,
    )
    far = [send(value, plan, afar) for value in far]
    def deal_on(pairs, count, bit):
        while count > 2:
            count, bit = count // 2, bit * 2
            made = [
                after(functools.partial(deal_kernel, plan), dealt(count), pair, [], "deal", 0.3)
                for pair in pairs
            ]
            pairs = [[keep, send(value, plan, lambda d, m=bit: d ^ m)] for keep, value in made]
        return pairs, count // 2, bit * 2

    others, count, bit = deal_on(others, plan.rels // 2, 1)
    keeps, arrived, made = combine(
        keeps,
        arrived,
        1,
        "combine_first",
        lambda plan, *refs: share(plan, len(others), *refs),
        [source] + far + sum(others, []),
        dealt(plan.rels // 2) + dealt(count) * len(others),
    )
    mine = [[made[0], send(made[1], plan, lambda d: d ^ 1)]]
    others = [
        [made[at], send(made[at + 1], plan, lambda d: d ^ bit)] for at in range(2, len(made), 2)
    ]
    (mine,), count, bit = deal_on(mine, plan.rels // 2, 1)
    totals, _, made = combine(
        keeps,
        arrived,
        2,
        "combine_last",
        lambda plan, *refs: deal_and_settle(plan, len(others), *refs),
        mine + sum(others, []),
        dealt(count) + [shape((width + 16, lanes), i16)] * len(others),
    )
    mine, came = made[0], send(made[1], plan, lambda d: d ^ bit)
    crossing = exchanged(made[2:], range(0, plan.rels * buckets, plan.rels))
    pieces = [
        [total] + exchanged([total] * (len(part.masks[1]) - 1), part.masks[1])
        for part, total in zip(plan.parts, totals)
    ]
    flat = sum(pieces, [])
    made = after(
        functools.partial(stack_kernel, plan, [len(group) for group in pieces]),
        [
            shape((len(group),) + part.packed[1:], i16)
            for part, group in zip(plan.parts, pieces)
        ]
        + [shape((width + 16, lanes), i16)],
        flat + [mine, came] + crossing,
        [],
        "stack",
        0.5,
    )
    blocks, owners = made[:-1], {0: made[-1]}
    pieces = [
        [block] + exchanged([block] * (len(part.masks[0]) - 1), part.masks[0])
        for part, block in zip(plan.parts, blocks)
    ]
    while bit:
        for mask in sorted(owners):
            owners[mask | bit] = send(owners[mask], plan, lambda d, m=bit: d ^ m)
        bit //= 2
    (grad_partitions,) = after(
        functools.partial(part_out_kernel, plan),
        [shape((width, prows), F32)],
        [owners[mask] for mask in range(plan.rels)],
        [],
        "part_out",
        1.0,
    )
    if lanes % LANES:
        order = jnp.arange(plan.rels) ^ lax.axis_index("rel")
        split_lanes = grad_partitions.reshape(width, plan.rels, lanes)
        grad_partitions = jnp.take(split_lanes, order, axis=1).reshape(width, prows)

    crossed = [[send(piece, plan, lambda d: d ^ 1) for piece in group] for group in pieces]
    side = lax.axis_index("rel") & 1
    outs = [shape((width, plan.nrels), F32), shape((width, plan.rems), F32)]
    spec = lambda lanes: pl.BlockSpec((width, lanes), lambda i, half: (0, half[0]))
    made = []
    for turn, groups in enumerate([pieces, crossed]):
        flat = sum(groups, [])
        made = call(
            functools.partial(spread_kernel, plan, [len(group) for group in groups]),
            outs,
            [(side ^ turn).reshape(1), *flat, *made],
            "spread",
            2.0,
            16,
            grid_spec=pltpu.PrefetchScalarGridSpec(
                num_scalar_prefetch=1,
                grid=(1,),
                in_specs=[pl.BlockSpec(piece.shape, lambda i, half: (0, 0, 0)) for piece in flat]
                + [ANY] * len(made),
                out_specs=[spec(plan.half_rel), spec(plan.half_rem)],
                scratch_shapes=[pltpu.VMEM(part.packed, i16) for part in plan.parts],
            ),
            input_output_aliases={1 + len(flat) + at: at for at in range(len(made))},
        )
    grad_relations, grad_remainder = made
    return grad_partitions.T, grad_remainder.T, grad_relations.T


def solution(mesh):
    edge = P("dom", None, "rel", None)
    in_specs = (P("dom", None), P(), P(), P("dom", None, "rel")) + (edge,) * 7
    out_specs = (P("dom", None), P(), P())
    return jax.shard_map(body, mesh=mesh, in_specs=in_specs, out_specs=out_specs, check_vma=False)
```

```python
import functools

import jax
import jax.numpy as jnp
from jax import lax
from jax.experimental import pallas as pl
from jax.experimental.pallas import tpu as pltpu
from jax.sharding import PartitionSpec as P

F32 = jnp.float32
BF16 = jnp.bfloat16
LANES = 128
REACH = 32766.0
NT = (((1,), (1,)), ((), ()))
NN = (((1,), (0,)), ((), ()))
TN = (((0,), (0,)), ((), ()))


def bits_of(count):
    return count.bit_length() - 1


def reverse_bits(value, count):
    out = 0
    for bit in range(bits_of(count)):
        out = out * 2 + ((value >> bit) & 1)
    return out


def split(value):
    high = value.astype(BF16)
    low = (value - high.astype(F32)).astype(BF16)
    return high, low


def dot(left, right, dims):
    return lax.dot_general(left, right, dims, preferred_element_type=F32)


def dot3(left, right, dims):
    left_high, left_low = split(left)
    right_high, right_low = split(right)
    return (
        dot(left_high, right_high, dims)
        + dot(left_high, right_low, dims)
        + dot(left_low, right_high, dims)
    )


def one_hot(ids, rows, base=0):
    place = lax.broadcasted_iota(jnp.int32, (rows, ids.shape[1]), 0)
    return jnp.where(place == ids - base, 1.0, 0.0).astype(BF16)


def store_split(ref, cols, value):
    high, low = split(value)
    depth = value.shape[0]
    ref[0:depth, cols] = high
    ref[depth : 2 * depth, cols] = low


def folded(value):
    depth = value.shape[0] // 2
    return value[:depth] + value[depth:]


def quantized(value):
    top = jnp.max(jnp.abs(value), axis=0, keepdims=True)
    exponent = jnp.floor(jnp.log2(jnp.maximum(top, 1e-30))) + 1.0
    return jnp.round(value * (REACH * jnp.exp2(-exponent))), exponent


def scale_of(exponent):
    return jnp.exp2(exponent) * (1.0 / REACH)


def to_words(value):
    return value.astype(jnp.int32).astype(jnp.int16)


def from_words(words):
    return words.astype(jnp.int32).astype(F32)


def pack_table(value, rows=None):
    scaled, exponent = quantized(value)
    spare = (rows or value.shape[0] + 16) - value.shape[0]
    tail = jnp.broadcast_to(exponent, (spare, value.shape[1]))
    return to_words(jnp.concatenate([scaled, tail], axis=0))


def unpack_table(words, depth=None):
    depth = depth or words.shape[0] - 16
    value = from_words(words)
    return value[:depth] * scale_of(value[depth : depth + 1])


class Part:
    def __init__(self, plan, units, groups):
        self.units = units
        self.rows = (units + 2) // 2 * 16
        self.masks = [self.group_masks(bits) for bits in groups]
        order = [bit for group in groups for bit in reversed(group)]
        self.place = {bit: len(order) - 1 - at for at, bit in enumerate(order)}
        self.packed = (plan.half_chunks, self.rows, LANES)
        self.bare = (plan.half_chunks, 8 * units, LANES)

    @staticmethod
    def group_masks(bits):
        masks = []
        for index in range(2 ** len(bits)):
            masks.append(sum(((index >> at) & 1) << bit for at, bit in enumerate(bits)))
        return masks

    def position(self, chunk, me):
        relative = chunk ^ (me >> 1)
        out = 0
        for bit, at in self.place.items():
            out = out + (((relative >> (bit - 1)) & 1) << at)
        return out

    def shares(self, count, size):
        count = count // size
        return [shape((count,) + self.bare[1:], F32)] + [
            shape((count,) + self.packed[1:], jnp.int16)
        ] * (size - 1)


class Plan:
    def __init__(self, doms, rels, prows, width, rems, nrels, maxb):
        self.doms, self.rels, self.maxb = doms, rels, maxb
        self.devices = doms * rels
        self.prows, self.width, self.rems, self.nrels = prows, width, rems, nrels
        self.buckets = doms // rels
        self.slots = rels * maxb
        self.bucket_edges = self.slots * LANES
        self.edges = self.buckets * self.bucket_edges
        self.part_lanes = prows // rels
        self.half_rel, self.half_rem = nrels // 2, rems // 2
        self.half_lanes = self.half_rel + self.half_rem
        self.subs = width // 8
        self.units = (self.half_lanes // LANES) * self.subs
        self.half_chunks = self.devices // 2
        self.chunk_units = -(-self.units // self.half_chunks)
        rel_bits = bits_of(rels)
        all_bits = rel_bits + bits_of(doms)
        near = list(range(1, rel_bits + 1))
        far = list(range(rel_bits + 1, all_bits))
        self.parts = [Part(self, self.chunk_units, [near, far])]

    def chunk_blocks(self, chunk, part):
        first = chunk * self.chunk_units + (self.parts[0].units if part else 0)
        blocks = []
        for unit in range(first, first + self.parts[part].units):
            lane, sub = divmod(unit, self.subs)
            blocks.append((lane * LANES, 8 * sub) if unit < self.units else None)
        return blocks

    def row(self, labels, bucket, kinds, first, count):
        rows = []
        for slot in range(first, first + count):
            rows += [labels[bucket][slot, kind : kind + 1, :] for kind in kinds]
        return jnp.concatenate(rows, axis=1) if len(rows) > 1 else rows[0]

    def whole_row(self, labels, kinds):
        rows = [
            self.row(labels, bucket, kinds, 0, self.slots) for bucket in range(self.buckets)
        ]
        return jnp.concatenate(rows, axis=1) if len(rows) > 1 else rows[0]

    def me(self):
        return lax.axis_index("dom") * self.rels + lax.axis_index("rel")

    def target_mask(self, rel):
        return reverse_bits(rel, self.rels) * self.buckets

    def dynamic_mask(self, rel):
        out = 0
        width = bits_of(self.rels)
        for bit in range(width):
            out = out + (((rel >> bit) & 1) << (width - 1 - bit))
        return out * self.buckets


def send(value, plan, target):
    pairs = [(device, target(device)) for device in range(plan.devices)]
    return lax.ppermute(value, ("dom", "rel"), pairs)


def lists_kernel(plan, *refs):
    tables, counts, outs = refs[:7], refs[7], refs[8:]
    source = lax.axis_index("dom")
    rel = lax.axis_index("rel")
    for mask, out in enumerate(outs):
        for bucket in range(plan.buckets):
            target = source ^ bucket ^ plan.dynamic_mask(rel ^ mask)
            stop = lax.rem(source - target + plan.doms, plan.doms)
            for turn in range(plan.maxb):
                at = bucket * plan.maxb + turn
                for kind, table in enumerate(tables):
                    out[at, kind : kind + 1, :] = table[0, stop, turn : turn + 1, :]
                live = jnp.where(turn < counts[stop], 1, 0)
                out[at, 7:8, :] = jnp.full((1, LANES), live, jnp.int32)


def forward_kernel(plan, *refs):
    lists, outs = refs[: plan.rels], refs[plan.rels :]
    for bucket, out in enumerate(outs):
        for mask, ref in enumerate(lists):
            for turn in range(plan.maxb):
                out[mask * plan.maxb + turn] = ref[bucket * plan.maxb + turn]


def split_kernel(relations, out):
    depth = relations.shape[0]
    high, low = split(relations[...])
    out[0:depth, :] = high
    out[depth : 2 * depth, :] = low


def relation_kernel(plan, *refs):
    labels, relations, out = refs[:1], refs[1], refs[-1]
    for pair in range(0, plan.slots, 2):
        count = min(2, plan.slots - pair)
        start = pair * LANES
        ids = plan.row(labels, 0, (2,), pair, count)
        out[:, start : start + count * LANES] = folded(
            dot(relations[...], one_hot(ids, plan.nrels), NN)
        )


def rows_kernel(plan, *refs):
    labels, (own, rem) = refs[:1], refs[1:3]
    lhs_out, rem_out = refs[-2:]
    for pair in range(0, plan.slots, 2):
        count = min(2, plan.slots - pair)
        row = lambda *kinds: plan.row(labels, 0, kinds, pair, count)
        start = pair * LANES
        end = start + count * LANES
        lhs_out[:, start:end] = dot(own[...], one_hot(row(0), plan.prows), NN) + dot(
            rem[...], one_hot(row(1), plan.rems), NN
        )
        rem_out[:, 2 * start : 2 * end] = dot(
            rem[...], one_hot(row(4, 6), plan.rems), NN
        ).astype(BF16)


def conjugate_parts(grad, other):
    half = grad.shape[0] // 2
    grad_re, grad_im = grad[:half], grad[half:]
    other_re, other_im = other[:half], other[half:]
    return jnp.concatenate(
        [grad_re * other_re + grad_im * other_im, grad_im * other_re - grad_re * other_im], 0
    )


def complex_product(left, right):
    half = left.shape[0] // 2
    left_re, left_im = left[:half], left[half:]
    right_re, right_im = right[:half], right[half:]
    return jnp.concatenate(
        [left_re * right_re - left_im * right_im, left_re * right_im + left_im * right_re], 0
    )


def bucket_grads(plan, labels, target, lhs_in, rel_in, rem_in, lhs_out, rel_out, cand_out, base):
    total = 2 * LANES
    edge = lax.broadcasted_iota(jnp.int32, (LANES, total), 0)
    column = lax.broadcasted_iota(jnp.int32, (LANES, total), 1)
    keep = jnp.where(edge == column, 0.0, 1.0 / total)
    for slot in range(plan.slots):
        cols = slice(slot * LANES, (slot + 1) * LANES)
        wide = slice(slot * total, (slot + 1) * total)
        ids = plan.row(labels, 0, (3, 5), slot, 1)
        cand = dot(target[...], one_hot(ids, plan.prows), NN) + rem_in[:, wide].astype(F32)
        rhs = cand[:, :LANES]
        lhs, vec = lhs_in[:, cols], rel_in[:, cols]
        u_vec = complex_product(lhs, vec)
        live = plan.row(labels, 0, (7,), slot, 1).astype(F32)
        positive = jnp.sum(u_vec * rhs, axis=0, keepdims=True)
        negative = dot3(u_vec, cand, TN)
        grad_pos = -jax.nn.sigmoid(-positive) * live
        grad_neg = jax.nn.sigmoid(negative) * keep * live[0:1, 0:1]
        grad_u = grad_pos * rhs + dot3(cand, grad_neg, NT)
        from_neg = dot3(u_vec, grad_neg, NN)
        grad_cand = jnp.concatenate(
            [from_neg[:, :LANES] + grad_pos * u_vec, from_neg[:, LANES:]], axis=1
        )
        at = base + slot
        cols = slice(at * LANES, (at + 1) * LANES)
        wide = slice(at * total, (at + 1) * total)
        store_split(lhs_out, cols, conjugate_parts(grad_u, vec))
        store_split(rel_out, cols, conjugate_parts(grad_u, lhs))
        store_split(cand_out, wide, grad_cand)


def bucket_kernel(plan, *refs):
    bucket_grads(plan, refs[:1], *refs[1:], 0)


def last_kernel(plan, *refs):
    labels, refs = refs[: plan.buckets], refs[plan.buckets :]
    before, refs = refs[: 3 * (plan.buckets - 1)], refs[3 * (plan.buckets - 1) :]
    inputs, refs = refs[:4], refs[4:]
    away, rem_part, outs, table = refs[: len(plan.parts)], refs[-5], refs[-4:-1], refs[-1]
    base = (plan.buckets - 1) * plan.slots
    bucket_grads(plan, labels[-1:], *inputs, *outs, base)
    for at, ref in enumerate(before):
        wide = ref.shape[1]
        start = at // 3 * wide
        outs[at % 3][:, start : start + wide] = ref[...]
    lhs_grads, rel_grads, cand_grads = outs
    first = one_hot(plan.whole_row(labels, (1,)), plan.rems)
    second = one_hot(plan.whole_row(labels, (4, 6)), plan.rems)
    rem = folded(dot(lhs_grads[...], first, NT) + dot(cand_grads[...], second, NT))
    low, high = rem[:, : plan.half_rem], rem[:, plan.half_rem :]
    core = lax.axis_index("rel") & 1
    rem_part[...] = jnp.where(core == 0, low, high)
    table[:, plan.half_rel :] = jnp.where(core == 0, high, low)
    reduce_half(plan, True, labels, rel_grads, table, away)


def home_kernel(plan, *refs):
    count = plan.buckets
    outs, table = refs[-1 - len(plan.parts) : -1], refs[-1]
    table[:, plan.half_rel :] = refs[count + 1][...]
    reduce_half(plan, False, refs[:count], refs[count], table, outs)


def reduce_half(plan, away, labels, rel_grads, table, outs):
    me = plan.me()
    half = (me & 1) ^ (1 if away else 0)
    step = 2 * LANES if plan.half_rel % (2 * LANES) == 0 else LANES
    ids = plan.whole_row(labels, (2,)) - half * plan.half_rel
    for start in range(0, plan.half_rel, step):
        hot = one_hot(ids, step, start)
        table[:, start : start + step] = folded(dot(rel_grads[...], hot, NT))
    for chunk in range(plan.half_chunks):
        for which, (part, out) in enumerate(zip(plan.parts, outs)):
            value = jnp.concatenate(
                [
                    table[block[1] : block[1] + 8, block[0] : block[0] + LANES]
                    if block
                    else jnp.zeros((8, LANES), F32)
                    for block in plan.chunk_blocks(chunk, which)
                ],
                axis=0,
            )
            out[part.position(chunk, me)] = pack_table(value, part.rows) if away else value


def rows_sum(plan, ids, grads):
    shift = lax.axis_index("rel") * plan.part_lanes
    return folded(dot(grads, one_hot(ids ^ shift, plan.prows), NT))


def target_kernel(plan, *refs):
    count = plan.buckets
    ids = plan.whole_row(refs[:count], (3, 5))
    refs[-1][...] = pack_table(rows_sum(plan, ids, refs[count][...]))


def source_sum(plan, labels, grads):
    return rows_sum(plan, plan.row([labels], 0, (0,), 0, plan.slots), grads)


def deal(plan, value, keep, away):
    lanes = plan.part_lanes
    for at in range(value.shape[1] // lanes):
        share = value[:, at * lanes : (at + 1) * lanes]
        to = slice(at // 2 * lanes, (at // 2 + 1) * lanes)
        if at % 2:
            away[:, to] = pack_table(share)
        else:
            keep[:, to] = share


def source_kernel(plan, bucket, *refs):
    start = bucket * plan.bucket_edges
    grads = refs[1][:, start : start + plan.bucket_edges]
    deal(plan, source_sum(plan, refs[0], grads), *refs[-2:])


def own_source_kernel(plan, *refs):
    refs[-1][...] = source_sum(plan, refs[0], refs[1][:, : plan.bucket_edges])


def share(plan, count, *refs):
    source, far, others = refs[0], refs[1], refs[2 : 2 + 2 * count]
    outs = refs[2 + 2 * count :]
    deal(plan, source[...] + unpack_table(far[...]), *outs[:2])
    for at in range(0, 2 * count, 2):
        deal_again(plan, *others[at : at + 2], *outs[at + 2 : at + 4])


def deal_again(plan, keep, came, *outs):
    deal(plan, keep[...] + unpack_table(came[...]), *outs)


def deal_and_settle(plan, count, *refs):
    ins, outs = refs[: 2 + 2 * count], refs[2 + 2 * count :]
    deal_again(plan, *ins[:2], *outs[:2])
    for at in range(count):
        add_kernel(2, *ins[2 + 2 * at : 4 + 2 * at], outs[2 + at])


def deal_kernel(plan, *refs):
    deal_again(plan, *refs)


def add_kernel(count, *refs):
    value = refs[0][...]
    for ref in refs[1:count]:
        value = value + unpack_table(ref[...])
    refs[-1][...] = pack_table(value)


def combine_kernel(plan, arrivals, sizes, beside, after, *refs):
    at, out_at = 0, sum(arrivals) + len(arrivals) + after
    if beside:
        step, ins, outs = beside
        step(plan, *refs[out_at : out_at + ins], *refs[len(refs) - outs :])
        out_at += ins
    for part, count, size in zip(plan.parts, arrivals, sizes):
        keep, arrived = refs[at], refs[at + 1 : at + 1 + count]
        outs = refs[out_at : out_at + size]
        at, out_at = at + 1 + count, out_at + size
        share = keep.shape[0] // size
        for place in range(keep.shape[0]):
            value = keep[place]
            for ref in arrived:
                value = value + unpack_table(ref[place], 8 * part.units)
            which, inner = divmod(place, share)
            packed = which or size == 1
            outs[which][inner] = pack_table(value, part.rows) if packed else value


def stack_kernel(plan, counts, *refs):
    outs = refs[-1 - len(counts) : -1]
    add = refs[sum(counts) : -1 - len(counts)]
    add_kernel(len(add), *add, refs[-1])
    first = 0
    for count, out in zip(counts, outs):
        for at in range(count):
            out[at] = refs[first + at][0]
        first += count


def spread_kernel(plan, counts, side, *refs):
    helds = refs[len(refs) - len(counts) :]
    rel_out, rem_out = refs[-2 - len(counts) : len(refs) - len(counts)]
    me = plan.me()
    first = 0
    for count, held in zip(counts, helds):
        at = 0
        for piece in refs[first : first + count]:
            held[at : at + piece.shape[0]] = piece[...]
            at += piece.shape[0]
        first += count
    for chunk in range(plan.half_chunks):
        for which, (part, held) in enumerate(zip(plan.parts, helds)):
            value = unpack_table(held[part.position(chunk, me)], 8 * part.units)
            for index, block in enumerate(plan.chunk_blocks(chunk, which)):
                if block is None:
                    break
                lane, sub = block
                rows = slice(sub, sub + 8)
                piece = value[8 * index : 8 * index + 8]
                if lane < plan.half_rel:
                    rel_out[rows, lane : lane + LANES] = piece
                else:
                    lane -= plan.half_rel
                    rem_out[rows, lane : lane + LANES] = piece


def relay_kernel(*refs):
    pass


def part_out_kernel(plan, *refs):
    out = refs[-1]
    rel = lax.axis_index("rel")
    lanes = plan.part_lanes
    for mask, ref in enumerate(refs[: plan.rels]):
        if lanes % LANES:
            out[:, mask * lanes : (mask + 1) * lanes] = unpack_table(ref[...])
        else:
            start = pl.multiple_of((rel ^ mask) * lanes, lanes)
            out[:, pl.ds(start, lanes)] = unpack_table(ref[...])


def shape(extent, kind):
    return jax.ShapeDtypeStruct(extent, kind)


VMEM = pl.BlockSpec(memory_space=pltpu.VMEM)
ANY = pl.BlockSpec(memory_space=pl.ANY)


def call(kernel, outs, args, name, cost, limit, scratch=(), in_specs=None, out_specs=None, **more):
    work = pl.CostEstimate(flops=int(cost * 1e9), bytes_accessed=int(cost * 3e6), transcendentals=0)
    if "grid_spec" not in more:
        more["in_specs"] = in_specs or [VMEM] * len(args)
        more["out_specs"] = out_specs or [VMEM] * len(outs)
        more["scratch_shapes"] = list(scratch)
    return pl.pallas_call(
        kernel,
        out_shape=outs,
        compiler_params=pltpu.CompilerParams(vmem_limit_bytes=int(limit * 2**20)),
        cost_estimate=work,
        name=name,
        **more,
    )(*args)


def body(
    partitions,
    remainder,
    relations,
    counts,
    lhs_rows,
    lhs_rems,
    rel_ids,
    rhs_rows,
    rhs_rems,
    neg_rows,
    neg_rems,
):
    prows, width = partitions.shape
    plan = Plan(
        lax.axis_size("dom"),
        lax.axis_size("rel"),
        prows,
        width,
        remainder.shape[0],
        relations.shape[0],
        lhs_rows.shape[2],
    )
    smem = pl.BlockSpec(memory_space=pltpu.SMEM)
    own, rem, rels = partitions.T, remainder.T, relations.T
    edges, wide = plan.edges, plan.bucket_edges
    grow = max(1, edges // 1024)
    buckets = plan.buckets
    afar = lambda d: d ^ (plan.target_mask(d % plan.rels) * plan.rels)
    i16 = jnp.int16

    def exchanged(values, masks):
        return [
            send(value, plan, lambda d, m=mask: d ^ m) for value, mask in zip(values, masks[1:])
        ]

    def after(kernel, outs, args, others, name, cost, limit=12, **more):
        return call(
            kernel,
            outs,
            list(args) + list(others),
            name,
            cost,
            limit,
            in_specs=[VMEM] * len(args) + [ANY] * len(others),
            **more,
        )

    tables = [lhs_rows, lhs_rems, rel_ids, rhs_rows, rhs_rems, neg_rows, neg_rems]
    target = send(own, plan, afar)
    sources = [own] + [
        send(own, plan, lambda d, b=bucket: d ^ (b * plan.rels)) for bucket in range(1, buckets)
    ]
    lists = call(
        functools.partial(lists_kernel, plan),
        [shape((buckets * plan.maxb, 8, LANES), jnp.int32)] * plan.rels,
        tables + [counts.reshape(-1)],
        "lists",
        0.5,
        60,
        in_specs=[VMEM] * 7 + [smem],
    )
    lists = [lists[0]] + exchanged(lists[1:], range(plan.rels))
    (rel_split,) = call(
        split_kernel,
        [shape((2 * width, plan.nrels), BF16)],
        [rels],
        "rel_split",
        2.0,
        50,
    )
    labels = call(
        functools.partial(forward_kernel, plan),
        [shape((plan.slots, 8, LANES), jnp.int32)] * buckets,
        lists,
        "forward",
        0.2,
        8,
    )
    labels = [labels[0]] + [
        send(labels[bucket], plan, lambda d, b=bucket: d ^ (b * plan.rels))
        for bucket in range(1, buckets)
    ]
    labels_of = lambda bucket: [labels[bucket]]
    grad_shapes = lambda count: [
        shape((2 * width, count), BF16),
        shape((2 * width, count), BF16),
        shape((2 * width, 2 * count), BF16),
    ]
    inputs = []
    for bucket in range(buckets):
        (vec,) = call(
            functools.partial(relation_kernel, plan),
            [shape((width, wide), F32)],
            labels_of(bucket) + [rel_split],
            "relation",
            2.0,
            16 * grow,
        )
        lhs, cand_rem = call(
            functools.partial(rows_kernel, plan),
            [shape((width, wide), F32), shape((width, 2 * wide), BF16)],
            labels_of(bucket) + [sources[bucket], rem],
            "rows",
            0.7,
            12 * grow,
        )
        inputs.append([lhs, vec, cand_rem])
    lanes = plan.part_lanes
    dealt = lambda count: [
        shape((width, count * lanes), F32),
        shape((width + 16, count * lanes), i16),
    ]
    grads = []
    for bucket in range(buckets - 1):
        grads += call(
            functools.partial(bucket_kernel, plan),
            grad_shapes(wide),
            labels_of(bucket) + [target] + inputs[bucket],
            "bucket",
            4.0,
            16 * grow,
        )
    table = [pltpu.VMEM((width, plan.half_lanes), F32)]
    made = call(
        functools.partial(last_kernel, plan),
        [shape(part.packed, i16) for part in plan.parts]
        + [shape((width, plan.half_rem), F32)]
        + grad_shapes(edges),
        labels + grads + [target] + inputs[-1],
        "last",
        9.0,
        20 * grow,
        scratch=table,
    )
    made, grads = list(made[:-3]), list(made[-3:])
    away, rem_part = made[:-1], made[-1]
    cores = [send(value, plan, lambda d: d ^ 1) for value in away]

    keeps = after(
        functools.partial(home_kernel, plan),
        [shape(part.bare, F32) for part in plan.parts],
        labels + [grads[1], rem_part],
        list(away),
        "home",
        3.0,
        16 * grow,
        scratch=table,
    )

    def combine(keeps, arrived, level, name, step=None, step_args=(), step_outs=(), order=()):
        sizes = [len(part.masks[level]) if level < 2 else 1 for part in plan.parts]
        outs, args = [], []
        for part, keep, pieces, size in zip(plan.parts, keeps, arrived, sizes):
            args += [keep] + pieces
            if level < 2:
                outs += part.shares(keep.shape[0], size)
            else:
                outs.append(shape((1,) + part.packed[1:], i16))
        beside = (step, len(step_args), len(step_outs)) if step else None
        count = [len(pieces) for pieces in arrived]
        made = after(
            functools.partial(combine_kernel, plan, count, sizes, beside, len(order)),
            outs + list(step_outs),
            args + list(step_args),
            order,
            name,
            0.6,
        )
        made, beside = made[: len(outs)], made[len(outs) :]
        if level == 2:
            return made, [], beside
        keeps, arrived = [], []
        for part, size in zip(plan.parts, sizes):
            group, made = made[:size], made[size:]
            keeps.append(group[0])
            arrived.append(exchanged(group[1:], part.masks[level]))
        return keeps, arrived, beside

    keeps, arrived, _ = combine(
        keeps, [[core] for core in cores], 0, "combine_cores"
    )
    far = after(
        functools.partial(target_kernel, plan),
        [shape((width + 16, prows), i16)],
        labels + [grads[2]],
        [keeps[0]],
        "target",
        1.8,
        16 * grow,
    )
    others, order = [], [far[0]]
    for bucket in range(1, buckets):
        keep, value = after(
            functools.partial(source_kernel, plan, bucket),
            dealt(plan.rels // 2),
            labels_of(bucket) + [grads[0]],
            order,
            "source",
            0.8,
            12 * grow,
        )
        others.append([keep, send(value, plan, lambda d: d ^ 1)])
        order = [keep]
    (source,) = after(
        functools.partial(own_source_kernel, plan),
        [shape((width, prows), F32)],
        labels_of(0) + [grads[0]],
        order,
        "own_source",
        0.8,
        16 * grow,
    )
    far = [send(value, plan, afar) for value in far]
    def deal_on(pairs, count, bit):
        while count > 2:
            count, bit = count // 2, bit * 2
            made = [
                after(functools.partial(deal_kernel, plan), dealt(count), pair, [], "deal", 0.3)
                for pair in pairs
            ]
            pairs = [[keep, send(value, plan, lambda d, m=bit: d ^ m)] for keep, value in made]
        return pairs, count // 2, bit * 2

    others, count, bit = deal_on(others, plan.rels // 2, 1)
    keeps, arrived, made = combine(
        keeps,
        arrived,
        1,
        "combine_first",
        lambda plan, *refs: share(plan, len(others), *refs),
        [source] + far + sum(others, []),
        dealt(plan.rels // 2) + dealt(count) * len(others),
    )
    mine = [[made[0], send(made[1], plan, lambda d: d ^ 1)]]
    others = [
        [made[at], send(made[at + 1], plan, lambda d: d ^ bit)] for at in range(2, len(made), 2)
    ]
    (mine,), count, bit = deal_on(mine, plan.rels // 2, 1)
    totals, _, made = combine(
        keeps,
        arrived,
        2,
        "combine_last",
        lambda plan, *refs: deal_and_settle(plan, len(others), *refs),
        mine + sum(others, []),
        dealt(count) + [shape((width + 16, lanes), i16)] * len(others),
    )
    mine, came = made[0], send(made[1], plan, lambda d: d ^ bit)
    crossing = exchanged(made[2:], range(0, plan.rels * buckets, plan.rels))
    pieces = [
        [total] + exchanged([total] * (len(part.masks[1]) - 1), part.masks[1])
        for part, total in zip(plan.parts, totals)
    ]
    flat = sum(pieces, [])
    made = after(
        functools.partial(stack_kernel, plan, [len(group) for group in pieces]),
        [
            shape((len(group),) + part.packed[1:], i16)
            for part, group in zip(plan.parts, pieces)
        ]
        + [shape((width + 16, lanes), i16)],
        flat + [mine, came] + crossing,
        [],
        "stack",
        0.5,
    )
    blocks, owners = made[:-1], {0: made[-1]}
    pieces = [
        [block] + exchanged([block] * (len(part.masks[0]) - 1), part.masks[0])
        for part, block in zip(plan.parts, blocks)
    ]
    while bit:
        masks = sorted(owners)
        if bit == 1:
            held = call(
                relay_kernel,
                [shape((width + 16, lanes), i16)] * len(masks),
                [owners[mask] for mask in masks] + pieces[0][1:],
                "relay",
                0.1,
                1,
                in_specs=[ANY] * (len(masks) + len(pieces[0]) - 1),
                out_specs=[ANY] * len(masks),
                input_output_aliases={at: at for at in range(len(masks))},
            )
            owners = dict(zip(masks, held))
        for mask in masks:
            owners[mask | bit] = send(owners[mask], plan, lambda d, m=bit: d ^ m)
        bit //= 2
    (grad_partitions,) = after(
        functools.partial(part_out_kernel, plan),
        [shape((width, prows), F32)],
        [owners[mask] for mask in range(plan.rels)],
        [],
        "part_out",
        1.0,
    )
    if lanes % LANES:
        order = jnp.arange(plan.rels) ^ lax.axis_index("rel")
        split_lanes = grad_partitions.reshape(width, plan.rels, lanes)
        grad_partitions = jnp.take(split_lanes, order, axis=1).reshape(width, prows)

    crossed = [[send(piece, plan, lambda d: d ^ 1) for piece in group] for group in pieces]
    side = lax.axis_index("rel") & 1
    outs = [shape((width, plan.nrels), F32), shape((width, plan.rems), F32)]
    spec = lambda lanes: pl.BlockSpec((width, lanes), lambda i, half: (0, half[0]))
    made = []
    for turn, groups in enumerate([pieces, crossed]):
        flat = sum(groups, [])
        made = call(
            functools.partial(spread_kernel, plan, [len(group) for group in groups]),
            outs,
            [(side ^ turn).reshape(1), *flat, *made],
            "spread",
            2.0,
            16,
            grid_spec=pltpu.PrefetchScalarGridSpec(
                num_scalar_prefetch=1,
                grid=(1,),
                in_specs=[pl.BlockSpec(piece.shape, lambda i, half: (0, 0, 0)) for piece in flat]
                + [ANY] * len(made),
                out_specs=[spec(plan.half_rel), spec(plan.half_rem)],
                scratch_shapes=[pltpu.VMEM(part.packed, i16) for part in plan.parts],
            ),
            input_output_aliases={1 + len(flat) + at: at for at in range(len(made))},
        )
    grad_relations, grad_remainder = made
    return grad_partitions.T, grad_remainder.T, grad_relations.T


def solution(mesh):
    edge = P("dom", None, "rel", None)
    in_specs = (P("dom", None), P(), P(), P("dom", None, "rel")) + (edge,) * 7
    out_specs = (P("dom", None), P(), P())
    return jax.shard_map(body, mesh=mesh, in_specs=in_specs, out_specs=out_specs, check_vma=False)
```

```python
import functools

import jax
import jax.numpy as jnp
from jax import lax
from jax.experimental import pallas as pl
from jax.experimental.pallas import tpu as pltpu
from jax.sharding import PartitionSpec as P

F32 = jnp.float32
BF16 = jnp.bfloat16
LANES = 128
REACH = 32766.0
NT = (((1,), (1,)), ((), ()))
NN = (((1,), (0,)), ((), ()))
TN = (((0,), (0,)), ((), ()))


def bits_of(count):
    return count.bit_length() - 1


def reverse_bits(value, count):
    out = 0
    for bit in range(bits_of(count)):
        out = out * 2 + ((value >> bit) & 1)
    return out


def split(value):
    high = value.astype(BF16)
    low = (value - high.astype(F32)).astype(BF16)
    return high, low


def dot(left, right, dims):
    return lax.dot_general(left, right, dims, preferred_element_type=F32)


def dot3(left, right, dims):
    left_high, left_low = split(left)
    right_high, right_low = split(right)
    return (
        dot(left_high, right_high, dims)
        + dot(left_high, right_low, dims)
        + dot(left_low, right_high, dims)
    )


def one_hot(ids, rows, base=0):
    place = lax.broadcasted_iota(jnp.int32, (rows, ids.shape[1]), 0)
    return jnp.where(place == ids - base, 1.0, 0.0).astype(BF16)


def store_split(ref, cols, value):
    high, low = split(value)
    depth = value.shape[0]
    ref[0:depth, cols] = high
    ref[depth : 2 * depth, cols] = low


def folded(value):
    depth = value.shape[0] // 2
    return value[:depth] + value[depth:]


def quantized(value):
    top = jnp.max(jnp.abs(value), axis=0, keepdims=True)
    exponent = jnp.floor(jnp.log2(jnp.maximum(top, 1e-30))) + 1.0
    return jnp.round(value * (REACH * jnp.exp2(-exponent))), exponent


def scale_of(exponent):
    return jnp.exp2(exponent) * (1.0 / REACH)


def to_words(value):
    return value.astype(jnp.int32).astype(jnp.int16)


def from_words(words):
    return words.astype(jnp.int32).astype(F32)


def pack_table(value, rows=None):
    scaled, exponent = quantized(value)
    spare = (rows or value.shape[0] + 16) - value.shape[0]
    tail = jnp.broadcast_to(exponent, (spare, value.shape[1]))
    return to_words(jnp.concatenate([scaled, tail], axis=0))


def unpack_table(words, depth=None):
    depth = depth or words.shape[0] - 16
    value = from_words(words)
    return value[:depth] * scale_of(value[depth : depth + 1])


class Part:
    def __init__(self, plan, units, groups):
        self.units = units
        self.rows = (units + 2) // 2 * 16
        self.masks = [self.group_masks(bits) for bits in groups]
        order = [bit for group in groups for bit in reversed(group)]
        self.place = {bit: len(order) - 1 - at for at, bit in enumerate(order)}
        self.packed = (plan.half_chunks, self.rows, LANES)
        self.bare = (plan.half_chunks, 8 * units, LANES)

    @staticmethod
    def group_masks(bits):
        masks = []
        for index in range(2 ** len(bits)):
            masks.append(sum(((index >> at) & 1) << bit for at, bit in enumerate(bits)))
        return masks

    def position(self, chunk, me):
        relative = chunk ^ (me >> 1)
        out = 0
        for bit, at in self.place.items():
            out = out + (((relative >> (bit - 1)) & 1) << at)
        return out

    def shares(self, count, size):
        count = count // size
        return [shape((count,) + self.bare[1:], F32)] + [
            shape((count,) + self.packed[1:], jnp.int16)
        ] * (size - 1)


class Plan:
    def __init__(self, doms, rels, prows, width, rems, nrels, maxb):
        self.doms, self.rels, self.maxb = doms, rels, maxb
        self.devices = doms * rels
        self.prows, self.width, self.rems, self.nrels = prows, width, rems, nrels
        self.buckets = doms // rels
        self.slots = rels * maxb
        self.bucket_edges = self.slots * LANES
        self.edges = self.buckets * self.bucket_edges
        self.part_lanes = prows // rels
        self.half_rel, self.half_rem = nrels // 2, rems // 2
        self.half_lanes = self.half_rel + self.half_rem
        self.subs = width // 8
        self.units = (self.half_lanes // LANES) * self.subs
        self.half_chunks = self.devices // 2
        self.chunk_units = -(-self.units // self.half_chunks)
        rel_bits = bits_of(rels)
        all_bits = rel_bits + bits_of(doms)
        near = list(range(1, rel_bits + 1))
        far = list(range(rel_bits + 1, all_bits))
        self.parts = [Part(self, self.chunk_units, [near, far])]

    def chunk_blocks(self, chunk, part):
        first = chunk * self.chunk_units + (self.parts[0].units if part else 0)
        blocks = []
        for unit in range(first, first + self.parts[part].units):
            lane, sub = divmod(unit, self.subs)
            blocks.append((lane * LANES, 8 * sub) if unit < self.units else None)
        return blocks

    def row(self, labels, bucket, kinds, first, count):
        rows = []
        for slot in range(first, first + count):
            rows += [labels[bucket][slot, kind : kind + 1, :] for kind in kinds]
        return jnp.concatenate(rows, axis=1) if len(rows) > 1 else rows[0]

    def whole_row(self, labels, kinds):
        rows = [
            self.row(labels, bucket, kinds, 0, self.slots) for bucket in range(self.buckets)
        ]
        return jnp.concatenate(rows, axis=1) if len(rows) > 1 else rows[0]

    def me(self):
        return lax.axis_index("dom") * self.rels + lax.axis_index("rel")

    def target_mask(self, rel):
        return reverse_bits(rel, self.rels) * self.buckets

    def dynamic_mask(self, rel):
        out = 0
        width = bits_of(self.rels)
        for bit in range(width):
            out = out + (((rel >> bit) & 1) << (width - 1 - bit))
        return out * self.buckets


def send(value, plan, target):
    pairs = [(device, target(device)) for device in range(plan.devices)]
    return lax.ppermute(value, ("dom", "rel"), pairs)


def lists_kernel(plan, *refs):
    tables, counts, outs = refs[:7], refs[7], refs[8:]
    source = lax.axis_index("dom")
    rel = lax.axis_index("rel")
    for mask, out in enumerate(outs):
        for bucket in range(plan.buckets):
            target = source ^ bucket ^ plan.dynamic_mask(rel ^ mask)
            stop = lax.rem(source - target + plan.doms, plan.doms)
            for turn in range(plan.maxb):
                at = bucket * plan.maxb + turn
                for kind, table in enumerate(tables):
                    out[at, kind : kind + 1, :] = table[0, stop, turn : turn + 1, :]
                live = jnp.where(turn < counts[stop], 1, 0)
                out[at, 7:8, :] = jnp.full((1, LANES), live, jnp.int32)


def forward_kernel(plan, *refs):
    lists, outs = refs[: plan.rels], refs[plan.rels :]
    for bucket, out in enumerate(outs):
        for mask, ref in enumerate(lists):
            for turn in range(plan.maxb):
                out[mask * plan.maxb + turn] = ref[bucket * plan.maxb + turn]


def split_kernel(relations, out):
    depth = relations.shape[0]
    high, low = split(relations[...])
    out[0:depth, :] = high
    out[depth : 2 * depth, :] = low


def relation_kernel(plan, *refs):
    labels, relations, out = refs[:1], refs[1], refs[-1]
    for pair in range(0, plan.slots, 2):
        count = min(2, plan.slots - pair)
        start = pair * LANES
        ids = plan.row(labels, 0, (2,), pair, count)
        out[:, start : start + count * LANES] = folded(
            dot(relations[...], one_hot(ids, plan.nrels), NN)
        )


def rows_kernel(plan, *refs):
    labels, (own, rem) = refs[:1], refs[1:3]
    lhs_out, rem_out = refs[-2:]
    for pair in range(0, plan.slots, 2):
        count = min(2, plan.slots - pair)
        row = lambda *kinds: plan.row(labels, 0, kinds, pair, count)
        start = pair * LANES
        end = start + count * LANES
        lhs_out[:, start:end] = dot(own[...], one_hot(row(0), plan.prows), NN) + dot(
            rem[...], one_hot(row(1), plan.rems), NN
        )
        rem_out[:, 2 * start : 2 * end] = dot(
            rem[...], one_hot(row(4, 6), plan.rems), NN
        ).astype(BF16)


def conjugate_parts(grad, other):
    half = grad.shape[0] // 2
    grad_re, grad_im = grad[:half], grad[half:]
    other_re, other_im = other[:half], other[half:]
    return jnp.concatenate(
        [grad_re * other_re + grad_im * other_im, grad_im * other_re - grad_re * other_im], 0
    )


def complex_product(left, right):
    half = left.shape[0] // 2
    left_re, left_im = left[:half], left[half:]
    right_re, right_im = right[:half], right[half:]
    return jnp.concatenate(
        [left_re * right_re - left_im * right_im, left_re * right_im + left_im * right_re], 0
    )


def bucket_grads(plan, labels, target, lhs_in, rel_in, rem_in, lhs_out, rel_out, cand_out, base):
    total = 2 * LANES
    edge = lax.broadcasted_iota(jnp.int32, (LANES, total), 0)
    column = lax.broadcasted_iota(jnp.int32, (LANES, total), 1)
    keep = jnp.where(edge == column, 0.0, 1.0 / total)
    for slot in range(plan.slots):
        cols = slice(slot * LANES, (slot + 1) * LANES)
        wide = slice(slot * total, (slot + 1) * total)
        ids = plan.row(labels, 0, (3, 5), slot, 1)
        cand = dot(target[...], one_hot(ids, plan.prows), NN) + rem_in[:, wide].astype(F32)
        rhs = cand[:, :LANES]
        lhs, vec = lhs_in[:, cols], rel_in[:, cols]
        u_vec = complex_product(lhs, vec)
        live = plan.row(labels, 0, (7,), slot, 1).astype(F32)
        positive = jnp.sum(u_vec * rhs, axis=0, keepdims=True)
        negative = dot3(u_vec, cand, TN)
        grad_pos = -jax.nn.sigmoid(-positive) * live
        grad_neg = jax.nn.sigmoid(negative) * keep * live[0:1, 0:1]
        grad_u = grad_pos * rhs + dot3(cand, grad_neg, NT)
        from_neg = dot3(u_vec, grad_neg, NN)
        grad_cand = jnp.concatenate(
            [from_neg[:, :LANES] + grad_pos * u_vec, from_neg[:, LANES:]], axis=1
        )
        at = base + slot
        cols = slice(at * LANES, (at + 1) * LANES)
        wide = slice(at * total, (at + 1) * total)
        store_split(lhs_out, cols, conjugate_parts(grad_u, vec))
        store_split(rel_out, cols, conjugate_parts(grad_u, lhs))
        store_split(cand_out, wide, grad_cand)


def bucket_kernel(plan, *refs):
    bucket_grads(plan, refs[:1], *refs[1:], 0)


def last_kernel(plan, *refs):
    labels, refs = refs[: plan.buckets], refs[plan.buckets :]
    before, refs = refs[: 3 * (plan.buckets - 1)], refs[3 * (plan.buckets - 1) :]
    inputs, refs = refs[:4], refs[4:]
    away, rem_part, outs, table = refs[: len(plan.parts)], refs[-5], refs[-4:-1], refs[-1]
    base = (plan.buckets - 1) * plan.slots
    bucket_grads(plan, labels[-1:], *inputs, *outs, base)
    for at, ref in enumerate(before):
        wide = ref.shape[1]
        start = at // 3 * wide
        outs[at % 3][:, start : start + wide] = ref[...]
    lhs_grads, rel_grads, cand_grads = outs
    first = one_hot(plan.whole_row(labels, (1,)), plan.rems)
    second = one_hot(plan.whole_row(labels, (4, 6)), plan.rems)
    rem = folded(dot(lhs_grads[...], first, NT) + dot(cand_grads[...], second, NT))
    low, high = rem[:, : plan.half_rem], rem[:, plan.half_rem :]
    core = lax.axis_index("rel") & 1
    rem_part[...] = jnp.where(core == 0, low, high)
    table[:, plan.half_rel :] = jnp.where(core == 0, high, low)
    reduce_half(plan, True, labels, rel_grads, table, away)


def home_kernel(plan, *refs):
    count = plan.buckets
    outs, table = refs[-1 - len(plan.parts) : -1], refs[-1]
    table[:, plan.half_rel :] = refs[count + 1][...]
    reduce_half(plan, False, refs[:count], refs[count], table, outs)


def reduce_half(plan, away, labels, rel_grads, table, outs):
    me = plan.me()
    half = (me & 1) ^ (1 if away else 0)
    step = 2 * LANES if plan.half_rel % (2 * LANES) == 0 else LANES
    ids = plan.whole_row(labels, (2,)) - half * plan.half_rel
    for start in range(0, plan.half_rel, step):
        hot = one_hot(ids, step, start)
        table[:, start : start + step] = folded(dot(rel_grads[...], hot, NT))
    for chunk in range(plan.half_chunks):
        for which, (part, out) in enumerate(zip(plan.parts, outs)):
            value = jnp.concatenate(
                [
                    table[block[1] : block[1] + 8, block[0] : block[0] + LANES]
                    if block
                    else jnp.zeros((8, LANES), F32)
                    for block in plan.chunk_blocks(chunk, which)
                ],
                axis=0,
            )
            out[part.position(chunk, me)] = pack_table(value, part.rows) if away else value


def rows_sum(plan, ids, grads):
    shift = lax.axis_index("rel") * plan.part_lanes
    return folded(dot(grads, one_hot(ids ^ shift, plan.prows), NT))


def target_kernel(plan, *refs):
    count = plan.buckets
    ids = plan.whole_row(refs[:count], (3, 5))
    value = pack_table(rows_sum(plan, ids, refs[count][...]))
    for at, out in enumerate(refs[-2:]):
        lanes = out.shape[1]
        out[...] = value[:, at * lanes : (at + 1) * lanes]


def source_sum(plan, labels, grads):
    return rows_sum(plan, plan.row([labels], 0, (0,), 0, plan.slots), grads)


def deal(plan, value, keep, away):
    lanes = plan.part_lanes
    for at in range(value.shape[1] // lanes):
        share = value[:, at * lanes : (at + 1) * lanes]
        to = slice(at // 2 * lanes, (at // 2 + 1) * lanes)
        if at % 2:
            away[:, to] = pack_table(share)
        else:
            keep[:, to] = share


def source_kernel(plan, bucket, *refs):
    start = bucket * plan.bucket_edges
    grads = refs[1][:, start : start + plan.bucket_edges]
    deal(plan, source_sum(plan, refs[0], grads), *refs[-2:])


def own_source_kernel(plan, *refs):
    refs[-1][...] = source_sum(plan, refs[0], refs[1][:, : plan.bucket_edges])


def share(plan, count, *refs):
    source, fars, others = refs[0], refs[1:3], refs[3 : 3 + 2 * count]
    outs = refs[3 + 2 * count :]
    far = jnp.concatenate([unpack_table(ref[...]) for ref in fars], axis=1)
    deal(plan, source[...] + far, *outs[:2])
    for at in range(0, 2 * count, 2):
        deal_again(plan, *others[at : at + 2], *outs[at + 2 : at + 4])


def deal_again(plan, keep, came, *outs):
    deal(plan, keep[...] + unpack_table(came[...]), *outs)


def deal_and_settle(plan, count, *refs):
    ins, outs = refs[: 2 + 2 * count], refs[2 + 2 * count :]
    deal_again(plan, *ins[:2], *outs[:2])
    for at in range(count):
        add_kernel(2, *ins[2 + 2 * at : 4 + 2 * at], outs[2 + at])


def deal_kernel(plan, *refs):
    deal_again(plan, *refs)


def add_kernel(count, *refs):
    value = refs[0][...]
    for ref in refs[1:count]:
        value = value + unpack_table(ref[...])
    refs[-1][...] = pack_table(value)


def combine_kernel(plan, arrivals, sizes, beside, after, *refs):
    at, out_at = 0, sum(arrivals) + len(arrivals) + after
    if beside:
        step, ins, outs = beside
        step(plan, *refs[out_at : out_at + ins], *refs[len(refs) - outs :])
        out_at += ins
    for part, count, size in zip(plan.parts, arrivals, sizes):
        keep, arrived = refs[at], refs[at + 1 : at + 1 + count]
        outs = refs[out_at : out_at + size]
        at, out_at = at + 1 + count, out_at + size
        share = keep.shape[0] // size
        for place in range(keep.shape[0]):
            value = keep[place]
            for ref in arrived:
                value = value + unpack_table(ref[place], 8 * part.units)
            which, inner = divmod(place, share)
            packed = which or size == 1
            outs[which][inner] = pack_table(value, part.rows) if packed else value


def stack_kernel(plan, counts, *refs):
    outs = refs[-1 - len(counts) : -1]
    add = refs[sum(counts) : -1 - len(counts)]
    add_kernel(len(add), *add, refs[-1])
    first = 0
    for count, out in zip(counts, outs):
        for at in range(count):
            out[at] = refs[first + at][0]
        first += count


def spread_kernel(plan, counts, side, *refs):
    helds = refs[len(refs) - len(counts) :]
    rel_out, rem_out = refs[-2 - len(counts) : len(refs) - len(counts)]
    me = plan.me()
    first = 0
    for count, held in zip(counts, helds):
        at = 0
        for piece in refs[first : first + count]:
            held[at : at + piece.shape[0]] = piece[...]
            at += piece.shape[0]
        first += count
    for chunk in range(plan.half_chunks):
        for which, (part, held) in enumerate(zip(plan.parts, helds)):
            value = unpack_table(held[part.position(chunk, me)], 8 * part.units)
            for index, block in enumerate(plan.chunk_blocks(chunk, which)):
                if block is None:
                    break
                lane, sub = block
                rows = slice(sub, sub + 8)
                piece = value[8 * index : 8 * index + 8]
                if lane < plan.half_rel:
                    rel_out[rows, lane : lane + LANES] = piece
                else:
                    lane -= plan.half_rel
                    rem_out[rows, lane : lane + LANES] = piece


def part_out_kernel(plan, *refs):
    out = refs[-1]
    rel = lax.axis_index("rel")
    lanes = plan.part_lanes
    for mask, ref in enumerate(refs[: plan.rels]):
        if lanes % LANES:
            out[:, mask * lanes : (mask + 1) * lanes] = unpack_table(ref[...])
        else:
            start = pl.multiple_of((rel ^ mask) * lanes, lanes)
            out[:, pl.ds(start, lanes)] = unpack_table(ref[...])


def shape(extent, kind):
    return jax.ShapeDtypeStruct(extent, kind)


VMEM = pl.BlockSpec(memory_space=pltpu.VMEM)
ANY = pl.BlockSpec(memory_space=pl.ANY)


def call(kernel, outs, args, name, cost, limit, scratch=(), in_specs=None, out_specs=None, **more):
    work = pl.CostEstimate(flops=int(cost * 1e9), bytes_accessed=int(cost * 3e6), transcendentals=0)
    if "grid_spec" not in more:
        more["in_specs"] = in_specs or [VMEM] * len(args)
        more["out_specs"] = out_specs or [VMEM] * len(outs)
        more["scratch_shapes"] = list(scratch)
    return pl.pallas_call(
        kernel,
        out_shape=outs,
        compiler_params=pltpu.CompilerParams(vmem_limit_bytes=int(limit * 2**20)),
        cost_estimate=work,
        name=name,
        **more,
    )(*args)


def body(
    partitions,
    remainder,
    relations,
    counts,
    lhs_rows,
    lhs_rems,
    rel_ids,
    rhs_rows,
    rhs_rems,
    neg_rows,
    neg_rems,
):
    prows, width = partitions.shape
    plan = Plan(
        lax.axis_size("dom"),
        lax.axis_size("rel"),
        prows,
        width,
        remainder.shape[0],
        relations.shape[0],
        lhs_rows.shape[2],
    )
    smem = pl.BlockSpec(memory_space=pltpu.SMEM)
    own, rem, rels = partitions.T, remainder.T, relations.T
    edges, wide = plan.edges, plan.bucket_edges
    grow = max(1, edges // 1024)
    buckets = plan.buckets
    afar = lambda d: d ^ (plan.target_mask(d % plan.rels) * plan.rels)
    i16 = jnp.int16

    def exchanged(values, masks):
        return [
            send(value, plan, lambda d, m=mask: d ^ m) for value, mask in zip(values, masks[1:])
        ]

    def after(kernel, outs, args, others, name, cost, limit=12, **more):
        return call(
            kernel,
            outs,
            list(args) + list(others),
            name,
            cost,
            limit,
            in_specs=[VMEM] * len(args) + [ANY] * len(others),
            **more,
        )

    tables = [lhs_rows, lhs_rems, rel_ids, rhs_rows, rhs_rems, neg_rows, neg_rems]
    target = send(own, plan, afar)
    sources = [own] + [
        send(own, plan, lambda d, b=bucket: d ^ (b * plan.rels)) for bucket in range(1, buckets)
    ]
    lists = call(
        functools.partial(lists_kernel, plan),
        [shape((buckets * plan.maxb, 8, LANES), jnp.int32)] * plan.rels,
        tables + [counts.reshape(-1)],
        "lists",
        0.5,
        60,
        in_specs=[VMEM] * 7 + [smem],
    )
    lists = [lists[0]] + exchanged(lists[1:], range(plan.rels))
    (rel_split,) = call(
        split_kernel,
        [shape((2 * width, plan.nrels), BF16)],
        [rels],
        "rel_split",
        2.0,
        50,
    )
    labels = call(
        functools.partial(forward_kernel, plan),
        [shape((plan.slots, 8, LANES), jnp.int32)] * buckets,
        lists,
        "forward",
        0.2,
        8,
    )
    labels = [labels[0]] + [
        send(labels[bucket], plan, lambda d, b=bucket: d ^ (b * plan.rels))
        for bucket in range(1, buckets)
    ]
    labels_of = lambda bucket: [labels[bucket]]
    grad_shapes = lambda count: [
        shape((2 * width, count), BF16),
        shape((2 * width, count), BF16),
        shape((2 * width, 2 * count), BF16),
    ]
    inputs = []
    for bucket in range(buckets):
        (vec,) = call(
            functools.partial(relation_kernel, plan),
            [shape((width, wide), F32)],
            labels_of(bucket) + [rel_split],
            "relation",
            2.0,
            16 * grow,
        )
        lhs, cand_rem = call(
            functools.partial(rows_kernel, plan),
            [shape((width, wide), F32), shape((width, 2 * wide), BF16)],
            labels_of(bucket) + [sources[bucket], rem],
            "rows",
            0.7,
            12 * grow,
        )
        inputs.append([lhs, vec, cand_rem])
    lanes = plan.part_lanes
    dealt = lambda count: [
        shape((width, count * lanes), F32),
        shape((width + 16, count * lanes), i16),
    ]
    grads = []
    for bucket in range(buckets - 1):
        grads += call(
            functools.partial(bucket_kernel, plan),
            grad_shapes(wide),
            labels_of(bucket) + [target] + inputs[bucket],
            "bucket",
            4.0,
            16 * grow,
        )
    table = [pltpu.VMEM((width, plan.half_lanes), F32)]
    made = call(
        functools.partial(last_kernel, plan),
        [shape(part.packed, i16) for part in plan.parts]
        + [shape((width, plan.half_rem), F32)]
        + grad_shapes(edges),
        labels + grads + [target] + inputs[-1],
        "last",
        9.0,
        20 * grow,
        scratch=table,
    )
    made, grads = list(made[:-3]), list(made[-3:])
    away, rem_part = made[:-1], made[-1]
    cores = [send(value, plan, lambda d: d ^ 1) for value in away]

    others, order = [], list(away)
    for bucket in range(1, buckets):
        keep, value = after(
            functools.partial(source_kernel, plan, bucket),
            dealt(plan.rels // 2),
            labels_of(bucket) + [grads[0]],
            order,
            "source",
            0.8,
            12 * grow,
        )
        others.append([keep, send(value, plan, lambda d: d ^ 1)])
        order = [keep]
    keeps = after(
        functools.partial(home_kernel, plan),
        [shape(part.bare, F32) for part in plan.parts],
        labels + [grads[1], rem_part],
        order,
        "home",
        3.0,
        16 * grow,
        scratch=table,
    )

    def combine(keeps, arrived, level, name, step=None, step_args=(), step_outs=(), order=()):
        sizes = [len(part.masks[level]) if level < 2 else 1 for part in plan.parts]
        outs, args = [], []
        for part, keep, pieces, size in zip(plan.parts, keeps, arrived, sizes):
            args += [keep] + pieces
            if level < 2:
                outs += part.shares(keep.shape[0], size)
            else:
                outs.append(shape((1,) + part.packed[1:], i16))
        beside = (step, len(step_args), len(step_outs)) if step else None
        count = [len(pieces) for pieces in arrived]
        made = after(
            functools.partial(combine_kernel, plan, count, sizes, beside, len(order)),
            outs + list(step_outs),
            args + list(step_args),
            order,
            name,
            0.6,
        )
        made, beside = made[: len(outs)], made[len(outs) :]
        if level == 2:
            return made, [], beside
        keeps, arrived = [], []
        for part, size in zip(plan.parts, sizes):
            group, made = made[:size], made[size:]
            keeps.append(group[0])
            arrived.append(exchanged(group[1:], part.masks[level]))
        return keeps, arrived, beside

    keeps, arrived, _ = combine(
        keeps, [[core] for core in cores], 0, "combine_cores", order=[other[1] for other in others]
    )
    far = after(
        functools.partial(target_kernel, plan),
        [shape((width + 16, prows // 2), i16)] * 2,
        labels + [grads[2]],
        [keeps[0]],
        "target",
        1.8,
        16 * grow,
    )
    (source,) = after(
        functools.partial(own_source_kernel, plan),
        [shape((width, prows), F32)],
        labels_of(0) + [grads[0]],
        [far[0]],
        "own_source",
        0.8,
        16 * grow,
    )
    far = [send(value, plan, afar) for value in far]
    def deal_on(pairs, count, bit):
        while count > 2:
            count, bit = count // 2, bit * 2
            made = [
                after(functools.partial(deal_kernel, plan), dealt(count), pair, [], "deal", 0.3)
                for pair in pairs
            ]
            pairs = [[keep, send(value, plan, lambda d, m=bit: d ^ m)] for keep, value in made]
        return pairs, count // 2, bit * 2

    others, count, bit = deal_on(others, plan.rels // 2, 1)
    keeps, arrived, made = combine(
        keeps,
        arrived,
        1,
        "combine_first",
        lambda plan, *refs: share(plan, len(others), *refs),
        [source] + far + sum(others, []),
        dealt(plan.rels // 2) + dealt(count) * len(others),
    )
    mine = [[made[0], send(made[1], plan, lambda d: d ^ 1)]]
    others = [
        [made[at], send(made[at + 1], plan, lambda d: d ^ bit)] for at in range(2, len(made), 2)
    ]
    (mine,), count, bit = deal_on(mine, plan.rels // 2, 1)
    totals, _, made = combine(
        keeps,
        arrived,
        2,
        "combine_last",
        lambda plan, *refs: deal_and_settle(plan, len(others), *refs),
        mine + sum(others, []),
        dealt(count) + [shape((width + 16, lanes), i16)] * len(others),
    )
    mine, came = made[0], send(made[1], plan, lambda d: d ^ bit)
    crossing = exchanged(made[2:], range(0, plan.rels * buckets, plan.rels))
    pieces = [
        [total] + exchanged([total] * (len(part.masks[1]) - 1), part.masks[1])
        for part, total in zip(plan.parts, totals)
    ]
    flat = sum(pieces, [])
    made = after(
        functools.partial(stack_kernel, plan, [len(group) for group in pieces]),
        [
            shape((len(group),) + part.packed[1:], i16)
            for part, group in zip(plan.parts, pieces)
        ]
        + [shape((width + 16, lanes), i16)],
        flat + [mine, came] + crossing,
        [],
        "stack",
        0.5,
    )
    blocks, owners = made[:-1], {0: made[-1]}
    def gathered(block, masks):
        if len(masks) != 4:
            return [block] + exchanged([block] * (len(masks) - 1), masks)
        half = block.shape[0] // 2
        first, second = exchanged([block] * 2, masks[:3])
        over_first = send(first[:half], plan, lambda d: d ^ masks[2])
        over_second = send(second[half:], plan, lambda d: d ^ masks[1])
        return [block, first, second, over_first, over_second]

    pieces = [gathered(block, part.masks[0]) for part, block in zip(plan.parts, blocks)]
    while bit:
        for mask in sorted(owners):
            owners[mask | bit] = send(owners[mask], plan, lambda d, m=bit: d ^ m)
        bit //= 2
    (grad_partitions,) = after(
        functools.partial(part_out_kernel, plan),
        [shape((width, prows), F32)],
        [owners[mask] for mask in range(plan.rels)],
        [],
        "part_out",
        1.0,
    )
    if lanes % LANES:
        order = jnp.arange(plan.rels) ^ lax.axis_index("rel")
        split_lanes = grad_partitions.reshape(width, plan.rels, lanes)
        grad_partitions = jnp.take(split_lanes, order, axis=1).reshape(width, prows)

    crossed = [[send(piece, plan, lambda d: d ^ 1) for piece in group] for group in pieces]
    side = lax.axis_index("rel") & 1
    outs = [shape((width, plan.nrels), F32), shape((width, plan.rems), F32)]
    spec = lambda lanes: pl.BlockSpec((width, lanes), lambda i, half: (0, half[0]))
    made = []
    for turn, groups in enumerate([pieces, crossed]):
        flat = sum(groups, [])
        made = call(
            functools.partial(spread_kernel, plan, [len(group) for group in groups]),
            outs,
            [(side ^ turn).reshape(1), *flat, *made],
            "spread",
            2.0,
            16,
            grid_spec=pltpu.PrefetchScalarGridSpec(
                num_scalar_prefetch=1,
                grid=(1,),
                in_specs=[pl.BlockSpec(piece.shape, lambda i, half: (0, 0, 0)) for piece in flat]
                + [ANY] * len(made),
                out_specs=[spec(plan.half_rel), spec(plan.half_rem)],
                scratch_shapes=[pltpu.VMEM(part.packed, i16) for part in plan.parts],
            ),
            input_output_aliases={1 + len(flat) + at: at for at in range(len(made))},
        )
    grad_relations, grad_remainder = made
    return grad_partitions.T, grad_remainder.T, grad_relations.T


def solution(mesh):
    edge = P("dom", None, "rel", None)
    in_specs = (P("dom", None), P(), P(), P("dom", None, "rel")) + (edge,) * 7
    out_specs = (P("dom", None), P(), P())
    return jax.shard_map(body, mesh=mesh, in_specs=in_specs, out_specs=out_specs, check_vma=False)
```

```python
import functools

import jax
import jax.numpy as jnp
from jax import lax
from jax.experimental import pallas as pl
from jax.experimental.pallas import tpu as pltpu
from jax.sharding import PartitionSpec as P

F32 = jnp.float32
BF16 = jnp.bfloat16
LANES = 128
REACH = 32766.0
NT = (((1,), (1,)), ((), ()))
NN = (((1,), (0,)), ((), ()))
TN = (((0,), (0,)), ((), ()))


def bits_of(count):
    return count.bit_length() - 1


def reverse_bits(value, count):
    out = 0
    for bit in range(bits_of(count)):
        out = out * 2 + ((value >> bit) & 1)
    return out


def split(value):
    high = value.astype(BF16)
    low = (value - high.astype(F32)).astype(BF16)
    return high, low


def dot(left, right, dims):
    return lax.dot_general(left, right, dims, preferred_element_type=F32)


def dot3(left, right, dims):
    left_high, left_low = split(left)
    right_high, right_low = split(right)
    return (
        dot(left_high, right_high, dims)
        + dot(left_high, right_low, dims)
        + dot(left_low, right_high, dims)
    )


def one_hot(ids, rows, base=0):
    place = lax.broadcasted_iota(jnp.int32, (rows, ids.shape[1]), 0)
    return jnp.where(place == ids - base, 1.0, 0.0).astype(BF16)


def store_split(ref, cols, value):
    high, low = split(value)
    depth = value.shape[0]
    ref[0:depth, cols] = high
    ref[depth : 2 * depth, cols] = low


def folded(value):
    depth = value.shape[0] // 2
    return value[:depth] + value[depth:]


def quantized(value):
    top = jnp.max(jnp.abs(value), axis=0, keepdims=True)
    exponent = jnp.floor(jnp.log2(jnp.maximum(top, 1e-30))) + 1.0
    return jnp.round(value * (REACH * jnp.exp2(-exponent))), exponent


def scale_of(exponent):
    return jnp.exp2(exponent) * (1.0 / REACH)


def to_words(value):
    return value.astype(jnp.int32).astype(jnp.int16)


def from_words(words):
    return words.astype(jnp.int32).astype(F32)


def pack_table(value, rows=None):
    scaled, exponent = quantized(value)
    spare = (rows or value.shape[0] + 16) - value.shape[0]
    tail = jnp.broadcast_to(exponent, (spare, value.shape[1]))
    return to_words(jnp.concatenate([scaled, tail], axis=0))


def unpack_table(words, depth=None):
    depth = depth or words.shape[0] - 16
    value = from_words(words)
    return value[:depth] * scale_of(value[depth : depth + 1])


class Part:
    def __init__(self, plan, units, groups):
        self.units = units
        self.rows = (units + 2) // 2 * 16
        self.masks = [self.group_masks(bits) for bits in groups]
        order = [bit for group in groups for bit in reversed(group)]
        self.place = {bit: len(order) - 1 - at for at, bit in enumerate(order)}
        self.packed = (plan.half_chunks, self.rows, LANES)
        self.bare = (plan.half_chunks, 8 * units, LANES)

    @staticmethod
    def group_masks(bits):
        masks = []
        for index in range(2 ** len(bits)):
            masks.append(sum(((index >> at) & 1) << bit for at, bit in enumerate(bits)))
        return masks

    def position(self, chunk, me):
        relative = chunk ^ (me >> 1)
        out = 0
        for bit, at in self.place.items():
            out = out + (((relative >> (bit - 1)) & 1) << at)
        return out

    def shares(self, count, size):
        count = count // size
        return [shape((count,) + self.bare[1:], F32)] + [
            shape((count,) + self.packed[1:], jnp.int16)
        ] * (size - 1)


class Plan:
    def __init__(self, doms, rels, prows, width, rems, nrels, maxb):
        self.doms, self.rels, self.maxb = doms, rels, maxb
        self.devices = doms * rels
        self.prows, self.width, self.rems, self.nrels = prows, width, rems, nrels
        self.buckets = doms // rels
        self.slots = rels * maxb
        self.bucket_edges = self.slots * LANES
        self.edges = self.buckets * self.bucket_edges
        self.part_lanes = prows // rels
        self.half_rel, self.half_rem = nrels // 2, rems // 2
        self.half_lanes = self.half_rel + self.half_rem
        self.subs = width // 8
        self.units = (self.half_lanes // LANES) * self.subs
        self.half_chunks = self.devices // 2
        self.chunk_units = -(-self.units // self.half_chunks)
        rel_bits = bits_of(rels)
        all_bits = rel_bits + bits_of(doms)
        near = list(range(1, rel_bits + 1))
        far = list(range(rel_bits + 1, all_bits))
        self.parts = [Part(self, self.chunk_units, [near, far])]

    def chunk_blocks(self, chunk, part):
        first = chunk * self.chunk_units + (self.parts[0].units if part else 0)
        blocks = []
        for unit in range(first, first + self.parts[part].units):
            lane, sub = divmod(unit, self.subs)
            blocks.append((lane * LANES, 8 * sub) if unit < self.units else None)
        return blocks

    def row(self, labels, bucket, kinds, first, count):
        rows = []
        for slot in range(first, first + count):
            rows += [labels[bucket][slot, kind : kind + 1, :] for kind in kinds]
        return jnp.concatenate(rows, axis=1) if len(rows) > 1 else rows[0]

    def whole_row(self, labels, kinds):
        rows = [
            self.row(labels, bucket, kinds, 0, self.slots) for bucket in range(self.buckets)
        ]
        return jnp.concatenate(rows, axis=1) if len(rows) > 1 else rows[0]

    def me(self):
        return lax.axis_index("dom") * self.rels + lax.axis_index("rel")

    def target_mask(self, rel):
        return reverse_bits(rel, self.rels) * self.buckets

    def dynamic_mask(self, rel):
        out = 0
        width = bits_of(self.rels)
        for bit in range(width):
            out = out + (((rel >> bit) & 1) << (width - 1 - bit))
        return out * self.buckets


def send(value, plan, target):
    pairs = [(device, target(device)) for device in range(plan.devices)]
    return lax.ppermute(value, ("dom", "rel"), pairs)


def lists_kernel(plan, *refs):
    tables, counts, outs = refs[:7], refs[7], refs[8:]
    source = lax.axis_index("dom")
    rel = lax.axis_index("rel")
    for mask, out in enumerate(outs):
        for bucket in range(plan.buckets):
            target = source ^ bucket ^ plan.dynamic_mask(rel ^ mask)
            stop = lax.rem(source - target + plan.doms, plan.doms)
            for turn in range(plan.maxb):
                at = bucket * plan.maxb + turn
                for kind, table in enumerate(tables):
                    out[at, kind : kind + 1, :] = table[0, stop, turn : turn + 1, :]
                live = jnp.where(turn < counts[stop], 1, 0)
                out[at, 7:8, :] = jnp.full((1, LANES), live, jnp.int32)


def forward_kernel(plan, *refs):
    lists, outs = refs[: plan.rels], refs[plan.rels :]
    for bucket, out in enumerate(outs):
        for mask, ref in enumerate(lists):
            for turn in range(plan.maxb):
                out[mask * plan.maxb + turn] = ref[bucket * plan.maxb + turn]


def split_kernel(relations, out, held, sems):
    depth, total = relations.shape
    step = 4 * LANES
    loads = [
        pltpu.make_async_copy(
            relations.at[:, start : start + step], held.at[:, start : start + step], sems.at[at]
        )
        for at, start in enumerate(range(0, total, step))
    ]
    for load in loads:
        load.start()
    for at, load in enumerate(loads):
        load.wait()
        cols = slice(at * step, (at + 1) * step)
        high, low = split(held[:, cols])
        out[0:depth, cols] = high
        out[depth : 2 * depth, cols] = low


def relation_kernel(plan, *refs):
    labels, relations, out = refs[:1], refs[1], refs[-1]
    for pair in range(0, plan.slots, 2):
        count = min(2, plan.slots - pair)
        start = pair * LANES
        ids = plan.row(labels, 0, (2,), pair, count)
        out[:, start : start + count * LANES] = folded(
            dot(relations[...], one_hot(ids, plan.nrels), NN)
        )


def rows_kernel(plan, *refs):
    labels, (own, rem) = refs[:1], refs[1:3]
    lhs_out, rem_out = refs[-2:]
    for pair in range(0, plan.slots, 2):
        count = min(2, plan.slots - pair)
        row = lambda *kinds: plan.row(labels, 0, kinds, pair, count)
        start = pair * LANES
        end = start + count * LANES
        lhs_out[:, start:end] = dot(own[...], one_hot(row(0), plan.prows), NN) + dot(
            rem[...], one_hot(row(1), plan.rems), NN
        )
        rem_out[:, 2 * start : 2 * end] = dot(
            rem[...], one_hot(row(4, 6), plan.rems), NN
        ).astype(BF16)


def conjugate_parts(grad, other):
    half = grad.shape[0] // 2
    grad_re, grad_im = grad[:half], grad[half:]
    other_re, other_im = other[:half], other[half:]
    return jnp.concatenate(
        [grad_re * other_re + grad_im * other_im, grad_im * other_re - grad_re * other_im], 0
    )


def complex_product(left, right):
    half = left.shape[0] // 2
    left_re, left_im = left[:half], left[half:]
    right_re, right_im = right[:half], right[half:]
    return jnp.concatenate(
        [left_re * right_re - left_im * right_im, left_re * right_im + left_im * right_re], 0
    )


def bucket_grads(plan, labels, target, lhs_in, rel_in, rem_in, lhs_out, rel_out, cand_out, base):
    total = 2 * LANES
    edge = lax.broadcasted_iota(jnp.int32, (LANES, total), 0)
    column = lax.broadcasted_iota(jnp.int32, (LANES, total), 1)
    keep = jnp.where(edge == column, 0.0, 1.0 / total)
    for slot in range(plan.slots):
        cols = slice(slot * LANES, (slot + 1) * LANES)
        wide = slice(slot * total, (slot + 1) * total)
        ids = plan.row(labels, 0, (3, 5), slot, 1)
        cand = dot(target[...], one_hot(ids, plan.prows), NN) + rem_in[:, wide].astype(F32)
        rhs = cand[:, :LANES]
        lhs, vec = lhs_in[:, cols], rel_in[:, cols]
        u_vec = complex_product(lhs, vec)
        live = plan.row(labels, 0, (7,), slot, 1).astype(F32)
        positive = jnp.sum(u_vec * rhs, axis=0, keepdims=True)
        negative = dot3(u_vec, cand, TN)
        grad_pos = -jax.nn.sigmoid(-positive) * live
        grad_neg = jax.nn.sigmoid(negative) * keep * live[0:1, 0:1]
        grad_u = grad_pos * rhs + dot3(cand, grad_neg, NT)
        from_neg = dot3(u_vec, grad_neg, NN)
        grad_cand = jnp.concatenate(
            [from_neg[:, :LANES] + grad_pos * u_vec, from_neg[:, LANES:]], axis=1
        )
        at = base + slot
        cols = slice(at * LANES, (at + 1) * LANES)
        wide = slice(at * total, (at + 1) * total)
        store_split(lhs_out, cols, conjugate_parts(grad_u, vec))
        store_split(rel_out, cols, conjugate_parts(grad_u, lhs))
        store_split(cand_out, wide, grad_cand)


def bucket_kernel(plan, *refs):
    bucket_grads(plan, refs[:1], *refs[1:], 0)


def last_kernel(plan, *refs):
    labels, refs = refs[: plan.buckets], refs[plan.buckets :]
    before, refs = refs[: 3 * (plan.buckets - 1)], refs[3 * (plan.buckets - 1) :]
    inputs, refs = refs[:4], refs[4:]
    away, rem_part, outs, table = refs[: len(plan.parts)], refs[-5], refs[-4:-1], refs[-1]
    base = (plan.buckets - 1) * plan.slots
    bucket_grads(plan, labels[-1:], *inputs, *outs, base)
    for at, ref in enumerate(before):
        wide = ref.shape[1]
        start = at // 3 * wide
        outs[at % 3][:, start : start + wide] = ref[...]
    lhs_grads, rel_grads, cand_grads = outs
    first = one_hot(plan.whole_row(labels, (1,)), plan.rems)
    second = one_hot(plan.whole_row(labels, (4, 6)), plan.rems)
    rem = folded(dot(lhs_grads[...], first, NT) + dot(cand_grads[...], second, NT))
    low, high = rem[:, : plan.half_rem], rem[:, plan.half_rem :]
    core = lax.axis_index("rel") & 1
    rem_part[...] = jnp.where(core == 0, low, high)
    table[:, plan.half_rel :] = jnp.where(core == 0, high, low)
    reduce_half(plan, True, labels, rel_grads, table, away)


def home_kernel(plan, *refs):
    count = plan.buckets
    outs, table = refs[-1 - len(plan.parts) : -1], refs[-1]
    table[:, plan.half_rel :] = refs[count + 1][...]
    reduce_half(plan, False, refs[:count], refs[count], table, outs)


def reduce_half(plan, away, labels, rel_grads, table, outs):
    me = plan.me()
    half = (me & 1) ^ (1 if away else 0)
    step = 2 * LANES if plan.half_rel % (2 * LANES) == 0 else LANES
    ids = plan.whole_row(labels, (2,)) - half * plan.half_rel
    for start in range(0, plan.half_rel, step):
        hot = one_hot(ids, step, start)
        table[:, start : start + step] = folded(dot(rel_grads[...], hot, NT))
    for chunk in range(plan.half_chunks):
        for which, (part, out) in enumerate(zip(plan.parts, outs)):
            value = jnp.concatenate(
                [
                    table[block[1] : block[1] + 8, block[0] : block[0] + LANES]
                    if block
                    else jnp.zeros((8, LANES), F32)
                    for block in plan.chunk_blocks(chunk, which)
                ],
                axis=0,
            )
            out[part.position(chunk, me)] = pack_table(value, part.rows) if away else value


def rows_sum(plan, ids, grads):
    shift = lax.axis_index("rel") * plan.part_lanes
    return folded(dot(grads, one_hot(ids ^ shift, plan.prows), NT))


def target_kernel(plan, *refs):
    count = plan.buckets
    ids = plan.whole_row(refs[:count], (3, 5))
    value = pack_table(rows_sum(plan, ids, refs[count][...]))
    for at, out in enumerate(refs[-2:]):
        lanes = out.shape[1]
        out[...] = value[:, at * lanes : (at + 1) * lanes]


def source_sum(plan, labels, grads):
    return rows_sum(plan, plan.row([labels], 0, (0,), 0, plan.slots), grads)


def deal(plan, value, keep, away):
    lanes = plan.part_lanes
    for at in range(value.shape[1] // lanes):
        share = value[:, at * lanes : (at + 1) * lanes]
        to = slice(at // 2 * lanes, (at // 2 + 1) * lanes)
        if at % 2:
            away[:, to] = pack_table(share)
        else:
            keep[:, to] = share


def source_kernel(plan, bucket, *refs):
    start = bucket * plan.bucket_edges
    grads = refs[1][:, start : start + plan.bucket_edges]
    deal(plan, source_sum(plan, refs[0], grads), *refs[-2:])


def own_source_kernel(plan, *refs):
    refs[-1][...] = source_sum(plan, refs[0], refs[1][:, : plan.bucket_edges])


def share(plan, count, *refs):
    source, fars, others = refs[0], refs[1:3], refs[3 : 3 + 2 * count]
    outs = refs[3 + 2 * count :]
    far = jnp.concatenate([unpack_table(ref[...]) for ref in fars], axis=1)
    deal(plan, source[...] + far, *outs[:2])
    for at in range(0, 2 * count, 2):
        deal_again(plan, *others[at : at + 2], *outs[at + 2 : at + 4])


def deal_again(plan, keep, came, *outs):
    deal(plan, keep[...] + unpack_table(came[...]), *outs)


def deal_and_settle(plan, count, *refs):
    ins, outs = refs[: 2 + 2 * count], refs[2 + 2 * count :]
    deal_again(plan, *ins[:2], *outs[:2])
    for at in range(count):
        add_kernel(2, *ins[2 + 2 * at : 4 + 2 * at], outs[2 + at])


def deal_kernel(plan, *refs):
    deal_again(plan, *refs)


def add_kernel(count, *refs):
    value = refs[0][...]
    for ref in refs[1:count]:
        value = value + unpack_table(ref[...])
    refs[-1][...] = pack_table(value)


def combine_kernel(plan, arrivals, sizes, beside, after, *refs):
    at, out_at = 0, sum(arrivals) + len(arrivals) + after
    if beside:
        step, ins, outs = beside
        step(plan, *refs[out_at : out_at + ins], *refs[len(refs) - outs :])
        out_at += ins
    for part, count, size in zip(plan.parts, arrivals, sizes):
        keep, arrived = refs[at], refs[at + 1 : at + 1 + count]
        outs = refs[out_at : out_at + size]
        at, out_at = at + 1 + count, out_at + size
        share = keep.shape[0] // size
        for place in range(keep.shape[0]):
            value = keep[place]
            for ref in arrived:
                value = value + unpack_table(ref[place], 8 * part.units)
            which, inner = divmod(place, share)
            packed = which or size == 1
            outs[which][inner] = pack_table(value, part.rows) if packed else value


def stack_kernel(plan, counts, *refs):
    outs = refs[-1 - len(counts) : -1]
    add = refs[sum(counts) : -1 - len(counts)]
    add_kernel(len(add), *add, refs[-1])
    first = 0
    for count, out in zip(counts, outs):
        for at in range(count):
            out[at] = refs[first + at][0]
        first += count


def spread_kernel(plan, counts, side, *refs):
    helds = refs[len(refs) - len(counts) :]
    rel_out, rem_out = refs[-2 - len(counts) : len(refs) - len(counts)]
    me = plan.me()
    first = 0
    for count, held in zip(counts, helds):
        at = 0
        for piece in refs[first : first + count]:
            held[at : at + piece.shape[0]] = piece[...]
            at += piece.shape[0]
        first += count
    for chunk in range(plan.half_chunks):
        for which, (part, held) in enumerate(zip(plan.parts, helds)):
            value = unpack_table(held[part.position(chunk, me)], 8 * part.units)
            for index, block in enumerate(plan.chunk_blocks(chunk, which)):
                if block is None:
                    break
                lane, sub = block
                rows = slice(sub, sub + 8)
                piece = value[8 * index : 8 * index + 8]
                if lane < plan.half_rel:
                    rel_out[rows, lane : lane + LANES] = piece
                else:
                    lane -= plan.half_rel
                    rem_out[rows, lane : lane + LANES] = piece


def part_out_kernel(plan, *refs):
    out = refs[-1]
    rel = lax.axis_index("rel")
    lanes = plan.part_lanes
    for mask, ref in enumerate(refs[: plan.rels]):
        if lanes % LANES:
            out[:, mask * lanes : (mask + 1) * lanes] = unpack_table(ref[...])
        else:
            start = pl.multiple_of((rel ^ mask) * lanes, lanes)
            out[:, pl.ds(start, lanes)] = unpack_table(ref[...])


def shape(extent, kind):
    return jax.ShapeDtypeStruct(extent, kind)


VMEM = pl.BlockSpec(memory_space=pltpu.VMEM)
ANY = pl.BlockSpec(memory_space=pl.ANY)


def call(kernel, outs, args, name, cost, limit, scratch=(), in_specs=None, out_specs=None, **more):
    work = pl.CostEstimate(flops=int(cost * 1e9), bytes_accessed=int(cost * 3e6), transcendentals=0)
    if "grid_spec" not in more:
        more["in_specs"] = in_specs or [VMEM] * len(args)
        more["out_specs"] = out_specs or [VMEM] * len(outs)
        more["scratch_shapes"] = list(scratch)
    return pl.pallas_call(
        kernel,
        out_shape=outs,
        compiler_params=pltpu.CompilerParams(vmem_limit_bytes=int(limit * 2**20)),
        cost_estimate=work,
        name=name,
        **more,
    )(*args)


def body(
    partitions,
    remainder,
    relations,
    counts,
    lhs_rows,
    lhs_rems,
    rel_ids,
    rhs_rows,
    rhs_rems,
    neg_rows,
    neg_rems,
):
    prows, width = partitions.shape
    plan = Plan(
        lax.axis_size("dom"),
        lax.axis_size("rel"),
        prows,
        width,
        remainder.shape[0],
        relations.shape[0],
        lhs_rows.shape[2],
    )
    smem = pl.BlockSpec(memory_space=pltpu.SMEM)
    own, rem, rels = partitions.T, remainder.T, relations.T
    edges, wide = plan.edges, plan.bucket_edges
    grow = max(1, edges // 1024)
    buckets = plan.buckets
    afar = lambda d: d ^ (plan.target_mask(d % plan.rels) * plan.rels)
    i16 = jnp.int16

    def exchanged(values, masks):
        return [
            send(value, plan, lambda d, m=mask: d ^ m) for value, mask in zip(values, masks[1:])
        ]

    def after(kernel, outs, args, others, name, cost, limit=12, **more):
        return call(
            kernel,
            outs,
            list(args) + list(others),
            name,
            cost,
            limit,
            in_specs=[VMEM] * len(args) + [ANY] * len(others),
            **more,
        )

    tables = [lhs_rows, lhs_rems, rel_ids, rhs_rows, rhs_rems, neg_rows, neg_rems]
    target = send(own, plan, afar)
    sources = [own] + [
        send(own, plan, lambda d, b=bucket: d ^ (b * plan.rels)) for bucket in range(1, buckets)
    ]
    lists = call(
        functools.partial(lists_kernel, plan),
        [shape((buckets * plan.maxb, 8, LANES), jnp.int32)] * plan.rels,
        tables + [counts.reshape(-1)],
        "lists",
        0.5,
        60,
        in_specs=[VMEM] * 7 + [smem],
    )
    lists = [lists[0]] + exchanged(lists[1:], range(plan.rels))
    (rel_split,) = call(
        split_kernel,
        [shape((2 * width, plan.nrels), BF16)],
        [rels],
        "rel_split",
        2.0,
        50,
        in_specs=[ANY],
        scratch=[
            pltpu.VMEM((width, plan.nrels), F32),
            pltpu.SemaphoreType.DMA((plan.nrels // (4 * LANES),)),
        ],
    )
    labels = call(
        functools.partial(forward_kernel, plan),
        [shape((plan.slots, 8, LANES), jnp.int32)] * buckets,
        lists,
        "forward",
        0.2,
        8,
    )
    labels = [labels[0]] + [
        send(labels[bucket], plan, lambda d, b=bucket: d ^ (b * plan.rels))
        for bucket in range(1, buckets)
    ]
    labels_of = lambda bucket: [labels[bucket]]
    grad_shapes = lambda count: [
        shape((2 * width, count), BF16),
        shape((2 * width, count), BF16),
        shape((2 * width, 2 * count), BF16),
    ]
    inputs = []
    for bucket in range(buckets):
        (vec,) = call(
            functools.partial(relation_kernel, plan),
            [shape((width, wide), F32)],
            labels_of(bucket) + [rel_split],
            "relation",
            2.0,
            16 * grow,
        )
        lhs, cand_rem = call(
            functools.partial(rows_kernel, plan),
            [shape((width, wide), F32), shape((width, 2 * wide), BF16)],
            labels_of(bucket) + [sources[bucket], rem],
            "rows",
            0.7,
            12 * grow,
        )
        inputs.append([lhs, vec, cand_rem])
    lanes = plan.part_lanes
    dealt = lambda count: [
        shape((width, count * lanes), F32),
        shape((width + 16, count * lanes), i16),
    ]
    grads = []
    for bucket in range(buckets - 1):
        grads += call(
            functools.partial(bucket_kernel, plan),
            grad_shapes(wide),
            labels_of(bucket) + [target] + inputs[bucket],
            "bucket",
            4.0,
            16 * grow,
        )
    table = [pltpu.VMEM((width, plan.half_lanes), F32)]
    made = call(
        functools.partial(last_kernel, plan),
        [shape(part.packed, i16) for part in plan.parts]
        + [shape((width, plan.half_rem), F32)]
        + grad_shapes(edges),
        labels + grads + [target] + inputs[-1],
        "last",
        9.0,
        20 * grow,
        scratch=table,
    )
    made, grads = list(made[:-3]), list(made[-3:])
    away, rem_part = made[:-1], made[-1]
    cores = [send(value, plan, lambda d: d ^ 1) for value in away]

    others, order = [], list(away)
    for bucket in range(1, buckets):
        keep, value = after(
            functools.partial(source_kernel, plan, bucket),
            dealt(plan.rels // 2),
            labels_of(bucket) + [grads[0]],
            order,
            "source",
            0.8,
            12 * grow,
        )
        others.append([keep, send(value, plan, lambda d: d ^ 1)])
        order = [keep]
    keeps = after(
        functools.partial(home_kernel, plan),
        [shape(part.bare, F32) for part in plan.parts],
        labels + [grads[1], rem_part],
        order,
        "home",
        3.0,
        16 * grow,
        scratch=table,
    )

    def combine(keeps, arrived, level, name, step=None, step_args=(), step_outs=(), order=()):
        sizes = [len(part.masks[level]) if level < 2 else 1 for part in plan.parts]
        outs, args = [], []
        for part, keep, pieces, size in zip(plan.parts, keeps, arrived, sizes):
            args += [keep] + pieces
            if level < 2:
                outs += part.shares(keep.shape[0], size)
            else:
                outs.append(shape((1,) + part.packed[1:], i16))
        beside = (step, len(step_args), len(step_outs)) if step else None
        count = [len(pieces) for pieces in arrived]
        made = after(
            functools.partial(combine_kernel, plan, count, sizes, beside, len(order)),
            outs + list(step_outs),
            args + list(step_args),
            order,
            name,
            0.6,
        )
        made, beside = made[: len(outs)], made[len(outs) :]
        if level == 2:
            return made, [], beside
        keeps, arrived = [], []
        for part, size in zip(plan.parts, sizes):
            group, made = made[:size], made[size:]
            keeps.append(group[0])
            arrived.append(exchanged(group[1:], part.masks[level]))
        return keeps, arrived, beside

    keeps, arrived, _ = combine(
        keeps, [[core] for core in cores], 0, "combine_cores", order=[other[1] for other in others]
    )
    far = after(
        functools.partial(target_kernel, plan),
        [shape((width + 16, prows // 2), i16)] * 2,
        labels + [grads[2]],
        [keeps[0]],
        "target",
        1.8,
        16 * grow,
    )
    (source,) = after(
        functools.partial(own_source_kernel, plan),
        [shape((width, prows), F32)],
        labels_of(0) + [grads[0]],
        [far[0]],
        "own_source",
        0.8,
        16 * grow,
    )
    far = [send(value, plan, afar) for value in far]
    def deal_on(pairs, count, bit):
        while count > 2:
            count, bit = count // 2, bit * 2
            made = [
                after(functools.partial(deal_kernel, plan), dealt(count), pair, [], "deal", 0.3)
                for pair in pairs
            ]
            pairs = [[keep, send(value, plan, lambda d, m=bit: d ^ m)] for keep, value in made]
        return pairs, count // 2, bit * 2

    others, count, bit = deal_on(others, plan.rels // 2, 1)
    keeps, arrived, made = combine(
        keeps,
        arrived,
        1,
        "combine_first",
        lambda plan, *refs: share(plan, len(others), *refs),
        [source] + far + sum(others, []),
        dealt(plan.rels // 2) + dealt(count) * len(others),
    )
    mine = [[made[0], send(made[1], plan, lambda d: d ^ 1)]]
    others = [
        [made[at], send(made[at + 1], plan, lambda d: d ^ bit)] for at in range(2, len(made), 2)
    ]
    (mine,), count, bit = deal_on(mine, plan.rels // 2, 1)
    totals, _, made = combine(
        keeps,
        arrived,
        2,
        "combine_last",
        lambda plan, *refs: deal_and_settle(plan, len(others), *refs),
        mine + sum(others, []),
        dealt(count) + [shape((width + 16, lanes), i16)] * len(others),
    )
    mine, came = made[0], send(made[1], plan, lambda d: d ^ bit)
    crossing = exchanged(made[2:], range(0, plan.rels * buckets, plan.rels))
    pieces = [
        [total] + exchanged([total] * (len(part.masks[1]) - 1), part.masks[1])
        for part, total in zip(plan.parts, totals)
    ]
    flat = sum(pieces, [])
    made = after(
        functools.partial(stack_kernel, plan, [len(group) for group in pieces]),
        [
            shape((len(group),) + part.packed[1:], i16)
            for part, group in zip(plan.parts, pieces)
        ]
        + [shape((width + 16, lanes), i16)],
        flat + [mine, came] + crossing,
        [],
        "stack",
        0.5,
    )
    blocks, owners = made[:-1], {0: made[-1]}
    def gathered(block, masks):
        if len(masks) != 4:
            return [block] + exchanged([block] * (len(masks) - 1), masks)
        half = block.shape[0] // 2
        first, second = exchanged([block] * 2, masks[:3])
        over_first = send(first[:half], plan, lambda d: d ^ masks[2])
        over_second = send(second[half:], plan, lambda d: d ^ masks[1])
        return [block, first, second, over_first, over_second]

    pieces = [gathered(block, part.masks[0]) for part, block in zip(plan.parts, blocks)]
    while bit:
        for mask in sorted(owners):
            owners[mask | bit] = send(owners[mask], plan, lambda d, m=bit: d ^ m)
        bit //= 2
    (grad_partitions,) = after(
        functools.partial(part_out_kernel, plan),
        [shape((width, prows), F32)],
        [owners[mask] for mask in range(plan.rels)],
        [],
        "part_out",
        1.0,
    )
    if lanes % LANES:
        order = jnp.arange(plan.rels) ^ lax.axis_index("rel")
        split_lanes = grad_partitions.reshape(width, plan.rels, lanes)
        grad_partitions = jnp.take(split_lanes, order, axis=1).reshape(width, prows)

    crossed = [[send(piece, plan, lambda d: d ^ 1) for piece in group] for group in pieces]
    side = lax.axis_index("rel") & 1
    outs = [shape((width, plan.nrels), F32), shape((width, plan.rems), F32)]
    spec = lambda lanes: pl.BlockSpec((width, lanes), lambda i, half: (0, half[0]))
    made = []
    for turn, groups in enumerate([pieces, crossed]):
        flat = sum(groups, [])
        made = call(
            functools.partial(spread_kernel, plan, [len(group) for group in groups]),
            outs,
            [(side ^ turn).reshape(1), *flat, *made],
            "spread",
            2.0,
            16,
            grid_spec=pltpu.PrefetchScalarGridSpec(
                num_scalar_prefetch=1,
                grid=(1,),
                in_specs=[VMEM] * len(flat) + [ANY] * len(made),
                out_specs=[spec(plan.half_rel), spec(plan.half_rem)],
                scratch_shapes=[pltpu.VMEM(part.packed, i16) for part in plan.parts],
            ),
            input_output_aliases={1 + len(flat) + at: at for at in range(len(made))},
        )
    grad_relations, grad_remainder = made
    return grad_partitions.T, grad_remainder.T, grad_relations.T


def solution(mesh):
    edge = P("dom", None, "rel", None)
    in_specs = (P("dom", None), P(), P(), P("dom", None, "rel")) + (edge,) * 7
    out_specs = (P("dom", None), P(), P())
    return jax.shard_map(body, mesh=mesh, in_specs=in_specs, out_specs=out_specs, check_vma=False)
```

```python
import functools

import jax
import jax.numpy as jnp
from jax import lax
from jax.experimental import pallas as pl
from jax.experimental.pallas import tpu as pltpu
from jax.sharding import PartitionSpec as P

F32 = jnp.float32
BF16 = jnp.bfloat16
LANES = 128
REACH = 32766.0
NT = (((1,), (1,)), ((), ()))
NN = (((1,), (0,)), ((), ()))
TN = (((0,), (0,)), ((), ()))


def bits_of(count):
    return count.bit_length() - 1


def reverse_bits(value, count):
    out = 0
    for bit in range(bits_of(count)):
        out = out * 2 + ((value >> bit) & 1)
    return out


def split(value):
    high = value.astype(BF16)
    low = (value - high.astype(F32)).astype(BF16)
    return high, low


def dot(left, right, dims):
    return lax.dot_general(left, right, dims, preferred_element_type=F32)


def dot3(left, right, dims):
    left_high, left_low = split(left)
    right_high, right_low = split(right)
    return (
        dot(left_high, right_high, dims)
        + dot(left_high, right_low, dims)
        + dot(left_low, right_high, dims)
    )


def one_hot(ids, rows, base=0):
    place = lax.broadcasted_iota(jnp.int32, (rows, ids.shape[1]), 0)
    return jnp.where(place == ids - base, 1.0, 0.0).astype(BF16)


def store_split(ref, cols, value):
    high, low = split(value)
    depth = value.shape[0]
    ref[0:depth, cols] = high
    ref[depth : 2 * depth, cols] = low


def folded(value):
    depth = value.shape[0] // 2
    return value[:depth] + value[depth:]


def quantized(value):
    top = jnp.max(jnp.abs(value), axis=0, keepdims=True)
    exponent = jnp.floor(jnp.log2(jnp.maximum(top, 1e-30))) + 1.0
    return jnp.round(value * (REACH * jnp.exp2(-exponent))), exponent


def scale_of(exponent):
    return jnp.exp2(exponent) * (1.0 / REACH)


def to_words(value):
    return value.astype(jnp.int32).astype(jnp.int16)


def from_words(words):
    return words.astype(jnp.int32).astype(F32)


def pack_table(value, rows=None):
    scaled, exponent = quantized(value)
    spare = (rows or value.shape[0] + 16) - value.shape[0]
    tail = jnp.broadcast_to(exponent, (spare, value.shape[1]))
    return to_words(jnp.concatenate([scaled, tail], axis=0))


def unpack_table(words, depth=None):
    depth = depth or words.shape[0] - 16
    value = from_words(words)
    return value[:depth] * scale_of(value[depth : depth + 1])


class Part:
    def __init__(self, plan, units, groups):
        self.units = units
        self.rows = (units + 2) // 2 * 16
        self.masks = [self.group_masks(bits) for bits in groups]
        order = [bit for group in groups for bit in reversed(group)]
        self.place = {bit: len(order) - 1 - at for at, bit in enumerate(order)}
        self.packed = (plan.half_chunks, self.rows, LANES)
        self.bare = (plan.half_chunks, 8 * units, LANES)

    @staticmethod
    def group_masks(bits):
        masks = []
        for index in range(2 ** len(bits)):
            masks.append(sum(((index >> at) & 1) << bit for at, bit in enumerate(bits)))
        return masks

    def position(self, chunk, me):
        relative = chunk ^ (me >> 1)
        out = 0
        for bit, at in self.place.items():
            out = out + (((relative >> (bit - 1)) & 1) << at)
        return out

    def shares(self, count, size):
        count = count // size
        return [shape((count,) + self.bare[1:], F32)] + [
            shape((count,) + self.packed[1:], jnp.int16)
        ] * (size - 1)


class Plan:
    def __init__(self, doms, rels, prows, width, rems, nrels, maxb):
        self.doms, self.rels, self.maxb = doms, rels, maxb
        self.devices = doms * rels
        self.prows, self.width, self.rems, self.nrels = prows, width, rems, nrels
        self.buckets = doms // rels
        self.slots = rels * maxb
        self.bucket_edges = self.slots * LANES
        self.edges = self.buckets * self.bucket_edges
        self.part_lanes = prows // rels
        self.half_rel, self.half_rem = nrels // 2, rems // 2
        self.half_lanes = self.half_rel + self.half_rem
        self.subs = width // 8
        self.units = (self.half_lanes // LANES) * self.subs
        self.half_chunks = self.devices // 2
        self.chunk_units = -(-self.units // self.half_chunks)
        rel_bits = bits_of(rels)
        all_bits = rel_bits + bits_of(doms)
        near = list(range(1, rel_bits + 1))
        far = list(range(rel_bits + 1, all_bits))
        self.parts = [Part(self, self.chunk_units, [near, far])]

    def chunk_blocks(self, chunk, part):
        first = chunk * self.chunk_units + (self.parts[0].units if part else 0)
        blocks = []
        for unit in range(first, first + self.parts[part].units):
            lane, sub = divmod(unit, self.subs)
            blocks.append((lane * LANES, 8 * sub) if unit < self.units else None)
        return blocks

    def row(self, labels, bucket, kinds, first, count):
        rows = []
        for slot in range(first, first + count):
            rows += [labels[bucket][slot, kind : kind + 1, :] for kind in kinds]
        return jnp.concatenate(rows, axis=1) if len(rows) > 1 else rows[0]

    def whole_row(self, labels, kinds):
        rows = [
            self.row(labels, bucket, kinds, 0, self.slots) for bucket in range(self.buckets)
        ]
        return jnp.concatenate(rows, axis=1) if len(rows) > 1 else rows[0]

    def me(self):
        return lax.axis_index("dom") * self.rels + lax.axis_index("rel")

    def target_mask(self, rel):
        return reverse_bits(rel, self.rels) * self.buckets

    def dynamic_mask(self, rel):
        out = 0
        width = bits_of(self.rels)
        for bit in range(width):
            out = out + (((rel >> bit) & 1) << (width - 1 - bit))
        return out * self.buckets


def send(value, plan, target):
    pairs = [(device, target(device)) for device in range(plan.devices)]
    return lax.ppermute(value, ("dom", "rel"), pairs)


def lists_kernel(plan, *refs):
    tables, counts, outs = refs[:7], refs[7], refs[8:]
    source = lax.axis_index("dom")
    rel = lax.axis_index("rel")
    for mask, out in enumerate(outs):
        for bucket in range(plan.buckets):
            target = source ^ bucket ^ plan.dynamic_mask(rel ^ mask)
            stop = lax.rem(source - target + plan.doms, plan.doms)
            for turn in range(plan.maxb):
                at = bucket * plan.maxb + turn
                for kind, table in enumerate(tables):
                    out[at, kind : kind + 1, :] = table[0, stop, turn : turn + 1, :]
                live = jnp.where(turn < counts[stop], 1, 0)
                out[at, 7:8, :] = jnp.full((1, LANES), live, jnp.int32)


def forward_kernel(plan, *refs):
    lists, outs = refs[: plan.rels], refs[plan.rels :]
    for bucket, out in enumerate(outs):
        for mask, ref in enumerate(lists):
            for turn in range(plan.maxb):
                out[mask * plan.maxb + turn] = ref[bucket * plan.maxb + turn]


def split_kernel(relations, out, held, sems):
    depth, total = relations.shape
    step = 4 * LANES
    loads = [
        pltpu.make_async_copy(
            relations.at[:, start : start + step], held.at[:, start : start + step], sems.at[at]
        )
        for at, start in enumerate(range(0, total, step))
    ]
    for load in loads:
        load.start()
    for at, load in enumerate(loads):
        load.wait()
        cols = slice(at * step, (at + 1) * step)
        high, low = split(held[:, cols])
        out[0:depth, cols] = high
        out[depth : 2 * depth, cols] = low


def relation_kernel(plan, *refs):
    labels, relations, out = refs[:1], refs[1], refs[-1]
    for pair in range(0, plan.slots, 2):
        count = min(2, plan.slots - pair)
        start = pair * LANES
        ids = plan.row(labels, 0, (2,), pair, count)
        out[:, start : start + count * LANES] = folded(
            dot(relations[...], one_hot(ids, plan.nrels), NN)
        )


def rows_kernel(plan, *refs):
    labels, (own, rem) = refs[:1], refs[1:3]
    lhs_out, rem_out = refs[-2:]
    for pair in range(0, plan.slots, 2):
        count = min(2, plan.slots - pair)
        row = lambda *kinds: plan.row(labels, 0, kinds, pair, count)
        start = pair * LANES
        end = start + count * LANES
        lhs_out[:, start:end] = dot(own[...], one_hot(row(0), plan.prows), NN) + dot(
            rem[...], one_hot(row(1), plan.rems), NN
        )
        rem_out[:, 2 * start : 2 * end] = dot(
            rem[...], one_hot(row(4, 6), plan.rems), NN
        ).astype(BF16)


def conjugate_parts(grad, other):
    half = grad.shape[0] // 2
    grad_re, grad_im = grad[:half], grad[half:]
    other_re, other_im = other[:half], other[half:]
    return jnp.concatenate(
        [grad_re * other_re + grad_im * other_im, grad_im * other_re - grad_re * other_im], 0
    )


def complex_product(left, right):
    half = left.shape[0] // 2
    left_re, left_im = left[:half], left[half:]
    right_re, right_im = right[:half], right[half:]
    return jnp.concatenate(
        [left_re * right_re - left_im * right_im, left_re * right_im + left_im * right_re], 0
    )


def bucket_grads(plan, labels, target, lhs_in, rel_in, rem_in, lhs_out, rel_out, cand_out, base):
    total = 2 * LANES
    edge = lax.broadcasted_iota(jnp.int32, (LANES, total), 0)
    column = lax.broadcasted_iota(jnp.int32, (LANES, total), 1)
    keep = jnp.where(edge == column, 0.0, 1.0 / total)
    for slot in range(plan.slots):
        cols = slice(slot * LANES, (slot + 1) * LANES)
        wide = slice(slot * total, (slot + 1) * total)
        ids = plan.row(labels, 0, (3, 5), slot, 1)
        cand = dot(target[...], one_hot(ids, plan.prows), NN) + rem_in[:, wide].astype(F32)
        rhs = cand[:, :LANES]
        lhs, vec = lhs_in[:, cols], rel_in[:, cols]
        u_vec = complex_product(lhs, vec)
        live = plan.row(labels, 0, (7,), slot, 1).astype(F32)
        positive = jnp.sum(u_vec * rhs, axis=0, keepdims=True)
        negative = dot3(u_vec, cand, TN)
        grad_pos = -jax.nn.sigmoid(-positive) * live
        grad_neg = jax.nn.sigmoid(negative) * keep * live[0:1, 0:1]
        grad_u = grad_pos * rhs + dot3(cand, grad_neg, NT)
        from_neg = dot3(u_vec, grad_neg, NN)
        grad_cand = jnp.concatenate(
            [from_neg[:, :LANES] + grad_pos * u_vec, from_neg[:, LANES:]], axis=1
        )
        at = base + slot
        cols = slice(at * LANES, (at + 1) * LANES)
        wide = slice(at * total, (at + 1) * total)
        store_split(lhs_out, cols, conjugate_parts(grad_u, vec))
        store_split(rel_out, cols, conjugate_parts(grad_u, lhs))
        store_split(cand_out, wide, grad_cand)


def bucket_kernel(plan, *refs):
    bucket_grads(plan, refs[:1], *refs[1:], 0)


def last_kernel(plan, *refs):
    labels, refs = refs[: plan.buckets], refs[plan.buckets :]
    before, refs = refs[: 3 * (plan.buckets - 1)], refs[3 * (plan.buckets - 1) :]
    inputs, refs = refs[:4], refs[4:]
    away, rem_part, outs, table = refs[: len(plan.parts)], refs[-5], refs[-4:-1], refs[-1]
    base = (plan.buckets - 1) * plan.slots
    bucket_grads(plan, labels[-1:], *inputs, *outs, base)
    for at, ref in enumerate(before):
        wide = ref.shape[1]
        start = at // 3 * wide
        outs[at % 3][:, start : start + wide] = ref[...]
    lhs_grads, rel_grads, cand_grads = outs
    first = one_hot(plan.whole_row(labels, (1,)), plan.rems)
    second = one_hot(plan.whole_row(labels, (4, 6)), plan.rems)
    rem = folded(dot(lhs_grads[...], first, NT) + dot(cand_grads[...], second, NT))
    low, high = rem[:, : plan.half_rem], rem[:, plan.half_rem :]
    core = lax.axis_index("rel") & 1
    rem_part[...] = jnp.where(core == 0, low, high)
    table[:, plan.half_rel :] = jnp.where(core == 0, high, low)
    reduce_half(plan, True, labels, rel_grads, table, away)


def home_kernel(plan, *refs):
    count = plan.buckets
    outs, table = refs[-1 - len(plan.parts) : -1], refs[-1]
    table[:, plan.half_rel :] = refs[count + 1][...]
    reduce_half(plan, False, refs[:count], refs[count], table, outs)


def reduce_half(plan, away, labels, rel_grads, table, outs):
    me = plan.me()
    half = (me & 1) ^ (1 if away else 0)
    step = 2 * LANES if plan.half_rel % (2 * LANES) == 0 else LANES
    ids = plan.whole_row(labels, (2,)) - half * plan.half_rel
    for start in range(0, plan.half_rel, step):
        hot = one_hot(ids, step, start)
        table[:, start : start + step] = folded(dot(rel_grads[...], hot, NT))
    for chunk in range(plan.half_chunks):
        for which, (part, out) in enumerate(zip(plan.parts, outs)):
            value = jnp.concatenate(
                [
                    table[block[1] : block[1] + 8, block[0] : block[0] + LANES]
                    if block
                    else jnp.zeros((8, LANES), F32)
                    for block in plan.chunk_blocks(chunk, which)
                ],
                axis=0,
            )
            out[part.position(chunk, me)] = pack_table(value, part.rows) if away else value


def rows_sum(plan, ids, grads):
    shift = lax.axis_index("rel") * plan.part_lanes
    return folded(dot(grads, one_hot(ids ^ shift, plan.prows), NT))


def target_kernel(plan, *refs):
    count = plan.buckets
    ids = plan.whole_row(refs[:count], (3, 5))
    value = pack_table(rows_sum(plan, ids, refs[count][...]))
    for at, out in enumerate(refs[-2:]):
        lanes = out.shape[1]
        out[...] = value[:, at * lanes : (at + 1) * lanes]


def source_sum(plan, labels, grads):
    return rows_sum(plan, plan.row([labels], 0, (0,), 0, plan.slots), grads)


def deal(plan, value, keep, away):
    lanes = plan.part_lanes
    for at in range(value.shape[1] // lanes):
        share = value[:, at * lanes : (at + 1) * lanes]
        to = slice(at // 2 * lanes, (at // 2 + 1) * lanes)
        if at % 2:
            away[:, to] = pack_table(share)
        else:
            keep[:, to] = share


def source_kernel(plan, bucket, *refs):
    start = bucket * plan.bucket_edges
    grads = refs[1][:, start : start + plan.bucket_edges]
    deal(plan, source_sum(plan, refs[0], grads), *refs[-2:])


def own_source_kernel(plan, *refs):
    refs[-1][...] = source_sum(plan, refs[0], refs[1][:, : plan.bucket_edges])


def share(plan, count, *refs):
    source, fars, others = refs[0], refs[1:3], refs[3 : 3 + 2 * count]
    outs = refs[3 + 2 * count :]
    far = jnp.concatenate([unpack_table(ref[...]) for ref in fars], axis=1)
    deal(plan, source[...] + far, *outs[:2])
    for at in range(0, 2 * count, 2):
        deal_again(plan, *others[at : at + 2], *outs[at + 2 : at + 4])


def deal_again(plan, keep, came, *outs):
    deal(plan, keep[...] + unpack_table(came[...]), *outs)


def deal_and_settle(plan, count, *refs):
    ins, outs = refs[: 2 + 2 * count], refs[2 + 2 * count :]
    deal_again(plan, *ins[:2], *outs[:2])
    for at in range(count):
        add_kernel(2, *ins[2 + 2 * at : 4 + 2 * at], outs[2 + at])


def deal_kernel(plan, *refs):
    deal_again(plan, *refs)


def add_kernel(count, *refs):
    value = refs[0][...]
    for ref in refs[1:count]:
        value = value + unpack_table(ref[...])
    refs[-1][...] = pack_table(value)


def combine_kernel(plan, arrivals, sizes, beside, after, *refs):
    at, out_at = 0, sum(arrivals) + len(arrivals) + after
    if beside:
        step, ins, outs = beside
        step(plan, *refs[out_at : out_at + ins], *refs[len(refs) - outs :])
        out_at += ins
    for part, count, size in zip(plan.parts, arrivals, sizes):
        keep, arrived = refs[at], refs[at + 1 : at + 1 + count]
        outs = refs[out_at : out_at + size]
        at, out_at = at + 1 + count, out_at + size
        share = keep.shape[0] // size
        for place in range(keep.shape[0]):
            value = keep[place]
            for ref in arrived:
                value = value + unpack_table(ref[place], 8 * part.units)
            which, inner = divmod(place, share)
            packed = which or size == 1
            outs[which][inner] = pack_table(value, part.rows) if packed else value


def stack_kernel(plan, counts, *refs):
    outs = refs[-1 - len(counts) : -1]
    add = refs[sum(counts) : -1 - len(counts)]
    add_kernel(len(add), *add, refs[-1])
    first = 0
    for count, out in zip(counts, outs):
        for at in range(count):
            out[at] = refs[first + at][0]
        first += count


def spread_kernel(plan, counts, other, *refs):
    scratch = len(counts) + 2
    helds, table, sems = refs[len(refs) - scratch : -2], refs[-2], refs[-1]
    rel_out, rem_out = refs[-2 - scratch : len(refs) - scratch]
    me = plan.me()
    half = (me & 1) ^ other
    first = 0
    for count, held in zip(counts, helds):
        at = 0
        for piece in refs[first : first + count]:
            held[at : at + piece.shape[0]] = piece[...]
            at += piece.shape[0]
        first += count
    stores = []
    for chunk in range(plan.half_chunks):
        for which, (part, held) in enumerate(zip(plan.parts, helds)):
            value = unpack_table(held[part.position(chunk, me)], 8 * part.units)
            for index, block in enumerate(plan.chunk_blocks(chunk, which)):
                if block is None:
                    break
                lane, sub = block
                table[sub : sub + 8, lane : lane + LANES] = value[8 * index : 8 * index + 8]
        whole = min((chunk + 1) * plan.chunk_units, plan.units) // plan.subs
        for block in range(len(stores), whole):
            lane = block * LANES
            if lane < plan.half_rel:
                out, start = rel_out, half * plan.half_rel + lane
            else:
                out, start = rem_out, half * plan.half_rem + lane - plan.half_rel
            stores.append(
                pltpu.make_async_copy(
                    table.at[:, lane : lane + LANES],
                    out.at[:, pl.ds(pl.multiple_of(start, LANES), LANES)],
                    sems.at[block],
                )
            )
            stores[-1].start()
    for store in stores:
        store.wait()


def part_out_kernel(plan, *refs):
    out = refs[-1]
    rel = lax.axis_index("rel")
    lanes = plan.part_lanes
    for mask, ref in enumerate(refs[: plan.rels]):
        if lanes % LANES:
            out[:, mask * lanes : (mask + 1) * lanes] = unpack_table(ref[...])
        else:
            start = pl.multiple_of((rel ^ mask) * lanes, lanes)
            out[:, pl.ds(start, lanes)] = unpack_table(ref[...])


def shape(extent, kind):
    return jax.ShapeDtypeStruct(extent, kind)


VMEM = pl.BlockSpec(memory_space=pltpu.VMEM)
ANY = pl.BlockSpec(memory_space=pl.ANY)


def call(kernel, outs, args, name, cost, limit, scratch=(), in_specs=None, out_specs=None, **more):
    work = pl.CostEstimate(flops=int(cost * 1e9), bytes_accessed=int(cost * 3e6), transcendentals=0)
    return pl.pallas_call(
        kernel,
        out_shape=outs,
        in_specs=in_specs or [VMEM] * len(args),
        out_specs=out_specs or [VMEM] * len(outs),
        scratch_shapes=list(scratch),
        compiler_params=pltpu.CompilerParams(vmem_limit_bytes=int(limit * 2**20)),
        cost_estimate=work,
        name=name,
        **more,
    )(*args)


def body(
    partitions,
    remainder,
    relations,
    counts,
    lhs_rows,
    lhs_rems,
    rel_ids,
    rhs_rows,
    rhs_rems,
    neg_rows,
    neg_rems,
):
    prows, width = partitions.shape
    plan = Plan(
        lax.axis_size("dom"),
        lax.axis_size("rel"),
        prows,
        width,
        remainder.shape[0],
        relations.shape[0],
        lhs_rows.shape[2],
    )
    smem = pl.BlockSpec(memory_space=pltpu.SMEM)
    own, rem, rels = partitions.T, remainder.T, relations.T
    edges, wide = plan.edges, plan.bucket_edges
    grow = max(1, edges // 1024)
    buckets = plan.buckets
    afar = lambda d: d ^ (plan.target_mask(d % plan.rels) * plan.rels)
    i16 = jnp.int16

    def exchanged(values, masks):
        return [
            send(value, plan, lambda d, m=mask: d ^ m) for value, mask in zip(values, masks[1:])
        ]

    def after(kernel, outs, args, others, name, cost, limit=12, **more):
        return call(
            kernel,
            outs,
            list(args) + list(others),
            name,
            cost,
            limit,
            in_specs=[VMEM] * len(args) + [ANY] * len(others),
            **more,
        )

    tables = [lhs_rows, lhs_rems, rel_ids, rhs_rows, rhs_rems, neg_rows, neg_rems]
    target = send(own, plan, afar)
    sources = [own] + [
        send(own, plan, lambda d, b=bucket: d ^ (b * plan.rels)) for bucket in range(1, buckets)
    ]
    lists = call(
        functools.partial(lists_kernel, plan),
        [shape((buckets * plan.maxb, 8, LANES), jnp.int32)] * plan.rels,
        tables + [counts.reshape(-1)],
        "lists",
        0.5,
        60,
        in_specs=[VMEM] * 7 + [smem],
    )
    lists = [lists[0]] + exchanged(lists[1:], range(plan.rels))
    (rel_split,) = call(
        split_kernel,
        [shape((2 * width, plan.nrels), BF16)],
        [rels],
        "rel_split",
        2.0,
        50,
        in_specs=[ANY],
        scratch=[
            pltpu.VMEM((width, plan.nrels), F32),
            pltpu.SemaphoreType.DMA((plan.nrels // (4 * LANES),)),
        ],
    )
    labels = call(
        functools.partial(forward_kernel, plan),
        [shape((plan.slots, 8, LANES), jnp.int32)] * buckets,
        lists,
        "forward",
        0.2,
        8,
    )
    labels = [labels[0]] + [
        send(labels[bucket], plan, lambda d, b=bucket: d ^ (b * plan.rels))
        for bucket in range(1, buckets)
    ]
    labels_of = lambda bucket: [labels[bucket]]
    grad_shapes = lambda count: [
        shape((2 * width, count), BF16),
        shape((2 * width, count), BF16),
        shape((2 * width, 2 * count), BF16),
    ]
    inputs = []
    for bucket in range(buckets):
        (vec,) = call(
            functools.partial(relation_kernel, plan),
            [shape((width, wide), F32)],
            labels_of(bucket) + [rel_split],
            "relation",
            2.0,
            16 * grow,
        )
        lhs, cand_rem = call(
            functools.partial(rows_kernel, plan),
            [shape((width, wide), F32), shape((width, 2 * wide), BF16)],
            labels_of(bucket) + [sources[bucket], rem],
            "rows",
            0.7,
            12 * grow,
        )
        inputs.append([lhs, vec, cand_rem])
    lanes = plan.part_lanes
    dealt = lambda count: [
        shape((width, count * lanes), F32),
        shape((width + 16, count * lanes), i16),
    ]
    grads = []
    for bucket in range(buckets - 1):
        grads += call(
            functools.partial(bucket_kernel, plan),
            grad_shapes(wide),
            labels_of(bucket) + [target] + inputs[bucket],
            "bucket",
            4.0,
            16 * grow,
        )
    table = [pltpu.VMEM((width, plan.half_lanes), F32)]
    made = call(
        functools.partial(last_kernel, plan),
        [shape(part.packed, i16) for part in plan.parts]
        + [shape((width, plan.half_rem), F32)]
        + grad_shapes(edges),
        labels + grads + [target] + inputs[-1],
        "last",
        9.0,
        20 * grow,
        scratch=table,
    )
    made, grads = list(made[:-3]), list(made[-3:])
    away, rem_part = made[:-1], made[-1]
    cores = [send(value, plan, lambda d: d ^ 1) for value in away]

    others, order = [], list(away)
    for bucket in range(1, buckets):
        keep, value = after(
            functools.partial(source_kernel, plan, bucket),
            dealt(plan.rels // 2),
            labels_of(bucket) + [grads[0]],
            order,
            "source",
            0.8,
            12 * grow,
        )
        others.append([keep, send(value, plan, lambda d: d ^ 1)])
        order = [keep]
    keeps = after(
        functools.partial(home_kernel, plan),
        [shape(part.bare, F32) for part in plan.parts],
        labels + [grads[1], rem_part],
        order,
        "home",
        3.0,
        16 * grow,
        scratch=table,
    )

    def combine(keeps, arrived, level, name, step=None, step_args=(), step_outs=(), order=()):
        sizes = [len(part.masks[level]) if level < 2 else 1 for part in plan.parts]
        outs, args = [], []
        for part, keep, pieces, size in zip(plan.parts, keeps, arrived, sizes):
            args += [keep] + pieces
            if level < 2:
                outs += part.shares(keep.shape[0], size)
            else:
                outs.append(shape((1,) + part.packed[1:], i16))
        beside = (step, len(step_args), len(step_outs)) if step else None
        count = [len(pieces) for pieces in arrived]
        made = after(
            functools.partial(combine_kernel, plan, count, sizes, beside, len(order)),
            outs + list(step_outs),
            args + list(step_args),
            order,
            name,
            0.6,
        )
        made, beside = made[: len(outs)], made[len(outs) :]
        if level == 2:
            return made, [], beside
        keeps, arrived = [], []
        for part, size in zip(plan.parts, sizes):
            group, made = made[:size], made[size:]
            keeps.append(group[0])
            arrived.append(exchanged(group[1:], part.masks[level]))
        return keeps, arrived, beside

    keeps, arrived, _ = combine(
        keeps, [[core] for core in cores], 0, "combine_cores", order=[other[1] for other in others]
    )
    far = after(
        functools.partial(target_kernel, plan),
        [shape((width + 16, prows // 2), i16)] * 2,
        labels + [grads[2]],
        [keeps[0]],
        "target",
        1.8,
        16 * grow,
    )
    (source,) = after(
        functools.partial(own_source_kernel, plan),
        [shape((width, prows), F32)],
        labels_of(0) + [grads[0]],
        [far[0]],
        "own_source",
        0.8,
        16 * grow,
    )
    far = [send(value, plan, afar) for value in far]
    def deal_on(pairs, count, bit):
        while count > 2:
            count, bit = count // 2, bit * 2
            made = [
                after(functools.partial(deal_kernel, plan), dealt(count), pair, [], "deal", 0.3)
                for pair in pairs
            ]
            pairs = [[keep, send(value, plan, lambda d, m=bit: d ^ m)] for keep, value in made]
        return pairs, count // 2, bit * 2

    others, count, bit = deal_on(others, plan.rels // 2, 1)
    keeps, arrived, made = combine(
        keeps,
        arrived,
        1,
        "combine_first",
        lambda plan, *refs: share(plan, len(others), *refs),
        [source] + far + sum(others, []),
        dealt(plan.rels // 2) + dealt(count) * len(others),
    )
    mine = [[made[0], send(made[1], plan, lambda d: d ^ 1)]]
    others = [
        [made[at], send(made[at + 1], plan, lambda d: d ^ bit)] for at in range(2, len(made), 2)
    ]
    (mine,), count, bit = deal_on(mine, plan.rels // 2, 1)
    totals, _, made = combine(
        keeps,
        arrived,
        2,
        "combine_last",
        lambda plan, *refs: deal_and_settle(plan, len(others), *refs),
        mine + sum(others, []),
        dealt(count) + [shape((width + 16, lanes), i16)] * len(others),
    )
    mine, came = made[0], send(made[1], plan, lambda d: d ^ bit)
    crossing = exchanged(made[2:], range(0, plan.rels * buckets, plan.rels))
    pieces = [
        [total] + exchanged([total] * (len(part.masks[1]) - 1), part.masks[1])
        for part, total in zip(plan.parts, totals)
    ]
    flat = sum(pieces, [])
    made = after(
        functools.partial(stack_kernel, plan, [len(group) for group in pieces]),
        [
            shape((len(group),) + part.packed[1:], i16)
            for part, group in zip(plan.parts, pieces)
        ]
        + [shape((width + 16, lanes), i16)],
        flat + [mine, came] + crossing,
        [],
        "stack",
        0.5,
    )
    blocks, owners = made[:-1], {0: made[-1]}
    def gathered(block, masks):
        if len(masks) != 4:
            return [block] + exchanged([block] * (len(masks) - 1), masks)
        half = block.shape[0] // 2
        first, second = exchanged([block] * 2, masks[:3])
        over_first = send(first[:half], plan, lambda d: d ^ masks[2])
        over_second = send(second[half:], plan, lambda d: d ^ masks[1])
        return [block, first, second, over_first, over_second]

    pieces = [gathered(block, part.masks[0]) for part, block in zip(plan.parts, blocks)]
    while bit:
        for mask in sorted(owners):
            owners[mask | bit] = send(owners[mask], plan, lambda d, m=bit: d ^ m)
        bit //= 2
    (grad_partitions,) = after(
        functools.partial(part_out_kernel, plan),
        [shape((width, prows), F32)],
        [owners[mask] for mask in range(plan.rels)],
        [],
        "part_out",
        1.0,
    )
    if lanes % LANES:
        order = jnp.arange(plan.rels) ^ lax.axis_index("rel")
        split_lanes = grad_partitions.reshape(width, plan.rels, lanes)
        grad_partitions = jnp.take(split_lanes, order, axis=1).reshape(width, prows)

    crossed = [[send(piece, plan, lambda d: d ^ 1) for piece in group] for group in pieces]
    outs = [shape((width, plan.nrels), F32), shape((width, plan.rems), F32)]
    made = []
    for turn, groups in enumerate([pieces, crossed]):
        flat = sum(groups, [])
        made = after(
            functools.partial(spread_kernel, plan, [len(group) for group in groups], turn),
            outs,
            flat,
            made,
            "spread",
            2.0,
            16,
            out_specs=[ANY] * 2,
            scratch=[pltpu.VMEM(part.packed, i16) for part in plan.parts]
            + [
                pltpu.VMEM((width, plan.half_lanes), F32),
                pltpu.SemaphoreType.DMA((plan.half_lanes // LANES,)),
            ],
            input_output_aliases={len(flat) + at: at for at in range(len(made))},
        )
    grad_relations, grad_remainder = made
    return grad_partitions.T, grad_remainder.T, grad_relations.T


def solution(mesh):
    edge = P("dom", None, "rel", None)
    in_specs = (P("dom", None), P(), P(), P("dom", None, "rel")) + (edge,) * 7
    out_specs = (P("dom", None), P(), P())
    return jax.shard_map(body, mesh=mesh, in_specs=in_specs, out_specs=out_specs, check_vma=False)
```

```python
import functools

import jax
import jax.numpy as jnp
from jax import lax
from jax.experimental import pallas as pl
from jax.experimental.pallas import tpu as pltpu
from jax.sharding import PartitionSpec as P

F32 = jnp.float32
BF16 = jnp.bfloat16
LANES = 128
REACH = 32766.0
NT = (((1,), (1,)), ((), ()))
NN = (((1,), (0,)), ((), ()))
TN = (((0,), (0,)), ((), ()))


def bits_of(count):
    return count.bit_length() - 1


def reverse_bits(value, count):
    out = 0
    for bit in range(bits_of(count)):
        out = out * 2 + ((value >> bit) & 1)
    return out


def split(value):
    high = value.astype(BF16)
    low = (value - high.astype(F32)).astype(BF16)
    return high, low


def dot(left, right, dims):
    return lax.dot_general(left, right, dims, preferred_element_type=F32)


def dot3(left, right, dims):
    left_high, left_low = split(left)
    right_high, right_low = split(right)
    return (
        dot(left_high, right_high, dims)
        + dot(left_high, right_low, dims)
        + dot(left_low, right_high, dims)
    )


def one_hot(ids, rows, base=0):
    place = lax.broadcasted_iota(jnp.int32, (rows, ids.shape[1]), 0)
    return jnp.where(place == ids - base, 1.0, 0.0).astype(BF16)


def store_split(ref, cols, value):
    high, low = split(value)
    depth = value.shape[0]
    ref[0:depth, cols] = high
    ref[depth : 2 * depth, cols] = low


def folded(value):
    depth = value.shape[0] // 2
    return value[:depth] + value[depth:]


def quantized(value):
    top = jnp.max(jnp.abs(value), axis=0, keepdims=True)
    exponent = jnp.floor(jnp.log2(jnp.maximum(top, 1e-30))) + 1.0
    return jnp.round(value * (REACH * jnp.exp2(-exponent))), exponent


def scale_of(exponent):
    return jnp.exp2(exponent) * (1.0 / REACH)


def to_words(value):
    return value.astype(jnp.int32).astype(jnp.int16)


def from_words(words):
    return words.astype(jnp.int32).astype(F32)


def pack_table(value, rows=None):
    scaled, exponent = quantized(value)
    spare = (rows or value.shape[0] + 16) - value.shape[0]
    tail = jnp.broadcast_to(exponent, (spare, value.shape[1]))
    return to_words(jnp.concatenate([scaled, tail], axis=0))


def unpack_table(words, depth=None):
    depth = depth or words.shape[0] - 16
    value = from_words(words)
    return value[:depth] * scale_of(value[depth : depth + 1])


class Part:
    def __init__(self, plan, units, groups):
        self.units = units
        self.rows = (units + 2) // 2 * 16
        self.masks = [self.group_masks(bits) for bits in groups]
        order = [bit for group in groups for bit in reversed(group)]
        self.place = {bit: len(order) - 1 - at for at, bit in enumerate(order)}
        self.packed = (plan.half_chunks, self.rows, LANES)
        self.bare = (plan.half_chunks, 8 * units, LANES)

    @staticmethod
    def group_masks(bits):
        masks = []
        for index in range(2 ** len(bits)):
            masks.append(sum(((index >> at) & 1) << bit for at, bit in enumerate(bits)))
        return masks

    def position(self, chunk, me):
        relative = chunk ^ (me >> 1)
        out = 0
        for bit, at in self.place.items():
            out = out + (((relative >> (bit - 1)) & 1) << at)
        return out

    def shares(self, count, size):
        count = count // size
        return [shape((count,) + self.bare[1:], F32)] + [
            shape((count,) + self.packed[1:], jnp.int16)
        ] * (size - 1)


class Plan:
    def __init__(self, doms, rels, prows, width, rems, nrels, maxb):
        self.doms, self.rels, self.maxb = doms, rels, maxb
        self.devices = doms * rels
        self.prows, self.width, self.rems, self.nrels = prows, width, rems, nrels
        self.buckets = doms // rels
        self.slots = rels * maxb
        self.bucket_edges = self.slots * LANES
        self.edges = self.buckets * self.bucket_edges
        self.part_lanes = prows // rels
        self.half_rel, self.half_rem = nrels // 2, rems // 2
        self.half_lanes = self.half_rel + self.half_rem
        self.subs = width // 8
        self.units = (self.half_lanes // LANES) * self.subs
        self.half_chunks = self.devices // 2
        self.chunk_units = -(-self.units // self.half_chunks)
        rel_bits = bits_of(rels)
        all_bits = rel_bits + bits_of(doms)
        near = list(range(1, rel_bits + 1))
        far = list(range(rel_bits + 1, all_bits))
        self.parts = [Part(self, self.chunk_units, [near, far])]

    def chunk_blocks(self, chunk, part):
        first = chunk * self.chunk_units + (self.parts[0].units if part else 0)
        blocks = []
        for unit in range(first, first + self.parts[part].units):
            lane, sub = divmod(unit, self.subs)
            blocks.append((lane * LANES, 8 * sub) if unit < self.units else None)
        return blocks

    def row(self, labels, bucket, kinds, first, count):
        rows = []
        for slot in range(first, first + count):
            rows += [labels[bucket][slot, kind : kind + 1, :] for kind in kinds]
        return jnp.concatenate(rows, axis=1) if len(rows) > 1 else rows[0]

    def whole_row(self, labels, kinds):
        rows = [
            self.row(labels, bucket, kinds, 0, self.slots) for bucket in range(self.buckets)
        ]
        return jnp.concatenate(rows, axis=1) if len(rows) > 1 else rows[0]

    def me(self):
        return lax.axis_index("dom") * self.rels + lax.axis_index("rel")

    def target_mask(self, rel):
        return reverse_bits(rel, self.rels) * self.buckets

    def dynamic_mask(self, rel):
        out = 0
        width = bits_of(self.rels)
        for bit in range(width):
            out = out + (((rel >> bit) & 1) << (width - 1 - bit))
        return out * self.buckets


def send(value, plan, target):
    pairs = [(device, target(device)) for device in range(plan.devices)]
    return lax.ppermute(value, ("dom", "rel"), pairs)


def lists_kernel(plan, *refs):
    tables, counts, outs = refs[:7], refs[7], refs[8:]
    source = lax.axis_index("dom")
    rel = lax.axis_index("rel")
    for mask, out in enumerate(outs):
        for bucket in range(plan.buckets):
            target = source ^ bucket ^ plan.dynamic_mask(rel ^ mask)
            stop = lax.rem(source - target + plan.doms, plan.doms)
            for turn in range(plan.maxb):
                at = bucket * plan.maxb + turn
                for kind, table in enumerate(tables):
                    out[at, kind : kind + 1, :] = table[0, stop, turn : turn + 1, :]
                live = jnp.where(turn < counts[stop], 1, 0)
                out[at, 7:8, :] = jnp.full((1, LANES), live, jnp.int32)


def forward_kernel(plan, *refs):
    lists, outs = refs[: plan.rels], refs[plan.rels :]
    for bucket, out in enumerate(outs):
        for mask, ref in enumerate(lists):
            for turn in range(plan.maxb):
                out[mask * plan.maxb + turn] = ref[bucket * plan.maxb + turn]


def split_kernel(relations, out, held, sems):
    depth, total = relations.shape
    step = 4 * LANES
    loads = [
        pltpu.make_async_copy(
            relations.at[:, start : start + step], held.at[:, start : start + step], sems.at[at]
        )
        for at, start in enumerate(range(0, total, step))
    ]
    for load in loads:
        load.start()
    for at, load in enumerate(loads):
        load.wait()
        cols = slice(at * step, (at + 1) * step)
        high, low = split(held[:, cols])
        out[0:depth, cols] = high
        out[depth : 2 * depth, cols] = low


def relation_kernel(plan, *refs):
    labels, relations, out = refs[:1], refs[1], refs[-1]
    for pair in range(0, plan.slots, 2):
        count = min(2, plan.slots - pair)
        start = pair * LANES
        ids = plan.row(labels, 0, (2,), pair, count)
        out[:, start : start + count * LANES] = folded(
            dot(relations[...], one_hot(ids, plan.nrels), NN)
        )


def rows_kernel(plan, *refs):
    labels, (own, rem) = refs[:1], refs[1:3]
    lhs_out, rem_out = refs[-2:]
    for pair in range(0, plan.slots, 2):
        count = min(2, plan.slots - pair)
        row = lambda *kinds: plan.row(labels, 0, kinds, pair, count)
        start = pair * LANES
        end = start + count * LANES
        lhs_out[:, start:end] = dot(own[...], one_hot(row(0), plan.prows), NN) + dot(
            rem[...], one_hot(row(1), plan.rems), NN
        )
        rem_out[:, 2 * start : 2 * end] = dot(
            rem[...], one_hot(row(4, 6), plan.rems), NN
        ).astype(BF16)


def conjugate_parts(grad, other):
    half = grad.shape[0] // 2
    grad_re, grad_im = grad[:half], grad[half:]
    other_re, other_im = other[:half], other[half:]
    return jnp.concatenate(
        [grad_re * other_re + grad_im * other_im, grad_im * other_re - grad_re * other_im], 0
    )


def complex_product(left, right):
    half = left.shape[0] // 2
    left_re, left_im = left[:half], left[half:]
    right_re, right_im = right[:half], right[half:]
    return jnp.concatenate(
        [left_re * right_re - left_im * right_im, left_re * right_im + left_im * right_re], 0
    )


def bucket_grads(plan, labels, target, lhs_in, rel_in, rem_in, lhs_out, rel_out, cand_out, base):
    total = 2 * LANES
    edge = lax.broadcasted_iota(jnp.int32, (LANES, total), 0)
    column = lax.broadcasted_iota(jnp.int32, (LANES, total), 1)
    keep = jnp.where(edge == column, 0.0, 1.0 / total)
    for slot in range(plan.slots):
        cols = slice(slot * LANES, (slot + 1) * LANES)
        wide = slice(slot * total, (slot + 1) * total)
        ids = plan.row(labels, 0, (3, 5), slot, 1)
        cand = dot(target[...], one_hot(ids, plan.prows), NN) + rem_in[:, wide].astype(F32)
        rhs = cand[:, :LANES]
        lhs, vec = lhs_in[:, cols], rel_in[:, cols]
        u_vec = complex_product(lhs, vec)
        live = plan.row(labels, 0, (7,), slot, 1).astype(F32)
        positive = jnp.sum(u_vec * rhs, axis=0, keepdims=True)
        negative = dot3(u_vec, cand, TN)
        grad_pos = -jax.nn.sigmoid(-positive) * live
        grad_neg = jax.nn.sigmoid(negative) * keep * live[0:1, 0:1]
        grad_u = grad_pos * rhs + dot3(cand, grad_neg, NT)
        from_neg = dot3(u_vec, grad_neg, NN)
        grad_cand = jnp.concatenate(
            [from_neg[:, :LANES] + grad_pos * u_vec, from_neg[:, LANES:]], axis=1
        )
        at = base + slot
        cols = slice(at * LANES, (at + 1) * LANES)
        wide = slice(at * total, (at + 1) * total)
        store_split(lhs_out, cols, conjugate_parts(grad_u, vec))
        store_split(rel_out, cols, conjugate_parts(grad_u, lhs))
        store_split(cand_out, wide, grad_cand)


def bucket_kernel(plan, *refs):
    bucket_grads(plan, refs[:1], *refs[1:], 0)


def last_kernel(plan, *refs):
    labels, refs = refs[: plan.buckets], refs[plan.buckets :]
    before, refs = refs[: 3 * (plan.buckets - 1)], refs[3 * (plan.buckets - 1) :]
    inputs, refs = refs[:4], refs[4:]
    away, rem_part, outs, table = refs[: len(plan.parts)], refs[-5], refs[-4:-1], refs[-1]
    base = (plan.buckets - 1) * plan.slots
    bucket_grads(plan, labels[-1:], *inputs, *outs, base)
    for at, ref in enumerate(before):
        wide = ref.shape[1]
        start = at // 3 * wide
        outs[at % 3][:, start : start + wide] = ref[...]
    lhs_grads, rel_grads, cand_grads = outs
    first = one_hot(plan.whole_row(labels, (1,)), plan.rems)
    second = one_hot(plan.whole_row(labels, (4, 6)), plan.rems)
    rem = folded(dot(lhs_grads[...], first, NT) + dot(cand_grads[...], second, NT))
    low, high = rem[:, : plan.half_rem], rem[:, plan.half_rem :]
    core = lax.axis_index("rel") & 1
    rem_part[...] = jnp.where(core == 0, low, high)
    table[:, plan.half_rel :] = jnp.where(core == 0, high, low)
    reduce_half(plan, True, labels, rel_grads, table, away)


def home_kernel(plan, *refs):
    count = plan.buckets
    outs, table = refs[-1 - len(plan.parts) : -1], refs[-1]
    table[:, plan.half_rel :] = refs[count + 1][...]
    reduce_half(plan, False, refs[:count], refs[count], table, outs)


def reduce_half(plan, away, labels, rel_grads, table, outs):
    me = plan.me()
    half = (me & 1) ^ (1 if away else 0)
    step = 2 * LANES if plan.half_rel % (2 * LANES) == 0 else LANES
    ids = plan.whole_row(labels, (2,)) - half * plan.half_rel
    for start in range(0, plan.half_rel, step):
        hot = one_hot(ids, step, start)
        table[:, start : start + step] = folded(dot(rel_grads[...], hot, NT))
    for chunk in range(plan.half_chunks):
        for which, (part, out) in enumerate(zip(plan.parts, outs)):
            value = jnp.concatenate(
                [
                    table[block[1] : block[1] + 8, block[0] : block[0] + LANES]
                    if block
                    else jnp.zeros((8, LANES), F32)
                    for block in plan.chunk_blocks(chunk, which)
                ],
                axis=0,
            )
            out[part.position(chunk, me)] = pack_table(value, part.rows) if away else value


def rows_sum(plan, ids, grads):
    shift = lax.axis_index("rel") * plan.part_lanes
    return folded(dot(grads, one_hot(ids ^ shift, plan.prows), NT))


def target_kernel(plan, *refs):
    count = plan.buckets
    ids = plan.whole_row(refs[:count], (3, 5))
    value = pack_table(rows_sum(plan, ids, refs[count][...]))
    for at, out in enumerate(refs[-2:]):
        lanes = out.shape[1]
        out[...] = value[:, at * lanes : (at + 1) * lanes]


def source_sum(plan, labels, grads):
    return rows_sum(plan, plan.row([labels], 0, (0,), 0, plan.slots), grads)


def deal(plan, value, keep, away):
    lanes = plan.part_lanes
    for at in range(value.shape[1] // lanes):
        share = value[:, at * lanes : (at + 1) * lanes]
        to = slice(at // 2 * lanes, (at // 2 + 1) * lanes)
        if at % 2:
            away[:, to] = pack_table(share)
        else:
            keep[:, to] = share


def source_kernel(plan, bucket, *refs):
    start = bucket * plan.bucket_edges
    grads = refs[1][:, start : start + plan.bucket_edges]
    deal(plan, source_sum(plan, refs[0], grads), *refs[-2:])


def own_source_kernel(plan, *refs):
    refs[-1][...] = source_sum(plan, refs[0], refs[1][:, : plan.bucket_edges])


def share(plan, count, *refs):
    source, fars, others = refs[0], refs[1:3], refs[3 : 3 + 2 * count]
    outs = refs[3 + 2 * count :]
    far = jnp.concatenate([unpack_table(ref[...]) for ref in fars], axis=1)
    deal(plan, source[...] + far, *outs[:2])
    for at in range(0, 2 * count, 2):
        deal_again(plan, *others[at : at + 2], *outs[at + 2 : at + 4])


def deal_again(plan, keep, came, *outs):
    deal(plan, keep[...] + unpack_table(came[...]), *outs)


def deal_and_settle(plan, count, *refs):
    ins, outs = refs[: 2 + 2 * count], refs[2 + 2 * count :]
    deal_again(plan, *ins[:2], *outs[:2])
    for at in range(count):
        add_kernel(2, *ins[2 + 2 * at : 4 + 2 * at], outs[2 + at])


def deal_kernel(plan, *refs):
    deal_again(plan, *refs)


def add_kernel(count, *refs):
    value = refs[0][...]
    for ref in refs[1:count]:
        value = value + unpack_table(ref[...])
    refs[-1][...] = pack_table(value)


def combine_kernel(plan, arrivals, sizes, beside, after, *refs):
    at, out_at = 0, sum(arrivals) + len(arrivals) + after
    if beside:
        step, ins, outs = beside
        step(plan, *refs[out_at : out_at + ins], *refs[len(refs) - outs :])
        out_at += ins
    for part, count, size in zip(plan.parts, arrivals, sizes):
        keep, arrived = refs[at], refs[at + 1 : at + 1 + count]
        outs = refs[out_at : out_at + size]
        at, out_at = at + 1 + count, out_at + size
        share = keep.shape[0] // size
        for place in range(keep.shape[0]):
            value = keep[place]
            for ref in arrived:
                value = value + unpack_table(ref[place], 8 * part.units)
            which, inner = divmod(place, share)
            packed = which or size == 1
            outs[which][inner] = pack_table(value, part.rows) if packed else value


def stack_kernel(plan, counts, *refs):
    outs = refs[-1 - len(counts) : -1]
    add = refs[sum(counts) : -1 - len(counts)]
    add_kernel(len(add), *add, refs[-1])
    first = 0
    for count, out in zip(counts, outs):
        for at in range(count):
            out[at] = refs[first + at][0]
        first += count


def spread_kernel(plan, counts, other, *refs):
    scratch = len(counts) + 2
    helds, table, sems = refs[len(refs) - scratch : -2], refs[-2], refs[-1]
    rel_out, rem_out = refs[-2 - scratch : len(refs) - scratch]
    me = plan.me()
    half = (me & 1) ^ other
    first = 0
    for count, held in zip(counts, helds):
        at = 0
        for piece in refs[first : first + count]:
            held[at : at + piece.shape[0]] = piece[...]
            at += piece.shape[0]
        first += count
    stores = []
    for chunk in range(plan.half_chunks):
        for which, (part, held) in enumerate(zip(plan.parts, helds)):
            value = unpack_table(held[part.position(chunk, me)], 8 * part.units)
            for index, block in enumerate(plan.chunk_blocks(chunk, which)):
                if block is None:
                    break
                lane, sub = block
                table[sub : sub + 8, lane : lane + LANES] = value[8 * index : 8 * index + 8]
        whole = min((chunk + 1) * plan.chunk_units, plan.units) // plan.subs
        for block in range(len(stores), whole):
            lane = block * LANES
            if lane < plan.half_rel:
                out, start = rel_out, half * plan.half_rel + lane
            else:
                out, start = rem_out, half * plan.half_rem + lane - plan.half_rel
            stores.append(
                pltpu.make_async_copy(
                    table.at[:, lane : lane + LANES],
                    out.at[:, pl.ds(pl.multiple_of(start, LANES), LANES)],
                    sems.at[block],
                )
            )
            stores[-1].start()
    for store in stores:
        store.wait()


def part_out_kernel(plan, *refs):
    out = refs[-1]
    rel = lax.axis_index("rel")
    lanes = plan.part_lanes
    for mask, ref in enumerate(refs[: plan.rels]):
        if lanes % LANES:
            out[:, mask * lanes : (mask + 1) * lanes] = unpack_table(ref[...])
        else:
            start = pl.multiple_of((rel ^ mask) * lanes, lanes)
            out[:, pl.ds(start, lanes)] = unpack_table(ref[...])


def shape(extent, kind):
    return jax.ShapeDtypeStruct(extent, kind)


VMEM = pl.BlockSpec(memory_space=pltpu.VMEM)
ANY = pl.BlockSpec(memory_space=pl.ANY)


def call(kernel, outs, args, name, cost, limit, scratch=(), in_specs=None, out_specs=None, **more):
    work = pl.CostEstimate(flops=int(cost * 1e9), bytes_accessed=int(cost * 3e6), transcendentals=0)
    return pl.pallas_call(
        kernel,
        out_shape=outs,
        in_specs=in_specs or [VMEM] * len(args),
        out_specs=out_specs or [VMEM] * len(outs),
        scratch_shapes=list(scratch),
        compiler_params=pltpu.CompilerParams(vmem_limit_bytes=int(limit * 2**20)),
        cost_estimate=work,
        name=name,
        **more,
    )(*args)


def body(
    partitions,
    remainder,
    relations,
    counts,
    lhs_rows,
    lhs_rems,
    rel_ids,
    rhs_rows,
    rhs_rems,
    neg_rows,
    neg_rems,
):
    prows, width = partitions.shape
    plan = Plan(
        lax.axis_size("dom"),
        lax.axis_size("rel"),
        prows,
        width,
        remainder.shape[0],
        relations.shape[0],
        lhs_rows.shape[2],
    )
    smem = pl.BlockSpec(memory_space=pltpu.SMEM)
    own, rem, rels = partitions.T, remainder.T, relations.T
    edges, wide = plan.edges, plan.bucket_edges
    grow = max(1, edges // 1024)
    buckets = plan.buckets
    afar = lambda d: d ^ (plan.target_mask(d % plan.rels) * plan.rels)
    i16 = jnp.int16

    def exchanged(values, masks):
        return [
            send(value, plan, lambda d, m=mask: d ^ m) for value, mask in zip(values, masks[1:])
        ]

    def after(kernel, outs, args, others, name, cost, limit=12, **more):
        return call(
            kernel,
            outs,
            list(args) + list(others),
            name,
            cost,
            limit,
            in_specs=[VMEM] * len(args) + [ANY] * len(others),
            **more,
        )

    tables = [lhs_rows, lhs_rems, rel_ids, rhs_rows, rhs_rems, neg_rows, neg_rems]
    target = send(own, plan, afar)
    sources = [own] + [
        send(own, plan, lambda d, b=bucket: d ^ (b * plan.rels)) for bucket in range(1, buckets)
    ]
    lists = call(
        functools.partial(lists_kernel, plan),
        [shape((buckets * plan.maxb, 8, LANES), jnp.int32)] * plan.rels,
        tables + [counts.reshape(-1)],
        "lists",
        0.5,
        60,
        in_specs=[VMEM] * 7 + [smem],
    )
    lists = [lists[0]] + exchanged(lists[1:], range(plan.rels))
    (rel_split,) = call(
        split_kernel,
        [shape((2 * width, plan.nrels), BF16)],
        [rels],
        "rel_split",
        2.0,
        50,
        in_specs=[ANY],
        scratch=[
            pltpu.VMEM((width, plan.nrels), F32),
            pltpu.SemaphoreType.DMA((plan.nrels // (4 * LANES),)),
        ],
    )
    labels = call(
        functools.partial(forward_kernel, plan),
        [shape((plan.slots, 8, LANES), jnp.int32)] * buckets,
        lists,
        "forward",
        0.2,
        8,
    )
    labels = [labels[0]] + [
        send(labels[bucket], plan, lambda d, b=bucket: d ^ (b * plan.rels))
        for bucket in range(1, buckets)
    ]
    labels_of = lambda bucket: [labels[bucket]]
    grad_shapes = lambda count: [
        shape((2 * width, count), BF16),
        shape((2 * width, count), BF16),
        shape((2 * width, 2 * count), BF16),
    ]
    inputs = []
    for bucket in range(buckets):
        (vec,) = call(
            functools.partial(relation_kernel, plan),
            [shape((width, wide), F32)],
            labels_of(bucket) + [rel_split],
            "relation",
            2.0,
            16 * grow,
        )
        lhs, cand_rem = call(
            functools.partial(rows_kernel, plan),
            [shape((width, wide), F32), shape((width, 2 * wide), BF16)],
            labels_of(bucket) + [sources[bucket], rem],
            "rows",
            0.7,
            12 * grow,
        )
        inputs.append([lhs, vec, cand_rem])
    lanes = plan.part_lanes
    dealt = lambda count: [
        shape((width, count * lanes), F32),
        shape((width + 16, count * lanes), i16),
    ]
    grads = []
    for bucket in range(buckets - 1):
        grads += call(
            functools.partial(bucket_kernel, plan),
            grad_shapes(wide),
            labels_of(bucket) + [target] + inputs[bucket],
            "bucket",
            4.0,
            16 * grow,
        )
    table = [pltpu.VMEM((width, plan.half_lanes), F32)]
    made = call(
        functools.partial(last_kernel, plan),
        [shape(part.packed, i16) for part in plan.parts]
        + [shape((width, plan.half_rem), F32)]
        + grad_shapes(edges),
        labels + grads + [target] + inputs[-1],
        "last",
        9.0,
        20 * grow,
        scratch=table,
    )
    made, grads = list(made[:-3]), list(made[-3:])
    away, rem_part = made[:-1], made[-1]
    cores = [send(value, plan, lambda d: d ^ 1) for value in away]

    others, order = [], list(away)
    for bucket in range(1, buckets):
        keep, value = after(
            functools.partial(source_kernel, plan, bucket),
            dealt(plan.rels // 2),
            labels_of(bucket) + [grads[0]],
            order,
            "source",
            0.8,
            12 * grow,
        )
        others.append([keep, send(value, plan, lambda d: d ^ 1)])
        order = [keep]
    keeps = after(
        functools.partial(home_kernel, plan),
        [shape(part.bare, F32) for part in plan.parts],
        labels + [grads[1], rem_part],
        order,
        "home",
        3.0,
        16 * grow,
        scratch=table,
    )

    def combine(keeps, arrived, level, name, step=None, step_args=(), step_outs=(), order=()):
        sizes = [len(part.masks[level]) if level < 2 else 1 for part in plan.parts]
        outs, args = [], []
        for part, keep, pieces, size in zip(plan.parts, keeps, arrived, sizes):
            args += [keep] + pieces
            if level < 2:
                outs += part.shares(keep.shape[0], size)
            else:
                outs.append(shape((1,) + part.packed[1:], i16))
        beside = (step, len(step_args), len(step_outs)) if step else None
        count = [len(pieces) for pieces in arrived]
        made = after(
            functools.partial(combine_kernel, plan, count, sizes, beside, len(order)),
            outs + list(step_outs),
            args + list(step_args),
            order,
            name,
            0.6,
        )
        made, beside = made[: len(outs)], made[len(outs) :]
        if level == 2:
            return made, [], beside
        keeps, arrived = [], []
        for part, size in zip(plan.parts, sizes):
            group, made = made[:size], made[size:]
            keeps.append(group[0])
            arrived.append(exchanged(group[1:], part.masks[level]))
        return keeps, arrived, beside

    keeps, arrived, _ = combine(
        keeps, [[core] for core in cores], 0, "combine_cores", order=[other[1] for other in others]
    )
    far = after(
        functools.partial(target_kernel, plan),
        [shape((width + 16, prows // 2), i16)] * 2,
        labels + [grads[2]],
        [keeps[0]],
        "target",
        1.8,
        16 * grow,
    )
    (source,) = after(
        functools.partial(own_source_kernel, plan),
        [shape((width, prows), F32)],
        labels_of(0) + [grads[0]],
        [far[0]],
        "own_source",
        0.8,
        16 * grow,
    )
    far = [send(value, plan, afar) for value in far]
    def deal_on(pairs, count, bit):
        while count > 2:
            count, bit = count // 2, bit * 2
            made = [
                after(functools.partial(deal_kernel, plan), dealt(count), pair, [], "deal", 0.3)
                for pair in pairs
            ]
            pairs = [[keep, send(value, plan, lambda d, m=bit: d ^ m)] for keep, value in made]
        return pairs, count // 2, bit * 2

    others, count, bit = deal_on(others, plan.rels // 2, 1)
    keeps, arrived, made = combine(
        keeps,
        arrived,
        1,
        "combine_first",
        lambda plan, *refs: share(plan, len(others), *refs),
        [source] + far + sum(others, []),
        dealt(plan.rels // 2) + dealt(count) * len(others),
    )
    mine = [[made[0], send(made[1], plan, lambda d: d ^ 1)]]
    others = [
        [made[at], send(made[at + 1], plan, lambda d: d ^ bit)] for at in range(2, len(made), 2)
    ]
    (mine,), count, bit = deal_on(mine, plan.rels // 2, 1)
    totals, _, made = combine(
        keeps,
        arrived,
        2,
        "combine_last",
        lambda plan, *refs: deal_and_settle(plan, len(others), *refs),
        mine + sum(others, []),
        dealt(count) + [shape((width + 16, lanes), i16)] * len(others),
    )
    mine, came = made[0], send(made[1], plan, lambda d: d ^ bit)
    crossing = exchanged(made[2:], range(0, plan.rels * buckets, plan.rels))
    pieces = [
        [total] + exchanged([total] * (len(part.masks[1]) - 1), part.masks[1])
        for part, total in zip(plan.parts, totals)
    ]
    flat = sum(pieces, [])
    made = after(
        functools.partial(stack_kernel, plan, [len(group) for group in pieces]),
        [
            shape((len(group),) + part.packed[1:], i16)
            for part, group in zip(plan.parts, pieces)
        ]
        + [shape((width + 16, lanes), i16)],
        flat + [mine, came] + crossing,
        [],
        "stack",
        0.5,
    )
    blocks, owners = made[:-1], {0: made[-1]}
    def gathered(block, masks):
        if len(masks) != 4:
            return [block] + exchanged([block] * (len(masks) - 1), masks)
        half = block.shape[0] // 2
        second = send(block, plan, lambda d: d ^ masks[2])
        first = send(block, plan, lambda d: d ^ masks[1])
        over_first = send(first[:half], plan, lambda d: d ^ masks[2])
        over_second = send(second[half:], plan, lambda d: d ^ masks[1])
        return [block, first, second, over_first, over_second]

    pieces = [gathered(block, part.masks[0]) for part, block in zip(plan.parts, blocks)]
    while bit:
        for mask in sorted(owners):
            owners[mask | bit] = send(owners[mask], plan, lambda d, m=bit: d ^ m)
        bit //= 2
    (grad_partitions,) = after(
        functools.partial(part_out_kernel, plan),
        [shape((width, prows), F32)],
        [owners[mask] for mask in range(plan.rels)],
        [],
        "part_out",
        1.0,
    )
    if lanes % LANES:
        order = jnp.arange(plan.rels) ^ lax.axis_index("rel")
        split_lanes = grad_partitions.reshape(width, plan.rels, lanes)
        grad_partitions = jnp.take(split_lanes, order, axis=1).reshape(width, prows)

    crossed = [[send(piece, plan, lambda d: d ^ 1) for piece in group] for group in pieces]
    outs = [shape((width, plan.nrels), F32), shape((width, plan.rems), F32)]
    made = []
    for turn, groups in enumerate([pieces, crossed]):
        flat = sum(groups, [])
        made = after(
            functools.partial(spread_kernel, plan, [len(group) for group in groups], turn),
            outs,
            flat,
            made,
            "spread",
            2.0,
            16,
            out_specs=[ANY] * 2,
            scratch=[pltpu.VMEM(part.packed, i16) for part in plan.parts]
            + [
                pltpu.VMEM((width, plan.half_lanes), F32),
                pltpu.SemaphoreType.DMA((plan.half_lanes // LANES,)),
            ],
            input_output_aliases={len(flat) + at: at for at in range(len(made))},
        )
    grad_relations, grad_remainder = made
    return grad_partitions.T, grad_remainder.T, grad_relations.T


def solution(mesh):
    edge = P("dom", None, "rel", None)
    in_specs = (P("dom", None), P(), P(), P("dom", None, "rel")) + (edge,) * 7
    out_specs = (P("dom", None), P(), P())
    return jax.shard_map(body, mesh=mesh, in_specs=in_specs, out_specs=out_specs, check_vma=False)
```
